32 devices in a mesh: members: 2 (over y), tiles: 4 (over z), rows: 2 (over x), lev: 2 (over core).
Axes of the slice: x: 2, y: 2, z: 4, core: 2. Of those that a mesh axis runs over, the one named last changes fastest.
Arguments:
- air_state: float32 [64, 48, 1536], P(('members', 'lev'), 'rows', 'tiles'), parts along dimension 0, may hold values from -6 to 6
- wind_east: float32 [64, 48, 1536], P(('members', 'lev'), 'rows', 'tiles'), parts along dimension 0, may hold values from -0.4 to 0.4
- wind_north: float32 [64, 48, 1536], P(('members', 'lev'), 'rows', 'tiles'), parts along dimension 0, may hold values from -0.4 to 0.4
- feedback_weight: float32 [32], P('lev'), may hold values from 0.2 to 1
- nest_west: int32 [4], P('members'), parts along dimension 0, may hold values from 1 to 1023
- nest_south: int32 [4], P('members'), parts along dimension 0, may hold values from 1 to 31
Outputs:
- new_state: float32 [64, 48, 1536], P(('members', 'lev'), 'rows', 'tiles'), parts along dimension 0
The draws below stay inside these ranges and needn't reach their ends.
There are 2 independent parts, one for each index of `members`. The reference program is written for one: setup_inputs(seed, part) draws one part's arguments, and reference() takes and returns one part's arrays. A program takes and returns all parts, laid end to end along the dimension named above; an argument that names none is the same for every part. Nothing has to cross between parts.
Inputs may be any that keep to these rules, and one draw needn't show every extreme that they name: `nest_west`: the nest's footprint with one cell of margin lies inside the parent grid in both substeps.
All inputs are finite; a program needn't handle non-finite values.
Results may differ from the reference program's by a relative error of at most 0.000086.
Values sent between devices are 32-bit elements; how exact they have to be, the bound alone decides.
No kernel may reach another device: no remote copies, remote signals or barrier semaphores. Data moves between devices by JAX's collectives and lax.ppermute only.
A program may use at most 64 MiB of HBM per device.

```python
import math
import jax
import jax.numpy as jnp
from jax import lax

LEV = 32
NXALL = 1536
PX = 1152
NXN = 384
FX = 128
NY = 48
FY = 16


def block_levels(own_key, dims, cuts, least, top_value):
    loudness = 1.0
    for axis_at, shards_of in cuts:
        steps = jax.random.uniform(jax.random.fold_in(jax.random.fold_in(own_key, 6), axis_at), (shards_of,), jnp.float32, least / len(cuts), top_value / len(cuts))
        loudness = loudness * jnp.repeat(jnp.exp(steps), dims[axis_at] // shards_of).reshape((-1,) + (1,) * (len(dims) - 1 - axis_at))
    return loudness


def normal_values(key, dims, deviation, limit, cuts=(), kind=jnp.bfloat16):
    gain = block_levels(key, dims, cuts, -0.22, 0.18) if cuts else 1.0
    array = jax.random.normal(key, dims, jnp.float32) * deviation * gain
    return jnp.minimum(jnp.maximum(array, -limit), limit).astype(kind)


def setup_inputs(seed: int = 0, part: int = 0) -> dict:
    keys = jax.random.split(jax.random.key(seed), 7)
    part_keys = jax.random.split(jax.random.fold_in(keys[6], part), 7)
    air_state = normal_values(part_keys[0], (LEV, NY, NXALL), 1.0, 6.0, ((0, 2), (1, 2), (2, 4)), jnp.float32)
    wind_east = jnp.clip(jax.random.uniform(part_keys[1], (LEV, NY, NXALL), jnp.float32, -0.4, 0.4) * block_levels(part_keys[1], (LEV, NY, NXALL), ((0, 2), (1, 2), (2, 4)), -0.4, 0.0), -0.4, 0.4)
    wind_north = jnp.clip(jax.random.uniform(part_keys[2], (LEV, NY, NXALL), jnp.float32, -0.4, 0.4) * block_levels(part_keys[2], (LEV, NY, NXALL), ((0, 2), (1, 2), (2, 4)), -0.4, 0.0), -0.4, 0.4)
    feedback_weight = jnp.clip(jnp.exp(math.log(1.0) - 1.609438 * jax.random.uniform(keys[3], (LEV,), jnp.float32) ** block_levels(keys[3], (LEV,), ((0, 2),), -0.2, 0.2)), 0.2, 1.0)
    nest_west = jax.random.randint(part_keys[4], (2,), 1, PX - FX).astype(jnp.int32)
    nest_south = jax.random.randint(part_keys[5], (2,), 1, NY - FY).astype(jnp.int32)
    return dict(air_state=air_state, wind_east=wind_east, wind_north=wind_north, feedback_weight=feedback_weight, nest_west=nest_west, nest_south=nest_south)


VERTICAL_MIX = 0.1
PARENT_MIXING = 0.04
NEST_MIXING = 0.18
NEST_ADVECT = 1.5
NUDGING = 0.2


def interp_table(cells):
    extended = jnp.arange(cells + 2, dtype=jnp.int32) - 1
    coarse = jnp.floor_divide(extended, 3)
    offset = extended - 3 * coarse
    fraction = jnp.abs(offset - 1).astype(jnp.float32) / 3.0
    nearest = coarse + 1
    beside = nearest + (offset - 1)
    slots = jnp.arange(cells // 3 + 2, dtype=jnp.int32)[:, None]
    first_part = jnp.where(slots == nearest[None, :], 1.0 - fraction[None, :], jnp.zeros((), jnp.float32))
    second_part = jnp.where(slots == beside[None, :], fraction[None, :], jnp.zeros((), jnp.float32))
    return first_part + second_part


def tendency(padded, speed_east, speed_north, advect_scale, mixing_scale):
    centre = padded[1:-1, 1:-1, 1:-1]
    eastern = padded[1:-1, 1:-1, 2:]
    western = padded[1:-1, 1:-1, :-2]
    southern = padded[1:-1, 2:, 1:-1]
    northern = padded[1:-1, :-2, 1:-1]
    upper = padded[2:, 1:-1, 1:-1]
    lower = padded[:-2, 1:-1, 1:-1]
    advect = speed_east * (eastern - western) + speed_north * (southern - northern)
    horizontal = eastern + western + southern + northern - 4.0 * centre
    vertical = upper + lower - 2.0 * centre
    return -0.5 * advect_scale * advect + mixing_scale * horizontal + VERTICAL_MIX * vertical


def reference(air_state, wind_east, wind_north, feedback_weight, nest_west, nest_south):
    parent = air_state[:, :, :PX]
    nest_field = air_state[:, :, PX:]
    table_x = interp_table(NXN)
    table_y = interp_table(NY)

    def refine(source, substep):
        start = (jnp.int32(0), (nest_south[substep] - 1).astype(jnp.int32), (nest_west[substep] - 1).astype(jnp.int32))
        window = lax.dynamic_slice(source, start, (LEV, FY + 2, FX + 2))
        along = jnp.einsum("lwj,je->lwe", window, table_x, precision=lax.Precision.HIGHEST)
        return jnp.einsum("lwe,wf->lfe", along, table_y, precision=lax.Precision.HIGHEST)

    def nest_step(current, source, substep):
        fine = refine(source, substep)
        joined = fine.at[:, 1:-1, 1:-1].set(current)
        padded = jnp.pad(joined, ((1, 1), (0, 0), (0, 0)))
        change = tendency(padded, wind_east[:, :, PX:], wind_north[:, :, PX:], NEST_ADVECT, NEST_MIXING)
        return current + change + NUDGING * (fine[:, 1:-1, 1:-1] - current)

    parent_new = parent + tendency(jnp.pad(parent, 1), wind_east[:, :, :PX], wind_north[:, :, :PX], 1.0, PARENT_MIXING)
    nest_one = nest_step(nest_field, parent, 0)
    nest_two = nest_step(nest_one, parent_new, 1)
    averaged = nest_two.reshape(LEV, FY, 3, FX, 3).mean(axis=(2, 4))
    corner = (jnp.int32(0), nest_south[1].astype(jnp.int32), nest_west[1].astype(jnp.int32))
    region = lax.dynamic_slice(parent_new, corner, (LEV, FY, FX))
    blended = region + feedback_weight[:, None, None] * (averaged - region)
    parent_out = lax.dynamic_update_slice(parent_new, blended, corner)
    return jnp.concatenate([parent_out, nest_two], axis=2)
```

```python
import functools

import jax
import jax.numpy as jnp
from jax import lax
from jax.experimental import pallas as pl
from jax.experimental.pallas import tpu as pltpu
from jax.sharding import PartitionSpec as P

VERTICAL_MIX = 0.1
PARENT_MIXING = 0.04
NEST_MIXING = 0.18
NEST_ADVECT = 1.5
NUDGING = 0.2


def padded_2(array, sides, width):
    for axis, dim in sides:
        size, length = (lax.axis_size(axis), array.shape[dim])
        up = [(i, (i + 1) % size) for i in range(size - 1)]
        down = [(j, i) for i, j in up]
        last = lax.slice_in_dim(array, length - width, length, axis=dim)
        first = lax.slice_in_dim(array, 0, width, axis=dim)
        before = lax.ppermute(last, axis, up)
        after = lax.ppermute(first, axis, down)
        array = jnp.concatenate([before, array, after], axis=dim)
    return array


def interp_table(cells):
    extended = jnp.arange(cells + 2, dtype=jnp.int32) - 1
    coarse = jnp.floor_divide(extended, 3)
    offset = extended - 3 * coarse
    fraction = jnp.abs(offset - 1).astype(jnp.float32) / 3.0
    nearest = coarse + 1
    beside = nearest + (offset - 1)
    slots = jnp.arange(cells // 3 + 2, dtype=jnp.int32)[:, None]
    first_part = jnp.where(
        slots == nearest[None, :], 1.0 - fraction[None, :], jnp.zeros((), jnp.float32)
    )
    second_part = jnp.where(slots == beside[None, :], fraction[None, :], jnp.zeros((), jnp.float32))
    return first_part + second_part


def tendency(padded, speed_east, speed_north, advect_scale, mixing_scale):
    centre = padded[1:-1, 1:-1, 1:-1]
    eastern = padded[1:-1, 1:-1, 2:]
    western = padded[1:-1, 1:-1, :-2]
    southern = padded[1:-1, 2:, 1:-1]
    northern = padded[1:-1, :-2, 1:-1]
    upper = padded[2:, 1:-1, 1:-1]
    lower = padded[:-2, 1:-1, 1:-1]
    advect = speed_east * (eastern - western) + speed_north * (southern - northern)
    horizontal = eastern + western + southern + northern - 4.0 * centre
    vertical = upper + lower - 2.0 * centre
    return -0.5 * advect_scale * advect + mixing_scale * horizontal + VERTICAL_MIX * vertical


def padded_block(block_field):
    return padded_2(block_field, (("tiles", 2), ("rows", 1), ("lev", 0)), 1)


def per_device(air_state, wind_east, wind_north, feedback_weight, nest_west, nest_south):
    levels, height, breadth = air_state.shape
    tile_count = lax.axis_size("tiles")
    row_count = lax.axis_size("rows")
    tile_index = lax.axis_index("tiles")
    row_index = lax.axis_index("rows")
    parent_tiles = 3 * tile_count // 4
    nest_tiles = tile_count - parent_tiles
    in_nest = tile_index >= parent_tiles
    nest_tile = tile_index - parent_tiles
    cross_x = breadth // 3 + 2
    cross_y = height // 3 + 2
    third_x = breadth // 3
    third_y = height // 3
    first_x = tile_index * breadth
    first_y = row_index * height
    columns = jnp.arange(breadth, dtype=jnp.int32)
    lines = jnp.arange(height, dtype=jnp.int32)
    targets_x = jnp.arange(tile_count, dtype=jnp.int32)
    targets_y = jnp.arange(row_count, dtype=jnp.int32)
    highest = lax.Precision.HIGHEST
    table_x = interp_table(breadth)
    table_y = interp_table(height)
    zero_value = jnp.zeros((), jnp.float32)

    def boundary(source, substep):
        anchor_x = nest_west[substep] + (targets_x - parent_tiles) * third_x - 1
        slot_x = jnp.arange(cross_x, dtype=jnp.int32)
        pick_x = (
            (first_x + columns)[None, :, None] == anchor_x[:, None, None] + slot_x[None, None, :]
        ) & (targets_x >= parent_tiles)[:, None, None]
        pick_x = pick_x.astype(jnp.float32)
        anchor_y = nest_south[substep] + targets_y * third_y - 1
        slot_y = jnp.arange(cross_y, dtype=jnp.int32)
        pick_y = (
            (first_y + lines)[None, :, None] == anchor_y[:, None, None] + slot_y[None, None, :]
        ).astype(jnp.float32)
        pieces = jnp.einsum("lyi,tij->tlyj", source, pick_x, precision=highest)
        merged = lax.all_to_all(pieces, "tiles", split_axis=0, concat_axis=0, tiled=True).sum(
            axis=0
        )
        pieces = jnp.einsum("lyj,ryw->rlwj", merged, pick_y, precision=highest)
        window = lax.all_to_all(pieces, "rows", split_axis=0, concat_axis=0, tiled=True).sum(axis=0)
        along = jnp.einsum("lwj,je->lwe", window, table_x, precision=highest)
        return jnp.einsum("lwe,wf->lfe", along, table_y, precision=highest)

    def assemble(block_field, fine):
        padded = padded_block(block_field)
        fine_padded = jnp.pad(fine, ((1, 1), (0, 0), (0, 0)))
        column_place = lax.broadcasted_iota(jnp.int32, padded.shape, 2)
        line_place = lax.broadcasted_iota(jnp.int32, padded.shape, 1)
        outside = (column_place == 0) & (nest_tile == 0) | (column_place == breadth + 1) & (
            nest_tile == nest_tiles - 1
        )
        outside = (
            outside
            | (line_place == 0) & (row_index == 0)
            | (line_place == height + 1) & (row_index == row_count - 1)
        )
        padded = jnp.where(outside & in_nest, fine_padded, padded)
        seam_cells = (column_place == breadth + 1) & (tile_index == parent_tiles - 1)
        return jnp.where(seam_cells, zero_value, padded)

    advect_scale = jnp.where(in_nest, jnp.float32(NEST_ADVECT), jnp.float32(1.0))
    mixing_scale = jnp.where(in_nest, jnp.float32(NEST_MIXING), jnp.float32(PARENT_MIXING))
    fine_first = boundary(air_state, 0)
    change = tendency(
        assemble(air_state, fine_first), wind_east, wind_north, advect_scale, mixing_scale
    )
    nudging_term = jnp.where(in_nest, NUDGING * (fine_first[:, 1:-1, 1:-1] - air_state), zero_value)
    step_one = air_state + change + nudging_term
    fine_second = boundary(step_one, 1)
    change = tendency(
        assemble(step_one, fine_second), wind_east, wind_north, advect_scale, mixing_scale
    )
    nested_two = step_one + change + NUDGING * (fine_second[:, 1:-1, 1:-1] - step_one)
    step_two = jnp.where(in_nest, nested_two, step_one)
    coarse = step_two.reshape(levels, third_y, 3, third_x, 3).mean(axis=(2, 4))
    avg_columns = jnp.arange(third_x, dtype=jnp.int32)
    avg_lines = jnp.arange(third_y, dtype=jnp.int32)
    west_last = nest_west[1]
    south_last = nest_south[1]
    place_x = (
        (west_last + (targets_x - parent_tiles) * third_x)[:, None, None]
        + avg_columns[None, :, None]
        == (first_x + columns)[None, None, :]
    ) & (targets_x >= parent_tiles)[:, None, None]
    place_x = place_x.astype(jnp.float32)
    place_y = (
        (south_last + targets_y * third_y)[:, None, None] + avg_lines[None, :, None]
        == (first_y + lines)[None, None, :]
    ).astype(jnp.float32)
    parent_y = south_last + row_index * third_y + avg_lines
    send_y = (jnp.floor_divide(parent_y, height)[None, :] == targets_y[:, None]) & in_nest
    pieces = jnp.where(send_y[:, None, :, None], coarse[None], zero_value)
    received = lax.all_to_all(pieces, "rows", split_axis=0, concat_axis=0, tiled=True)
    spread = jnp.einsum("slba,sby->lya", received, place_y, precision=highest)
    parent_x = west_last + nest_tile * third_x + avg_columns
    send_x = jnp.floor_divide(parent_x, breadth)[None, :] == targets_x[:, None]
    pieces = jnp.where(send_x[:, None, None, :], spread[None], zero_value)
    received = lax.all_to_all(pieces, "tiles", split_axis=0, concat_axis=0, tiled=True)
    placed = jnp.einsum("slya,sai->lyi", received, place_x, precision=highest)
    global_x = (first_x + columns)[None, None, :]
    global_y = (first_y + lines)[None, :, None]
    covered = (global_x >= west_last) & (global_x < west_last + nest_tiles * third_x)
    covered = covered & (global_y >= south_last) & (global_y < south_last + row_count * third_y)
    covered = covered & jnp.logical_not(in_nest)
    blended = step_two + feedback_weight[:, None, None] * (placed - step_two)
    return jnp.where(covered, blended, step_two)


LANES = 128
FIRST_LANE = 48
LAST_LANE = 80


def iota(shape, dim):
    return lax.broadcasted_iota(jnp.int32, shape, dim)


def split_level(place, height):
    level = ((place.astype(jnp.float32) + 0.5) * (1.0 / height)).astype(jnp.int32)
    return level, place - level * height


def table(values):
    return values.astype(jnp.float32).astype(jnp.bfloat16)


def parts_of(array):
    high = array.astype(jnp.bfloat16)
    rest = array - high.astype(jnp.float32)
    middle = rest.astype(jnp.bfloat16)
    low = (rest - middle.astype(jnp.float32)).astype(jnp.bfloat16)
    return high, middle, low


def dot(left, right):
    return jnp.dot(left, right, preferred_element_type=jnp.float32)


def from_left(weights, array):
    high, middle, low = parts_of(array)
    return dot(weights, high) + (dot(weights, middle) + dot(weights, low))


def from_right(array, weights):
    high, middle, low = parts_of(array)
    return dot(high, weights) + (dot(middle, weights) + dot(low, weights))


def hat(distance):
    return jnp.maximum(0, 3 - jnp.abs(distance - 1))


def place():
    return lax.axis_index("tiles"), lax.axis_index("rows"), lax.axis_index("lev")


def level_table(levels, height):
    shape = (levels, levels * height)
    level, _ = split_level(iota(shape, 1), height)
    return table(iota(shape, 0) == level)


def spread_table(levels, height):
    shape = (levels * height, levels)
    level, _ = split_level(iota(shape, 0), height)
    return table(iota(shape, 1) == level)


def row_table(levels, height, row):
    shape = (levels, levels * height)
    level, line = split_level(iota(shape, 1), height)
    return table((iota(shape, 0) == level) & (line == row))


def column_table(breadth, third, first_x, west):
    shape = (breadth, third + LANES)
    slot = iota(shape, 1)
    target = jnp.where(
        slot < third, west + slot, jnp.where(slot == third, west - 1, west + third)
    )
    return table((iota(shape, 0) + first_x == target) & (slot < third + 2))


def window_rows_table(count, levels, height, first_y, top):
    shape = (count * levels, levels * height)
    taken = iota(shape, 0)
    slot = taken // levels
    level, line = split_level(iota(shape, 1), height)
    return table((taken - slot * levels == level) & (line + first_y == top + slot))


def store_window(ref, window, count, levels, third):
    extra = jnp.zeros((levels, LANES), jnp.float32)
    for slot in range(count):
        rows = window[slot * levels : (slot + 1) * levels]
        ref[slot] = rows[:, :third]
        beside = rows[:, third:]
        extra = extra + (pltpu.roll(beside, 2 * slot, 1) if slot else beside)
    return extra


def pack_edges(flat, levels, height):
    breadth = flat.shape[1]
    shape = (levels * height, LANES)
    lane = iota(shape, 1)
    _, line = split_level(iota(shape, 0), height)
    columns = jnp.where(lane == line + FIRST_LANE, flat[:, 0:1], 0.0)
    columns = jnp.where(lane == line + LAST_LANE, flat[:, breadth - 1 : breadth], columns)
    return from_left(level_table(levels, height), columns)


def neighbour_columns(by_one, by_three, parent_tiles, tile):
    odd = tile % 2 == 1
    west = jnp.where(odd, by_one, by_three)
    east = jnp.where(odd, by_three, by_one)
    west = jnp.where(tile == 0, jnp.zeros_like(west), west)
    east = jnp.where(tile >= parent_tiles - 1, jnp.zeros_like(east), east)
    return jnp.where(iota(west.shape, 1) < LAST_LANE, east, west)


def unpack_edges(columns, levels, height):
    wide = from_left(spread_table(levels, height), columns)
    lane = iota(wide.shape, 1)
    _, line = split_level(iota(wide.shape, 0), height)
    west = jnp.sum(jnp.where(lane == line + LAST_LANE, wide, 0.0), axis=1, keepdims=True)
    east = jnp.sum(jnp.where(lane == line + FIRST_LANE, wide, 0.0), axis=1, keepdims=True)
    return jnp.where(lane == 0, west, jnp.where(lane == 1, east, 0.0))


def join_row(ref, first, count):
    return jnp.concatenate([ref[first + i] for i in range(count)], axis=1)


def unpack_window(slabs, extra):
    beside = [pltpu.roll(extra, (LANES - 2 * s) % LANES, 1) if s else extra for s in range(len(slabs))]
    return jnp.concatenate(
        [jnp.concatenate(slabs, axis=0), jnp.concatenate(beside, axis=0)], axis=1
    )


def refine(window, levels, height, breadth, row):
    slots = window.shape[0] // levels
    third = breadth // 3
    shape = (third + LANES, breadth + LANES)
    slot, cell = iota(shape, 0), iota(shape, 1)
    at = jnp.where(slot < third, slot, jnp.where(slot == third, -1, third))
    cell = jnp.where(cell == breadth, -1, jnp.where(cell == breadth + 1, breadth, cell))
    across = jnp.where((slot < third + 2) & (cell <= breadth), hat(cell - 3 * at), 0)
    wide = from_right(window, table(across))
    shape = (levels * height, slots * levels)
    taken = iota(shape, 1)
    slot = taken // levels
    level, line = split_level(iota(shape, 0), height)
    along = jnp.where(taken - slot * levels == level, hat(line - 3 * (slot - 1)), 0)
    shape = (levels, slots * levels)
    taken = iota(shape, 1)
    slot = taken // levels
    line = jnp.where(row == 0, -1, height)
    outer = jnp.where(taken - slot * levels == iota(shape, 0), hat(line - 3 * (slot - 1)), 0)
    high, middle, low = parts_of(wide)
    along, outer = table(along), table(outer)
    cells = dot(along, high) + (dot(along, middle) + dot(along, low))
    ring = dot(outer, high) + (dot(outer, middle) + dot(outer, low))
    return cells * (1.0 / 9.0), ring[:, :breadth] * (1.0 / 9.0)


def beside_rows(x, north, south):
    height = x.shape[0]
    line = iota(x.shape, 0)
    northern = jnp.where(line == 0, north, pltpu.roll(x, 1, 0))
    southern = jnp.where(line == height - 1, south, pltpu.roll(x, height - 1, 0))
    return northern, southern


def beside_columns(x, west, east):
    breadth = x.shape[1]
    column = iota(x.shape, 1)
    western = jnp.where(column == 0, west, pltpu.roll(x, 1, 1))
    eastern = jnp.where(column == breadth - 1, east, pltpu.roll(x, breadth - 1, 1))
    return western, eastern


def change_of(x, sides, u, v, upper, lower, advect_scale, mixing_scale):
    northern, southern, western, eastern = sides
    advect = u * (eastern - western) + v * (southern - northern)
    horizontal = eastern + western + southern + northern - 4.0 * x
    vertical = upper + lower - 2.0 * x
    return -0.5 * advect_scale * advect + mixing_scale * horizontal + VERTICAL_MIX * vertical


def vertical_sides(ref, l, level_ref, lev):
    levels = ref.shape[0]
    zero = jnp.zeros(ref.shape[1:], jnp.float32)
    lower = ref[l - 1] if l > 0 else jnp.where(lev == 1, level_ref[...], zero)
    upper = ref[l + 1] if l < levels - 1 else jnp.where(lev == 0, level_ref[...], zero)
    return upper, lower


def full_step(
    out_ref, field_ref, u_ref, v_ref, level_ref, north_ref, south_ref, side_ref, fine_ref, lev, nest
):
    levels, height, breadth = field_ref.shape
    for l in range(levels):
        x = field_ref[l]
        upper, lower = vertical_sides(field_ref, l, level_ref, lev)
        side = side_ref[pl.ds(l * height, height)]
        northern, southern = beside_rows(x, north_ref[pl.ds(l, 1)], south_ref[pl.ds(l, 1)])
        western, eastern = beside_columns(x, side[:, 0:1], side[:, 1:2])
        change = change_of(
            x,
            (northern, southern, western, eastern),
            u_ref[l],
            v_ref[l],
            upper,
            lower,
            NEST_ADVECT if nest else 1.0,
            NEST_MIXING if nest else PARENT_MIXING,
        )
        fresh = x + change
        if nest:
            fresh = fresh + NUDGING * (fine_ref[pl.ds(l * height, height)] - x)
        out_ref[l] = fresh


def inner_row(height, row):
    return jnp.where(row == 0, height - 1, 0)


def pack_kernel(slots, west_ref, south_ref, air_ref, north_ref, rows_ref, own_ref, level_ref):
    levels, height, breadth = air_ref.shape
    third_x, third_y = breadth // 3, height // 3
    pieces = breadth // LANES
    tile, row, lev = place()
    nest = tile == lax.axis_size("tiles") - 1
    level_ref[...] = jnp.where(lev == 0, air_ref[levels - 1], air_ref[0])
    flat = air_ref[...].reshape(levels * height, breadth)
    edge = row_table(levels, height, inner_row(height, row))
    shared = from_left(edge, flat)
    for i in range(pieces):
        rows_ref[slots + 1 + i] = shared[:, i * LANES : (i + 1) * LANES]

    @pl.when(nest)
    def _():
        speed = from_left(edge, north_ref[...].reshape(levels * height, breadth))
        for i in range(pieces):
            rows_ref[i] = speed[:, i * LANES : (i + 1) * LANES]
        for i in range(pieces, slots + 1):
            rows_ref[i] = jnp.zeros((levels, LANES), jnp.float32)
        own_ref[...] = jnp.zeros_like(own_ref)

    @pl.when(jnp.logical_not(nest))
    def _():
        columns = column_table(breadth, third_x, tile * breadth, west_ref[0])
        high, middle, low = parts_of(from_right(flat, columns))
        for ref, block in ((rows_ref, 1 - row), (own_ref, row)):
            top = south_ref[0] + block * third_y - 1
            picked = window_rows_table(slots, levels, height, row * height, top)
            window = dot(picked, high) + (dot(picked, middle) + dot(picked, low))
            extra = store_window(ref, window, slots, levels, third_x)
            ref[slots] = extra
        own_ref[slots] = own_ref[slots] + pack_edges(flat, levels, height)


def first_kernel(
    slots,
    west_ref,
    south_ref,
    air_ref,
    east_ref,
    north_ref,
    rows_ref,
    level_ref,
    one_ref,
    two_ref,
    three_ref,
    out_ref,
    edge_ref,
    message_ref,
    fine_ref,
    side_ref,
    northern_ref,
    southern_ref,
):
    levels, height, breadth = air_ref.shape
    third_x, third_y = breadth // 3, height // 3
    pieces = breadth // LANES
    tile_count = lax.axis_size("tiles")
    tile, row, lev = place()
    nest = tile == tile_count - 1
    halo = join_row(rows_ref, slots + 1, pieces)

    @pl.when(nest)
    def _():
        slabs = [one_ref[s] + two_ref[s] + three_ref[s] for s in range(slots + 1)]
        window = unpack_window(slabs[:slots], slabs[slots])
        cells, ring = refine(window, levels, height, breadth, row)
        fine_ref[...] = cells[:, :breadth]
        side_ref[...] = cells[:, breadth:]
        northern_ref[...] = jnp.where(row == 0, ring, halo)
        southern_ref[...] = jnp.where(row == 0, halo, ring)
        full_step(
            out_ref, air_ref, east_ref, north_ref, level_ref, northern_ref, southern_ref, side_ref, fine_ref, lev, True
        )

    @pl.when(jnp.logical_not(nest))
    def _():
        columns = neighbour_columns(one_ref[slots], three_ref[slots], tile_count - 1, tile)
        side_ref[...] = unpack_edges(columns, levels, height)
        zero = jnp.zeros_like(halo)
        northern_ref[...] = jnp.where(row == 0, zero, halo)
        southern_ref[...] = jnp.where(row == 0, halo, zero)
        full_step(
            out_ref, air_ref, east_ref, north_ref, level_ref, northern_ref, southern_ref, side_ref, fine_ref, lev, False
        )
        flat = out_ref[...].reshape(levels * height, breadth)
        picked = column_table(breadth, third_x, tile * breadth, west_ref[1])
        count = message_ref.shape[0] - 1
        rows = window_rows_table(count, levels, height, row * height, south_ref[1] - 1)
        window = from_left(rows, from_right(flat, picked))
        extra = store_window(message_ref, window, count, levels, third_x)
        message_ref[count] = extra + pack_edges(flat, levels, height)

    edge_ref[...] = jnp.where(lev == 0, out_ref[levels - 1], out_ref[0])


def average_kernel(slots, field_ref, east_ref, north_ref, rows_ref, level_ref, given_ref, message_ref, part_ref):
    levels, height, breadth = field_ref.shape
    third_x, third_y = breadth // 3, height // 3
    pieces = breadth // LANES
    size = levels * height
    tile, row, lev = place()
    nest = tile == lax.axis_size("tiles") - 1

    @pl.when(jnp.logical_not(nest))
    def _():
        message_ref[...] = given_ref[...]

    @pl.when(nest)
    def _():
        for l in range(levels):
            x = field_ref[l]
            upper, lower = vertical_sides(field_ref, l, level_ref, lev)
            sides = beside_rows(x, 0.0, 0.0) + beside_columns(x, 0.0, 0.0)
            change = change_of(x, sides, east_ref[l], north_ref[l], upper, lower, NEST_ADVECT, NEST_MIXING)
            part_ref[pl.ds(l * height, height)] = x + change - NUDGING * x
        cell, third = iota((breadth, third_x), 0), iota((breadth, third_x), 1)
        offset = cell - 3 * third
        sums = table((offset >= 0) & (offset <= 2))
        shape = (third_y * levels, size)
        taken = iota(shape, 0)
        block = taken // levels
        level, line = split_level(iota(shape, 1), height)
        offset_y = line - 3 * block
        rows = table((taken - block * levels == level) & (offset_y >= 0) & (offset_y <= 2))
        means = from_left(rows, from_right(part_ref[...], sums)) * (1.0 / 9.0)
        for m in range(third_y):
            message_ref[m] = means[m * levels : (m + 1) * levels]
        flat = field_ref[...].reshape(size, breadth)
        speed = north_ref[...].reshape(size, breadth)
        inner = inner_row(height, row)
        outer = height - 1 - inner
        sign = jnp.where(row == 0, 0.5 * NEST_ADVECT, -0.5 * NEST_ADVECT)
        shared = from_left(row_table(levels, height, inner), flat)
        shared = (sign * join_row(rows_ref, 0, pieces) + NEST_MIXING) * shared
        ghost = sign * from_left(row_table(levels, height, outer), speed) + NEST_MIXING
        message_ref[third_y + 4] = from_right(shared, sums) * (1.0 / 9.0)
        weights = (
            table(offset == 0),
            table(jnp.where(offset == 1, 3, jnp.where((offset == 0) | (offset == 2), 2, 0))),
            table(offset == 2),
        )
        for q in range(3):
            message_ref[third_y + q] = from_right(ghost, weights[q]) * (1.0 / 27.0)
        shape = (size, LANES)
        lane = iota(shape, 1)
        _, line = split_level(iota(shape, 0), height)
        block = lane // 8
        inside = lane - block * 8
        eastern = inside >= 3
        kind = jnp.where(eastern, inside - 3, inside)
        offset = line - 3 * block
        weight = jnp.where(
            kind == 1,
            jnp.where(offset == 1, 3, jnp.where((offset == 0) | (offset == 2), 2, 0)),
            jnp.where(offset == kind, 1, 0),
        )
        weight = jnp.where((inside < 6) & (block < third_y), weight, 0).astype(jnp.float32)
        speed = east_ref[...].reshape(size, breadth)
        first = 0.5 * NEST_ADVECT * speed[:, 0:1] + NEST_MIXING
        last = -0.5 * NEST_ADVECT * speed[:, breadth - 1 : breadth] + NEST_MIXING
        columns = jnp.where(eastern, last, first) * weight
        message_ref[third_y + 3] = from_left(level_table(levels, height), columns) * (1.0 / 27.0)
        for i in range(third_y + 5, message_ref.shape[0]):
            message_ref[i] = jnp.zeros((levels, LANES), jnp.float32)


def nest_message(tile, one_ref, two_ref, three_ref, i):
    return jnp.where(tile == 0, three_ref[i], jnp.where(tile == 1, two_ref[i], one_ref[i]))


def swap_kernel(slots, field_ref, one_ref, two_ref, three_ref, rows_ref):
    levels, height, breadth = field_ref.shape
    third_y = height // 3
    pieces = breadth // LANES
    tile_count = lax.axis_size("tiles")
    tile, row, _ = place()
    nest = tile == tile_count - 1
    last = one_ref.shape[0] - 1
    flat = field_ref[...].reshape(levels * height, breadth)
    edge = from_left(row_table(levels, height, inner_row(height, row)), flat)
    base = third_y + 5
    for i in range(pieces):
        rows_ref[base + i] = edge[:, i * LANES : (i + 1) * LANES]

    @pl.when(nest)
    def _():
        first = jnp.where(row == 0, third_y, 0)
        for s in range(slots):
            rows_ref[s] = one_ref[first + s] + two_ref[first + s] + three_ref[first + s]
        extra = one_ref[last] + two_ref[last] + three_ref[last]
        rows_ref[slots] = jnp.where(row == 0, pltpu.roll(extra, LANES - 2 * third_y, 1), extra)
        for i in range(slots + 1, base):
            rows_ref[i] = jnp.zeros((levels, LANES), jnp.float32)
        rows_ref[base + pieces] = jnp.zeros((levels, LANES), jnp.float32)

    @pl.when(jnp.logical_not(nest))
    def _():
        for i in range(base):
            rows_ref[i] = nest_message(tile, one_ref, two_ref, three_ref, i)
        columns = neighbour_columns(one_ref[last], three_ref[last], tile_count - 1, tile)

        def moved(lane, to):
            low = pltpu.roll(columns, (LANES + to - lane) % LANES, 1)
            high = pltpu.roll(columns, (LANES + to - lane - height + 1) % LANES, 1)
            return jnp.where(row == 0, high, low)

        lane = iota(columns.shape, 1)
        corners = jnp.where(lane == 1, moved(FIRST_LANE, 1), 0.0)
        rows_ref[base + pieces] = jnp.where(lane == 0, moved(LAST_LANE, 0), corners)


def last_kernel(
    slots,
    west_ref,
    south_ref,
    weight_ref,
    field_ref,
    east_ref,
    north_ref,
    level_ref,
    rows_ref,
    one_ref,
    two_ref,
    three_ref,
    out_ref,
    fine_ref,
    side_ref,
    northern_ref,
    southern_ref,
    placed_ref,
    coef_ref,
    edge_coef_ref,
):
    levels, height, breadth = field_ref.shape
    third_x, third_y = breadth // 3, height // 3
    pieces = breadth // LANES
    size = levels * height
    tile_count = lax.axis_size("tiles")
    tile, row, lev = place()
    nest = tile == tile_count - 1
    last = one_ref.shape[0] - 1
    base = third_y + 5
    halo = join_row(rows_ref, base, pieces)

    @pl.when(nest)
    def _():
        first = jnp.where(row == 0, 0, third_y)
        slabs = [
            one_ref[first + s] + two_ref[first + s] + three_ref[first + s] + rows_ref[s]
            for s in range(slots)
        ]
        extra = one_ref[last] + two_ref[last] + three_ref[last]
        extra = jnp.where(row == 0, extra, pltpu.roll(extra, LANES - 2 * third_y, 1))
        window = unpack_window(slabs, extra + rows_ref[slots])
        cells, ring = refine(window, levels, height, breadth, row)
        fine_ref[...] = cells[:, :breadth]
        side_ref[...] = cells[:, breadth:]
        northern_ref[...] = jnp.where(row == 0, ring, halo)
        southern_ref[...] = jnp.where(row == 0, halo, ring)
        full_step(
            out_ref, field_ref, east_ref, north_ref, level_ref, northern_ref, southern_ref, side_ref, fine_ref, lev, True
        )

    @pl.when(jnp.logical_not(nest))
    def _():
        west, south = west_ref[1], south_ref[1]
        columns = neighbour_columns(one_ref[last], three_ref[last], tile_count - 1, tile)
        side_ref[...] = unpack_edges(columns, levels, height)
        zero = jnp.zeros_like(halo)
        northern_ref[...] = jnp.where(row == 0, zero, halo)
        southern_ref[...] = jnp.where(row == 0, halo, zero)

        def block_slab(block, i):
            mine = nest_message(tile, one_ref, two_ref, three_ref, i)
            return jnp.where(row == block, mine, rows_ref[i])

        means, beside = [], []
        for block in range(2):
            slabs = [block_slab(block, m) for m in range(third_y)]
            correction = block_slab(1 - block, third_y + 4)
            near = third_y - 1 if block == 0 else 0
            slabs[near] = slabs[near] + correction
            means += slabs
            edges = block_slab(block, third_y + 3)
            beside += [pltpu.roll(edges, LANES - 8 * m, 1) if m else edges for m in range(third_y)]
        ghosts = [block_slab(block, third_y + q) for q in range(3) for block in range(2)]
        shape = (third_x, breadth)
        spread = table(iota(shape, 1) + tile * breadth == west + iota(shape, 0))
        wide = from_right(jnp.concatenate(means + ghosts, axis=0), spread)
        count = 2 * third_y * levels
        both = jnp.concatenate([wide[:count], jnp.concatenate(beside, axis=0)], axis=1)
        shape = (size, count)
        taken = iota(shape, 1)
        block = taken // levels
        level, line = split_level(iota(shape, 0), height)
        rows = (taken - block * levels == level) & (line + row * height == south + block)
        both = from_left(table(rows), both)
        placed_ref[...] = both[:, :breadth]
        edge_coef_ref[...] = both[:, breadth:]
        shape = (size, 2 * levels)
        taken = iota(shape, 1)
        block = taken // levels
        level, line = split_level(iota(shape, 0), height)
        target = south + block * (2 * third_y - 1)
        rows = table((taken - block * levels == level) & (line + row * height == target))
        for q in range(3):
            piece = wide[count + 2 * q * levels : count + 2 * (q + 1) * levels]
            coef_ref[q] = from_left(rows, piece)
        line = iota((height, breadth), 0) + row * height
        column = iota((height, breadth), 1) + tile * breadth
        covered = (column >= west) & (column < west + third_x)
        covered = covered & (line >= south) & (line < south + 2 * third_y)
        top_row = line == south
        first_column = column == west
        last_column = column == west + third_x - 1
        two, one = 2.0 / 3.0, 1.0 / 3.0
        for l in range(levels):
            part = pl.ds(l * height, height)
            x = field_ref[l]
            side = side_ref[part]
            corner = rows_ref[base + pieces, pl.ds(l, 1)]
            xn, xs = beside_rows(x, northern_ref[pl.ds(l, 1)], southern_ref[pl.ds(l, 1)])
            sn, ss = beside_rows(side, corner, corner)
            xw, xe = beside_columns(x, side[:, 0:1], side[:, 1:2])
            xnw, xne = beside_columns(xn, sn[:, 0:1], sn[:, 1:2])
            xsw, xse = beside_columns(xs, ss[:, 0:1], ss[:, 1:2])
            q, qw, qe = xn + 7.0 * x + xs, xnw + 7.0 * xw + xsw, xne + 7.0 * xe + xse
            value = placed_ref[part] + (NUDGING / 81.0) * (qw + 7.0 * q + qe)

            def outward(n, c, s):
                return two * jnp.where(top_row, n, s) + one * c

            value = value + coef_ref[0, part] * outward(xnw, xw, xsw)
            value = value + coef_ref[1, part] * outward(xn, x, xs)
            value = value + coef_ref[2, part] * outward(xne, xe, xse)
            ec = edge_coef_ref[part]

            def sideward(w, c, e):
                return two * jnp.where(first_column, w, e) + one * c

            def coefficient(q):
                return jnp.where(
                    first_column, ec[:, q : q + 1], jnp.where(last_column, ec[:, q + 3 : q + 4], 0.0)
                )

            value = value + coefficient(0) * sideward(xnw, xn, xne)
            value = value + coefficient(1) * sideward(xw, x, xe)
            value = value + coefficient(2) * sideward(xsw, xs, xse)
            out_ref[l] = jnp.where(covered, x + weight_ref[l] * (value - x), x)


def call(kernel, outs, inputs, scalars, scratch=()):
    smem = pl.BlockSpec(memory_space=pltpu.SMEM)
    vmem = pl.BlockSpec(memory_space=pltpu.VMEM)
    shapes = [jax.ShapeDtypeStruct(shape, jnp.float32) for shape in outs]
    return pl.pallas_call(
        kernel,
        out_shape=shapes,
        in_specs=[smem] * scalars + [vmem] * (len(inputs) - scalars),
        out_specs=[vmem] * len(outs),
        scratch_shapes=[pltpu.VMEM(shape, jnp.float32) for shape in scratch],
        compiler_params=pltpu.CompilerParams(vmem_limit_bytes=48 * 1024 * 1024),
    )(*inputs)


def per_device_paired(air_state, wind_east, wind_north, feedback_weight, nest_west, nest_south):
    levels, height, breadth = air_state.shape
    third_y = height // 3
    pieces = breadth // LANES
    slots = third_y + 2
    tile_count = lax.axis_size("tiles")
    size = levels * height
    block = (levels, height, breadth)
    swap = [(0, 1), (1, 0)]

    def slabs(count):
        return (count, levels, LANES)

    def over_tiles(message):
        return [
            lax.ppermute(message, "tiles", [(t, t ^ step) for t in range(tile_count)])
            for step in (1, 2, 3)
        ]

    rows, own, level = call(
        functools.partial(pack_kernel, slots),
        [slabs(slots + 1 + pieces), slabs(slots + 1), block[1:]],
        [nest_west, nest_south, air_state, wind_north],
        2,
    )
    rows = lax.ppermute(rows, "rows", swap)
    level = lax.ppermute(level, "lev", swap)
    received = over_tiles(own + rows[: slots + 1])
    steps = [(size, breadth), (size, LANES), (levels, breadth), (levels, breadth)]
    field, edge, message = call(
        functools.partial(first_kernel, slots),
        [block, block[1:], slabs(2 * third_y + 3)],
        [nest_west, nest_south, air_state, wind_east, wind_north, rows, level, *received],
        2,
        steps,
    )
    level = lax.ppermute(edge, "lev", swap)
    (message,) = call(
        functools.partial(average_kernel, slots),
        [slabs(2 * third_y + 3)],
        [field, wind_east, wind_north, rows, level, message],
        0,
        [(size, breadth)],
    )
    received = over_tiles(message)
    (rows,) = call(
        functools.partial(swap_kernel, slots),
        [slabs(third_y + 6 + pieces)],
        [field, *received],
        0,
    )
    rows = lax.ppermute(rows, "rows", swap)
    (out,) = call(
        functools.partial(last_kernel, slots),
        [block],
        [nest_west, nest_south, feedback_weight, field, wind_east, wind_north, level, rows, *received],
        3,
        steps + [(size, breadth), (3, size, breadth), (size, LANES)],
    )
    return out


def solution(mesh):
    in_specs = (
        P(("members", "lev"), "rows", "tiles"),
        P(("members", "lev"), "rows", "tiles"),
        P(("members", "lev"), "rows", "tiles"),
        P("lev"),
        P("members"),
        P("members"),
    )
    out_specs = P(("members", "lev"), "rows", "tiles")
    paired = mesh.shape["tiles"] == 4 and mesh.shape["rows"] == 2 and mesh.shape["lev"] == 2
    return jax.shard_map(
        per_device_paired if paired else per_device, mesh=mesh, in_specs=in_specs, out_specs=out_specs, check_vma=False
    )
```

```python
import functools
import math

import jax
import jax.numpy as jnp
from jax import lax
from jax.experimental import pallas as pl
from jax.experimental.pallas import tpu as pltpu
from jax.sharding import PartitionSpec as P

VERTICAL_MIX = 0.1
PARENT_MIXING = 0.04
NEST_MIXING = 0.18
NEST_ADVECT = 1.5
NUDGING = 0.2


def padded_2(array, sides, width):
    for axis, dim in sides:
        size, length = (lax.axis_size(axis), array.shape[dim])
        up = [(i, (i + 1) % size) for i in range(size - 1)]
        down = [(j, i) for i, j in up]
        last = lax.slice_in_dim(array, length - width, length, axis=dim)
        first = lax.slice_in_dim(array, 0, width, axis=dim)
        before = lax.ppermute(last, axis, up)
        after = lax.ppermute(first, axis, down)
        array = jnp.concatenate([before, array, after], axis=dim)
    return array


def interp_table(cells):
    extended = jnp.arange(cells + 2, dtype=jnp.int32) - 1
    coarse = jnp.floor_divide(extended, 3)
    offset = extended - 3 * coarse
    fraction = jnp.abs(offset - 1).astype(jnp.float32) / 3.0
    nearest = coarse + 1
    beside = nearest + (offset - 1)
    slots = jnp.arange(cells // 3 + 2, dtype=jnp.int32)[:, None]
    first_part = jnp.where(
        slots == nearest[None, :], 1.0 - fraction[None, :], jnp.zeros((), jnp.float32)
    )
    second_part = jnp.where(slots == beside[None, :], fraction[None, :], jnp.zeros((), jnp.float32))
    return first_part + second_part


def tendency(padded, speed_east, speed_north, advect_scale, mixing_scale):
    centre = padded[1:-1, 1:-1, 1:-1]
    eastern = padded[1:-1, 1:-1, 2:]
    western = padded[1:-1, 1:-1, :-2]
    southern = padded[1:-1, 2:, 1:-1]
    northern = padded[1:-1, :-2, 1:-1]
    upper = padded[2:, 1:-1, 1:-1]
    lower = padded[:-2, 1:-1, 1:-1]
    advect = speed_east * (eastern - western) + speed_north * (southern - northern)
    horizontal = eastern + western + southern + northern - 4.0 * centre
    vertical = upper + lower - 2.0 * centre
    return -0.5 * advect_scale * advect + mixing_scale * horizontal + VERTICAL_MIX * vertical


def padded_block(block_field):
    return padded_2(block_field, (("tiles", 2), ("rows", 1), ("lev", 0)), 1)


def per_device(air_state, wind_east, wind_north, feedback_weight, nest_west, nest_south):
    levels, height, breadth = air_state.shape
    tile_count = lax.axis_size("tiles")
    row_count = lax.axis_size("rows")
    tile_index = lax.axis_index("tiles")
    row_index = lax.axis_index("rows")
    parent_tiles = 3 * tile_count // 4
    nest_tiles = tile_count - parent_tiles
    in_nest = tile_index >= parent_tiles
    nest_tile = tile_index - parent_tiles
    cross_x = breadth // 3 + 2
    cross_y = height // 3 + 2
    third_x = breadth // 3
    third_y = height // 3
    first_x = tile_index * breadth
    first_y = row_index * height
    columns = jnp.arange(breadth, dtype=jnp.int32)
    lines = jnp.arange(height, dtype=jnp.int32)
    targets_x = jnp.arange(tile_count, dtype=jnp.int32)
    targets_y = jnp.arange(row_count, dtype=jnp.int32)
    highest = lax.Precision.HIGHEST
    table_x = interp_table(breadth)
    table_y = interp_table(height)
    zero_value = jnp.zeros((), jnp.float32)

    def boundary(source, substep):
        anchor_x = nest_west[substep] + (targets_x - parent_tiles) * third_x - 1
        slot_x = jnp.arange(cross_x, dtype=jnp.int32)
        pick_x = (
            (first_x + columns)[None, :, None] == anchor_x[:, None, None] + slot_x[None, None, :]
        ) & (targets_x >= parent_tiles)[:, None, None]
        pick_x = pick_x.astype(jnp.float32)
        anchor_y = nest_south[substep] + targets_y * third_y - 1
        slot_y = jnp.arange(cross_y, dtype=jnp.int32)
        pick_y = (
            (first_y + lines)[None, :, None] == anchor_y[:, None, None] + slot_y[None, None, :]
        ).astype(jnp.float32)
        pieces = jnp.einsum("lyi,tij->tlyj", source, pick_x, precision=highest)
        merged = lax.all_to_all(pieces, "tiles", split_axis=0, concat_axis=0, tiled=True).sum(
            axis=0
        )
        pieces = jnp.einsum("lyj,ryw->rlwj", merged, pick_y, precision=highest)
        window = lax.all_to_all(pieces, "rows", split_axis=0, concat_axis=0, tiled=True).sum(axis=0)
        along = jnp.einsum("lwj,je->lwe", window, table_x, precision=highest)
        return jnp.einsum("lwe,wf->lfe", along, table_y, precision=highest)

    def assemble(block_field, fine):
        padded = padded_block(block_field)
        fine_padded = jnp.pad(fine, ((1, 1), (0, 0), (0, 0)))
        column_place = lax.broadcasted_iota(jnp.int32, padded.shape, 2)
        line_place = lax.broadcasted_iota(jnp.int32, padded.shape, 1)
        outside = (column_place == 0) & (nest_tile == 0) | (column_place == breadth + 1) & (
            nest_tile == nest_tiles - 1
        )
        outside = (
            outside
            | (line_place == 0) & (row_index == 0)
            | (line_place == height + 1) & (row_index == row_count - 1)
        )
        padded = jnp.where(outside & in_nest, fine_padded, padded)
        seam_cells = (column_place == breadth + 1) & (tile_index == parent_tiles - 1)
        return jnp.where(seam_cells, zero_value, padded)

    advect_scale = jnp.where(in_nest, jnp.float32(NEST_ADVECT), jnp.float32(1.0))
    mixing_scale = jnp.where(in_nest, jnp.float32(NEST_MIXING), jnp.float32(PARENT_MIXING))
    fine_first = boundary(air_state, 0)
    change = tendency(
        assemble(air_state, fine_first), wind_east, wind_north, advect_scale, mixing_scale
    )
    nudging_term = jnp.where(in_nest, NUDGING * (fine_first[:, 1:-1, 1:-1] - air_state), zero_value)
    step_one = air_state + change + nudging_term
    fine_second = boundary(step_one, 1)
    change = tendency(
        assemble(step_one, fine_second), wind_east, wind_north, advect_scale, mixing_scale
    )
    nested_two = step_one + change + NUDGING * (fine_second[:, 1:-1, 1:-1] - step_one)
    step_two = jnp.where(in_nest, nested_two, step_one)
    coarse = step_two.reshape(levels, third_y, 3, third_x, 3).mean(axis=(2, 4))
    avg_columns = jnp.arange(third_x, dtype=jnp.int32)
    avg_lines = jnp.arange(third_y, dtype=jnp.int32)
    west_last = nest_west[1]
    south_last = nest_south[1]
    place_x = (
        (west_last + (targets_x - parent_tiles) * third_x)[:, None, None]
        + avg_columns[None, :, None]
        == (first_x + columns)[None, None, :]
    ) & (targets_x >= parent_tiles)[:, None, None]
    place_x = place_x.astype(jnp.float32)
    place_y = (
        (south_last + targets_y * third_y)[:, None, None] + avg_lines[None, :, None]
        == (first_y + lines)[None, None, :]
    ).astype(jnp.float32)
    parent_y = south_last + row_index * third_y + avg_lines
    send_y = (jnp.floor_divide(parent_y, height)[None, :] == targets_y[:, None]) & in_nest
    pieces = jnp.where(send_y[:, None, :, None], coarse[None], zero_value)
    received = lax.all_to_all(pieces, "rows", split_axis=0, concat_axis=0, tiled=True)
    spread = jnp.einsum("slba,sby->lya", received, place_y, precision=highest)
    parent_x = west_last + nest_tile * third_x + avg_columns
    send_x = jnp.floor_divide(parent_x, breadth)[None, :] == targets_x[:, None]
    pieces = jnp.where(send_x[:, None, None, :], spread[None], zero_value)
    received = lax.all_to_all(pieces, "tiles", split_axis=0, concat_axis=0, tiled=True)
    placed = jnp.einsum("slya,sai->lyi", received, place_x, precision=highest)
    global_x = (first_x + columns)[None, None, :]
    global_y = (first_y + lines)[None, :, None]
    covered = (global_x >= west_last) & (global_x < west_last + nest_tiles * third_x)
    covered = covered & (global_y >= south_last) & (global_y < south_last + row_count * third_y)
    covered = covered & jnp.logical_not(in_nest)
    blended = step_two + feedback_weight[:, None, None] * (placed - step_two)
    return jnp.where(covered, blended, step_two)


LANES = 128
FIRST_LANE = 32
LAST_LANE = 96
EAST_LANE = 64


def iota(shape, dim):
    return lax.broadcasted_iota(jnp.int32, shape, dim)


def split_level(place, height):
    level = ((place.astype(jnp.float32) + 0.5) * (1.0 / height)).astype(jnp.int32)
    return level, place - level * height


def table(values):
    return values.astype(jnp.float32).astype(jnp.bfloat16)


def parts_of(array):
    high = array.astype(jnp.bfloat16)
    low = (array - high.astype(jnp.float32)).astype(jnp.bfloat16)
    return high, low


def dot(left, right):
    return jnp.dot(left, right, preferred_element_type=jnp.float32)


def from_left(weights, array):
    high, low = parts_of(array)
    return dot(weights, high) + dot(weights, low)


def from_right(array, weights):
    high, low = parts_of(array)
    return dot(high, weights) + dot(low, weights)


def hat(distance):
    return jnp.maximum(0, 3 - jnp.abs(distance - 1))


def place():
    return lax.axis_index("tiles"), lax.axis_index("rows"), lax.axis_index("lev")


def level_table(levels, height):
    shape = (levels, levels * height)
    level, _ = split_level(iota(shape, 1), height)
    return table(iota(shape, 0) == level)


def spread_table(levels, height):
    shape = (levels * height, levels)
    level, _ = split_level(iota(shape, 0), height)
    return table(iota(shape, 1) == level)


def load_line(ref, levels, line):
    rows = pl.ds(line, levels, stride=ref.shape[1] // levels)
    return jnp.concatenate([ref[c, rows, :] for c in range(ref.shape[0])], axis=1)


def store_line(ref, levels, line, value):
    rows = pl.ds(line, levels, stride=ref.shape[1] // levels)
    for c in range(ref.shape[0]):
        ref[c, rows, :] = value[:, c * LANES : (c + 1) * LANES]


def load_level(ref, height, l):
    rows = pl.ds(l * height, height)
    if len(ref.shape) == 2:
        return ref[rows, :]
    return jnp.concatenate([ref[c, rows, :] for c in range(ref.shape[0])], axis=1)


def store_level(ref, height, l, value):
    rows = pl.ds(l * height, height)
    if len(ref.shape) == 2:
        ref[rows, :] = value
    else:
        for c in range(ref.shape[0]):
            ref[c, rows, :] = value[:, c * LANES : (c + 1) * LANES]


def store_slabs(ref, first, wide):
    for i in range(wide.shape[1] // LANES):
        ref[first + i] = wide[:, i * LANES : (i + 1) * LANES]


def join_slabs(ref, first, count):
    return jnp.concatenate([ref[first + i] for i in range(count)], axis=1)


def pack_window(ref, field_ref, levels, top, start):
    height = field_ref.shape[1] // levels
    breadth = field_ref.shape[0] * LANES
    slots = ref.shape[0] - 1
    lane = iota((levels, breadth), 1)
    column = jnp.where(lane == breadth - 1, start - 1, start + lane)
    inside = (column >= 0) & (column < breadth)
    turn = lax.rem(4 * breadth - start, breadth)
    lane = iota((levels, LANES), 1)
    extra = jnp.zeros((levels, LANES), jnp.float32)
    for slot in range(slots):
        line = top + slot
        there = (line >= 0) & (line < height)
        rows = load_line(field_ref, levels, jnp.clip(line, 0, height - 1))
        rows = jnp.where(inside & there, pltpu.roll(rows, turn, 1), 0.0)
        ref[slot] = rows[:, :LANES]
        east = rows[:, LANES : 2 * LANES]
        west = rows[:, breadth - LANES :]
        extra = jnp.where(lane == slot, pltpu.roll(west, slot + 1, 1), extra)
        extra = jnp.where(lane == EAST_LANE + slot, pltpu.roll(east, EAST_LANE + slot, 1), extra)
    ref[slots] = extra


def pack_edges(field_ref, levels):
    height = field_ref.shape[1] // levels
    lane = iota((levels, LANES), 1)
    packed = jnp.zeros((levels, LANES), jnp.float32)
    for line in range(height):
        rows = pl.ds(line, levels, stride=height)
        first = field_ref[0, rows, :]
        last = field_ref[field_ref.shape[0] - 1, rows, :]
        packed = jnp.where(lane == FIRST_LANE + line, pltpu.roll(first, FIRST_LANE + line, 1), packed)
        packed = jnp.where(lane == LAST_LANE + line, pltpu.roll(last, LAST_LANE + line + 1, 1), packed)
    return packed


def neighbour_columns(even, odd, parent_tiles, tile):
    is_odd = tile % 2 == 1
    west = jnp.where(is_odd, even, odd)
    east = jnp.where(is_odd, odd, even)
    west = jnp.where(tile == 0, jnp.zeros_like(west), west)
    east = jnp.where(tile >= parent_tiles - 1, jnp.zeros_like(east), east)
    return jnp.where(iota(west.shape, 1) < LAST_LANE, east, west)


def unpack_edges(columns, levels, height):
    wide = from_left(spread_table(levels, height), columns)
    lane = iota(wide.shape, 1)
    _, line = split_level(iota(wide.shape, 0), height)
    west = jnp.sum(jnp.where(lane == line + LAST_LANE, wide, 0.0), axis=1, keepdims=True)
    east = jnp.sum(jnp.where(lane == line + FIRST_LANE, wide, 0.0), axis=1, keepdims=True)
    return jnp.where(lane == 0, west, jnp.where(lane == 1, east, 0.0))


def refine(slabs, extra, height, breadth, row):
    slots, levels = len(slabs), extra.shape[0]
    beside = [pltpu.roll(extra, LANES - s, 1) if s else extra for s in range(slots)]
    window = jnp.concatenate([jnp.concatenate(slabs, axis=0), jnp.concatenate(beside, axis=0)], axis=1)
    shape = (2 * LANES, breadth + LANES)
    slot, cell = iota(shape, 0), iota(shape, 1)
    held = (slot <= LANES) | (slot == LANES + EAST_LANE)
    at = jnp.where(slot < LANES, slot, jnp.where(slot == LANES, -1, LANES))
    cell = jnp.where(cell == breadth, -1, jnp.where(cell == breadth + 1, breadth, cell))
    across = jnp.where(held & (cell <= breadth), hat(cell - 3 * at), 0)
    wide = from_right(window, table(across)) * (1.0 / 9.0)
    shape = (levels * height, slots * levels)
    taken = iota(shape, 1)
    slot = taken // levels
    level, line = split_level(iota(shape, 0), height)
    along = jnp.where(taken - slot * levels == level, hat(line - 3 * (slot - 1)), 0)
    cells = from_left(table(along), wide)
    ring = jnp.where(
        row == 0,
        2.0 * wide[:levels] + wide[levels : 2 * levels],
        2.0 * wide[(slots - 1) * levels :] + wide[(slots - 2) * levels : (slots - 1) * levels],
    )
    return cells, ring[:, :breadth]


def beside_rows(x, north, south):
    height = x.shape[0]
    line = iota(x.shape, 0)
    northern = jnp.where(line == 0, north, pltpu.roll(x, 1, 0))
    southern = jnp.where(line == height - 1, south, pltpu.roll(x, height - 1, 0))
    return northern, southern


def beside_columns(x, west, east):
    breadth = x.shape[1]
    column = iota(x.shape, 1)
    western = jnp.where(column == 0, west, pltpu.roll(x, 1, 1))
    eastern = jnp.where(column == breadth - 1, east, pltpu.roll(x, breadth - 1, 1))
    return western, eastern


def change_of(x, sides, u, v, upper, lower, nest):
    advect_scale = NEST_ADVECT if nest else 1.0
    mixing_scale = NEST_MIXING if nest else PARENT_MIXING
    northern, southern, western, eastern = sides
    advect = u * (eastern - western) + v * (southern - northern)
    horizontal = eastern + western + southern + northern - 4.0 * x
    vertical = upper + lower - 2.0 * x
    return -0.5 * advect_scale * advect + mixing_scale * horizontal + VERTICAL_MIX * vertical


def ghost_weight(speed, before):
    return jnp.where(before, 0.5 * NEST_ADVECT, -0.5 * NEST_ADVECT) * speed + NEST_MIXING


def full_step(out_ref, field_ref, u_ref, v_ref, level_ref, levels, lev, nest, north, south, side, fine):
    height, breadth = level_ref.shape
    zero = jnp.zeros((height, breadth), jnp.float32)

    def block(ref, l):
        return load_level(ref, height, l)

    for l in range(levels):
        x = block(field_ref, l)
        lower = block(field_ref, l - 1) if l else jnp.where(lev == 1, level_ref[...], zero)
        upper = block(field_ref, l + 1) if l < levels - 1 else jnp.where(lev == 0, level_ref[...], zero)
        rows = [0.0 if ref is None else ref[pl.ds(l, 1), :] for ref in (north, south)]
        if side is None:
            columns = (0.0, 0.0)
        else:
            beside = side[pl.ds(l * height, height), :]
            columns = (beside[:, 0:1], beside[:, 1:2])
        sides = beside_rows(x, *rows) + beside_columns(x, *columns)
        fresh = x + change_of(x, sides, block(u_ref, l), block(v_ref, l), upper, lower, nest)
        if nest:
            fresh = fresh - NUDGING * x if fine is None else fresh + NUDGING * (block(fine, l) - x)
        store_level(out_ref, height, l, fresh)


def inner_line(height, row):
    return jnp.where(row == 0, height - 1, 0)


def edge_level(ref, height, lev):
    last = ref.shape[1] // height - 1
    return jnp.where(lev == 0, load_level(ref, height, last), load_level(ref, height, 0))


def pack_kernel(
    levels,
    west_hbm,
    south_hbm,
    air_hbm,
    north_hbm,
    rows_ref,
    own_ref,
    edges_ref,
    level_ref,
    west_ref,
    south_ref,
    air_ref,
    north_ref,
    sems,
):
    pieces, size, _ = air_ref.shape
    height, breadth = level_ref.shape
    third_y = height // 3
    slots = own_ref.shape[0] - 1
    tile, row, lev = place()
    nest = tile == lax.axis_size("tiles") - 1

    def column_copies(source, target, first):
        return [
            pltpu.make_async_copy(source.at[:, pl.ds(c * LANES, LANES)], target.at[c], sems.at[first + c])
            for c in range(pieces)
        ]

    copies = column_copies(air_hbm, air_ref, 0)
    copies.append(pltpu.make_async_copy(west_hbm, west_ref, sems.at[2 * pieces]))
    copies.append(pltpu.make_async_copy(south_hbm, south_ref, sems.at[2 * pieces + 1]))
    speeds = column_copies(north_hbm, north_ref, pieces)
    for copy in copies + speeds:
        copy.start()
    for copy in copies + speeds:
        copy.wait()
    inner = inner_line(height, row)
    level_ref[...] = edge_level(air_ref, height, lev)
    store_slabs(rows_ref, slots + 1, load_line(air_ref, levels, inner))

    @pl.when(nest)
    def _():
        speed = load_line(north_ref, levels, inner)
        store_slabs(rows_ref, 0, speed)
        for i in range(pieces, slots + 1):
            rows_ref[i] = jnp.zeros((levels, LANES), jnp.float32)
        store_slabs(own_ref, 0, load_line(north_ref, levels, height - 1 - inner))
        store_slabs(own_ref, pieces, speed)
        edges_ref[...] = jnp.zeros_like(edges_ref)

    @pl.when(jnp.logical_not(nest))
    def _():
        start = west_ref[0] - tile * breadth
        top = south_ref[0] - 1 - row * height
        part = rows_ref.at[pl.ds(0, slots + 1)]
        pack_window(part, air_ref, levels, top + (1 - row) * third_y, start)
        pack_window(own_ref, air_ref, levels, top + row * third_y, start)
        edges_ref[...] = pack_edges(air_ref, levels)


def early_kernel(
    levels,
    west_ref,
    south_ref,
    air_ref,
    east_ref,
    north_ref,
    rows_ref,
    level_ref,
    even_ref,
    odd_ref,
    speeds_ref,
    field_ref,
    own_ref,
    other_ref,
    coef_ref,
    side_ref,
    northern_ref,
    southern_ref,
):
    size, breadth = air_ref.shape
    height = size // levels
    third_y = height // 3
    pieces = breadth // LANES
    slots = own_ref.shape[0] - 1
    tile_count = lax.axis_size("tiles")
    tile, row, lev = place()
    nest = tile == tile_count - 1
    halo = join_slabs(rows_ref, slots + 1, pieces)
    zero = jnp.zeros_like(halo)
    northern_ref[...] = jnp.where(row == 0, zero, halo)
    southern_ref[...] = jnp.where(row == 0, halo, zero)
    shared = (field_ref, air_ref, east_ref, north_ref, level_ref, levels, lev)

    @pl.when(nest)
    def _():
        full_step(*shared, True, northern_ref, southern_ref, None, None)
        ghost = ghost_weight(join_slabs(speeds_ref, 0, pieces), row == 0)
        cell, third = iota((breadth, 3 * LANES), 0), iota((breadth, 3 * LANES), 1)
        kind = third // LANES
        offset = cell - 3 * (third - kind * LANES)
        middle = jnp.where(offset == 1, 3, jnp.where((offset == 0) | (offset == 2), 2, 0))
        weight = jnp.where(kind == 1, middle, jnp.where(offset == kind, 1, 0))
        store_slabs(coef_ref, 0, from_right(ghost, table(weight)) * (1.0 / 27.0))
        shape = (size, LANES)
        lane = iota(shape, 1)
        _, line = split_level(iota(shape, 0), height)
        block = lane // 8
        inside = lane - block * 8
        eastern = inside >= 3
        kind = jnp.where(eastern, inside - 3, inside)
        offset = line - 3 * block
        middle = jnp.where(offset == 1, 3, jnp.where((offset == 0) | (offset == 2), 2, 0))
        weight = jnp.where(kind == 1, middle, jnp.where(offset == kind, 1, 0))
        weight = jnp.where((inside < 6) & (block < third_y), weight, 0).astype(jnp.float32)
        first = ghost_weight(east_ref[:, 0:1], True)
        last = ghost_weight(east_ref[:, breadth - 1 : breadth], False)
        columns = jnp.where(eastern, last, first) * weight
        coef_ref[3] = from_left(level_table(levels, height), columns) * (1.0 / 27.0)
        own_ref[...] = jnp.zeros_like(own_ref)
        other_ref[...] = jnp.zeros_like(other_ref)

    @pl.when(jnp.logical_not(nest))
    def _():
        columns = neighbour_columns(even_ref[...], odd_ref[...], tile_count - 1, tile)
        side_ref[...] = unpack_edges(columns, levels, height)
        full_step(*shared, False, northern_ref, southern_ref, side_ref, None)
        start = west_ref[1] - tile * breadth
        top = south_ref[1] - 1 - row * height
        pack_window(other_ref, field_ref, levels, top + (1 - row) * third_y, start)
        pack_window(own_ref, field_ref, levels, top + row * third_y, start)
        coef_ref[...] = jnp.zeros_like(coef_ref)


def first_kernel(
    levels, early_ref, east_ref, speeds_ref, one_ref, two_ref, three_ref, own_ref, other_ref, field_ref, edge_ref, window_ref
):
    pieces, size, _ = early_ref.shape
    height, breadth = edge_ref.shape
    slots = own_ref.shape[0] - 1
    tile, row, lev = place()
    nest = tile == lax.axis_size("tiles") - 1

    @pl.when(jnp.logical_not(nest))
    def _():
        window_ref[...] = own_ref[...] + other_ref[...]
        edge_ref[...] = jnp.zeros_like(edge_ref)

    @pl.when(nest)
    def _():
        slabs = [one_ref[s] + two_ref[s] + three_ref[s] for s in range(slots + 1)]
        cells, ring = refine(slabs[:slots], slabs[slots], height, breadth, row)
        lane = iota((size, LANES), 1)
        for c in range(pieces):
            piece = slice(c * LANES, (c + 1) * LANES)
            value = early_ref[c] + NUDGING * cells[:, piece]
            if c == 0:
                ghost = ghost_weight(east_ref[:, piece], True) * cells[:, breadth : breadth + 1]
                value = value + jnp.where(lane == 0, ghost, 0.0)
            if c == pieces - 1:
                ghost = ghost_weight(east_ref[:, piece], False) * cells[:, breadth + 1 : breadth + 2]
                value = value + jnp.where(lane == LANES - 1, ghost, 0.0)
            field_ref[c] = value
        outer = height - 1 - inner_line(height, row)
        ghost = ghost_weight(join_slabs(speeds_ref, 0, pieces), row == 0) * ring
        store_line(field_ref, levels, outer, load_line(field_ref, levels, outer) + ghost)
        edge_ref[...] = edge_level(field_ref, height, lev)


def average_kernel(
    levels, field_ref, east_ref, north_ref, rows_ref, level_ref, coef_ref, window_ref, message_ref, part_ref
):
    pieces, size, _ = field_ref.shape
    height, breadth = level_ref.shape
    third_y = height // 3
    tile, row, lev = place()
    nest = tile == lax.axis_size("tiles") - 1

    @pl.when(jnp.logical_not(nest))
    def _():
        slots = window_ref.shape[0]
        message_ref[pl.ds(0, slots)] = window_ref[...]
        for i in range(slots, message_ref.shape[0]):
            message_ref[i] = jnp.zeros((levels, LANES), jnp.float32)

    @pl.when(nest)
    def _():
        full_step(part_ref, field_ref, east_ref, north_ref, level_ref, levels, lev, True, None, None, None, None)
        cell, third = iota((breadth, LANES), 0), iota((breadth, LANES), 1)
        offset = cell - 3 * third
        sums = table((offset >= 0) & (offset <= 2))
        shape = (third_y * levels, size)
        taken = iota(shape, 0)
        block = taken // levels
        level, line = split_level(iota(shape, 1), height)
        offset = line - 3 * block
        rows = table((taken - block * levels == level) & (offset >= 0) & (offset <= 2))
        means = from_left(rows, from_right(part_ref[...], sums)) * (1.0 / 9.0)
        for m in range(third_y):
            message_ref[m] = means[m * levels : (m + 1) * levels]
        message_ref[pl.ds(third_y, 4)] = coef_ref[...]
        shared = load_line(field_ref, levels, inner_line(height, row))
        shared = ghost_weight(join_slabs(rows_ref, 0, pieces), row == 0) * shared
        message_ref[third_y + 4] = from_right(shared, sums) * (1.0 / 9.0)


def blend_kernel(levels, weight_ref, field_ref, window_ref, one_ref, two_ref, three_ref, rows_ref):
    pieces, size, _ = field_ref.shape
    height = size // levels
    third_y = height // 3
    slots = third_y + 2
    tile_count = lax.axis_size("tiles")
    tile, row, _ = place()
    nest = tile == tile_count - 1

    @pl.when(nest)
    def _():
        store_slabs(rows_ref, 0, load_line(field_ref, levels, inner_line(height, row)))
        for i in range(pieces, rows_ref.shape[0]):
            rows_ref[i] = jnp.zeros((levels, LANES), jnp.float32)

    @pl.when(jnp.logical_not(nest))
    def _():
        def mine(i):
            return jnp.where(tile == 0, three_ref[i], jnp.where(tile == 1, two_ref[i], one_ref[i]))

        def whole(i):
            odd = tile % 2 == 1
            west = jnp.where(odd, one_ref[i], three_ref[i])
            east = jnp.where(odd, three_ref[i], one_ref[i])
            part = jnp.where(tile == 0, window_ref[i], window_ref[i] + west)
            return jnp.where(tile == tile_count - 2, part, part + east)

        weight = weight_ref[:, 0:1]
        extra = whole(slots)
        lane = iota(extra.shape, 1)
        at_first, at_last = lane == 0, lane == LANES - 1
        lines = []
        for s in range(slots):
            x = whole(s)
            west = jnp.where(at_first, extra[:, s : s + 1], pltpu.roll(x, 1, 1))
            last = EAST_LANE + s
            east = jnp.where(at_last, extra[:, last : last + 1], pltpu.roll(x, LANES - 1, 1))
            lines.append((west, x, east))
        edges = mine(third_y + 3)
        ghosts = [mine(third_y + q) for q in range(3)]

        def outward(side, q):
            near = lines[1] if side == 0 else lines[slots - 2]
            far = lines[0] if side == 0 else lines[slots - 1]
            return (2.0 / 3.0) * far[q] + (1.0 / 3.0) * near[q]

        def sideward(s):
            west, x, east = lines[s]
            return (2.0 / 3.0) * jnp.where(at_first, west, east) + (1.0 / 3.0) * x

        sidewards = [sideward(s) for s in range(slots)]
        columns = [w + 7.0 * x + e for w, x, e in lines]
        for m in range(third_y):
            x = lines[m + 1][1]
            value = mine(m) + (NUDGING / 81.0) * (columns[m] + 7.0 * columns[m + 1] + columns[m + 2])
            for q in range(3):
                lane_of = 8 * m + q
                first, last = edges[:, lane_of : lane_of + 1], edges[:, lane_of + 3 : lane_of + 4]
                scale = jnp.where(at_first, first, jnp.where(at_last, last, 0.0))
                value = value + scale * sidewards[m + q]
            for side, at in ((0, 0), (1, third_y - 1)):
                if m == at:
                    for q in range(3):
                        value = value + jnp.where(row == side, ghosts[q], 0.0) * outward(side, q)
            rows_ref[m] = x + weight * (value - x)
        rows_ref[third_y] = weight * mine(third_y + 4)


def later_kernel(
    levels,
    field_ref,
    east_ref,
    north_ref,
    level_ref,
    one_ref,
    two_ref,
    three_ref,
    out_ref,
    fine_ref,
    side_ref,
    northern_ref,
    southern_ref,
):
    height, breadth = level_ref.shape
    slots = height // 3 + 2
    tile, row, lev = place()

    @pl.when(tile == lax.axis_size("tiles") - 1)
    def _():
        slabs = [one_ref[s] + two_ref[s] + three_ref[s] for s in range(slots + 1)]
        cells, ring = refine(slabs[:slots], slabs[slots], height, breadth, row)
        fine_ref[...] = cells[:, :breadth]
        side_ref[...] = cells[:, breadth:]
        zero = jnp.zeros_like(ring)
        northern_ref[...] = jnp.where(row == 0, ring, zero)
        southern_ref[...] = jnp.where(row == 0, zero, ring)
        full_step(
            out_ref,
            field_ref,
            east_ref,
            north_ref,
            level_ref,
            levels,
            lev,
            True,
            northern_ref,
            southern_ref,
            side_ref,
            fine_ref,
        )


def last_kernel(
    levels, west_ref, south_ref, parent_ref, nested_ref, speeds_ref, blend_ref, rows_ref, out_hbm, out_ref, sems
):
    pieces, size, _ = parent_ref.shape
    breadth = pieces * LANES
    height = size // levels
    third_y = height // 3
    tile, row, _ = place()
    nest = tile == lax.axis_size("tiles") - 1

    @pl.when(nest)
    def _():
        out_ref[...] = nested_ref[...]
        inner = inner_line(height, row)
        halo = ghost_weight(join_slabs(speeds_ref, pieces, pieces), row == 1) * join_slabs(rows_ref, 0, pieces)
        store_line(out_ref, levels, inner, load_line(out_ref, levels, inner) + halo)

    @pl.when(jnp.logical_not(nest))
    def _():
        out_ref[...] = parent_ref[...]
        start = west_ref[1] - tile * breadth
        top = south_ref[1] - row * height
        lane = iota((levels, breadth), 1)
        inside = (lane >= start) & (lane < start + LANES)
        turn = lax.rem(start + 4 * breadth, breadth)
        empty = jnp.zeros((levels, breadth - LANES), jnp.float32)
        for block in range(2):
            for m in range(third_y):
                line = top + block * third_y + m

                @pl.when((line >= 0) & (line < height))
                def _():
                    value = jnp.where(row == block, blend_ref[m], rows_ref[m])
                    if m == (third_y - 1 if block == 0 else 0):
                        value = value + jnp.where(row == block, rows_ref[third_y], blend_ref[third_y])
                    wide = pltpu.roll(jnp.concatenate([value, empty], axis=1), turn, 1)
                    kept = load_line(out_ref, levels, line)
                    store_line(out_ref, levels, line, jnp.where(inside, wide, kept))

    copies = [
        pltpu.make_async_copy(out_ref.at[c], out_hbm.at[:, pl.ds(c * LANES, LANES)], sems.at[c])
        for c in range(pieces)
    ]
    for copy in copies:
        copy.start()
    for copy in copies:
        copy.wait()


def call(kernel, outs, inputs, places, scratch=(), flops=0, out_place="v"):
    spaces = {"s": pltpu.SMEM, "v": pltpu.VMEM, "h": pltpu.HBM}
    moved = sum(4 * math.prod(shape) for shape in outs) + sum(array.nbytes for array in inputs)
    return pl.pallas_call(
        kernel,
        out_shape=[jax.ShapeDtypeStruct(shape, jnp.float32) for shape in outs],
        in_specs=[pl.BlockSpec(memory_space=spaces[p]) for p in places],
        out_specs=[pl.BlockSpec(memory_space=spaces[out_place])] * len(outs),
        scratch_shapes=[pltpu.VMEM(s, jnp.float32) if isinstance(s, tuple) else s for s in scratch],
        compiler_params=pltpu.CompilerParams(vmem_limit_bytes=32 * 1024 * 1024),
        cost_estimate=pl.CostEstimate(flops=flops, bytes_accessed=moved, transcendentals=0),
    )(*inputs)


def per_device_paired(air_state, wind_east, wind_north, feedback_weight, nest_west, nest_south):
    levels, height, breadth = air_state.shape
    third_y = height // 3
    pieces = breadth // LANES
    slots = third_y + 2
    tile_count = lax.axis_size("tiles")
    size = levels * height
    flat = (size, breadth)
    chunked = (pieces, size, LANES)
    air, east, north = (array.reshape(flat) for array in (air_state, wind_east, wind_north))
    weight = jnp.broadcast_to(feedback_weight[:, None], (levels, LANES))
    swap = [(0, 1), (1, 0)]
    last = tile_count - 1
    near = [(0, 1), (1, 0)]
    across = [(1, 2), (2, 1)]

    def slabs(count):
        return (count, levels, LANES)

    def kernel(body):
        return functools.partial(body, levels)

    rows, own, edges, level = call(
        kernel(pack_kernel),
        [slabs(slots + 1 + pieces), slabs(slots + 1), (levels, LANES), (height, breadth)],
        [nest_west, nest_south, air, north],
        "hhhh",
        [
            pltpu.SMEM((2,), jnp.int32),
            pltpu.SMEM((2,), jnp.int32),
            chunked,
            chunked,
            pltpu.SemaphoreType.DMA((2 * pieces + 2,)),
        ],
    )
    rows = lax.ppermute(rows, "rows", swap)
    even = lax.ppermute(edges, "tiles", near)
    odd = lax.ppermute(edges, "tiles", across)
    level = lax.ppermute(level, "lev", swap)
    window = own + rows[: slots + 1]
    speeds = own
    received = [lax.ppermute(window, "tiles", [(last - step, last)]) for step in (1, 2, 3)]
    sides = [(size, LANES), (levels, breadth), (levels, breadth)]
    early, own, other, coef = call(
        kernel(early_kernel),
        [chunked, slabs(slots + 1), slabs(slots + 1), slabs(4)],
        [nest_west, nest_south, air, east, north, rows, level, even, odd, speeds],
        "ssvvvvvvvv",
        sides,
        flops=30 * size * breadth,
    )
    other = lax.ppermute(other, "rows", swap)
    first, edge, window = call(
        kernel(first_kernel),
        [chunked, (height, breadth), slabs(slots + 1)],
        [early, east, speeds, *received, own, other],
        "vvvvvvvv",
    )
    level = lax.ppermute(edge, "lev", swap)
    (message,) = call(
        kernel(average_kernel),
        [slabs(third_y + 5)],
        [first, east, north, rows, level, coef, window],
        "vvvvvvv",
        [flat],
    )
    pairs = [[(0, 1), (1, 0), (2, 3), (3, 2)], [(1, 3), (3, 1)], [(0, 3), (3, 0), (1, 2), (2, 1)]]
    received = [lax.ppermute(message, "tiles", pair) for pair in pairs]
    (blend,) = call(
        kernel(blend_kernel),
        [slabs(third_y + 1)],
        [weight, first, window, *received],
        "vvvvvv",
    )
    rows = lax.ppermute(blend, "rows", swap)
    (later,) = call(
        kernel(later_kernel),
        [chunked],
        [first, east, north, level, *received],
        "vvvvvvv",
        [flat, *sides],
        flops=30 * size * breadth,
    )
    (out,) = call(
        kernel(last_kernel),
        [flat],
        [nest_west, nest_south, early, later, speeds, blend, rows],
        "ssvvvvv",
        [chunked, pltpu.SemaphoreType.DMA((pieces,))],
        out_place="h",
    )
    return out.reshape(air_state.shape)


def solution(mesh):
    in_specs = (
        P(("members", "lev"), "rows", "tiles"),
        P(("members", "lev"), "rows", "tiles"),
        P(("members", "lev"), "rows", "tiles"),
        P("lev"),
        P("members"),
        P("members"),
    )
    out_specs = P(("members", "lev"), "rows", "tiles")
    paired = mesh.shape["tiles"] == 4 and mesh.shape["rows"] == 2 and mesh.shape["lev"] == 2
    return jax.shard_map(
        per_device_paired if paired else per_device, mesh=mesh, in_specs=in_specs, out_specs=out_specs, check_vma=False
    )
```

```python
import functools
import math

import jax
import jax.numpy as jnp
from jax import lax
from jax.experimental import pallas as pl
from jax.experimental.pallas import tpu as pltpu
from jax.sharding import PartitionSpec as P

VERTICAL_MIX = 0.1
PARENT_MIXING = 0.04
NEST_MIXING = 0.18
NEST_ADVECT = 1.5
NUDGING = 0.2


def padded_2(array, sides, width):
    for axis, dim in sides:
        size, length = (lax.axis_size(axis), array.shape[dim])
        up = [(i, (i + 1) % size) for i in range(size - 1)]
        down = [(j, i) for i, j in up]
        last = lax.slice_in_dim(array, length - width, length, axis=dim)
        first = lax.slice_in_dim(array, 0, width, axis=dim)
        before = lax.ppermute(last, axis, up)
        after = lax.ppermute(first, axis, down)
        array = jnp.concatenate([before, array, after], axis=dim)
    return array


def interp_table(cells):
    extended = jnp.arange(cells + 2, dtype=jnp.int32) - 1
    coarse = jnp.floor_divide(extended, 3)
    offset = extended - 3 * coarse
    fraction = jnp.abs(offset - 1).astype(jnp.float32) / 3.0
    nearest = coarse + 1
    beside = nearest + (offset - 1)
    slots = jnp.arange(cells // 3 + 2, dtype=jnp.int32)[:, None]
    first_part = jnp.where(
        slots == nearest[None, :], 1.0 - fraction[None, :], jnp.zeros((), jnp.float32)
    )
    second_part = jnp.where(slots == beside[None, :], fraction[None, :], jnp.zeros((), jnp.float32))
    return first_part + second_part


def tendency(padded, speed_east, speed_north, advect_scale, mixing_scale):
    centre = padded[1:-1, 1:-1, 1:-1]
    eastern = padded[1:-1, 1:-1, 2:]
    western = padded[1:-1, 1:-1, :-2]
    southern = padded[1:-1, 2:, 1:-1]
    northern = padded[1:-1, :-2, 1:-1]
    upper = padded[2:, 1:-1, 1:-1]
    lower = padded[:-2, 1:-1, 1:-1]
    advect = speed_east * (eastern - western) + speed_north * (southern - northern)
    horizontal = eastern + western + southern + northern - 4.0 * centre
    vertical = upper + lower - 2.0 * centre
    return -0.5 * advect_scale * advect + mixing_scale * horizontal + VERTICAL_MIX * vertical


def padded_block(block_field):
    return padded_2(block_field, (("tiles", 2), ("rows", 1), ("lev", 0)), 1)


def per_device(air_state, wind_east, wind_north, feedback_weight, nest_west, nest_south):
    levels, height, breadth = air_state.shape
    tile_count = lax.axis_size("tiles")
    row_count = lax.axis_size("rows")
    tile_index = lax.axis_index("tiles")
    row_index = lax.axis_index("rows")
    parent_tiles = 3 * tile_count // 4
    nest_tiles = tile_count - parent_tiles
    in_nest = tile_index >= parent_tiles
    nest_tile = tile_index - parent_tiles
    cross_x = breadth // 3 + 2
    cross_y = height // 3 + 2
    third_x = breadth // 3
    third_y = height // 3
    first_x = tile_index * breadth
    first_y = row_index * height
    columns = jnp.arange(breadth, dtype=jnp.int32)
    lines = jnp.arange(height, dtype=jnp.int32)
    targets_x = jnp.arange(tile_count, dtype=jnp.int32)
    targets_y = jnp.arange(row_count, dtype=jnp.int32)
    highest = lax.Precision.HIGHEST
    table_x = interp_table(breadth)
    table_y = interp_table(height)
    zero_value = jnp.zeros((), jnp.float32)

    def boundary(source, substep):
        anchor_x = nest_west[substep] + (targets_x - parent_tiles) * third_x - 1
        slot_x = jnp.arange(cross_x, dtype=jnp.int32)
        pick_x = (
            (first_x + columns)[None, :, None] == anchor_x[:, None, None] + slot_x[None, None, :]
        ) & (targets_x >= parent_tiles)[:, None, None]
        pick_x = pick_x.astype(jnp.float32)
        anchor_y = nest_south[substep] + targets_y * third_y - 1
        slot_y = jnp.arange(cross_y, dtype=jnp.int32)
        pick_y = (
            (first_y + lines)[None, :, None] == anchor_y[:, None, None] + slot_y[None, None, :]
        ).astype(jnp.float32)
        pieces = jnp.einsum("lyi,tij->tlyj", source, pick_x, precision=highest)
        merged = lax.all_to_all(pieces, "tiles", split_axis=0, concat_axis=0, tiled=True).sum(
            axis=0
        )
        pieces = jnp.einsum("lyj,ryw->rlwj", merged, pick_y, precision=highest)
        window = lax.all_to_all(pieces, "rows", split_axis=0, concat_axis=0, tiled=True).sum(axis=0)
        along = jnp.einsum("lwj,je->lwe", window, table_x, precision=highest)
        return jnp.einsum("lwe,wf->lfe", along, table_y, precision=highest)

    def assemble(block_field, fine):
        padded = padded_block(block_field)
        fine_padded = jnp.pad(fine, ((1, 1), (0, 0), (0, 0)))
        column_place = lax.broadcasted_iota(jnp.int32, padded.shape, 2)
        line_place = lax.broadcasted_iota(jnp.int32, padded.shape, 1)
        outside = (column_place == 0) & (nest_tile == 0) | (column_place == breadth + 1) & (
            nest_tile == nest_tiles - 1
        )
        outside = (
            outside
            | (line_place == 0) & (row_index == 0)
            | (line_place == height + 1) & (row_index == row_count - 1)
        )
        padded = jnp.where(outside & in_nest, fine_padded, padded)
        seam_cells = (column_place == breadth + 1) & (tile_index == parent_tiles - 1)
        return jnp.where(seam_cells, zero_value, padded)

    advect_scale = jnp.where(in_nest, jnp.float32(NEST_ADVECT), jnp.float32(1.0))
    mixing_scale = jnp.where(in_nest, jnp.float32(NEST_MIXING), jnp.float32(PARENT_MIXING))
    fine_first = boundary(air_state, 0)
    change = tendency(
        assemble(air_state, fine_first), wind_east, wind_north, advect_scale, mixing_scale
    )
    nudging_term = jnp.where(in_nest, NUDGING * (fine_first[:, 1:-1, 1:-1] - air_state), zero_value)
    step_one = air_state + change + nudging_term
    fine_second = boundary(step_one, 1)
    change = tendency(
        assemble(step_one, fine_second), wind_east, wind_north, advect_scale, mixing_scale
    )
    nested_two = step_one + change + NUDGING * (fine_second[:, 1:-1, 1:-1] - step_one)
    step_two = jnp.where(in_nest, nested_two, step_one)
    coarse = step_two.reshape(levels, third_y, 3, third_x, 3).mean(axis=(2, 4))
    avg_columns = jnp.arange(third_x, dtype=jnp.int32)
    avg_lines = jnp.arange(third_y, dtype=jnp.int32)
    west_last = nest_west[1]
    south_last = nest_south[1]
    place_x = (
        (west_last + (targets_x - parent_tiles) * third_x)[:, None, None]
        + avg_columns[None, :, None]
        == (first_x + columns)[None, None, :]
    ) & (targets_x >= parent_tiles)[:, None, None]
    place_x = place_x.astype(jnp.float32)
    place_y = (
        (south_last + targets_y * third_y)[:, None, None] + avg_lines[None, :, None]
        == (first_y + lines)[None, None, :]
    ).astype(jnp.float32)
    parent_y = south_last + row_index * third_y + avg_lines
    send_y = (jnp.floor_divide(parent_y, height)[None, :] == targets_y[:, None]) & in_nest
    pieces = jnp.where(send_y[:, None, :, None], coarse[None], zero_value)
    received = lax.all_to_all(pieces, "rows", split_axis=0, concat_axis=0, tiled=True)
    spread = jnp.einsum("slba,sby->lya", received, place_y, precision=highest)
    parent_x = west_last + nest_tile * third_x + avg_columns
    send_x = jnp.floor_divide(parent_x, breadth)[None, :] == targets_x[:, None]
    pieces = jnp.where(send_x[:, None, None, :], spread[None], zero_value)
    received = lax.all_to_all(pieces, "tiles", split_axis=0, concat_axis=0, tiled=True)
    placed = jnp.einsum("slya,sai->lyi", received, place_x, precision=highest)
    global_x = (first_x + columns)[None, None, :]
    global_y = (first_y + lines)[None, :, None]
    covered = (global_x >= west_last) & (global_x < west_last + nest_tiles * third_x)
    covered = covered & (global_y >= south_last) & (global_y < south_last + row_count * third_y)
    covered = covered & jnp.logical_not(in_nest)
    blended = step_two + feedback_weight[:, None, None] * (placed - step_two)
    return jnp.where(covered, blended, step_two)


LANES = 128
FIRST_LANE = 32
LAST_LANE = 96
EAST_LANE = 64


def iota(shape, dim):
    return lax.broadcasted_iota(jnp.int32, shape, dim)


def split_level(place, height):
    level = ((place.astype(jnp.float32) + 0.5) * (1.0 / height)).astype(jnp.int32)
    return level, place - level * height


def table(values):
    return values.astype(jnp.float32).astype(jnp.bfloat16)


def parts_of(array):
    high = array.astype(jnp.bfloat16)
    low = (array - high.astype(jnp.float32)).astype(jnp.bfloat16)
    return high, low


def dot(left, right):
    return jnp.dot(left, right, preferred_element_type=jnp.float32)


def from_left(weights, array):
    high, low = parts_of(array)
    return dot(weights, high) + dot(weights, low)


def from_right(array, weights):
    high, low = parts_of(array)
    return dot(high, weights) + dot(low, weights)


def hat(distance):
    return jnp.maximum(0, 3 - jnp.abs(distance - 1))


def place():
    return lax.axis_index("tiles"), lax.axis_index("rows"), lax.axis_index("lev")


def level_table(levels, height):
    shape = (levels, levels * height)
    level, _ = split_level(iota(shape, 1), height)
    return table(iota(shape, 0) == level)


def spread_table(levels, height):
    shape = (levels * height, levels)
    level, _ = split_level(iota(shape, 0), height)
    return table(iota(shape, 1) == level)


def load_line(ref, levels, line):
    rows = pl.ds(line, levels, stride=ref.shape[1] // levels)
    return jnp.concatenate([ref[c, rows, :] for c in range(ref.shape[0])], axis=1)


def store_line(ref, levels, line, value):
    rows = pl.ds(line, levels, stride=ref.shape[1] // levels)
    for c in range(ref.shape[0]):
        ref[c, rows, :] = value[:, c * LANES : (c + 1) * LANES]


def load_level(ref, height, l):
    rows = pl.ds(l * height, height)
    if len(ref.shape) == 2:
        return ref[rows, :]
    return jnp.concatenate([ref[c, rows, :] for c in range(ref.shape[0])], axis=1)


def store_level(ref, height, l, value):
    rows = pl.ds(l * height, height)
    if len(ref.shape) == 2:
        ref[rows, :] = value
    else:
        for c in range(ref.shape[0]):
            ref[c, rows, :] = value[:, c * LANES : (c + 1) * LANES]


def store_slabs(ref, first, wide):
    for i in range(wide.shape[1] // LANES):
        ref[first + i] = wide[:, i * LANES : (i + 1) * LANES]


def join_slabs(ref, first, count):
    return jnp.concatenate([ref[first + i] for i in range(count)], axis=1)


def column_pieces(start, pieces):
    first = (start + 64 * LANES) // LANES - 64
    offset = start - first * LANES
    held = [(c >= 0) & (c < pieces) for c in (first, first + 1)]
    return [jnp.clip(c, 0, pieces - 1) for c in (first, first + 1)], held, offset


def pack_window(ref, field_ref, levels, top, start):
    pieces, size, _ = field_ref.shape
    height = size // levels
    slots = ref.shape[0] - 1
    lane = iota((levels, LANES), 1)
    (left, right), (left_held, right_held), offset = column_pieces(start, pieces)
    before = lax.rem(offset + LANES - 1, LANES)
    (beside, _), (beside_held, _), _ = column_pieces(start - 1, pieces)
    in_left = lane < LANES - offset
    held = jnp.where(in_left, left_held.astype(jnp.float32), right_held.astype(jnp.float32))
    west_held, east_held = beside_held.astype(jnp.float32), right_held.astype(jnp.float32)
    turn = lax.rem(LANES - offset, LANES)
    extra = jnp.zeros((levels, LANES), jnp.float32)
    for slot in range(slots):
        line = top + slot
        there = ((line >= 0) & (line < height)).astype(jnp.float32)
        rows = pl.ds(jnp.clip(line, 0, height - 1), levels, stride=height)
        near, far, west = field_ref[left, rows, :], field_ref[right, rows, :], field_ref[beside, rows, :]
        ref[slot] = jnp.where(in_left, pltpu.roll(near, turn, 1), pltpu.roll(far, turn, 1)) * (held * there)
        west = pltpu.roll(west, lax.rem(LANES + slot - before, LANES), 1) * (west_held * there)
        east = pltpu.roll(far, lax.rem(LANES + EAST_LANE + slot - offset, LANES), 1) * (east_held * there)
        extra = jnp.where(lane == slot, west, jnp.where(lane == EAST_LANE + slot, east, extra))
    ref[slots] = extra


def place_row(ref, levels, line, start, value):
    pieces, size, _ = ref.shape
    height = size // levels
    lane = iota((levels, LANES), 1)
    at, held, offset = column_pieces(start, pieces)
    value = pltpu.roll(value, offset, 1)
    there = (line >= 0) & (line < height)
    rows = pl.ds(jnp.clip(line, 0, height - 1), levels, stride=height)
    for c in range(2):
        mine = (lane >= offset) if c == 0 else (lane < offset)
        ref[at[c], rows, :] = jnp.where(mine & (held[c] & there), value, ref[at[c], rows, :])


def pack_edges(field_ref, levels):
    height = field_ref.shape[1] // levels
    lane = iota((levels, LANES), 1)
    packed = jnp.zeros((levels, LANES), jnp.float32)
    for line in range(height):
        rows = pl.ds(line, levels, stride=height)
        first = field_ref[0, rows, :]
        last = field_ref[field_ref.shape[0] - 1, rows, :]
        packed = jnp.where(lane == FIRST_LANE + line, pltpu.roll(first, FIRST_LANE + line, 1), packed)
        packed = jnp.where(lane == LAST_LANE + line, pltpu.roll(last, LAST_LANE + line + 1, 1), packed)
    return packed


def neighbour_columns(even, odd, parent_tiles, tile):
    is_odd = tile % 2 == 1
    west = jnp.where(is_odd, even, odd)
    east = jnp.where(is_odd, odd, even)
    west = jnp.where(tile == 0, jnp.zeros_like(west), west)
    east = jnp.where(tile >= parent_tiles - 1, jnp.zeros_like(east), east)
    return jnp.where(iota(west.shape, 1) < LAST_LANE, east, west)


def unpack_edges(columns, levels, height):
    wide = from_left(spread_table(levels, height), columns)
    lane = iota(wide.shape, 1)
    _, line = split_level(iota(wide.shape, 0), height)
    west = jnp.sum(jnp.where(lane == line + LAST_LANE, wide, 0.0), axis=1, keepdims=True)
    east = jnp.sum(jnp.where(lane == line + FIRST_LANE, wide, 0.0), axis=1, keepdims=True)
    return jnp.where(lane == 0, west, jnp.where(lane == 1, east, 0.0))


def refine(slabs, extra, height, breadth, row):
    slots, levels = len(slabs), extra.shape[0]
    beside = [pltpu.roll(extra, LANES - s, 1) if s else extra for s in range(slots)]
    window = jnp.concatenate([jnp.concatenate(slabs, axis=0), jnp.concatenate(beside, axis=0)], axis=1)
    shape = (2 * LANES, breadth + LANES)
    slot, cell = iota(shape, 0), iota(shape, 1)
    held = (slot <= LANES) | (slot == LANES + EAST_LANE)
    at = jnp.where(slot < LANES, slot, jnp.where(slot == LANES, -1, LANES))
    cell = jnp.where(cell == breadth, -1, jnp.where(cell == breadth + 1, breadth, cell))
    across = jnp.where(held & (cell <= breadth), hat(cell - 3 * at), 0)
    wide = from_right(window, table(across)) * (1.0 / 9.0)
    shape = (levels * height, slots * levels)
    taken = iota(shape, 1)
    slot = taken // levels
    level, line = split_level(iota(shape, 0), height)
    along = jnp.where(taken - slot * levels == level, hat(line - 3 * (slot - 1)), 0)
    cells = from_left(table(along), wide)
    ring = jnp.where(
        row == 0,
        2.0 * wide[:levels] + wide[levels : 2 * levels],
        2.0 * wide[(slots - 1) * levels :] + wide[(slots - 2) * levels : (slots - 1) * levels],
    )
    return cells, ring[:, :breadth]


def beside_rows(x, north, south):
    height = x.shape[0]
    line = iota(x.shape, 0)
    northern = jnp.where(line == 0, north, pltpu.roll(x, 1, 0))
    southern = jnp.where(line == height - 1, south, pltpu.roll(x, height - 1, 0))
    return northern, southern


def beside_columns(x, west, east):
    breadth = x.shape[1]
    column = iota(x.shape, 1)
    western = jnp.where(column == 0, west, pltpu.roll(x, 1, 1))
    eastern = jnp.where(column == breadth - 1, east, pltpu.roll(x, breadth - 1, 1))
    return western, eastern


def change_of(x, sides, u, v, upper, lower, nest):
    advect_scale = NEST_ADVECT if nest else 1.0
    mixing_scale = NEST_MIXING if nest else PARENT_MIXING
    northern, southern, western, eastern = sides
    advect = u * (eastern - western) + v * (southern - northern)
    horizontal = eastern + western + southern + northern - 4.0 * x
    vertical = upper + lower - 2.0 * x
    return -0.5 * advect_scale * advect + mixing_scale * horizontal + VERTICAL_MIX * vertical


def ghost_weight(speed, before):
    return jnp.where(before, 0.5 * NEST_ADVECT, -0.5 * NEST_ADVECT) * speed + NEST_MIXING


def full_step(out_ref, field_ref, u_ref, v_ref, level_ref, levels, lev, nest, north, south, side, fine):
    height, breadth = level_ref.shape
    zero = jnp.zeros((height, breadth), jnp.float32)

    def block(ref, l):
        return load_level(ref, height, l)

    for l in range(levels):
        x = block(field_ref, l)
        lower = block(field_ref, l - 1) if l else jnp.where(lev == 1, level_ref[...], zero)
        upper = block(field_ref, l + 1) if l < levels - 1 else jnp.where(lev == 0, level_ref[...], zero)
        rows = [0.0 if ref is None else ref[pl.ds(l, 1), :] for ref in (north, south)]
        if side is None:
            columns = (0.0, 0.0)
        else:
            beside = side[pl.ds(l * height, height), :]
            columns = (beside[:, 0:1], beside[:, 1:2])
        sides = beside_rows(x, *rows) + beside_columns(x, *columns)
        fresh = x + change_of(x, sides, block(u_ref, l), block(v_ref, l), upper, lower, nest)
        if nest:
            fresh = fresh - NUDGING * x if fine is None else fresh + NUDGING * (block(fine, l) - x)
        store_level(out_ref, height, l, fresh)


def inner_line(height, row):
    return jnp.where(row == 0, height - 1, 0)


def edge_level(ref, height, lev):
    last = ref.shape[1] // height - 1
    return jnp.where(lev == 0, load_level(ref, height, last), load_level(ref, height, 0))


def ghost_row_weights(ghost, breadth):
    cell, third = iota((breadth, 3 * LANES), 0), iota((breadth, 3 * LANES), 1)
    kind = third // LANES
    offset = cell - 3 * (third - kind * LANES)
    middle = jnp.where(offset == 1, 3, jnp.where((offset == 0) | (offset == 2), 2, 0))
    weight = jnp.where(kind == 1, middle, jnp.where(offset == kind, 1, 0))
    return from_right(ghost, table(weight)) * (1.0 / 27.0)


def ghost_column_weights(first, last, levels, height):
    shape = (levels * height, LANES)
    lane = iota(shape, 1)
    _, line = split_level(iota(shape, 0), height)
    block = lane // 8
    inside = lane - block * 8
    eastern = inside >= 3
    kind = jnp.where(eastern, inside - 3, inside)
    offset = line - 3 * block
    middle = jnp.where(offset == 1, 3, jnp.where((offset == 0) | (offset == 2), 2, 0))
    weight = jnp.where(kind == 1, middle, jnp.where(offset == kind, 1, 0))
    weight = jnp.where((inside < 6) & (block < height // 3), weight, 0).astype(jnp.float32)
    columns = jnp.where(eastern, last, first) * weight
    return from_left(level_table(levels, height), columns) * (1.0 / 27.0)


def pack_kernel(
    levels,
    west_hbm,
    south_hbm,
    air_hbm,
    east_hbm,
    north_hbm,
    rows_ref,
    own_ref,
    level_ref,
    speeds_ref,
    west_ref,
    south_ref,
    air_ref,
    east_ref,
    north_ref,
    sems,
):
    pieces, size, _ = air_ref.shape
    height, breadth = level_ref.shape
    third_y = height // 3
    slots = own_ref.shape[0] - 1
    tile, row, lev = place()
    nest = tile == lax.axis_size("tiles") - 1

    def column_copies(source, target, first):
        return [
            pltpu.make_async_copy(source.at[:, pl.ds(c * LANES, LANES)], target.at[c], sems.at[first + c])
            for c in range(pieces)
        ]

    copies = column_copies(air_hbm, air_ref, 0)
    copies.append(pltpu.make_async_copy(west_hbm, west_ref, sems.at[3 * pieces]))
    copies.append(pltpu.make_async_copy(south_hbm, south_ref, sems.at[3 * pieces + 1]))
    speeds = column_copies(east_hbm, east_ref, pieces) + column_copies(north_hbm, north_ref, 2 * pieces)
    for copy in copies:
        copy.start()

    @pl.when(nest)
    def _():
        for copy in speeds:
            copy.start()

    for copy in copies:
        copy.wait()
    inner = inner_line(height, row)
    level_ref[...] = edge_level(air_ref, height, lev)
    store_slabs(rows_ref, slots + 1, load_line(air_ref, levels, inner))

    @pl.when(nest)
    def _():
        for copy in speeds:
            copy.wait()
        speed = load_line(north_ref, levels, inner)
        outer = load_line(north_ref, levels, height - 1 - inner)
        own_ref[...] = jnp.zeros_like(own_ref)
        rows_ref[pl.ds(0, slots + 1)] = jnp.zeros_like(own_ref)
        store_slabs(rows_ref, 4, speed)
        store_slabs(speeds_ref, 0, outer)
        store_slabs(speeds_ref, pieces, speed)
        store_slabs(own_ref, 0, ghost_row_weights(ghost_weight(outer, row == 0), breadth))
        first = ghost_weight(east_ref[0, :, 0:1], True)
        last = ghost_weight(east_ref[pieces - 1, :, LANES - 1 : LANES], False)
        own_ref[3] = ghost_column_weights(first, last, levels, height)

    @pl.when(jnp.logical_not(nest))
    def _():
        start = west_ref[0] - tile * breadth
        top = south_ref[0] - 1 - row * height
        part = rows_ref.at[pl.ds(0, slots + 1)]
        pack_window(part, air_ref, levels, top + (1 - row) * third_y, start)
        pack_window(own_ref, air_ref, levels, top + row * third_y, start)
        own_ref[slots] = own_ref[slots] + pack_edges(air_ref, levels)
        speeds_ref[...] = jnp.zeros_like(speeds_ref)


def early_kernel(
    levels,
    west_ref,
    south_ref,
    air_ref,
    east_ref,
    north_ref,
    rows_ref,
    level_ref,
    one_ref,
    three_ref,
    field_ref,
    own_ref,
    other_ref,
    side_ref,
    northern_ref,
    southern_ref,
):
    size, breadth = air_ref.shape
    height = size // levels
    third_y = height // 3
    pieces = breadth // LANES
    slots = own_ref.shape[0] - 1
    tile_count = lax.axis_size("tiles")
    tile, row, lev = place()
    nest = tile == tile_count - 1
    halo = join_slabs(rows_ref, slots + 1, pieces)
    zero = jnp.zeros_like(halo)
    northern_ref[...] = jnp.where(row == 0, zero, halo)
    southern_ref[...] = jnp.where(row == 0, halo, zero)
    shared = (field_ref, air_ref, east_ref, north_ref, level_ref, levels, lev)

    @pl.when(nest)
    def _():
        full_step(*shared, True, northern_ref, southern_ref, None, None)
        own_ref[...] = jnp.zeros_like(own_ref)
        other_ref[...] = jnp.zeros_like(other_ref)

    @pl.when(jnp.logical_not(nest))
    def _():
        columns = neighbour_columns(one_ref[slots], three_ref[slots], tile_count - 1, tile)
        side_ref[...] = unpack_edges(columns, levels, height)
        full_step(*shared, False, northern_ref, southern_ref, side_ref, None)
        start = west_ref[1] - tile * breadth
        top = south_ref[1] - 1 - row * height
        pack_window(other_ref, field_ref, levels, top + (1 - row) * third_y, start)
        pack_window(own_ref, field_ref, levels, top + row * third_y, start)


def first_kernel(
    levels, early_ref, east_ref, speeds_ref, one_ref, two_ref, three_ref, field_ref, edge_ref
):
    pieces, size, _ = early_ref.shape
    height, breadth = edge_ref.shape
    slots = one_ref.shape[0] - 1
    tile, row, lev = place()
    nest = tile == lax.axis_size("tiles") - 1

    @pl.when(jnp.logical_not(nest))
    def _():
        edge_ref[...] = jnp.zeros_like(edge_ref)

    @pl.when(nest)
    def _():
        slabs = [one_ref[s] + two_ref[s] + three_ref[s] for s in range(slots + 1)]
        cells, ring = refine(slabs[:slots], slabs[slots], height, breadth, row)
        lane = iota((size, LANES), 1)
        for c in range(pieces):
            piece = slice(c * LANES, (c + 1) * LANES)
            value = early_ref[c] + NUDGING * cells[:, piece]
            if c == 0:
                ghost = ghost_weight(east_ref[:, piece], True) * cells[:, breadth : breadth + 1]
                value = value + jnp.where(lane == 0, ghost, 0.0)
            if c == pieces - 1:
                ghost = ghost_weight(east_ref[:, piece], False) * cells[:, breadth + 1 : breadth + 2]
                value = value + jnp.where(lane == LANES - 1, ghost, 0.0)
            field_ref[c] = value
        outer = height - 1 - inner_line(height, row)
        ghost = ghost_weight(join_slabs(speeds_ref, 0, pieces), row == 0) * ring
        store_line(field_ref, levels, outer, load_line(field_ref, levels, outer) + ghost)
        edge_ref[...] = edge_level(field_ref, height, lev)


def average_kernel(
    levels, field_ref, east_ref, north_ref, rows_ref, level_ref, own_ref, other_ref, message_ref, part_ref
):
    pieces, size, _ = field_ref.shape
    height, breadth = level_ref.shape
    third_y = height // 3
    tile, row, lev = place()
    nest = tile == lax.axis_size("tiles") - 1

    @pl.when(jnp.logical_not(nest))
    def _():
        message_ref[...] = own_ref[...] + other_ref[...]

    @pl.when(nest)
    def _():
        full_step(part_ref, field_ref, east_ref, north_ref, level_ref, levels, lev, True, None, None, None, None)
        cell, third = iota((breadth, LANES), 0), iota((breadth, LANES), 1)
        offset = cell - 3 * third
        sums = table((offset >= 0) & (offset <= 2))
        shape = (third_y * levels, size)
        taken = iota(shape, 0)
        block = taken // levels
        level, line = split_level(iota(shape, 1), height)
        offset = line - 3 * block
        rows = table((taken - block * levels == level) & (offset >= 0) & (offset <= 2))
        means = from_left(rows, from_right(part_ref[...], sums)) * (1.0 / 9.0)
        for m in range(third_y):
            message_ref[m] = means[m * levels : (m + 1) * levels]
        shared = load_line(field_ref, levels, inner_line(height, row))
        shared = ghost_weight(join_slabs(rows_ref, 4, pieces), row == 0) * shared
        message_ref[third_y] = from_right(shared, sums) * (1.0 / 9.0)
        for i in range(third_y + 1, message_ref.shape[0]):
            message_ref[i] = jnp.zeros((levels, LANES), jnp.float32)


def blend_kernel(
    levels,
    weight_ref,
    field_ref,
    window_ref,
    one_ref,
    two_ref,
    three_ref,
    coef_one_ref,
    coef_two_ref,
    coef_three_ref,
    rows_ref,
):
    pieces, size, _ = field_ref.shape
    height = size // levels
    third_y = height // 3
    slots = third_y + 2
    tile_count = lax.axis_size("tiles")
    tile, row, _ = place()
    nest = tile == tile_count - 1

    @pl.when(nest)
    def _():
        store_slabs(rows_ref, 0, load_line(field_ref, levels, inner_line(height, row)))
        for i in range(pieces, rows_ref.shape[0]):
            rows_ref[i] = jnp.zeros((levels, LANES), jnp.float32)

    @pl.when(jnp.logical_not(nest))
    def _():
        def of_nest(refs, i):
            one, two, three = refs
            return jnp.where(tile == 0, three[i], jnp.where(tile == 1, two[i], one[i]))

        def mine(i):
            return of_nest((one_ref, two_ref, three_ref), i)

        def coefficient(i):
            return of_nest((coef_one_ref, coef_two_ref, coef_three_ref), i)

        def whole(i):
            odd = tile % 2 == 1
            west = jnp.where(odd, one_ref[i], three_ref[i])
            east = jnp.where(odd, three_ref[i], one_ref[i])
            part = jnp.where(tile == 0, window_ref[i], window_ref[i] + west)
            return jnp.where(tile == tile_count - 2, part, part + east)

        weight = weight_ref[:, 0:1]
        extra = whole(slots)
        lane = iota(extra.shape, 1)
        at_first, at_last = lane == 0, lane == LANES - 1
        lines = []
        for s in range(slots):
            x = whole(s)
            west = jnp.where(at_first, extra[:, s : s + 1], pltpu.roll(x, 1, 1))
            last = EAST_LANE + s
            east = jnp.where(at_last, extra[:, last : last + 1], pltpu.roll(x, LANES - 1, 1))
            lines.append((west, x, east))
        edges = coefficient(3)
        ghosts = [coefficient(q) for q in range(3)]

        def outward(side, q):
            near = lines[1] if side == 0 else lines[slots - 2]
            far = lines[0] if side == 0 else lines[slots - 1]
            return (2.0 / 3.0) * far[q] + (1.0 / 3.0) * near[q]

        def sideward(s):
            west, x, east = lines[s]
            return (2.0 / 3.0) * jnp.where(at_first, west, east) + (1.0 / 3.0) * x

        sidewards = [sideward(s) for s in range(slots)]
        columns = [w + 7.0 * x + e for w, x, e in lines]
        for m in range(third_y):
            x = lines[m + 1][1]
            value = mine(m) + (NUDGING / 81.0) * (columns[m] + 7.0 * columns[m + 1] + columns[m + 2])
            for q in range(3):
                lane_of = 8 * m + q
                first, last = edges[:, lane_of : lane_of + 1], edges[:, lane_of + 3 : lane_of + 4]
                scale = jnp.where(at_first, first, jnp.where(at_last, last, 0.0))
                value = value + scale * sidewards[m + q]
            for side, at in ((0, 0), (1, third_y - 1)):
                if m == at:
                    for q in range(3):
                        value = value + jnp.where(row == side, ghosts[q], 0.0) * outward(side, q)
            rows_ref[m] = x + weight * (value - x)
        rows_ref[third_y] = weight * mine(third_y)


def later_kernel(
    levels,
    west_ref,
    south_ref,
    field_ref,
    east_ref,
    north_ref,
    level_ref,
    one_ref,
    two_ref,
    three_ref,
    parent_ref,
    blend_ref,
    out_ref,
    fine_ref,
    side_ref,
    northern_ref,
    southern_ref,
):
    height, breadth = level_ref.shape
    third_y = height // 3
    slots = third_y + 2
    tile, row, lev = place()
    nest = tile == lax.axis_size("tiles") - 1

    @pl.when(nest)
    def _():
        slabs = [one_ref[s] + two_ref[s] + three_ref[s] for s in range(slots + 1)]
        cells, ring = refine(slabs[:slots], slabs[slots], height, breadth, row)
        fine_ref[...] = cells[:, :breadth]
        side_ref[...] = cells[:, breadth:]
        zero = jnp.zeros_like(ring)
        northern_ref[...] = jnp.where(row == 0, ring, zero)
        southern_ref[...] = jnp.where(row == 0, zero, ring)
        full_step(
            out_ref,
            field_ref,
            east_ref,
            north_ref,
            level_ref,
            levels,
            lev,
            True,
            northern_ref,
            southern_ref,
            side_ref,
            fine_ref,
        )

    @pl.when(jnp.logical_not(nest))
    def _():
        out_ref[...] = parent_ref[...]
        start = west_ref[1] - tile * breadth
        top = south_ref[1] + row * third_y - row * height
        for m in range(third_y):
            place_row(out_ref, levels, top + m, start, blend_ref[m])


def last_kernel(
    levels, west_ref, south_ref, given_ref, speeds_ref, blend_ref, rows_ref, out_hbm, out_ref, sems
):
    pieces, size, _ = given_ref.shape
    breadth = pieces * LANES
    height = size // levels
    third_y = height // 3
    tile, row, _ = place()
    nest = tile == lax.axis_size("tiles") - 1
    out_ref[...] = given_ref[...]

    @pl.when(nest)
    def _():
        inner = inner_line(height, row)
        halo = ghost_weight(join_slabs(speeds_ref, pieces, pieces), row == 1) * join_slabs(rows_ref, 0, pieces)
        store_line(out_ref, levels, inner, load_line(out_ref, levels, inner) + halo)

    @pl.when(jnp.logical_not(nest))
    def _():
        start = west_ref[1] - tile * breadth
        top = south_ref[1] + (1 - row) * third_y - row * height
        for m in range(third_y):
            value = rows_ref[m]
            if m == 0:
                value = value + jnp.where(row == 0, blend_ref[third_y], 0.0)
            if m == third_y - 1:
                value = value + jnp.where(row == 1, blend_ref[third_y], 0.0)
            place_row(out_ref, levels, top + m, start, value)
        near = jnp.where(row == 0, third_y - 1, 0)
        line = south_ref[1] + row * third_y - row * height + near
        place_row(out_ref, levels, line, start, blend_ref[near] + rows_ref[third_y])

    copies = [
        pltpu.make_async_copy(out_ref.at[c], out_hbm.at[:, pl.ds(c * LANES, LANES)], sems.at[c])
        for c in range(pieces)
    ]
    for copy in copies:
        copy.start()
    for copy in copies:
        copy.wait()


def call(kernel, outs, inputs, places, scratch=(), flops=0, out_place="v", room=32 * 1024):
    spaces = {"s": pltpu.SMEM, "v": pltpu.VMEM, "h": pltpu.HBM}
    moved = sum(4 * math.prod(shape) for shape in outs) + sum(array.nbytes for array in inputs)
    inputs = [
        pltpu.with_memory_space_constraint(array, pltpu.HBM) if p == "h" else array
        for array, p in zip(inputs, places)
    ]
    return pl.pallas_call(
        kernel,
        out_shape=[spaces[out_place](shape, jnp.float32) for shape in outs],
        in_specs=[pl.BlockSpec(memory_space=spaces[p]) for p in places],
        out_specs=[pl.BlockSpec(memory_space=spaces[out_place])] * len(outs),
        scratch_shapes=[pltpu.VMEM(s, jnp.float32) if isinstance(s, tuple) else s for s in scratch],
        compiler_params=pltpu.CompilerParams(vmem_limit_bytes=room * 1024),
        cost_estimate=pl.CostEstimate(flops=flops, bytes_accessed=moved, transcendentals=0),
    )(*inputs)


def per_device_paired(air_state, wind_east, wind_north, feedback_weight, nest_west, nest_south):
    levels, height, breadth = air_state.shape
    third_y = height // 3
    pieces = breadth // LANES
    slots = third_y + 2
    size = levels * height
    flat = (size, breadth)
    chunked = (pieces, size, LANES)
    air, east, north = (array.reshape(flat) for array in (air_state, wind_east, wind_north))
    weight = jnp.broadcast_to(feedback_weight[:, None], (levels, LANES))
    swap = [(0, 1), (1, 0)]

    def slabs(count):
        return (count, levels, LANES)

    def kernel(body):
        return functools.partial(body, levels)

    rows, own, level, speeds = call(
        kernel(pack_kernel),
        [slabs(slots + 1 + pieces), slabs(slots + 1), (height, breadth), slabs(2 * pieces)],
        [nest_west, nest_south, air, east, north],
        "hhhhh",
        [
            pltpu.SMEM((2,), jnp.int32),
            pltpu.SMEM((2,), jnp.int32),
            chunked,
            chunked,
            chunked,
            pltpu.SemaphoreType.DMA((3 * pieces + 2,)),
        ],
    )
    rows = lax.ppermute(rows, "rows", swap)
    level = lax.ppermute(level, "lev", swap)
    pairs = [[(0, 1), (1, 0), (2, 3), (3, 2)], [(1, 3), (3, 1)], [(0, 3), (3, 0), (1, 2), (2, 1)]]

    def over_tiles(message):
        return [lax.ppermute(message, "tiles", pair) for pair in pairs]

    starting = over_tiles(own + rows[: slots + 1])
    sides = [(size, LANES), (levels, breadth), (levels, breadth)]
    early, own, other = call(
        kernel(early_kernel),
        [chunked, slabs(slots + 1), slabs(slots + 1)],
        [nest_west, nest_south, air, east, north, rows, level, starting[0], starting[2]],
        "ssvvvvvvv",
        sides,
        flops=30 * size * breadth,
    )
    other = lax.ppermute(other, "rows", swap)
    first, edge = call(
        kernel(first_kernel),
        [chunked, (height, breadth)],
        [early, east, speeds, *starting],
        "vvvvvv",
    )
    level = lax.ppermute(edge, "lev", swap)
    (message,) = call(
        kernel(average_kernel),
        [slabs(slots + 1)],
        [first, east, north, rows, level, own, other],
        "vvvvvvv",
        [flat],
    )
    received = over_tiles(message)
    (blend,) = call(
        kernel(blend_kernel),
        [slabs(third_y + 1)],
        [weight, first, message, *received, *starting],
        "v" * 9,
    )
    rows = lax.ppermute(blend, "rows", swap)
    (later,) = call(
        kernel(later_kernel),
        [chunked],
        [nest_west, nest_south, first, east, north, level, *received, early, blend],
        "ss" + "v" * 9,
        [flat, *sides],
        flops=30 * size * breadth,
    )
    (out,) = call(
        kernel(last_kernel),
        [flat],
        [nest_west, nest_south, later, speeds, blend, rows],
        "ssvvvv",
        [chunked, pltpu.SemaphoreType.DMA((pieces,))],
        out_place="h",
    )
    return out.reshape(air_state.shape)


def solution(mesh):
    in_specs = (
        P(("members", "lev"), "rows", "tiles"),
        P(("members", "lev"), "rows", "tiles"),
        P(("members", "lev"), "rows", "tiles"),
        P("lev"),
        P("members"),
        P("members"),
    )
    out_specs = P(("members", "lev"), "rows", "tiles")
    paired = mesh.shape["tiles"] == 4 and mesh.shape["rows"] == 2 and mesh.shape["lev"] == 2
    return jax.shard_map(
        per_device_paired if paired else per_device, mesh=mesh, in_specs=in_specs, out_specs=out_specs, check_vma=False
    )
```

```python
import functools
import math

import jax
import jax.numpy as jnp
from jax import lax
from jax.experimental import pallas as pl
from jax.experimental.pallas import tpu as pltpu
from jax.sharding import PartitionSpec as P

VERTICAL_MIX = 0.1
PARENT_MIXING = 0.04
NEST_MIXING = 0.18
NEST_ADVECT = 1.5
NUDGING = 0.2


def padded_2(array, sides, width):
    for axis, dim in sides:
        size, length = (lax.axis_size(axis), array.shape[dim])
        up = [(i, (i + 1) % size) for i in range(size - 1)]
        down = [(j, i) for i, j in up]
        last = lax.slice_in_dim(array, length - width, length, axis=dim)
        first = lax.slice_in_dim(array, 0, width, axis=dim)
        before = lax.ppermute(last, axis, up)
        after = lax.ppermute(first, axis, down)
        array = jnp.concatenate([before, array, after], axis=dim)
    return array


def interp_table(cells):
    extended = jnp.arange(cells + 2, dtype=jnp.int32) - 1
    coarse = jnp.floor_divide(extended, 3)
    offset = extended - 3 * coarse
    fraction = jnp.abs(offset - 1).astype(jnp.float32) / 3.0
    nearest = coarse + 1
    beside = nearest + (offset - 1)
    slots = jnp.arange(cells // 3 + 2, dtype=jnp.int32)[:, None]
    first_part = jnp.where(
        slots == nearest[None, :], 1.0 - fraction[None, :], jnp.zeros((), jnp.float32)
    )
    second_part = jnp.where(slots == beside[None, :], fraction[None, :], jnp.zeros((), jnp.float32))
    return first_part + second_part


def tendency(padded, speed_east, speed_north, advect_scale, mixing_scale):
    centre = padded[1:-1, 1:-1, 1:-1]
    eastern = padded[1:-1, 1:-1, 2:]
    western = padded[1:-1, 1:-1, :-2]
    southern = padded[1:-1, 2:, 1:-1]
    northern = padded[1:-1, :-2, 1:-1]
    upper = padded[2:, 1:-1, 1:-1]
    lower = padded[:-2, 1:-1, 1:-1]
    advect = speed_east * (eastern - western) + speed_north * (southern - northern)
    horizontal = eastern + western + southern + northern - 4.0 * centre
    vertical = upper + lower - 2.0 * centre
    return -0.5 * advect_scale * advect + mixing_scale * horizontal + VERTICAL_MIX * vertical


def padded_block(block_field):
    return padded_2(block_field, (("tiles", 2), ("rows", 1), ("lev", 0)), 1)


def per_device(air_state, wind_east, wind_north, feedback_weight, nest_west, nest_south):
    levels, height, breadth = air_state.shape
    tile_count = lax.axis_size("tiles")
    row_count = lax.axis_size("rows")
    tile_index = lax.axis_index("tiles")
    row_index = lax.axis_index("rows")
    parent_tiles = 3 * tile_count // 4
    nest_tiles = tile_count - parent_tiles
    in_nest = tile_index >= parent_tiles
    nest_tile = tile_index - parent_tiles
    cross_x = breadth // 3 + 2
    cross_y = height // 3 + 2
    third_x = breadth // 3
    third_y = height // 3
    first_x = tile_index * breadth
    first_y = row_index * height
    columns = jnp.arange(breadth, dtype=jnp.int32)
    lines = jnp.arange(height, dtype=jnp.int32)
    targets_x = jnp.arange(tile_count, dtype=jnp.int32)
    targets_y = jnp.arange(row_count, dtype=jnp.int32)
    highest = lax.Precision.HIGHEST
    table_x = interp_table(breadth)
    table_y = interp_table(height)
    zero_value = jnp.zeros((), jnp.float32)

    def boundary(source, substep):
        anchor_x = nest_west[substep] + (targets_x - parent_tiles) * third_x - 1
        slot_x = jnp.arange(cross_x, dtype=jnp.int32)
        pick_x = (
            (first_x + columns)[None, :, None] == anchor_x[:, None, None] + slot_x[None, None, :]
        ) & (targets_x >= parent_tiles)[:, None, None]
        pick_x = pick_x.astype(jnp.float32)
        anchor_y = nest_south[substep] + targets_y * third_y - 1
        slot_y = jnp.arange(cross_y, dtype=jnp.int32)
        pick_y = (
            (first_y + lines)[None, :, None] == anchor_y[:, None, None] + slot_y[None, None, :]
        ).astype(jnp.float32)
        pieces = jnp.einsum("lyi,tij->tlyj", source, pick_x, precision=highest)
        merged = lax.all_to_all(pieces, "tiles", split_axis=0, concat_axis=0, tiled=True).sum(
            axis=0
        )
        pieces = jnp.einsum("lyj,ryw->rlwj", merged, pick_y, precision=highest)
        window = lax.all_to_all(pieces, "rows", split_axis=0, concat_axis=0, tiled=True).sum(axis=0)
        along = jnp.einsum("lwj,je->lwe", window, table_x, precision=highest)
        return jnp.einsum("lwe,wf->lfe", along, table_y, precision=highest)

    def assemble(block_field, fine):
        padded = padded_block(block_field)
        fine_padded = jnp.pad(fine, ((1, 1), (0, 0), (0, 0)))
        column_place = lax.broadcasted_iota(jnp.int32, padded.shape, 2)
        line_place = lax.broadcasted_iota(jnp.int32, padded.shape, 1)
        outside = (column_place == 0) & (nest_tile == 0) | (column_place == breadth + 1) & (
            nest_tile == nest_tiles - 1
        )
        outside = (
            outside
            | (line_place == 0) & (row_index == 0)
            | (line_place == height + 1) & (row_index == row_count - 1)
        )
        padded = jnp.where(outside & in_nest, fine_padded, padded)
        seam_cells = (column_place == breadth + 1) & (tile_index == parent_tiles - 1)
        return jnp.where(seam_cells, zero_value, padded)

    advect_scale = jnp.where(in_nest, jnp.float32(NEST_ADVECT), jnp.float32(1.0))
    mixing_scale = jnp.where(in_nest, jnp.float32(NEST_MIXING), jnp.float32(PARENT_MIXING))
    fine_first = boundary(air_state, 0)
    change = tendency(
        assemble(air_state, fine_first), wind_east, wind_north, advect_scale, mixing_scale
    )
    nudging_term = jnp.where(in_nest, NUDGING * (fine_first[:, 1:-1, 1:-1] - air_state), zero_value)
    step_one = air_state + change + nudging_term
    fine_second = boundary(step_one, 1)
    change = tendency(
        assemble(step_one, fine_second), wind_east, wind_north, advect_scale, mixing_scale
    )
    nested_two = step_one + change + NUDGING * (fine_second[:, 1:-1, 1:-1] - step_one)
    step_two = jnp.where(in_nest, nested_two, step_one)
    coarse = step_two.reshape(levels, third_y, 3, third_x, 3).mean(axis=(2, 4))
    avg_columns = jnp.arange(third_x, dtype=jnp.int32)
    avg_lines = jnp.arange(third_y, dtype=jnp.int32)
    west_last = nest_west[1]
    south_last = nest_south[1]
    place_x = (
        (west_last + (targets_x - parent_tiles) * third_x)[:, None, None]
        + avg_columns[None, :, None]
        == (first_x + columns)[None, None, :]
    ) & (targets_x >= parent_tiles)[:, None, None]
    place_x = place_x.astype(jnp.float32)
    place_y = (
        (south_last + targets_y * third_y)[:, None, None] + avg_lines[None, :, None]
        == (first_y + lines)[None, None, :]
    ).astype(jnp.float32)
    parent_y = south_last + row_index * third_y + avg_lines
    send_y = (jnp.floor_divide(parent_y, height)[None, :] == targets_y[:, None]) & in_nest
    pieces = jnp.where(send_y[:, None, :, None], coarse[None], zero_value)
    received = lax.all_to_all(pieces, "rows", split_axis=0, concat_axis=0, tiled=True)
    spread = jnp.einsum("slba,sby->lya", received, place_y, precision=highest)
    parent_x = west_last + nest_tile * third_x + avg_columns
    send_x = jnp.floor_divide(parent_x, breadth)[None, :] == targets_x[:, None]
    pieces = jnp.where(send_x[:, None, None, :], spread[None], zero_value)
    received = lax.all_to_all(pieces, "tiles", split_axis=0, concat_axis=0, tiled=True)
    placed = jnp.einsum("slya,sai->lyi", received, place_x, precision=highest)
    global_x = (first_x + columns)[None, None, :]
    global_y = (first_y + lines)[None, :, None]
    covered = (global_x >= west_last) & (global_x < west_last + nest_tiles * third_x)
    covered = covered & (global_y >= south_last) & (global_y < south_last + row_count * third_y)
    covered = covered & jnp.logical_not(in_nest)
    blended = step_two + feedback_weight[:, None, None] * (placed - step_two)
    return jnp.where(covered, blended, step_two)


LANES = 128
FIRST_LANE = 32
LAST_LANE = 96
EAST_LANE = 64


def iota(shape, dim):
    return lax.broadcasted_iota(jnp.int32, shape, dim)


def split_level(place, height):
    level = ((place.astype(jnp.float32) + 0.5) * (1.0 / height)).astype(jnp.int32)
    return level, place - level * height


def table(values):
    return values.astype(jnp.float32).astype(jnp.bfloat16)


def parts_of(array):
    high = array.astype(jnp.bfloat16)
    low = (array - high.astype(jnp.float32)).astype(jnp.bfloat16)
    return high, low


def dot(left, right):
    return jnp.dot(left, right, preferred_element_type=jnp.float32)


def from_left(weights, array):
    high, low = parts_of(array)
    return dot(weights, high) + dot(weights, low)


def from_right(array, weights):
    high, low = parts_of(array)
    return dot(high, weights) + dot(low, weights)


def hat(distance):
    return jnp.maximum(0, 3 - jnp.abs(distance - 1))


def place():
    return lax.axis_index("tiles"), lax.axis_index("rows"), lax.axis_index("lev")


def level_table(levels, height):
    shape = (levels, levels * height)
    level, _ = split_level(iota(shape, 1), height)
    return table(iota(shape, 0) == level)


def spread_table(levels, height):
    shape = (levels * height, levels)
    level, _ = split_level(iota(shape, 0), height)
    return table(iota(shape, 1) == level)


def load_line(ref, levels, line):
    rows = pl.ds(line, levels, stride=ref.shape[1] // levels)
    return jnp.concatenate([ref[c, rows, :] for c in range(ref.shape[0])], axis=1)


def store_line(ref, levels, line, value):
    rows = pl.ds(line, levels, stride=ref.shape[1] // levels)
    for c in range(ref.shape[0]):
        ref[c, rows, :] = value[:, c * LANES : (c + 1) * LANES]


def load_level(ref, height, l):
    rows = pl.ds(l * height, height)
    if len(ref.shape) == 2:
        return ref[rows, :]
    return jnp.concatenate([ref[c, rows, :] for c in range(ref.shape[0])], axis=1)


def store_level(ref, height, l, value):
    rows = pl.ds(l * height, height)
    if len(ref.shape) == 2:
        ref[rows, :] = value
    else:
        for c in range(ref.shape[0]):
            ref[c, rows, :] = value[:, c * LANES : (c + 1) * LANES]


def store_slabs(ref, first, wide):
    for i in range(wide.shape[1] // LANES):
        ref[first + i] = wide[:, i * LANES : (i + 1) * LANES]


def join_slabs(ref, first, count):
    return jnp.concatenate([ref[first + i] for i in range(count)], axis=1)


def column_pieces(start, pieces):
    first = (start + 64 * LANES) // LANES - 64
    offset = start - first * LANES
    held = [(c >= 0) & (c < pieces) for c in (first, first + 1)]
    return [jnp.clip(c, 0, pieces - 1) for c in (first, first + 1)], held, offset


def pack_window(ref, field_ref, levels, top, start):
    pieces, size, _ = field_ref.shape
    height = size // levels
    slots = ref.shape[0] - 1
    lane = iota((levels, LANES), 1)
    (left, right), (left_held, right_held), offset = column_pieces(start, pieces)
    before = lax.rem(offset + LANES - 1, LANES)
    (beside, _), (beside_held, _), _ = column_pieces(start - 1, pieces)
    in_left = lane < LANES - offset
    held = jnp.where(in_left, left_held.astype(jnp.float32), right_held.astype(jnp.float32))
    west_held, east_held = beside_held.astype(jnp.float32), right_held.astype(jnp.float32)
    turn = lax.rem(LANES - offset, LANES)
    extra = jnp.zeros((levels, LANES), jnp.float32)
    for slot in range(slots):
        line = top + slot
        there = ((line >= 0) & (line < height)).astype(jnp.float32)
        rows = pl.ds(jnp.clip(line, 0, height - 1), levels, stride=height)
        near, far, west = field_ref[left, rows, :], field_ref[right, rows, :], field_ref[beside, rows, :]
        ref[slot] = jnp.where(in_left, pltpu.roll(near, turn, 1), pltpu.roll(far, turn, 1)) * (held * there)
        west = pltpu.roll(west, lax.rem(LANES + slot - before, LANES), 1) * (west_held * there)
        east = pltpu.roll(far, lax.rem(LANES + EAST_LANE + slot - offset, LANES), 1) * (east_held * there)
        extra = jnp.where(lane == slot, west, jnp.where(lane == EAST_LANE + slot, east, extra))
    ref[slots] = extra


def place_row(ref, levels, line, start, value):
    pieces, size, _ = ref.shape
    height = size // levels
    lane = iota((levels, LANES), 1)
    at, held, offset = column_pieces(start, pieces)
    value = pltpu.roll(value, offset, 1)
    there = (line >= 0) & (line < height)
    rows = pl.ds(jnp.clip(line, 0, height - 1), levels, stride=height)
    for c in range(2):
        mine = (lane >= offset) if c == 0 else (lane < offset)
        ref[at[c], rows, :] = jnp.where(mine & (held[c] & there), value, ref[at[c], rows, :])


def pack_edges(field_ref, levels):
    height = field_ref.shape[1] // levels
    lane = iota((levels, LANES), 1)
    packed = jnp.zeros((levels, LANES), jnp.float32)
    for line in range(height):
        rows = pl.ds(line, levels, stride=height)
        first = field_ref[0, rows, :]
        last = field_ref[field_ref.shape[0] - 1, rows, :]
        packed = jnp.where(lane == FIRST_LANE + line, pltpu.roll(first, FIRST_LANE + line, 1), packed)
        packed = jnp.where(lane == LAST_LANE + line, pltpu.roll(last, LAST_LANE + line + 1, 1), packed)
    return packed


def neighbour_columns(even, odd, parent_tiles, tile):
    is_odd = tile % 2 == 1
    west = jnp.where(is_odd, even, odd)
    east = jnp.where(is_odd, odd, even)
    west = jnp.where(tile == 0, jnp.zeros_like(west), west)
    east = jnp.where(tile >= parent_tiles - 1, jnp.zeros_like(east), east)
    return jnp.where(iota(west.shape, 1) < LAST_LANE, east, west)


def unpack_edges(columns, levels, height):
    wide = from_left(spread_table(levels, height), columns)
    lane = iota(wide.shape, 1)
    _, line = split_level(iota(wide.shape, 0), height)
    west = jnp.sum(jnp.where(lane == line + LAST_LANE, wide, 0.0), axis=1, keepdims=True)
    east = jnp.sum(jnp.where(lane == line + FIRST_LANE, wide, 0.0), axis=1, keepdims=True)
    return jnp.where(lane == 0, west, jnp.where(lane == 1, east, 0.0))


def refine(slabs, extra, height, breadth, row):
    slots, levels = len(slabs), extra.shape[0]
    beside = [pltpu.roll(extra, LANES - s, 1) if s else extra for s in range(slots)]
    window = jnp.concatenate([jnp.concatenate(slabs, axis=0), jnp.concatenate(beside, axis=0)], axis=1)
    shape = (2 * LANES, breadth + LANES)
    slot, cell = iota(shape, 0), iota(shape, 1)
    held = (slot <= LANES) | (slot == LANES + EAST_LANE)
    at = jnp.where(slot < LANES, slot, jnp.where(slot == LANES, -1, LANES))
    cell = jnp.where(cell == breadth, -1, jnp.where(cell == breadth + 1, breadth, cell))
    across = jnp.where(held & (cell <= breadth), hat(cell - 3 * at), 0)
    wide = from_right(window, table(across)) * (1.0 / 9.0)
    shape = (levels * height, slots * levels)
    taken = iota(shape, 1)
    slot = taken // levels
    level, line = split_level(iota(shape, 0), height)
    along = jnp.where(taken - slot * levels == level, hat(line - 3 * (slot - 1)), 0)
    cells = from_left(table(along), wide)
    ring = jnp.where(
        row == 0,
        2.0 * wide[:levels] + wide[levels : 2 * levels],
        2.0 * wide[(slots - 1) * levels :] + wide[(slots - 2) * levels : (slots - 1) * levels],
    )
    return cells, ring[:, :breadth]


def beside_rows(x, north, south):
    height = x.shape[0]
    line = iota(x.shape, 0)
    northern = jnp.where(line == 0, north, pltpu.roll(x, 1, 0))
    southern = jnp.where(line == height - 1, south, pltpu.roll(x, height - 1, 0))
    return northern, southern


def beside_columns(x, west, east):
    breadth = x.shape[1]
    column = iota(x.shape, 1)
    western = jnp.where(column == 0, west, pltpu.roll(x, 1, 1))
    eastern = jnp.where(column == breadth - 1, east, pltpu.roll(x, breadth - 1, 1))
    return western, eastern


def change_of(x, sides, u, v, upper, lower, nest):
    advect_scale = NEST_ADVECT if nest else 1.0
    mixing_scale = NEST_MIXING if nest else PARENT_MIXING
    northern, southern, western, eastern = sides
    advect = u * (eastern - western) + v * (southern - northern)
    horizontal = eastern + western + southern + northern - 4.0 * x
    vertical = upper + lower - 2.0 * x
    return -0.5 * advect_scale * advect + mixing_scale * horizontal + VERTICAL_MIX * vertical


def ghost_weight(speed, before):
    return jnp.where(before, 0.5 * NEST_ADVECT, -0.5 * NEST_ADVECT) * speed + NEST_MIXING


def full_step(out_ref, field_ref, u_ref, v_ref, level_ref, levels, lev, nest, north, south, side, fine):
    height, breadth = level_ref.shape
    zero = jnp.zeros((height, breadth), jnp.float32)

    def block(ref, l):
        return load_level(ref, height, l)

    for l in range(levels):
        x = block(field_ref, l)
        lower = block(field_ref, l - 1) if l else jnp.where(lev == 1, level_ref[...], zero)
        upper = block(field_ref, l + 1) if l < levels - 1 else jnp.where(lev == 0, level_ref[...], zero)
        rows = [0.0 if ref is None else ref[pl.ds(l, 1), :] for ref in (north, south)]
        if side is None:
            columns = (0.0, 0.0)
        else:
            beside = side[pl.ds(l * height, height), :]
            columns = (beside[:, 0:1], beside[:, 1:2])
        sides = beside_rows(x, *rows) + beside_columns(x, *columns)
        fresh = x + change_of(x, sides, block(u_ref, l), block(v_ref, l), upper, lower, nest)
        if nest:
            fresh = fresh - NUDGING * x if fine is None else fresh + NUDGING * (block(fine, l) - x)
        store_level(out_ref, height, l, fresh)


def inner_line(height, row):
    return jnp.where(row == 0, height - 1, 0)


def edge_level(ref, height, lev):
    last = ref.shape[1] // height - 1
    return jnp.where(lev == 0, load_level(ref, height, last), load_level(ref, height, 0))


def ghost_row_weights(ghost, breadth):
    cell, third = iota((breadth, 3 * LANES), 0), iota((breadth, 3 * LANES), 1)
    kind = third // LANES
    offset = cell - 3 * (third - kind * LANES)
    middle = jnp.where(offset == 1, 3, jnp.where((offset == 0) | (offset == 2), 2, 0))
    weight = jnp.where(kind == 1, middle, jnp.where(offset == kind, 1, 0))
    return from_right(ghost, table(weight)) * (1.0 / 27.0)


def ghost_column_weights(first, last, levels, height):
    shape = (levels * height, LANES)
    lane = iota(shape, 1)
    _, line = split_level(iota(shape, 0), height)
    block = lane // 8
    inside = lane - block * 8
    eastern = inside >= 3
    kind = jnp.where(eastern, inside - 3, inside)
    offset = line - 3 * block
    middle = jnp.where(offset == 1, 3, jnp.where((offset == 0) | (offset == 2), 2, 0))
    weight = jnp.where(kind == 1, middle, jnp.where(offset == kind, 1, 0))
    weight = jnp.where((inside < 6) & (block < height // 3), weight, 0).astype(jnp.float32)
    columns = jnp.where(eastern, last, first) * weight
    return from_left(level_table(levels, height), columns) * (1.0 / 27.0)


def pack_kernel(
    levels, west_hbm, south_hbm, air_hbm, rows_ref, air_ref, west_ref, south_ref, sems
):
    pieces, size, _ = air_ref.shape
    breadth = pieces * LANES
    height = size // levels
    third_y = height // 3
    slots = rows_ref.shape[0] - 1 - pieces
    tile, row, _ = place()
    nest = tile == lax.axis_size("tiles") - 1
    copies = [
        pltpu.make_async_copy(air_hbm.at[:, pl.ds(c * LANES, LANES)], air_ref.at[c], sems.at[c])
        for c in range(pieces)
    ]
    copies.append(pltpu.make_async_copy(west_hbm, west_ref, sems.at[pieces]))
    copies.append(pltpu.make_async_copy(south_hbm, south_ref, sems.at[pieces + 1]))
    for copy in copies:
        copy.start()
    for copy in copies:
        copy.wait()
    store_slabs(rows_ref, slots + 1, load_line(air_ref, levels, inner_line(height, row)))
    part = rows_ref.at[pl.ds(0, slots + 1)]

    @pl.when(nest)
    def _():
        part[...] = jnp.zeros_like(part)

    @pl.when(jnp.logical_not(nest))
    def _():
        start = west_ref[0] - tile * breadth
        top = south_ref[0] - 1 - row * height
        pack_window(part, air_ref, levels, top + (1 - row) * third_y, start)


def own_kernel(levels, west_ref, south_ref, air_ref, east_ref, north_ref, own_ref, level_ref, speeds_ref):
    pieces, size, _ = air_ref.shape
    breadth = pieces * LANES
    height = size // levels
    third_y = height // 3
    slots = own_ref.shape[0] - 1
    tile, row, lev = place()
    nest = tile == lax.axis_size("tiles") - 1
    level_ref[...] = edge_level(air_ref, height, lev)

    @pl.when(nest)
    def _():
        inner = inner_line(height, row)
        shape = (2 * levels, size)
        taken = iota(shape, 0)
        level, line = split_level(iota(shape, 1), height)
        wanted = jnp.where(taken < levels, height - 1 - inner, inner)
        picked = table((lax.rem(taken, levels) == level) & (line == wanted))
        speeds = from_left(picked, north_ref[...])
        outer = speeds[:levels]
        store_slabs(speeds_ref, 0, outer)
        store_slabs(speeds_ref, pieces, speeds[levels:])
        own_ref[...] = jnp.zeros_like(own_ref)
        store_slabs(own_ref, 0, ghost_row_weights(ghost_weight(outer, row == 0), breadth))
        first = ghost_weight(east_ref[:, 0:1], True)
        last = ghost_weight(east_ref[:, breadth - 1 : breadth], False)
        own_ref[3] = ghost_column_weights(first, last, levels, height)

    @pl.when(jnp.logical_not(nest))
    def _():
        start = west_ref[0] - tile * breadth
        top = south_ref[0] - 1 - row * height
        pack_window(own_ref, air_ref, levels, top + row * third_y, start)
        own_ref[slots] = own_ref[slots] + pack_edges(air_ref, levels)
        speeds_ref[...] = jnp.zeros_like(speeds_ref)


def set_halo(rows_ref, first, northern_ref, southern_ref, row):
    halo = join_slabs(rows_ref, first, rows_ref.shape[0] - first)
    zero = jnp.zeros_like(halo)
    northern_ref[...] = jnp.where(row == 0, zero, halo)
    southern_ref[...] = jnp.where(row == 0, halo, zero)


def parent_step(
    levels, west_ref, south_ref, shared, rows_ref, columns, field_ref, other_ref, side_ref, northern_ref, southern_ref
):
    height = side_ref.shape[0] // levels
    slots = other_ref.shape[0] - 1
    tile, row, lev = place()
    set_halo(rows_ref, slots + 1, northern_ref, southern_ref, row)
    side_ref[...] = unpack_edges(columns, levels, height)
    full_step(field_ref, *shared, levels, lev, False, northern_ref, southern_ref, side_ref, None)
    start = west_ref[1] - tile * field_ref.shape[0] * LANES
    top = south_ref[1] - 1 - row * height
    pack_window(other_ref, field_ref, levels, top + (1 - row) * (height // 3), start)


def early_kernel(
    levels,
    west_ref,
    south_ref,
    air_ref,
    east_ref,
    north_ref,
    rows_ref,
    level_ref,
    one_ref,
    speeds_ref,
    field_ref,
    other_ref,
    side_ref,
    northern_ref,
    southern_ref,
):
    pieces = field_ref.shape[0]
    slots = other_ref.shape[0] - 1
    tile_count = lax.axis_size("tiles")
    tile, row, lev = place()
    shared = (air_ref, east_ref, north_ref, level_ref)

    @pl.when(tile == tile_count - 1)
    def _():
        set_halo(rows_ref, slots + 1, northern_ref, southern_ref, row)
        full_step(field_ref, *shared, levels, lev, True, northern_ref, southern_ref, None, None)
        other_ref[...] = jnp.zeros_like(other_ref)
        other_ref[pl.ds(0, pieces)] = speeds_ref[pl.ds(pieces, pieces)]

    @pl.when(tile == 0)
    def _():
        columns = neighbour_columns(one_ref[slots], one_ref[slots], tile_count - 1, tile)
        refs = (field_ref, other_ref, side_ref, northern_ref, southern_ref)
        parent_step(levels, west_ref, south_ref, shared, rows_ref, columns, *refs)


def middle_kernel(
    levels,
    west_ref,
    south_ref,
    air_ref,
    east_ref,
    north_ref,
    rows_ref,
    level_ref,
    three_ref,
    one_ref,
    given_field_ref,
    given_other_ref,
    field_ref,
    other_ref,
    side_ref,
    northern_ref,
    southern_ref,
):
    slots = other_ref.shape[0] - 1
    tile_count = lax.axis_size("tiles")
    tile, _, _ = place()
    shared = (air_ref, east_ref, north_ref, level_ref)

    @pl.when((tile > 0) & (tile < tile_count - 1))
    def _():
        columns = neighbour_columns(one_ref[slots], three_ref[slots], tile_count - 1, tile)
        refs = (field_ref, other_ref, side_ref, northern_ref, southern_ref)
        parent_step(levels, west_ref, south_ref, shared, rows_ref, columns, *refs)


def first_kernel(
    levels,
    west_ref,
    south_ref,
    early_ref,
    east_ref,
    speeds_ref,
    three_ref,
    two_ref,
    one_ref,
    field_ref,
    edge_ref,
    own_ref,
):
    pieces, size, _ = early_ref.shape
    height, breadth = edge_ref.shape
    slots = one_ref.shape[0] - 1
    tile, row, lev = place()
    nest = tile == lax.axis_size("tiles") - 1

    @pl.when(jnp.logical_not(nest))
    def _():
        edge_ref[...] = jnp.zeros_like(edge_ref)
        start = west_ref[1] - tile * breadth
        top = south_ref[1] - 1 - row * height
        pack_window(own_ref, early_ref, levels, top + row * (height // 3), start)

    @pl.when(nest)
    def _():
        slabs = [one_ref[s] + two_ref[s] + three_ref[s] for s in range(slots + 1)]
        cells, ring = refine(slabs[:slots], slabs[slots], height, breadth, row)
        lane = iota((size, LANES), 1)
        for c in range(pieces):
            piece = slice(c * LANES, (c + 1) * LANES)
            value = early_ref[c] + NUDGING * cells[:, piece]
            if c == 0:
                ghost = ghost_weight(east_ref[:, piece], True) * cells[:, breadth : breadth + 1]
                value = value + jnp.where(lane == 0, ghost, 0.0)
            if c == pieces - 1:
                ghost = ghost_weight(east_ref[:, piece], False) * cells[:, breadth + 1 : breadth + 2]
                value = value + jnp.where(lane == LANES - 1, ghost, 0.0)
            field_ref[c] = value
        outer = height - 1 - inner_line(height, row)
        ghost = ghost_weight(join_slabs(speeds_ref, 0, pieces), row == 0) * ring
        store_line(field_ref, levels, outer, load_line(field_ref, levels, outer) + ghost)
        edge_ref[...] = edge_level(field_ref, height, lev)


def average_kernel(levels, field_ref, east_ref, north_ref, other_ref, message_ref, part_ref, nothing_ref):
    pieces, size, _ = field_ref.shape
    height, breadth = nothing_ref.shape
    third_y = height // 3
    tile, row, lev = place()

    @pl.when(tile == lax.axis_size("tiles") - 1)
    def _():
        nothing_ref[...] = jnp.zeros_like(nothing_ref)
        full_step(part_ref, field_ref, east_ref, north_ref, nothing_ref, levels, lev, True, None, None, None, None)
        sums = sums_table(breadth)
        shape = (third_y * levels, size)
        taken = iota(shape, 0)
        block = taken // levels
        level, line = split_level(iota(shape, 1), height)
        offset = line - 3 * block
        rows = table((taken - block * levels == level) & (offset >= 0) & (offset <= 2))
        means = from_left(rows, from_right(part_ref[...], sums)) * (1.0 / 9.0)
        for m in range(third_y):
            message_ref[m] = means[m * levels : (m + 1) * levels]
        shared = load_line(field_ref, levels, inner_line(height, row))
        shared = ghost_weight(join_slabs(other_ref, 0, pieces), row == 0) * shared
        message_ref[third_y] = from_right(shared, sums) * (1.0 / 9.0)
        for i in range(third_y + 1, message_ref.shape[0]):
            message_ref[i] = jnp.zeros((levels, LANES), jnp.float32)


def sums_table(breadth):
    offset = iota((breadth, LANES), 0) - 3 * iota((breadth, LANES), 1)
    return table((offset >= 0) & (offset <= 2))


def message_kernel(levels, level_ref, part_ref, own_ref, other_ref, message_ref):
    height, breadth = level_ref.shape
    third_y = height // 3
    tile, row, lev = place()
    nest = tile == lax.axis_size("tiles") - 1

    @pl.when(jnp.logical_not(nest))
    def _():
        message_ref[...] = own_ref[...] + other_ref[...]

    @pl.when(nest)
    def _():
        offset = iota((third_y, height), 1) - 3 * iota((third_y, height), 0)
        rows = table((offset >= 0) & (offset <= 2))
        across = from_left(rows, from_right(level_ref[...], sums_table(breadth))) * (VERTICAL_MIX / 9.0)
        at_edge = iota((levels, LANES), 0) == jnp.where(lev == 0, levels - 1, 0)
        for m in range(third_y):
            message_ref[m] = part_ref[m] + jnp.where(at_edge, across[m : m + 1], 0.0)
        for i in range(third_y, message_ref.shape[0]):
            message_ref[i] = part_ref[i]


def blend_kernel(
    levels,
    weight_ref,
    field_ref,
    window_ref,
    one_ref,
    two_ref,
    three_ref,
    coef_three_ref,
    coef_two_ref,
    coef_one_ref,
    rows_ref,
):
    pieces, size, _ = field_ref.shape
    height = size // levels
    third_y = height // 3
    slots = third_y + 2
    tile_count = lax.axis_size("tiles")
    tile, row, _ = place()
    nest = tile == tile_count - 1

    @pl.when(nest)
    def _():
        store_slabs(rows_ref, 0, load_line(field_ref, levels, inner_line(height, row)))
        for i in range(pieces, rows_ref.shape[0]):
            rows_ref[i] = jnp.zeros((levels, LANES), jnp.float32)

    @pl.when(jnp.logical_not(nest))
    def _():
        def of_nest(refs, i):
            one, two, three = refs
            return jnp.where(tile == 0, three[i], jnp.where(tile == 1, two[i], one[i]))

        def mine(i):
            return of_nest((one_ref, two_ref, three_ref), i)

        def coefficient(i):
            return of_nest((coef_one_ref, coef_two_ref, coef_three_ref), i)

        def whole(i):
            odd = tile % 2 == 1
            west = jnp.where(odd, one_ref[i], three_ref[i])
            east = jnp.where(odd, three_ref[i], one_ref[i])
            part = jnp.where(tile == 0, window_ref[i], window_ref[i] + west)
            return jnp.where(tile == tile_count - 2, part, part + east)

        weight = weight_ref[:, 0:1]
        extra = whole(slots)
        lane = iota(extra.shape, 1)
        at_first, at_last = lane == 0, lane == LANES - 1
        lines = []
        for s in range(slots):
            x = whole(s)
            west = jnp.where(at_first, extra[:, s : s + 1], pltpu.roll(x, 1, 1))
            last = EAST_LANE + s
            east = jnp.where(at_last, extra[:, last : last + 1], pltpu.roll(x, LANES - 1, 1))
            lines.append((west, x, east))
        edges = coefficient(3)
        ghosts = [coefficient(q) for q in range(3)]

        def outward(side, q):
            near = lines[1] if side == 0 else lines[slots - 2]
            far = lines[0] if side == 0 else lines[slots - 1]
            return (2.0 / 3.0) * far[q] + (1.0 / 3.0) * near[q]

        def sideward(s):
            west, x, east = lines[s]
            return (2.0 / 3.0) * jnp.where(at_first, west, east) + (1.0 / 3.0) * x

        sidewards = [sideward(s) for s in range(slots)]
        columns = [w + 7.0 * x + e for w, x, e in lines]
        for m in range(third_y):
            x = lines[m + 1][1]
            value = mine(m) + (NUDGING / 81.0) * (columns[m] + 7.0 * columns[m + 1] + columns[m + 2])
            for q in range(3):
                lane_of = 8 * m + q
                first, last = edges[:, lane_of : lane_of + 1], edges[:, lane_of + 3 : lane_of + 4]
                scale = jnp.where(at_first, first, jnp.where(at_last, last, 0.0))
                value = value + scale * sidewards[m + q]
            for side, at in ((0, 0), (1, third_y - 1)):
                if m == at:
                    for q in range(3):
                        value = value + jnp.where(row == side, ghosts[q], 0.0) * outward(side, q)
            rows_ref[m] = x + weight * (value - x)
        rows_ref[third_y] = weight * mine(third_y)


def later_kernel(
    levels,
    west_ref,
    south_ref,
    field_ref,
    east_ref,
    north_ref,
    level_ref,
    one_ref,
    two_ref,
    three_ref,
    parent_ref,
    blend_ref,
    out_ref,
    fine_ref,
    side_ref,
    northern_ref,
    southern_ref,
):
    height, breadth = level_ref.shape
    third_y = height // 3
    slots = third_y + 2
    tile, row, lev = place()
    nest = tile == lax.axis_size("tiles") - 1

    @pl.when(nest)
    def _():
        slabs = [one_ref[s] + two_ref[s] + three_ref[s] for s in range(slots + 1)]
        cells, ring = refine(slabs[:slots], slabs[slots], height, breadth, row)
        fine_ref[...] = cells[:, :breadth]
        side_ref[...] = cells[:, breadth:]
        zero = jnp.zeros_like(ring)
        northern_ref[...] = jnp.where(row == 0, ring, zero)
        southern_ref[...] = jnp.where(row == 0, zero, ring)
        full_step(
            out_ref,
            field_ref,
            east_ref,
            north_ref,
            level_ref,
            levels,
            lev,
            True,
            northern_ref,
            southern_ref,
            side_ref,
            fine_ref,
        )

    @pl.when(jnp.logical_not(nest))
    def _():
        out_ref[...] = parent_ref[...]
        start = west_ref[1] - tile * breadth
        top = south_ref[1] + row * third_y - row * height
        for m in range(third_y):
            place_row(out_ref, levels, top + m, start, blend_ref[m])


def last_kernel(
    levels, west_ref, south_ref, given_ref, speeds_ref, blend_ref, rows_ref, out_hbm, out_ref, sems
):
    pieces, size, _ = given_ref.shape
    breadth = pieces * LANES
    height = size // levels
    third_y = height // 3
    tile, row, _ = place()
    nest = tile == lax.axis_size("tiles") - 1
    out_ref[...] = given_ref[...]

    @pl.when(nest)
    def _():
        inner = inner_line(height, row)
        halo = ghost_weight(join_slabs(speeds_ref, pieces, pieces), row == 1) * join_slabs(rows_ref, 0, pieces)
        store_line(out_ref, levels, inner, load_line(out_ref, levels, inner) + halo)

    @pl.when(jnp.logical_not(nest))
    def _():
        start = west_ref[1] - tile * breadth
        top = south_ref[1] + (1 - row) * third_y - row * height
        for m in range(third_y):
            value = rows_ref[m]
            if m == 0:
                value = value + jnp.where(row == 0, blend_ref[third_y], 0.0)
            if m == third_y - 1:
                value = value + jnp.where(row == 1, blend_ref[third_y], 0.0)
            place_row(out_ref, levels, top + m, start, value)
        near = jnp.where(row == 0, third_y - 1, 0)
        line = south_ref[1] + row * third_y - row * height + near
        place_row(out_ref, levels, line, start, blend_ref[near] + rows_ref[third_y])

    copies = [
        pltpu.make_async_copy(out_ref.at[c], out_hbm.at[:, pl.ds(c * LANES, LANES)], sems.at[c])
        for c in range(pieces)
    ]
    for copy in copies:
        copy.start()
    for copy in copies:
        copy.wait()


def call(kernel, outs, inputs, places, scratch=(), flops=0, out_place="v", aliases=()):
    spaces = {"s": pltpu.SMEM, "v": pltpu.VMEM, "h": pltpu.HBM}
    outs = [spaces[out_place](out, jnp.float32) if isinstance(out, tuple) else out for out in outs]
    moved = sum(4 * math.prod(out.shape) for out in outs) + sum(array.nbytes for array in inputs)
    inputs = [
        array if p == "v" else pltpu.with_memory_space_constraint(array, spaces[p])
        for array, p in zip(inputs, places)
    ]
    return pl.pallas_call(
        kernel,
        out_shape=outs,
        in_specs=[pl.BlockSpec(memory_space=spaces[p]) for p in places],
        out_specs=[pl.BlockSpec(memory_space=out.memory_space) for out in outs],
        scratch_shapes=[pltpu.VMEM(s, jnp.float32) if isinstance(s, tuple) else s for s in scratch],
        input_output_aliases=dict(aliases),
        compiler_params=pltpu.CompilerParams(vmem_limit_bytes=32 * 1024 * 1024),
        cost_estimate=pl.CostEstimate(flops=flops, bytes_accessed=moved, transcendentals=0),
    )(*inputs)


def per_device_paired(air_state, wind_east, wind_north, feedback_weight, nest_west, nest_south):
    levels, height, breadth = air_state.shape
    third_y = height // 3
    pieces = breadth // LANES
    slots = third_y + 2
    size = levels * height
    flat = (size, breadth)
    chunked = (pieces, size, LANES)
    air, east, north = (array.reshape(flat) for array in (air_state, wind_east, wind_north))
    weight = jnp.broadcast_to(feedback_weight[:, None], (levels, LANES))
    swap = [(0, 1), (1, 0)]

    def slabs(count):
        return (count, levels, LANES)

    def kernel(body):
        return functools.partial(body, levels)

    rows, air_pieces, west, south = call(
        kernel(pack_kernel),
        [slabs(slots + 1 + pieces), chunked, pltpu.SMEM((2,), jnp.int32), pltpu.SMEM((2,), jnp.int32)],
        [nest_west, nest_south, air],
        "hhh",
        [pltpu.SemaphoreType.DMA((pieces + 2,))],
    )
    own, level, speeds = call(
        kernel(own_kernel),
        [slabs(slots + 1), (height, breadth), slabs(2 * pieces)],
        [west, south, air_pieces, east, north],
        "ssvvv",
        flops=30 * size * breadth,
    )
    rows = lax.ppermute(rows, "rows", swap)
    level = lax.ppermute(level, "lev", swap)
    pairs = [[(0, 1), (1, 0), (2, 3), (3, 2)], [(1, 3), (3, 1)], [(0, 3), (3, 0), (1, 2), (2, 1)]]

    def over_tiles(message):
        return [lax.ppermute(message, "tiles", pair) for pair in pairs]

    starting = over_tiles(own + rows[: slots + 1])
    sides = [(size, LANES), (levels, breadth), (levels, breadth)]
    early, other = call(
        kernel(early_kernel),
        [chunked, slabs(slots + 1)],
        [west, south, air, east, north, rows, level, starting[0], speeds],
        "ssvvvvvvv",
        sides,
        flops=30 * size * breadth,
    )
    early, other = call(
        kernel(middle_kernel),
        [chunked, slabs(slots + 1)],
        [west, south, air, east, north, rows, level, starting[2], starting[0], early, other],
        "ssvvvvvvvvv",
        sides,
        flops=30 * size * breadth,
        aliases=[(9, 0), (10, 1)],
    )
    other = lax.ppermute(other, "rows", swap)
    first, edge, own = call(
        kernel(first_kernel),
        [chunked, (height, breadth), slabs(slots + 1)],
        [west, south, early, east, speeds, *starting[::-1]],
        "ssvvvvvv",
        flops=10 * size * breadth,
    )
    level = lax.ppermute(edge, "lev", swap)
    (part,) = call(
        kernel(average_kernel),
        [slabs(slots + 1)],
        [first, east, north, other],
        "vvvv",
        [flat, (height, breadth)],
        flops=30 * size * breadth,
    )
    (message,) = call(
        kernel(message_kernel),
        [slabs(slots + 1)],
        [level, part, own, other],
        "vvvv",
    )
    received = over_tiles(message)
    (blend,) = call(
        kernel(blend_kernel),
        [slabs(third_y + 1)],
        [weight, first, message, *received, *starting[::-1]],
        "v" * 9,
    )
    rows = lax.ppermute(blend, "rows", swap)
    (later,) = call(
        kernel(later_kernel),
        [chunked],
        [west, south, first, east, north, level, *received, early, blend],
        "ss" + "v" * 9,
        [flat, *sides],
        flops=30 * size * breadth,
    )
    (out,) = call(
        kernel(last_kernel),
        [flat],
        [west, south, later, speeds, blend, rows],
        "ssvvvv",
        [chunked, pltpu.SemaphoreType.DMA((pieces,))],
        out_place="h",
    )
    return out.reshape(air_state.shape)


def solution(mesh):
    in_specs = (
        P(("members", "lev"), "rows", "tiles"),
        P(("members", "lev"), "rows", "tiles"),
        P(("members", "lev"), "rows", "tiles"),
        P("lev"),
        P("members"),
        P("members"),
    )
    out_specs = P(("members", "lev"), "rows", "tiles")
    paired = mesh.shape["tiles"] == 4 and mesh.shape["rows"] == 2 and mesh.shape["lev"] == 2
    return jax.shard_map(
        per_device_paired if paired else per_device, mesh=mesh, in_specs=in_specs, out_specs=out_specs, check_vma=False
    )
```

```python
import functools
import math

import jax
import jax.numpy as jnp
from jax import lax
from jax.experimental import pallas as pl
from jax.experimental.pallas import tpu as pltpu
from jax.sharding import PartitionSpec as P

VERTICAL_MIX = 0.1
PARENT_MIXING = 0.04
NEST_MIXING = 0.18
NEST_ADVECT = 1.5
NUDGING = 0.2


def padded_2(array, sides, width):
    for axis, dim in sides:
        size, length = (lax.axis_size(axis), array.shape[dim])
        up = [(i, (i + 1) % size) for i in range(size - 1)]
        down = [(j, i) for i, j in up]
        last = lax.slice_in_dim(array, length - width, length, axis=dim)
        first = lax.slice_in_dim(array, 0, width, axis=dim)
        before = lax.ppermute(last, axis, up)
        after = lax.ppermute(first, axis, down)
        array = jnp.concatenate([before, array, after], axis=dim)
    return array


def interp_table(cells):
    extended = jnp.arange(cells + 2, dtype=jnp.int32) - 1
    coarse = jnp.floor_divide(extended, 3)
    offset = extended - 3 * coarse
    fraction = jnp.abs(offset - 1).astype(jnp.float32) / 3.0
    nearest = coarse + 1
    beside = nearest + (offset - 1)
    slots = jnp.arange(cells // 3 + 2, dtype=jnp.int32)[:, None]
    first_part = jnp.where(
        slots == nearest[None, :], 1.0 - fraction[None, :], jnp.zeros((), jnp.float32)
    )
    second_part = jnp.where(slots == beside[None, :], fraction[None, :], jnp.zeros((), jnp.float32))
    return first_part + second_part


def tendency(padded, speed_east, speed_north, advect_scale, mixing_scale):
    centre = padded[1:-1, 1:-1, 1:-1]
    eastern = padded[1:-1, 1:-1, 2:]
    western = padded[1:-1, 1:-1, :-2]
    southern = padded[1:-1, 2:, 1:-1]
    northern = padded[1:-1, :-2, 1:-1]
    upper = padded[2:, 1:-1, 1:-1]
    lower = padded[:-2, 1:-1, 1:-1]
    advect = speed_east * (eastern - western) + speed_north * (southern - northern)
    horizontal = eastern + western + southern + northern - 4.0 * centre
    vertical = upper + lower - 2.0 * centre
    return -0.5 * advect_scale * advect + mixing_scale * horizontal + VERTICAL_MIX * vertical


def padded_block(block_field):
    return padded_2(block_field, (("tiles", 2), ("rows", 1), ("lev", 0)), 1)


def per_device(air_state, wind_east, wind_north, feedback_weight, nest_west, nest_south):
    levels, height, breadth = air_state.shape
    tile_count = lax.axis_size("tiles")
    row_count = lax.axis_size("rows")
    tile_index = lax.axis_index("tiles")
    row_index = lax.axis_index("rows")
    parent_tiles = 3 * tile_count // 4
    nest_tiles = tile_count - parent_tiles
    in_nest = tile_index >= parent_tiles
    nest_tile = tile_index - parent_tiles
    cross_x = breadth // 3 + 2
    cross_y = height // 3 + 2
    third_x = breadth // 3
    third_y = height // 3
    first_x = tile_index * breadth
    first_y = row_index * height
    columns = jnp.arange(breadth, dtype=jnp.int32)
    lines = jnp.arange(height, dtype=jnp.int32)
    targets_x = jnp.arange(tile_count, dtype=jnp.int32)
    targets_y = jnp.arange(row_count, dtype=jnp.int32)
    highest = lax.Precision.HIGHEST
    table_x = interp_table(breadth)
    table_y = interp_table(height)
    zero_value = jnp.zeros((), jnp.float32)

    def boundary(source, substep):
        anchor_x = nest_west[substep] + (targets_x - parent_tiles) * third_x - 1
        slot_x = jnp.arange(cross_x, dtype=jnp.int32)
        pick_x = (
            (first_x + columns)[None, :, None] == anchor_x[:, None, None] + slot_x[None, None, :]
        ) & (targets_x >= parent_tiles)[:, None, None]
        pick_x = pick_x.astype(jnp.float32)
        anchor_y = nest_south[substep] + targets_y * third_y - 1
        slot_y = jnp.arange(cross_y, dtype=jnp.int32)
        pick_y = (
            (first_y + lines)[None, :, None] == anchor_y[:, None, None] + slot_y[None, None, :]
        ).astype(jnp.float32)
        pieces = jnp.einsum("lyi,tij->tlyj", source, pick_x, precision=highest)
        merged = lax.all_to_all(pieces, "tiles", split_axis=0, concat_axis=0, tiled=True).sum(
            axis=0
        )
        pieces = jnp.einsum("lyj,ryw->rlwj", merged, pick_y, precision=highest)
        window = lax.all_to_all(pieces, "rows", split_axis=0, concat_axis=0, tiled=True).sum(axis=0)
        along = jnp.einsum("lwj,je->lwe", window, table_x, precision=highest)
        return jnp.einsum("lwe,wf->lfe", along, table_y, precision=highest)

    def assemble(block_field, fine):
        padded = padded_block(block_field)
        fine_padded = jnp.pad(fine, ((1, 1), (0, 0), (0, 0)))
        column_place = lax.broadcasted_iota(jnp.int32, padded.shape, 2)
        line_place = lax.broadcasted_iota(jnp.int32, padded.shape, 1)
        outside = (column_place == 0) & (nest_tile == 0) | (column_place == breadth + 1) & (
            nest_tile == nest_tiles - 1
        )
        outside = (
            outside
            | (line_place == 0) & (row_index == 0)
            | (line_place == height + 1) & (row_index == row_count - 1)
        )
        padded = jnp.where(outside & in_nest, fine_padded, padded)
        seam_cells = (column_place == breadth + 1) & (tile_index == parent_tiles - 1)
        return jnp.where(seam_cells, zero_value, padded)

    advect_scale = jnp.where(in_nest, jnp.float32(NEST_ADVECT), jnp.float32(1.0))
    mixing_scale = jnp.where(in_nest, jnp.float32(NEST_MIXING), jnp.float32(PARENT_MIXING))
    fine_first = boundary(air_state, 0)
    change = tendency(
        assemble(air_state, fine_first), wind_east, wind_north, advect_scale, mixing_scale
    )
    nudging_term = jnp.where(in_nest, NUDGING * (fine_first[:, 1:-1, 1:-1] - air_state), zero_value)
    step_one = air_state + change + nudging_term
    fine_second = boundary(step_one, 1)
    change = tendency(
        assemble(step_one, fine_second), wind_east, wind_north, advect_scale, mixing_scale
    )
    nested_two = step_one + change + NUDGING * (fine_second[:, 1:-1, 1:-1] - step_one)
    step_two = jnp.where(in_nest, nested_two, step_one)
    coarse = step_two.reshape(levels, third_y, 3, third_x, 3).mean(axis=(2, 4))
    avg_columns = jnp.arange(third_x, dtype=jnp.int32)
    avg_lines = jnp.arange(third_y, dtype=jnp.int32)
    west_last = nest_west[1]
    south_last = nest_south[1]
    place_x = (
        (west_last + (targets_x - parent_tiles) * third_x)[:, None, None]
        + avg_columns[None, :, None]
        == (first_x + columns)[None, None, :]
    ) & (targets_x >= parent_tiles)[:, None, None]
    place_x = place_x.astype(jnp.float32)
    place_y = (
        (south_last + targets_y * third_y)[:, None, None] + avg_lines[None, :, None]
        == (first_y + lines)[None, None, :]
    ).astype(jnp.float32)
    parent_y = south_last + row_index * third_y + avg_lines
    send_y = (jnp.floor_divide(parent_y, height)[None, :] == targets_y[:, None]) & in_nest
    pieces = jnp.where(send_y[:, None, :, None], coarse[None], zero_value)
    received = lax.all_to_all(pieces, "rows", split_axis=0, concat_axis=0, tiled=True)
    spread = jnp.einsum("slba,sby->lya", received, place_y, precision=highest)
    parent_x = west_last + nest_tile * third_x + avg_columns
    send_x = jnp.floor_divide(parent_x, breadth)[None, :] == targets_x[:, None]
    pieces = jnp.where(send_x[:, None, None, :], spread[None], zero_value)
    received = lax.all_to_all(pieces, "tiles", split_axis=0, concat_axis=0, tiled=True)
    placed = jnp.einsum("slya,sai->lyi", received, place_x, precision=highest)
    global_x = (first_x + columns)[None, None, :]
    global_y = (first_y + lines)[None, :, None]
    covered = (global_x >= west_last) & (global_x < west_last + nest_tiles * third_x)
    covered = covered & (global_y >= south_last) & (global_y < south_last + row_count * third_y)
    covered = covered & jnp.logical_not(in_nest)
    blended = step_two + feedback_weight[:, None, None] * (placed - step_two)
    return jnp.where(covered, blended, step_two)


LANES = 128
FIRST_LANE = 32
LAST_LANE = 96
EAST_LANE = 64
WEIGHTS = 4


def iota(shape, dim):
    return lax.broadcasted_iota(jnp.int32, shape, dim)


def split_level(place, height):
    level = ((place.astype(jnp.float32) + 0.5) * (1.0 / height)).astype(jnp.int32)
    return level, place - level * height


def table(values):
    return values.astype(jnp.float32).astype(jnp.bfloat16)


def parts_of(array):
    high = array.astype(jnp.bfloat16)
    low = (array - high.astype(jnp.float32)).astype(jnp.bfloat16)
    return high, low


def dot(left, right):
    return jnp.dot(left, right, preferred_element_type=jnp.float32)


def from_left(weights, array):
    high, low = parts_of(array)
    return dot(weights, high) + dot(weights, low)


def from_right(array, weights):
    high, low = parts_of(array)
    return dot(high, weights) + dot(low, weights)


def hat(distance):
    return jnp.maximum(0, 3 - jnp.abs(distance - 1))


def place():
    return lax.axis_index("tiles"), lax.axis_index("rows"), lax.axis_index("lev")


def level_table(levels, height):
    shape = (levels, levels * height)
    level, _ = split_level(iota(shape, 1), height)
    return table(iota(shape, 0) == level)


def spread_table(levels, height):
    shape = (levels * height, levels)
    level, _ = split_level(iota(shape, 0), height)
    return table(iota(shape, 1) == level)


def load_line(ref, levels, line):
    rows = pl.ds(line, levels, stride=ref.shape[1] // levels)
    return jnp.concatenate([ref[c, rows, :] for c in range(ref.shape[0])], axis=1)


def store_line(ref, levels, line, value):
    rows = pl.ds(line, levels, stride=ref.shape[1] // levels)
    for c in range(ref.shape[0]):
        ref[c, rows, :] = value[:, c * LANES : (c + 1) * LANES]


def load_level(ref, height, l):
    rows = pl.ds(l * height, height)
    if len(ref.shape) == 2:
        return ref[rows, :]
    return jnp.concatenate([ref[c, rows, :] for c in range(ref.shape[0])], axis=1)


def store_level(ref, height, l, value):
    rows = pl.ds(l * height, height)
    if len(ref.shape) == 2:
        ref[rows, :] = value
    else:
        for c in range(ref.shape[0]):
            ref[c, rows, :] = value[:, c * LANES : (c + 1) * LANES]


def store_slabs(ref, first, wide):
    for i in range(wide.shape[1] // LANES):
        ref[first + i] = wide[:, i * LANES : (i + 1) * LANES]


def join_slabs(ref, first, count):
    return jnp.concatenate([ref[first + i] for i in range(count)], axis=1)


def column_pieces(start, pieces):
    first = (start + 64 * LANES) // LANES - 64
    offset = start - first * LANES
    held = [(c >= 0) & (c < pieces) for c in (first, first + 1)]
    return [jnp.clip(c, 0, pieces - 1) for c in (first, first + 1)], held, offset


def pack_window(ref, field_ref, levels, top, start):
    pieces, size, _ = field_ref.shape
    height = size // levels
    slots = ref.shape[0] - 1
    lane = iota((levels, LANES), 1)
    (left, right), (left_held, right_held), offset = column_pieces(start, pieces)
    before = lax.rem(offset + LANES - 1, LANES)
    (beside, _), (beside_held, _), _ = column_pieces(start - 1, pieces)
    in_left = lane < LANES - offset
    held = jnp.where(in_left, left_held.astype(jnp.float32), right_held.astype(jnp.float32))
    west_held, east_held = beside_held.astype(jnp.float32), right_held.astype(jnp.float32)
    turn = lax.rem(LANES - offset, LANES)
    extra = jnp.zeros((levels, LANES), jnp.float32)
    for slot in range(slots):
        line = top + slot
        there = ((line >= 0) & (line < height)).astype(jnp.float32)
        rows = pl.ds(jnp.clip(line, 0, height - 1), levels, stride=height)
        near, far, west = field_ref[left, rows, :], field_ref[right, rows, :], field_ref[beside, rows, :]
        ref[slot] = jnp.where(in_left, pltpu.roll(near, turn, 1), pltpu.roll(far, turn, 1)) * (held * there)
        west = pltpu.roll(west, lax.rem(LANES + slot - before, LANES), 1) * (west_held * there)
        east = pltpu.roll(far, lax.rem(LANES + EAST_LANE + slot - offset, LANES), 1) * (east_held * there)
        extra = jnp.where(lane == slot, west, jnp.where(lane == EAST_LANE + slot, east, extra))
    ref[slots] = extra


def place_row(ref, levels, line, start, value):
    pieces, size, _ = ref.shape
    height = size // levels
    lane = iota((levels, LANES), 1)
    at, held, offset = column_pieces(start, pieces)
    value = pltpu.roll(value, offset, 1)
    there = (line >= 0) & (line < height)
    rows = pl.ds(jnp.clip(line, 0, height - 1), levels, stride=height)
    for c in range(2):
        mine = (lane >= offset) if c == 0 else (lane < offset)
        ref[at[c], rows, :] = jnp.where(mine & (held[c] & there), value, ref[at[c], rows, :])


def pack_edges(field_ref, levels):
    height = field_ref.shape[1] // levels
    lane = iota((levels, LANES), 1)
    packed = jnp.zeros((levels, LANES), jnp.float32)
    for line in range(height):
        rows = pl.ds(line, levels, stride=height)
        first = field_ref[0, rows, :]
        last = field_ref[field_ref.shape[0] - 1, rows, :]
        packed = jnp.where(lane == FIRST_LANE + line, pltpu.roll(first, FIRST_LANE + line, 1), packed)
        packed = jnp.where(lane == LAST_LANE + line, pltpu.roll(last, LAST_LANE + line + 1, 1), packed)
    return packed


def neighbour_columns(even, odd, parent_tiles, tile):
    is_odd = tile % 2 == 1
    west = jnp.where(is_odd, even, odd)
    east = jnp.where(is_odd, odd, even)
    west = jnp.where(tile == 0, jnp.zeros_like(west), west)
    east = jnp.where(tile >= parent_tiles - 1, jnp.zeros_like(east), east)
    return jnp.where(iota(west.shape, 1) < LAST_LANE, east, west)


def unpack_edges(columns, levels, height):
    wide = from_left(spread_table(levels, height), columns)
    lane = iota(wide.shape, 1)
    _, line = split_level(iota(wide.shape, 0), height)
    west = jnp.sum(jnp.where(lane == line + LAST_LANE, wide, 0.0), axis=1, keepdims=True)
    east = jnp.sum(jnp.where(lane == line + FIRST_LANE, wide, 0.0), axis=1, keepdims=True)
    return jnp.where(lane == 0, west, jnp.where(lane == 1, east, 0.0))


def refine(slabs, extra, height, breadth, row):
    slots, levels = len(slabs), extra.shape[0]
    beside = [pltpu.roll(extra, LANES - s, 1) if s else extra for s in range(slots)]
    window = jnp.concatenate([jnp.concatenate(slabs, axis=0), jnp.concatenate(beside, axis=0)], axis=1)
    shape = (2 * LANES, breadth + LANES)
    slot, cell = iota(shape, 0), iota(shape, 1)
    held = (slot <= LANES) | (slot == LANES + EAST_LANE)
    at = jnp.where(slot < LANES, slot, jnp.where(slot == LANES, -1, LANES))
    cell = jnp.where(cell == breadth, -1, jnp.where(cell == breadth + 1, breadth, cell))
    across = jnp.where(held & (cell <= breadth), hat(cell - 3 * at), 0)
    wide = from_right(window, table(across)) * (1.0 / 9.0)
    shape = (levels * height, slots * levels)
    taken = iota(shape, 1)
    slot = taken // levels
    level, line = split_level(iota(shape, 0), height)
    along = jnp.where(taken - slot * levels == level, hat(line - 3 * (slot - 1)), 0)
    cells = from_left(table(along), wide)
    ring = jnp.where(
        row == 0,
        2.0 * wide[:levels] + wide[levels : 2 * levels],
        2.0 * wide[(slots - 1) * levels :] + wide[(slots - 2) * levels : (slots - 1) * levels],
    )
    return cells, ring[:, :breadth]


def beside_rows(x, north, south):
    height = x.shape[0]
    line = iota(x.shape, 0)
    northern = jnp.where(line == 0, north, pltpu.roll(x, 1, 0))
    southern = jnp.where(line == height - 1, south, pltpu.roll(x, height - 1, 0))
    return northern, southern


def beside_columns(x, west, east):
    breadth = x.shape[1]
    column = iota(x.shape, 1)
    western = jnp.where(column == 0, west, pltpu.roll(x, 1, 1))
    eastern = jnp.where(column == breadth - 1, east, pltpu.roll(x, breadth - 1, 1))
    return western, eastern


def change_of(x, sides, u, v, upper, lower, nest):
    advect_scale = NEST_ADVECT if nest else 1.0
    mixing_scale = NEST_MIXING if nest else PARENT_MIXING
    northern, southern, western, eastern = sides
    advect = u * (eastern - western) + v * (southern - northern)
    horizontal = eastern + western + southern + northern - 4.0 * x
    vertical = upper + lower - 2.0 * x
    return -0.5 * advect_scale * advect + mixing_scale * horizontal + VERTICAL_MIX * vertical


def ghost_weight(speed, before):
    return jnp.where(before, 0.5 * NEST_ADVECT, -0.5 * NEST_ADVECT) * speed + NEST_MIXING


def full_step(out_ref, field_ref, u_ref, v_ref, level_ref, levels, lev, nest, north, south, side, fine):
    height, breadth = level_ref.shape
    zero = jnp.zeros((height, breadth), jnp.float32)

    def block(ref, l):
        return load_level(ref, height, l)

    for l in range(levels):
        x = block(field_ref, l)
        lower = block(field_ref, l - 1) if l else jnp.where(lev == 1, level_ref[...], zero)
        upper = block(field_ref, l + 1) if l < levels - 1 else jnp.where(lev == 0, level_ref[...], zero)
        rows = [0.0 if ref is None else ref[pl.ds(l, 1), :] for ref in (north, south)]
        if side is None:
            columns = (0.0, 0.0)
        else:
            beside = side[pl.ds(l * height, height), :]
            columns = (beside[:, 0:1], beside[:, 1:2])
        sides = beside_rows(x, *rows) + beside_columns(x, *columns)
        fresh = x + change_of(x, sides, block(u_ref, l), block(v_ref, l), upper, lower, nest)
        if nest:
            fresh = fresh - NUDGING * x if fine is None else fresh + NUDGING * (block(fine, l) - x)
        store_level(out_ref, height, l, fresh)


def inner_line(height, row):
    return jnp.where(row == 0, height - 1, 0)


def edge_level(ref, height, lev):
    last = ref.shape[1] // height - 1
    return jnp.where(lev == 0, load_level(ref, height, last), load_level(ref, height, 0))


def ghost_row_weights(ghost, breadth):
    cell, third = iota((breadth, 3 * LANES), 0), iota((breadth, 3 * LANES), 1)
    kind = third // LANES
    offset = cell - 3 * (third - kind * LANES)
    middle = jnp.where(offset == 1, 3, jnp.where((offset == 0) | (offset == 2), 2, 0))
    weight = jnp.where(kind == 1, middle, jnp.where(offset == kind, 1, 0))
    return from_right(ghost, table(weight)) * (1.0 / 27.0)


def ghost_column_weights(first, last, levels, height):
    shape = (levels * height, LANES)
    lane = iota(shape, 1)
    _, line = split_level(iota(shape, 0), height)
    block = lane // 8
    inside = lane - block * 8
    eastern = inside >= 3
    kind = jnp.where(eastern, inside - 3, inside)
    offset = line - 3 * block
    middle = jnp.where(offset == 1, 3, jnp.where((offset == 0) | (offset == 2), 2, 0))
    weight = jnp.where(kind == 1, middle, jnp.where(offset == kind, 1, 0))
    weight = jnp.where((inside < 6) & (block < height // 3), weight, 0).astype(jnp.float32)
    columns = jnp.where(eastern, last, first) * weight
    return from_left(level_table(levels, height), columns) * (1.0 / 27.0)


def pack_kernel(
    levels, west_hbm, south_hbm, air_hbm, north_hbm, rows_ref, air_ref, west_ref, south_ref, north_ref, sems
):
    pieces, size, _ = air_ref.shape
    breadth = pieces * LANES
    height = size // levels
    third_y = height // 3
    slots = rows_ref.shape[0] - 1 - pieces
    tile, row, _ = place()
    nest = tile == lax.axis_size("tiles") - 1
    inner = inner_line(height, row)

    def column_copies(source, target, first):
        return [
            pltpu.make_async_copy(source.at[:, pl.ds(c * LANES, LANES)], target.at[c], sems.at[first + c])
            for c in range(pieces)
        ]

    copies = column_copies(air_hbm, air_ref, 0)
    copies.append(pltpu.make_async_copy(west_hbm, west_ref, sems.at[2 * pieces]))
    copies.append(pltpu.make_async_copy(south_hbm, south_ref, sems.at[2 * pieces + 1]))
    speeds = column_copies(north_hbm, north_ref, pieces)
    for copy in copies:
        copy.start()

    @pl.when(nest)
    def _():
        for copy in speeds:
            copy.start()

    for copy in copies:
        copy.wait()
    store_slabs(rows_ref, slots + 1, load_line(air_ref, levels, inner))
    part = rows_ref.at[pl.ds(0, slots + 1)]

    @pl.when(nest)
    def _():
        for copy in speeds:
            copy.wait()
        part[...] = jnp.zeros_like(part)
        store_slabs(rows_ref, WEIGHTS, load_line(north_ref, levels, inner))

    @pl.when(jnp.logical_not(nest))
    def _():
        start = west_ref[0] - tile * breadth
        top = south_ref[0] - 1 - row * height
        pack_window(part, air_ref, levels, top + (1 - row) * third_y, start)


def own_kernel(
    levels, west_ref, south_ref, air_ref, east_ref, north_ref, own_ref, level_ref, speeds_ref, edges_ref
):
    pieces, size, _ = air_ref.shape
    breadth = pieces * LANES
    height = size // levels
    third_y = height // 3
    slots = own_ref.shape[0] - 1
    tile, row, lev = place()
    nest = tile == lax.axis_size("tiles") - 1
    level_ref[...] = edge_level(air_ref, height, lev)

    @pl.when(nest)
    def _():
        inner = inner_line(height, row)
        shape = (2 * levels, size)
        taken = iota(shape, 0)
        level, line = split_level(iota(shape, 1), height)
        wanted = jnp.where(taken < levels, height - 1 - inner, inner)
        picked = table((lax.rem(taken, levels) == level) & (line == wanted))
        speeds = from_left(picked, north_ref[...])
        outer = speeds[:levels]
        store_slabs(speeds_ref, 0, outer)
        store_slabs(speeds_ref, pieces, speeds[levels:])
        own_ref[...] = jnp.zeros_like(own_ref)
        edges_ref[...] = jnp.zeros_like(edges_ref)
        store_slabs(own_ref, 0, ghost_row_weights(ghost_weight(outer, row == 0), breadth))
        first = ghost_weight(east_ref[:, 0:1], True)
        last = ghost_weight(east_ref[:, breadth - 1 : breadth], False)
        own_ref[WEIGHTS - 1] = ghost_column_weights(first, last, levels, height)

    @pl.when(jnp.logical_not(nest))
    def _():
        start = west_ref[0] - tile * breadth
        top = south_ref[0] - 1 - row * height
        pack_window(own_ref, air_ref, levels, top + row * third_y, start)
        edges_ref[...] = pack_edges(air_ref, levels)
        own_ref[slots] = own_ref[slots] + edges_ref[...]
        speeds_ref[...] = jnp.zeros_like(speeds_ref)


def set_halo(rows_ref, first, northern_ref, southern_ref, row):
    halo = join_slabs(rows_ref, first, rows_ref.shape[0] - first)
    zero = jnp.zeros_like(halo)
    northern_ref[...] = jnp.where(row == 0, zero, halo)
    southern_ref[...] = jnp.where(row == 0, halo, zero)


def parent_step(
    levels, west_ref, south_ref, shared, rows_ref, columns, field_ref, other_ref, side_ref, northern_ref, southern_ref
):
    height = side_ref.shape[0] // levels
    slots = other_ref.shape[0] - 1
    tile, row, lev = place()
    set_halo(rows_ref, slots + 1, northern_ref, southern_ref, row)
    side_ref[...] = unpack_edges(columns, levels, height)
    full_step(field_ref, *shared, levels, lev, False, northern_ref, southern_ref, side_ref, None)
    start = west_ref[1] - tile * field_ref.shape[0] * LANES
    top = south_ref[1] - 1 - row * height
    pack_window(other_ref, field_ref, levels, top + (1 - row) * (height // 3), start)


def early_kernel(
    levels,
    west_ref,
    south_ref,
    air_ref,
    east_ref,
    north_ref,
    rows_ref,
    level_ref,
    one_ref,
    field_ref,
    other_ref,
    side_ref,
    northern_ref,
    southern_ref,
):
    slots = other_ref.shape[0] - 1
    tile_count = lax.axis_size("tiles")
    tile, row, lev = place()
    shared = (air_ref, east_ref, north_ref, level_ref)

    @pl.when(tile == tile_count - 1)
    def _():
        set_halo(rows_ref, slots + 1, northern_ref, southern_ref, row)
        full_step(field_ref, *shared, levels, lev, True, northern_ref, southern_ref, None, None)
        other_ref[...] = jnp.zeros_like(other_ref)

    @pl.when(tile == 0)
    def _():
        columns = neighbour_columns(one_ref[slots], one_ref[slots], tile_count - 1, tile)
        refs = (field_ref, other_ref, side_ref, northern_ref, southern_ref)
        parent_step(levels, west_ref, south_ref, shared, rows_ref, columns, *refs)


def middle_kernel(
    levels,
    west_ref,
    south_ref,
    air_ref,
    east_ref,
    north_ref,
    rows_ref,
    level_ref,
    three_ref,
    one_ref,
    given_field_ref,
    given_other_ref,
    field_ref,
    other_ref,
    side_ref,
    northern_ref,
    southern_ref,
):
    slots = other_ref.shape[0] - 1
    tile_count = lax.axis_size("tiles")
    tile, _, _ = place()
    shared = (air_ref, east_ref, north_ref, level_ref)

    @pl.when((tile > 0) & (tile < tile_count - 1))
    def _():
        columns = neighbour_columns(one_ref[slots], three_ref[...], tile_count - 1, tile)
        refs = (field_ref, other_ref, side_ref, northern_ref, southern_ref)
        parent_step(levels, west_ref, south_ref, shared, rows_ref, columns, *refs)


def first_kernel(
    levels,
    west_ref,
    south_ref,
    early_ref,
    east_ref,
    speeds_ref,
    three_ref,
    two_ref,
    one_ref,
    field_ref,
    edge_ref,
    own_ref,
):
    pieces, size, _ = early_ref.shape
    height, breadth = edge_ref.shape
    slots = one_ref.shape[0] - 1
    tile, row, lev = place()
    nest = tile == lax.axis_size("tiles") - 1

    @pl.when(jnp.logical_not(nest))
    def _():
        edge_ref[...] = jnp.zeros_like(edge_ref)
        start = west_ref[1] - tile * breadth
        top = south_ref[1] - 1 - row * height
        pack_window(own_ref, early_ref, levels, top + row * (height // 3), start)

    @pl.when(nest)
    def _():
        slabs = [one_ref[s] + two_ref[s] + three_ref[s] for s in range(slots + 1)]
        cells, ring = refine(slabs[:slots], slabs[slots], height, breadth, row)
        lane = iota((size, LANES), 1)
        for c in range(pieces):
            piece = slice(c * LANES, (c + 1) * LANES)
            value = early_ref[c] + NUDGING * cells[:, piece]
            if c == 0:
                ghost = ghost_weight(east_ref[:, piece], True) * cells[:, breadth : breadth + 1]
                value = value + jnp.where(lane == 0, ghost, 0.0)
            if c == pieces - 1:
                ghost = ghost_weight(east_ref[:, piece], False) * cells[:, breadth + 1 : breadth + 2]
                value = value + jnp.where(lane == LANES - 1, ghost, 0.0)
            field_ref[c] = value
        outer = height - 1 - inner_line(height, row)
        ghost = ghost_weight(join_slabs(speeds_ref, 0, pieces), row == 0) * ring
        store_line(field_ref, levels, outer, load_line(field_ref, levels, outer) + ghost)
        edge_ref[...] = edge_level(field_ref, height, lev)


def average_kernel(levels, field_ref, east_ref, north_ref, rows_ref, message_ref, part_ref, nothing_ref):
    pieces, size, _ = field_ref.shape
    height, breadth = nothing_ref.shape
    third_y = height // 3
    tile, row, lev = place()

    @pl.when(tile == lax.axis_size("tiles") - 1)
    def _():
        nothing_ref[...] = jnp.zeros_like(nothing_ref)
        full_step(part_ref, field_ref, east_ref, north_ref, nothing_ref, levels, lev, True, None, None, None, None)
        sums = sums_table(breadth)
        shape = (third_y * levels, size)
        taken = iota(shape, 0)
        block = taken // levels
        level, line = split_level(iota(shape, 1), height)
        offset = line - 3 * block
        rows = table((taken - block * levels == level) & (offset >= 0) & (offset <= 2))
        means = from_left(rows, from_right(part_ref[...], sums)) * (1.0 / 9.0)
        for m in range(third_y):
            message_ref[m] = means[m * levels : (m + 1) * levels]
        shared = load_line(field_ref, levels, inner_line(height, row))
        shared = ghost_weight(join_slabs(rows_ref, WEIGHTS, pieces), row == 0) * shared
        message_ref[third_y] = from_right(shared, sums) * (1.0 / 9.0)
        for i in range(third_y + 1, message_ref.shape[0]):
            message_ref[i] = jnp.zeros((levels, LANES), jnp.float32)


def sums_table(breadth):
    offset = iota((breadth, LANES), 0) - 3 * iota((breadth, LANES), 1)
    return table((offset >= 0) & (offset <= 2))


def message_kernel(levels, level_ref, part_ref, own_ref, other_ref, message_ref):
    height, breadth = level_ref.shape
    third_y = height // 3
    tile, row, lev = place()
    nest = tile == lax.axis_size("tiles") - 1

    @pl.when(jnp.logical_not(nest))
    def _():
        message_ref[...] = own_ref[...] + other_ref[...]

    @pl.when(nest)
    def _():
        offset = iota((third_y, height), 1) - 3 * iota((third_y, height), 0)
        rows = table((offset >= 0) & (offset <= 2))
        across = from_left(rows, from_right(level_ref[...], sums_table(breadth))) * (VERTICAL_MIX / 9.0)
        at_edge = iota((levels, LANES), 0) == jnp.where(lev == 0, levels - 1, 0)
        for m in range(third_y):
            message_ref[m] = part_ref[m] + jnp.where(at_edge, across[m : m + 1], 0.0)
        for i in range(third_y, message_ref.shape[0]):
            message_ref[i] = part_ref[i]


def blend_kernel(
    levels,
    weight_ref,
    field_ref,
    window_ref,
    one_ref,
    two_ref,
    three_ref,
    coef_three_ref,
    coef_two_ref,
    coef_one_ref,
    rows_ref,
):
    pieces, size, _ = field_ref.shape
    height = size // levels
    third_y = height // 3
    slots = third_y + 2
    tile_count = lax.axis_size("tiles")
    tile, row, _ = place()
    nest = tile == tile_count - 1

    @pl.when(nest)
    def _():
        store_slabs(rows_ref, 0, load_line(field_ref, levels, inner_line(height, row)))
        for i in range(pieces, rows_ref.shape[0]):
            rows_ref[i] = jnp.zeros((levels, LANES), jnp.float32)

    @pl.when(jnp.logical_not(nest))
    def _():
        def of_nest(refs, i):
            one, two, three = refs
            return jnp.where(tile == 0, three[i], jnp.where(tile == 1, two[i], one[i]))

        def mine(i):
            return of_nest((one_ref, two_ref, three_ref), i)

        def coefficient(i):
            return of_nest((coef_one_ref, coef_two_ref, coef_three_ref), i)

        def whole(i):
            odd = tile % 2 == 1
            west = jnp.where(odd, one_ref[i], three_ref[i])
            east = jnp.where(odd, three_ref[i], one_ref[i])
            part = jnp.where(tile == 0, window_ref[i], window_ref[i] + west)
            return jnp.where(tile == tile_count - 2, part, part + east)

        weight = weight_ref[:, 0:1]
        extra = whole(slots)
        lane = iota(extra.shape, 1)
        at_first, at_last = lane == 0, lane == LANES - 1
        lines = []
        for s in range(slots):
            x = whole(s)
            west = jnp.where(at_first, extra[:, s : s + 1], pltpu.roll(x, 1, 1))
            last = EAST_LANE + s
            east = jnp.where(at_last, extra[:, last : last + 1], pltpu.roll(x, LANES - 1, 1))
            lines.append((west, x, east))
        edges = coefficient(WEIGHTS - 1)
        ghosts = [coefficient(q) for q in range(3)]

        def outward(side, q):
            near = lines[1] if side == 0 else lines[slots - 2]
            far = lines[0] if side == 0 else lines[slots - 1]
            return (2.0 / 3.0) * far[q] + (1.0 / 3.0) * near[q]

        def sideward(s):
            west, x, east = lines[s]
            return (2.0 / 3.0) * jnp.where(at_first, west, east) + (1.0 / 3.0) * x

        sidewards = [sideward(s) for s in range(slots)]
        columns = [w + 7.0 * x + e for w, x, e in lines]
        for m in range(third_y):
            x = lines[m + 1][1]
            value = mine(m) + (NUDGING / 81.0) * (columns[m] + 7.0 * columns[m + 1] + columns[m + 2])
            for q in range(3):
                lane_of = 8 * m + q
                first, last = edges[:, lane_of : lane_of + 1], edges[:, lane_of + 3 : lane_of + 4]
                scale = jnp.where(at_first, first, jnp.where(at_last, last, 0.0))
                value = value + scale * sidewards[m + q]
            for side, at in ((0, 0), (1, third_y - 1)):
                if m == at:
                    for q in range(3):
                        value = value + jnp.where(row == side, ghosts[q], 0.0) * outward(side, q)
            rows_ref[m] = x + weight * (value - x)
        rows_ref[third_y] = weight * mine(third_y)


def later_kernel(
    levels,
    west_ref,
    south_ref,
    field_ref,
    east_ref,
    north_ref,
    level_ref,
    one_ref,
    two_ref,
    three_ref,
    parent_ref,
    blend_ref,
    out_ref,
    fine_ref,
    side_ref,
    northern_ref,
    southern_ref,
):
    height, breadth = level_ref.shape
    third_y = height // 3
    slots = third_y + 2
    tile, row, lev = place()
    nest = tile == lax.axis_size("tiles") - 1

    @pl.when(nest)
    def _():
        slabs = [one_ref[s] + two_ref[s] + three_ref[s] for s in range(slots + 1)]
        cells, ring = refine(slabs[:slots], slabs[slots], height, breadth, row)
        fine_ref[...] = cells[:, :breadth]
        side_ref[...] = cells[:, breadth:]
        zero = jnp.zeros_like(ring)
        northern_ref[...] = jnp.where(row == 0, ring, zero)
        southern_ref[...] = jnp.where(row == 0, zero, ring)
        full_step(
            out_ref,
            field_ref,
            east_ref,
            north_ref,
            level_ref,
            levels,
            lev,
            True,
            northern_ref,
            southern_ref,
            side_ref,
            fine_ref,
        )

    @pl.when(jnp.logical_not(nest))
    def _():
        out_ref[...] = parent_ref[...]
        start = west_ref[1] - tile * breadth
        top = south_ref[1] + row * third_y - row * height
        for m in range(third_y):
            place_row(out_ref, levels, top + m, start, blend_ref[m])


def last_kernel(
    levels, west_ref, south_ref, given_ref, speeds_ref, blend_ref, rows_ref, out_hbm, out_ref, sems
):
    pieces, size, _ = given_ref.shape
    breadth = pieces * LANES
    height = size // levels
    third_y = height // 3
    tile, row, _ = place()
    nest = tile == lax.axis_size("tiles") - 1
    out_ref[...] = given_ref[...]

    @pl.when(nest)
    def _():
        inner = inner_line(height, row)
        halo = ghost_weight(join_slabs(speeds_ref, pieces, pieces), row == 1) * join_slabs(rows_ref, 0, pieces)
        store_line(out_ref, levels, inner, load_line(out_ref, levels, inner) + halo)

    @pl.when(jnp.logical_not(nest))
    def _():
        start = west_ref[1] - tile * breadth
        top = south_ref[1] + (1 - row) * third_y - row * height
        for m in range(third_y):
            value = rows_ref[m]
            if m == 0:
                value = value + jnp.where(row == 0, blend_ref[third_y], 0.0)
            if m == third_y - 1:
                value = value + jnp.where(row == 1, blend_ref[third_y], 0.0)
            place_row(out_ref, levels, top + m, start, value)
        near = jnp.where(row == 0, third_y - 1, 0)
        line = south_ref[1] + row * third_y - row * height + near
        place_row(out_ref, levels, line, start, blend_ref[near] + rows_ref[third_y])

    copies = [
        pltpu.make_async_copy(out_ref.at[c], out_hbm.at[:, pl.ds(c * LANES, LANES)], sems.at[c])
        for c in range(pieces)
    ]
    for copy in copies:
        copy.start()
    for copy in copies:
        copy.wait()


def call(kernel, outs, inputs, places, scratch=(), flops=0, out_place="v", aliases=()):
    spaces = {"s": pltpu.SMEM, "v": pltpu.VMEM, "h": pltpu.HBM}
    outs = [spaces[out_place](out, jnp.float32) if isinstance(out, tuple) else out for out in outs]
    moved = sum(4 * math.prod(out.shape) for out in outs) + sum(array.nbytes for array in inputs)
    inputs = [
        array if p == "v" else pltpu.with_memory_space_constraint(array, spaces[p])
        for array, p in zip(inputs, places)
    ]
    return pl.pallas_call(
        kernel,
        out_shape=outs,
        in_specs=[pl.BlockSpec(memory_space=spaces[p]) for p in places],
        out_specs=[pl.BlockSpec(memory_space=out.memory_space) for out in outs],
        scratch_shapes=[pltpu.VMEM(s, jnp.float32) if isinstance(s, tuple) else s for s in scratch],
        input_output_aliases=dict(aliases),
        compiler_params=pltpu.CompilerParams(vmem_limit_bytes=32 * 1024 * 1024),
        cost_estimate=pl.CostEstimate(flops=flops, bytes_accessed=moved, transcendentals=0),
    )(*inputs)


def per_device_paired(air_state, wind_east, wind_north, feedback_weight, nest_west, nest_south):
    levels, height, breadth = air_state.shape
    third_y = height // 3
    pieces = breadth // LANES
    slots = third_y + 2
    tile_count = lax.axis_size("tiles")
    size = levels * height
    flat = (size, breadth)
    chunked = (pieces, size, LANES)
    air, east, north = (array.reshape(flat) for array in (air_state, wind_east, wind_north))
    weight = jnp.broadcast_to(feedback_weight[:, None], (levels, LANES))
    swap = [(0, 1), (1, 0)]

    def slabs(count):
        return (count, levels, LANES)

    def kernel(body):
        return functools.partial(body, levels)

    rows, air_pieces, west, south = call(
        kernel(pack_kernel),
        [slabs(slots + 1 + pieces), chunked, pltpu.SMEM((2,), jnp.int32), pltpu.SMEM((2,), jnp.int32)],
        [nest_west, nest_south, air, north],
        "hhhh",
        [chunked, pltpu.SemaphoreType.DMA((2 * pieces + 2,))],
    )
    own, level, speeds, edges = call(
        kernel(own_kernel),
        [slabs(slots + 1), (height, breadth), slabs(2 * pieces), (levels, LANES)],
        [west, south, air_pieces, east, north],
        "ssvvv",
        flops=30 * size * breadth,
    )
    rows = lax.ppermute(rows, "rows", swap)
    level = lax.ppermute(level, "lev", swap)
    where = [(t, r, l) for t in range(tile_count) for r in range(2) for l in range(2)]
    at = {position: i for i, position in enumerate(where)}

    def over_tiles(message, step, *without):
        pairs = []
        for t, r, l in where:
            idle = t in without or (t ^ step) in without
            pairs.append((at[t, r, l], at[(t, r, 1 - l) if idle else (t ^ step, r, l)]))
        return lax.ppermute(message, ("tiles", "rows", "lev"), pairs)

    window = own + rows[: slots + 1]
    starting = [over_tiles(window, 1), over_tiles(window, 2, 0), over_tiles(window, 3, 1)]
    halo = over_tiles(edges, 3, 0)
    sides = [(size, LANES), (levels, breadth), (levels, breadth)]
    early, other = call(
        kernel(early_kernel),
        [chunked, slabs(slots + 1)],
        [west, south, air, east, north, rows, level, starting[0]],
        "ssvvvvvv",
        sides,
        flops=30 * size * breadth,
    )
    early, other = call(
        kernel(middle_kernel),
        [chunked, slabs(slots + 1)],
        [west, south, air, east, north, rows, level, halo, starting[0], early, other],
        "ssvvvvvvvvv",
        sides,
        flops=30 * size * breadth,
        aliases=[(9, 0), (10, 1)],
    )
    other = lax.ppermute(other, "rows", swap)
    first, edge, own = call(
        kernel(first_kernel),
        [chunked, (height, breadth), slabs(slots + 1)],
        [west, south, early, east, speeds, *starting[::-1]],
        "ssvvvvvv",
        flops=10 * size * breadth,
    )
    level = lax.ppermute(edge, "lev", swap)
    (part,) = call(
        kernel(average_kernel),
        [slabs(slots + 1)],
        [first, east, north, rows],
        "vvvv",
        [flat, (height, breadth)],
        flops=30 * size * breadth,
    )
    (message,) = call(
        kernel(message_kernel),
        [slabs(slots + 1)],
        [level, part, own, other],
        "vvvv",
    )
    received = [over_tiles(message, 1), over_tiles(message, 2, 0), over_tiles(message, 3)]
    (blend,) = call(
        kernel(blend_kernel),
        [slabs(third_y + 1)],
        [weight, first, message, *received, *starting[::-1]],
        "v" * 9,
    )
    rows = lax.ppermute(blend, "rows", swap)
    (later,) = call(
        kernel(later_kernel),
        [chunked],
        [west, south, first, east, north, level, *received, early, blend],
        "ss" + "v" * 9,
        [flat, *sides],
        flops=30 * size * breadth,
    )
    (out,) = call(
        kernel(last_kernel),
        [flat],
        [west, south, later, speeds, blend, rows],
        "ssvvvv",
        [chunked, pltpu.SemaphoreType.DMA((pieces,))],
        out_place="h",
    )
    return out.reshape(air_state.shape)


def solution(mesh):
    in_specs = (
        P(("members", "lev"), "rows", "tiles"),
        P(("members", "lev"), "rows", "tiles"),
        P(("members", "lev"), "rows", "tiles"),
        P("lev"),
        P("members"),
        P("members"),
    )
    out_specs = P(("members", "lev"), "rows", "tiles")
    paired = mesh.shape["tiles"] == 4 and mesh.shape["rows"] == 2 and mesh.shape["lev"] == 2
    return jax.shard_map(
        per_device_paired if paired else per_device, mesh=mesh, in_specs=in_specs, out_specs=out_specs, check_vma=False
    )
```

```python
import functools
import math

import jax
import jax.numpy as jnp
from jax import lax
from jax.experimental import pallas as pl
from jax.experimental.pallas import tpu as pltpu
from jax.sharding import PartitionSpec as P

VERTICAL_MIX = 0.1
PARENT_MIXING = 0.04
NEST_MIXING = 0.18
NEST_ADVECT = 1.5
NUDGING = 0.2


def padded_2(array, sides, width):
    for axis, dim in sides:
        size, length = (lax.axis_size(axis), array.shape[dim])
        up = [(i, (i + 1) % size) for i in range(size - 1)]
        down = [(j, i) for i, j in up]
        last = lax.slice_in_dim(array, length - width, length, axis=dim)
        first = lax.slice_in_dim(array, 0, width, axis=dim)
        before = lax.ppermute(last, axis, up)
        after = lax.ppermute(first, axis, down)
        array = jnp.concatenate([before, array, after], axis=dim)
    return array


def interp_table(cells):
    extended = jnp.arange(cells + 2, dtype=jnp.int32) - 1
    coarse = jnp.floor_divide(extended, 3)
    offset = extended - 3 * coarse
    fraction = jnp.abs(offset - 1).astype(jnp.float32) / 3.0
    nearest = coarse + 1
    beside = nearest + (offset - 1)
    slots = jnp.arange(cells // 3 + 2, dtype=jnp.int32)[:, None]
    first_part = jnp.where(
        slots == nearest[None, :], 1.0 - fraction[None, :], jnp.zeros((), jnp.float32)
    )
    second_part = jnp.where(slots == beside[None, :], fraction[None, :], jnp.zeros((), jnp.float32))
    return first_part + second_part


def tendency(padded, speed_east, speed_north, advect_scale, mixing_scale):
    centre = padded[1:-1, 1:-1, 1:-1]
    eastern = padded[1:-1, 1:-1, 2:]
    western = padded[1:-1, 1:-1, :-2]
    southern = padded[1:-1, 2:, 1:-1]
    northern = padded[1:-1, :-2, 1:-1]
    upper = padded[2:, 1:-1, 1:-1]
    lower = padded[:-2, 1:-1, 1:-1]
    advect = speed_east * (eastern - western) + speed_north * (southern - northern)
    horizontal = eastern + western + southern + northern - 4.0 * centre
    vertical = upper + lower - 2.0 * centre
    return -0.5 * advect_scale * advect + mixing_scale * horizontal + VERTICAL_MIX * vertical


def padded_block(block_field):
    return padded_2(block_field, (("tiles", 2), ("rows", 1), ("lev", 0)), 1)


def per_device(air_state, wind_east, wind_north, feedback_weight, nest_west, nest_south):
    levels, height, breadth = air_state.shape
    tile_count = lax.axis_size("tiles")
    row_count = lax.axis_size("rows")
    tile_index = lax.axis_index("tiles")
    row_index = lax.axis_index("rows")
    parent_tiles = 3 * tile_count // 4
    nest_tiles = tile_count - parent_tiles
    in_nest = tile_index >= parent_tiles
    nest_tile = tile_index - parent_tiles
    cross_x = breadth // 3 + 2
    cross_y = height // 3 + 2
    third_x = breadth // 3
    third_y = height // 3
    first_x = tile_index * breadth
    first_y = row_index * height
    columns = jnp.arange(breadth, dtype=jnp.int32)
    lines = jnp.arange(height, dtype=jnp.int32)
    targets_x = jnp.arange(tile_count, dtype=jnp.int32)
    targets_y = jnp.arange(row_count, dtype=jnp.int32)
    highest = lax.Precision.HIGHEST
    table_x = interp_table(breadth)
    table_y = interp_table(height)
    zero_value = jnp.zeros((), jnp.float32)

    def boundary(source, substep):
        anchor_x = nest_west[substep] + (targets_x - parent_tiles) * third_x - 1
        slot_x = jnp.arange(cross_x, dtype=jnp.int32)
        pick_x = (
            (first_x + columns)[None, :, None] == anchor_x[:, None, None] + slot_x[None, None, :]
        ) & (targets_x >= parent_tiles)[:, None, None]
        pick_x = pick_x.astype(jnp.float32)
        anchor_y = nest_south[substep] + targets_y * third_y - 1
        slot_y = jnp.arange(cross_y, dtype=jnp.int32)
        pick_y = (
            (first_y + lines)[None, :, None] == anchor_y[:, None, None] + slot_y[None, None, :]
        ).astype(jnp.float32)
        pieces = jnp.einsum("lyi,tij->tlyj", source, pick_x, precision=highest)
        merged = lax.all_to_all(pieces, "tiles", split_axis=0, concat_axis=0, tiled=True).sum(
            axis=0
        )
        pieces = jnp.einsum("lyj,ryw->rlwj", merged, pick_y, precision=highest)
        window = lax.all_to_all(pieces, "rows", split_axis=0, concat_axis=0, tiled=True).sum(axis=0)
        along = jnp.einsum("lwj,je->lwe", window, table_x, precision=highest)
        return jnp.einsum("lwe,wf->lfe", along, table_y, precision=highest)

    def assemble(block_field, fine):
        padded = padded_block(block_field)
        fine_padded = jnp.pad(fine, ((1, 1), (0, 0), (0, 0)))
        column_place = lax.broadcasted_iota(jnp.int32, padded.shape, 2)
        line_place = lax.broadcasted_iota(jnp.int32, padded.shape, 1)
        outside = (column_place == 0) & (nest_tile == 0) | (column_place == breadth + 1) & (
            nest_tile == nest_tiles - 1
        )
        outside = (
            outside
            | (line_place == 0) & (row_index == 0)
            | (line_place == height + 1) & (row_index == row_count - 1)
        )
        padded = jnp.where(outside & in_nest, fine_padded, padded)
        seam_cells = (column_place == breadth + 1) & (tile_index == parent_tiles - 1)
        return jnp.where(seam_cells, zero_value, padded)

    advect_scale = jnp.where(in_nest, jnp.float32(NEST_ADVECT), jnp.float32(1.0))
    mixing_scale = jnp.where(in_nest, jnp.float32(NEST_MIXING), jnp.float32(PARENT_MIXING))
    fine_first = boundary(air_state, 0)
    change = tendency(
        assemble(air_state, fine_first), wind_east, wind_north, advect_scale, mixing_scale
    )
    nudging_term = jnp.where(in_nest, NUDGING * (fine_first[:, 1:-1, 1:-1] - air_state), zero_value)
    step_one = air_state + change + nudging_term
    fine_second = boundary(step_one, 1)
    change = tendency(
        assemble(step_one, fine_second), wind_east, wind_north, advect_scale, mixing_scale
    )
    nested_two = step_one + change + NUDGING * (fine_second[:, 1:-1, 1:-1] - step_one)
    step_two = jnp.where(in_nest, nested_two, step_one)
    coarse = step_two.reshape(levels, third_y, 3, third_x, 3).mean(axis=(2, 4))
    avg_columns = jnp.arange(third_x, dtype=jnp.int32)
    avg_lines = jnp.arange(third_y, dtype=jnp.int32)
    west_last = nest_west[1]
    south_last = nest_south[1]
    place_x = (
        (west_last + (targets_x - parent_tiles) * third_x)[:, None, None]
        + avg_columns[None, :, None]
        == (first_x + columns)[None, None, :]
    ) & (targets_x >= parent_tiles)[:, None, None]
    place_x = place_x.astype(jnp.float32)
    place_y = (
        (south_last + targets_y * third_y)[:, None, None] + avg_lines[None, :, None]
        == (first_y + lines)[None, None, :]
    ).astype(jnp.float32)
    parent_y = south_last + row_index * third_y + avg_lines
    send_y = (jnp.floor_divide(parent_y, height)[None, :] == targets_y[:, None]) & in_nest
    pieces = jnp.where(send_y[:, None, :, None], coarse[None], zero_value)
    received = lax.all_to_all(pieces, "rows", split_axis=0, concat_axis=0, tiled=True)
    spread = jnp.einsum("slba,sby->lya", received, place_y, precision=highest)
    parent_x = west_last + nest_tile * third_x + avg_columns
    send_x = jnp.floor_divide(parent_x, breadth)[None, :] == targets_x[:, None]
    pieces = jnp.where(send_x[:, None, None, :], spread[None], zero_value)
    received = lax.all_to_all(pieces, "tiles", split_axis=0, concat_axis=0, tiled=True)
    placed = jnp.einsum("slya,sai->lyi", received, place_x, precision=highest)
    global_x = (first_x + columns)[None, None, :]
    global_y = (first_y + lines)[None, :, None]
    covered = (global_x >= west_last) & (global_x < west_last + nest_tiles * third_x)
    covered = covered & (global_y >= south_last) & (global_y < south_last + row_count * third_y)
    covered = covered & jnp.logical_not(in_nest)
    blended = step_two + feedback_weight[:, None, None] * (placed - step_two)
    return jnp.where(covered, blended, step_two)


LANES = 128
FIRST_LANE = 32
LAST_LANE = 96
EAST_LANE = 64
WEIGHTS = 4


def iota(shape, dim):
    return lax.broadcasted_iota(jnp.int32, shape, dim)


def split_level(place, height):
    level = ((place.astype(jnp.float32) + 0.5) * (1.0 / height)).astype(jnp.int32)
    return level, place - level * height


def table(values):
    return values.astype(jnp.float32).astype(jnp.bfloat16)


def parts_of(array):
    high = array.astype(jnp.bfloat16)
    low = (array - high.astype(jnp.float32)).astype(jnp.bfloat16)
    return high, low


def dot(left, right):
    return jnp.dot(left, right, preferred_element_type=jnp.float32)


def from_left(weights, array):
    high, low = parts_of(array)
    return dot(weights, high) + dot(weights, low)


def from_right(array, weights):
    high, low = parts_of(array)
    return dot(high, weights) + dot(low, weights)


def hat(distance):
    return jnp.maximum(0, 3 - jnp.abs(distance - 1))


def place():
    return lax.axis_index("tiles"), lax.axis_index("rows"), lax.axis_index("lev")


def level_table(levels, height):
    shape = (levels, levels * height)
    level, _ = split_level(iota(shape, 1), height)
    return table(iota(shape, 0) == level)


def spread_table(levels, height):
    shape = (levels * height, levels)
    level, _ = split_level(iota(shape, 0), height)
    return table(iota(shape, 1) == level)


def load_line(ref, levels, line):
    rows = pl.ds(line, levels, stride=ref.shape[1] // levels)
    return jnp.concatenate([ref[c, rows, :] for c in range(ref.shape[0])], axis=1)


def store_line(ref, levels, line, value):
    rows = pl.ds(line, levels, stride=ref.shape[1] // levels)
    for c in range(ref.shape[0]):
        ref[c, rows, :] = value[:, c * LANES : (c + 1) * LANES]


def load_level(ref, height, l):
    rows = pl.ds(l * height, height)
    if len(ref.shape) == 2:
        return ref[rows, :]
    return jnp.concatenate([ref[c, rows, :] for c in range(ref.shape[0])], axis=1)


def store_level(ref, height, l, value):
    rows = pl.ds(l * height, height)
    if len(ref.shape) == 2:
        ref[rows, :] = value
    else:
        for c in range(ref.shape[0]):
            ref[c, rows, :] = value[:, c * LANES : (c + 1) * LANES]


def store_slabs(ref, first, wide):
    for i in range(wide.shape[1] // LANES):
        ref[first + i] = wide[:, i * LANES : (i + 1) * LANES]


def join_slabs(ref, first, count):
    return jnp.concatenate([ref[first + i] for i in range(count)], axis=1)


def column_pieces(start, pieces):
    first = (start + 64 * LANES) // LANES - 64
    offset = start - first * LANES
    held = [(c >= 0) & (c < pieces) for c in (first, first + 1)]
    return [jnp.clip(c, 0, pieces - 1) for c in (first, first + 1)], held, offset


def pack_window(ref, field_ref, levels, top, start):
    pieces, size, _ = field_ref.shape
    height = size // levels
    slots = ref.shape[0] - 1
    lane = iota((levels, LANES), 1)
    (left, right), (left_held, right_held), offset = column_pieces(start, pieces)
    before = lax.rem(offset + LANES - 1, LANES)
    (beside, _), (beside_held, _), _ = column_pieces(start - 1, pieces)
    in_left = lane < LANES - offset
    held = jnp.where(in_left, left_held.astype(jnp.float32), right_held.astype(jnp.float32))
    west_held, east_held = beside_held.astype(jnp.float32), right_held.astype(jnp.float32)
    turn = lax.rem(LANES - offset, LANES)
    extra = jnp.zeros((levels, LANES), jnp.float32)
    for slot in range(slots):
        line = top + slot
        there = ((line >= 0) & (line < height)).astype(jnp.float32)
        rows = pl.ds(jnp.clip(line, 0, height - 1), levels, stride=height)
        near, far, west = field_ref[left, rows, :], field_ref[right, rows, :], field_ref[beside, rows, :]
        ref[slot] = jnp.where(in_left, pltpu.roll(near, turn, 1), pltpu.roll(far, turn, 1)) * (held * there)
        west = pltpu.roll(west, lax.rem(LANES + slot - before, LANES), 1) * (west_held * there)
        east = pltpu.roll(far, lax.rem(LANES + EAST_LANE + slot - offset, LANES), 1) * (east_held * there)
        extra = jnp.where(lane == slot, west, jnp.where(lane == EAST_LANE + slot, east, extra))
    ref[slots] = extra


def place_row(ref, levels, line, start, value):
    pieces, size, _ = ref.shape
    height = size // levels
    lane = iota((levels, LANES), 1)
    at, held, offset = column_pieces(start, pieces)
    value = pltpu.roll(value, offset, 1)
    there = (line >= 0) & (line < height)
    rows = pl.ds(jnp.clip(line, 0, height - 1), levels, stride=height)
    for c in range(2):
        mine = (lane >= offset) if c == 0 else (lane < offset)
        ref[at[c], rows, :] = jnp.where(mine & (held[c] & there), value, ref[at[c], rows, :])


def pack_edges(field_ref, levels):
    height = field_ref.shape[1] // levels
    lane = iota((levels, LANES), 1)
    packed = jnp.zeros((levels, LANES), jnp.float32)
    for line in range(height):
        rows = pl.ds(line, levels, stride=height)
        first = field_ref[0, rows, :]
        last = field_ref[field_ref.shape[0] - 1, rows, :]
        packed = jnp.where(lane == FIRST_LANE + line, pltpu.roll(first, FIRST_LANE + line, 1), packed)
        packed = jnp.where(lane == LAST_LANE + line, pltpu.roll(last, LAST_LANE + line + 1, 1), packed)
    return packed


def neighbour_columns(even, odd, parent_tiles, tile):
    is_odd = tile % 2 == 1
    west = jnp.where(is_odd, even, odd)
    east = jnp.where(is_odd, odd, even)
    west = jnp.where(tile == 0, jnp.zeros_like(west), west)
    east = jnp.where(tile >= parent_tiles - 1, jnp.zeros_like(east), east)
    return jnp.where(iota(west.shape, 1) < LAST_LANE, east, west)


def unpack_edges(columns, levels, height):
    wide = from_left(spread_table(levels, height), columns)
    lane = iota(wide.shape, 1)
    _, line = split_level(iota(wide.shape, 0), height)
    west = jnp.sum(jnp.where(lane == line + LAST_LANE, wide, 0.0), axis=1, keepdims=True)
    east = jnp.sum(jnp.where(lane == line + FIRST_LANE, wide, 0.0), axis=1, keepdims=True)
    return jnp.where(lane == 0, west, jnp.where(lane == 1, east, 0.0))


def refine(slabs, extra, height, breadth, row):
    slots, levels = len(slabs), extra.shape[0]
    beside = [pltpu.roll(extra, LANES - s, 1) if s else extra for s in range(slots)]
    window = jnp.concatenate([jnp.concatenate(slabs, axis=0), jnp.concatenate(beside, axis=0)], axis=1)
    shape = (2 * LANES, breadth + LANES)
    slot, cell = iota(shape, 0), iota(shape, 1)
    held = (slot <= LANES) | (slot == LANES + EAST_LANE)
    at = jnp.where(slot < LANES, slot, jnp.where(slot == LANES, -1, LANES))
    cell = jnp.where(cell == breadth, -1, jnp.where(cell == breadth + 1, breadth, cell))
    across = jnp.where(held & (cell <= breadth), hat(cell - 3 * at), 0)
    wide = from_right(window, table(across)) * (1.0 / 9.0)
    shape = (levels * height, slots * levels)
    taken = iota(shape, 1)
    slot = taken // levels
    level, line = split_level(iota(shape, 0), height)
    along = jnp.where(taken - slot * levels == level, hat(line - 3 * (slot - 1)), 0)
    cells = from_left(table(along), wide)
    ring = jnp.where(
        row == 0,
        2.0 * wide[:levels] + wide[levels : 2 * levels],
        2.0 * wide[(slots - 1) * levels :] + wide[(slots - 2) * levels : (slots - 1) * levels],
    )
    return cells, ring[:, :breadth]


def beside_rows(x, north, south):
    height = x.shape[0]
    line = iota(x.shape, 0)
    northern = jnp.where(line == 0, north, pltpu.roll(x, 1, 0))
    southern = jnp.where(line == height - 1, south, pltpu.roll(x, height - 1, 0))
    return northern, southern


def beside_columns(x, west, east):
    breadth = x.shape[1]
    column = iota(x.shape, 1)
    western = jnp.where(column == 0, west, pltpu.roll(x, 1, 1))
    eastern = jnp.where(column == breadth - 1, east, pltpu.roll(x, breadth - 1, 1))
    return western, eastern


def change_of(x, sides, u, v, upper, lower, nest):
    advect_scale = NEST_ADVECT if nest else 1.0
    mixing_scale = NEST_MIXING if nest else PARENT_MIXING
    northern, southern, western, eastern = sides
    advect = u * (eastern - western) + v * (southern - northern)
    horizontal = eastern + western + southern + northern - 4.0 * x
    vertical = upper + lower - 2.0 * x
    return -0.5 * advect_scale * advect + mixing_scale * horizontal + VERTICAL_MIX * vertical


def ghost_weight(speed, before):
    return jnp.where(before, 0.5 * NEST_ADVECT, -0.5 * NEST_ADVECT) * speed + NEST_MIXING


def full_step(out_ref, field_ref, u_ref, v_ref, level_ref, levels, lev, nest, north, south, side, fine):
    height, breadth = level_ref.shape
    zero = jnp.zeros((height, breadth), jnp.float32)

    def block(ref, l):
        return load_level(ref, height, l)

    for l in range(levels):
        x = block(field_ref, l)
        lower = block(field_ref, l - 1) if l else jnp.where(lev == 1, level_ref[...], zero)
        upper = block(field_ref, l + 1) if l < levels - 1 else jnp.where(lev == 0, level_ref[...], zero)
        rows = [0.0 if ref is None else ref[pl.ds(l, 1), :] for ref in (north, south)]
        if side is None:
            columns = (0.0, 0.0)
        else:
            beside = side[pl.ds(l * height, height), :]
            columns = (beside[:, 0:1], beside[:, 1:2])
        sides = beside_rows(x, *rows) + beside_columns(x, *columns)
        fresh = x + change_of(x, sides, block(u_ref, l), block(v_ref, l), upper, lower, nest)
        if nest:
            fresh = fresh - NUDGING * x if fine is None else fresh + NUDGING * (block(fine, l) - x)
        store_level(out_ref, height, l, fresh)


def inner_line(height, row):
    return jnp.where(row == 0, height - 1, 0)


def edge_level(ref, height, lev):
    last = ref.shape[1] // height - 1
    return jnp.where(lev == 0, load_level(ref, height, last), load_level(ref, height, 0))


def ghost_row_weights(ghost, breadth):
    cell, third = iota((breadth, 3 * LANES), 0), iota((breadth, 3 * LANES), 1)
    kind = third // LANES
    offset = cell - 3 * (third - kind * LANES)
    middle = jnp.where(offset == 1, 3, jnp.where((offset == 0) | (offset == 2), 2, 0))
    weight = jnp.where(kind == 1, middle, jnp.where(offset == kind, 1, 0))
    return from_right(ghost, table(weight)) * (1.0 / 27.0)


def ghost_column_weights(first, last, levels, height):
    shape = (levels * height, LANES)
    lane = iota(shape, 1)
    _, line = split_level(iota(shape, 0), height)
    block = lane // 8
    inside = lane - block * 8
    eastern = inside >= 3
    kind = jnp.where(eastern, inside - 3, inside)
    offset = line - 3 * block
    middle = jnp.where(offset == 1, 3, jnp.where((offset == 0) | (offset == 2), 2, 0))
    weight = jnp.where(kind == 1, middle, jnp.where(offset == kind, 1, 0))
    weight = jnp.where((inside < 6) & (block < height // 3), weight, 0).astype(jnp.float32)
    columns = jnp.where(eastern, last, first) * weight
    return from_left(level_table(levels, height), columns) * (1.0 / 27.0)


def pack_kernel(
    levels, west_hbm, south_hbm, air_hbm, north_hbm, rows_ref, air_ref, west_ref, south_ref, north_ref, sems
):
    pieces, size, _ = air_ref.shape
    breadth = pieces * LANES
    height = size // levels
    third_y = height // 3
    slots = rows_ref.shape[0] - 1 - pieces
    tile, row, _ = place()
    nest = tile == lax.axis_size("tiles") - 1
    inner = inner_line(height, row)

    def column_copies(source, target, first):
        return [
            pltpu.make_async_copy(source.at[:, pl.ds(c * LANES, LANES)], target.at[c], sems.at[first + c])
            for c in range(pieces)
        ]

    copies = column_copies(air_hbm, air_ref, 0)
    copies.append(pltpu.make_async_copy(west_hbm, west_ref, sems.at[2 * pieces]))
    copies.append(pltpu.make_async_copy(south_hbm, south_ref, sems.at[2 * pieces + 1]))
    speeds = column_copies(north_hbm, north_ref, pieces)
    for copy in copies:
        copy.start()

    @pl.when(nest)
    def _():
        for copy in speeds:
            copy.start()

    for copy in copies:
        copy.wait()
    store_slabs(rows_ref, slots + 1, load_line(air_ref, levels, inner))
    part = rows_ref.at[pl.ds(0, slots + 1)]

    @pl.when(nest)
    def _():
        for copy in speeds:
            copy.wait()
        part[...] = jnp.zeros_like(part)
        store_slabs(rows_ref, WEIGHTS, load_line(north_ref, levels, inner))

    @pl.when(jnp.logical_not(nest))
    def _():
        start = west_ref[0] - tile * breadth
        top = south_ref[0] - 1 - row * height
        pack_window(part, air_ref, levels, top + (1 - row) * third_y, start)


def own_kernel(
    levels, west_ref, south_ref, air_ref, east_ref, north_ref, own_ref, level_ref, speeds_ref, edges_ref
):
    pieces, size, _ = air_ref.shape
    breadth = pieces * LANES
    height = size // levels
    third_y = height // 3
    slots = own_ref.shape[0] - 1
    tile, row, lev = place()
    nest = tile == lax.axis_size("tiles") - 1
    level_ref[...] = edge_level(air_ref, height, lev)

    @pl.when(nest)
    def _():
        inner = inner_line(height, row)
        shape = (2 * levels, size)
        taken = iota(shape, 0)
        level, line = split_level(iota(shape, 1), height)
        wanted = jnp.where(taken < levels, height - 1 - inner, inner)
        picked = table((lax.rem(taken, levels) == level) & (line == wanted))
        speeds = from_left(picked, north_ref[...])
        outer = speeds[:levels]
        store_slabs(speeds_ref, 0, outer)
        store_slabs(speeds_ref, pieces, speeds[levels:])
        own_ref[...] = jnp.zeros_like(own_ref)
        edges_ref[...] = jnp.zeros_like(edges_ref)
        store_slabs(own_ref, 0, ghost_row_weights(ghost_weight(outer, row == 0), breadth))
        first = ghost_weight(east_ref[:, 0:1], True)
        last = ghost_weight(east_ref[:, breadth - 1 : breadth], False)
        own_ref[WEIGHTS - 1] = ghost_column_weights(first, last, levels, height)

    @pl.when(jnp.logical_not(nest))
    def _():
        start = west_ref[0] - tile * breadth
        top = south_ref[0] - 1 - row * height
        pack_window(own_ref, air_ref, levels, top + row * third_y, start)
        edges_ref[...] = pack_edges(air_ref, levels)
        own_ref[slots] = own_ref[slots] + edges_ref[...]
        speeds_ref[...] = jnp.zeros_like(speeds_ref)


def set_halo(rows_ref, first, northern_ref, southern_ref, row):
    halo = join_slabs(rows_ref, first, rows_ref.shape[0] - first)
    zero = jnp.zeros_like(halo)
    northern_ref[...] = jnp.where(row == 0, zero, halo)
    southern_ref[...] = jnp.where(row == 0, halo, zero)


def parent_step(
    levels, west_ref, south_ref, shared, rows_ref, columns, field_ref, other_ref, side_ref, northern_ref, southern_ref
):
    height = side_ref.shape[0] // levels
    slots = other_ref.shape[0] - 1
    tile, row, lev = place()
    set_halo(rows_ref, slots + 1, northern_ref, southern_ref, row)
    side_ref[...] = unpack_edges(columns, levels, height)
    full_step(field_ref, *shared, levels, lev, False, northern_ref, southern_ref, side_ref, None)
    start = west_ref[1] - tile * field_ref.shape[0] * LANES
    top = south_ref[1] - 1 - row * height
    pack_window(other_ref, field_ref, levels, top + (1 - row) * (height // 3), start)


def early_kernel(
    levels,
    west_ref,
    south_ref,
    air_ref,
    east_ref,
    north_ref,
    rows_ref,
    level_ref,
    one_ref,
    field_ref,
    other_ref,
    side_ref,
    northern_ref,
    southern_ref,
):
    slots = other_ref.shape[0] - 1
    tile_count = lax.axis_size("tiles")
    tile, row, lev = place()
    shared = (air_ref, east_ref, north_ref, level_ref)

    @pl.when(tile == tile_count - 1)
    def _():
        set_halo(rows_ref, slots + 1, northern_ref, southern_ref, row)
        full_step(field_ref, *shared, levels, lev, True, northern_ref, southern_ref, None, None)
        other_ref[...] = jnp.zeros_like(other_ref)

    @pl.when(tile == 0)
    def _():
        columns = neighbour_columns(one_ref[slots], one_ref[slots], tile_count - 1, tile)
        refs = (field_ref, other_ref, side_ref, northern_ref, southern_ref)
        parent_step(levels, west_ref, south_ref, shared, rows_ref, columns, *refs)


def middle_kernel(
    levels,
    west_ref,
    south_ref,
    air_ref,
    east_ref,
    north_ref,
    rows_ref,
    level_ref,
    three_ref,
    one_ref,
    given_field_ref,
    given_other_ref,
    field_ref,
    other_ref,
    side_ref,
    northern_ref,
    southern_ref,
):
    slots = other_ref.shape[0] - 1
    tile_count = lax.axis_size("tiles")
    tile, _, _ = place()
    shared = (air_ref, east_ref, north_ref, level_ref)

    @pl.when((tile > 0) & (tile < tile_count - 1))
    def _():
        columns = neighbour_columns(one_ref[slots], three_ref[...], tile_count - 1, tile)
        refs = (field_ref, other_ref, side_ref, northern_ref, southern_ref)
        parent_step(levels, west_ref, south_ref, shared, rows_ref, columns, *refs)


def first_kernel(
    levels,
    west_ref,
    south_ref,
    early_ref,
    east_ref,
    speeds_ref,
    three_ref,
    two_ref,
    one_ref,
    field_ref,
    edge_ref,
    own_ref,
):
    pieces, size, _ = early_ref.shape
    height, breadth = edge_ref.shape
    slots = one_ref.shape[0] - 1
    tile, row, lev = place()
    nest = tile == lax.axis_size("tiles") - 1

    @pl.when(jnp.logical_not(nest))
    def _():
        edge_ref[...] = jnp.zeros_like(edge_ref)
        start = west_ref[1] - tile * breadth
        top = south_ref[1] - 1 - row * height
        pack_window(own_ref, early_ref, levels, top + row * (height // 3), start)

    @pl.when(nest)
    def _():
        slabs = [one_ref[s] + two_ref[s] + three_ref[s] for s in range(slots + 1)]
        cells, ring = refine(slabs[:slots], slabs[slots], height, breadth, row)
        lane = iota((size, LANES), 1)
        for c in range(pieces):
            piece = slice(c * LANES, (c + 1) * LANES)
            value = early_ref[c] + NUDGING * cells[:, piece]
            if c == 0:
                ghost = ghost_weight(east_ref[:, piece], True) * cells[:, breadth : breadth + 1]
                value = value + jnp.where(lane == 0, ghost, 0.0)
            if c == pieces - 1:
                ghost = ghost_weight(east_ref[:, piece], False) * cells[:, breadth + 1 : breadth + 2]
                value = value + jnp.where(lane == LANES - 1, ghost, 0.0)
            field_ref[c] = value
        outer = height - 1 - inner_line(height, row)
        ghost = ghost_weight(join_slabs(speeds_ref, 0, pieces), row == 0) * ring
        store_line(field_ref, levels, outer, load_line(field_ref, levels, outer) + ghost)
        edge_ref[...] = edge_level(field_ref, height, lev)


def average_kernel(levels, field_ref, east_ref, north_ref, rows_ref, message_ref, part_ref, nothing_ref):
    pieces, size, _ = field_ref.shape
    height, breadth = nothing_ref.shape
    third_y = height // 3
    tile, row, lev = place()

    @pl.when(tile == lax.axis_size("tiles") - 1)
    def _():
        nothing_ref[...] = jnp.zeros_like(nothing_ref)
        full_step(part_ref, field_ref, east_ref, north_ref, nothing_ref, levels, lev, True, None, None, None, None)
        sums = sums_table(breadth)
        shape = (third_y * levels, size)
        taken = iota(shape, 0)
        block = taken // levels
        level, line = split_level(iota(shape, 1), height)
        offset = line - 3 * block
        rows = table((taken - block * levels == level) & (offset >= 0) & (offset <= 2))
        means = from_left(rows, from_right(part_ref[...], sums)) * (1.0 / 9.0)
        for m in range(third_y):
            message_ref[m] = means[m * levels : (m + 1) * levels]
        shared = load_line(field_ref, levels, inner_line(height, row))
        shared = ghost_weight(join_slabs(rows_ref, WEIGHTS, pieces), row == 0) * shared
        message_ref[third_y] = from_right(shared, sums) * (1.0 / 9.0)
        for i in range(third_y + 1, message_ref.shape[0]):
            message_ref[i] = jnp.zeros((levels, LANES), jnp.float32)


def sums_table(breadth):
    offset = iota((breadth, LANES), 0) - 3 * iota((breadth, LANES), 1)
    return table((offset >= 0) & (offset <= 2))


def message_kernel(levels, level_ref, part_ref, coef_ref, own_ref, other_ref, message_ref, side_ref):
    height, breadth = level_ref.shape
    third_y = height // 3
    tile, row, lev = place()
    nest = tile == lax.axis_size("tiles") - 1

    @pl.when(jnp.logical_not(nest))
    def _():
        message_ref[...] = own_ref[...] + other_ref[...]

    @pl.when(nest)
    def _():
        offset = iota((third_y, height), 1) - 3 * iota((third_y, height), 0)
        rows = table((offset >= 0) & (offset <= 2))
        across = from_left(rows, from_right(level_ref[...], sums_table(breadth))) * (VERTICAL_MIX / 9.0)
        at_edge = iota((levels, LANES), 0) == jnp.where(lev == 0, levels - 1, 0)
        for m in range(third_y):
            message_ref[m] = part_ref[m] + jnp.where(at_edge, across[m : m + 1], 0.0)
        for i in range(third_y, message_ref.shape[0]):
            message_ref[i] = part_ref[i]

    side_ref[pl.ds(0, message_ref.shape[0])] = message_ref[...]
    side_ref[pl.ds(message_ref.shape[0], WEIGHTS)] = coef_ref[pl.ds(0, WEIGHTS)]


def blend_kernel(
    levels,
    western,
    weight_ref,
    field_ref,
    window_ref,
    beside_ref,
    middle_ref,
    other_ref,
    coef_middle_ref,
    coef_near_ref,
    rows_ref,
):
    pieces, size, _ = field_ref.shape
    height = size // levels
    third_y = height // 3
    slots = third_y + 2
    tile_count = lax.axis_size("tiles")
    tile, row, _ = place()
    nest = tile == tile_count - 1

    @pl.when(nest)
    def _():
        store_slabs(rows_ref, 0, load_line(field_ref, levels, inner_line(height, row)))
        for i in range(pieces, rows_ref.shape[0]):
            rows_ref[i] = jnp.zeros((levels, LANES), jnp.float32)

    @pl.when(jnp.logical_not(nest))
    def _():
        paired = (tile == 1) | (tile == (0 if western else 2))

        def mine(i):
            return jnp.where(tile == 1, middle_ref[i], other_ref[i])

        def coefficient(i):
            other = beside_ref[slots + 1 + i] if western else coef_near_ref[i]
            return jnp.where(tile == 1, coef_middle_ref[i], other)

        def whole(i):
            return jnp.where(paired, window_ref[i] + beside_ref[i], window_ref[i])

        weight = weight_ref[:, 0:1]
        extra = whole(slots)
        lane = iota(extra.shape, 1)
        at_first, at_last = lane == 0, lane == LANES - 1
        lines = []
        for s in range(slots):
            x = whole(s)
            west = jnp.where(at_first, extra[:, s : s + 1], pltpu.roll(x, 1, 1))
            last = EAST_LANE + s
            east = jnp.where(at_last, extra[:, last : last + 1], pltpu.roll(x, LANES - 1, 1))
            lines.append((west, x, east))
        edges = coefficient(WEIGHTS - 1)
        ghosts = [coefficient(q) for q in range(3)]

        def outward(side, q):
            near = lines[1] if side == 0 else lines[slots - 2]
            far = lines[0] if side == 0 else lines[slots - 1]
            return (2.0 / 3.0) * far[q] + (1.0 / 3.0) * near[q]

        def sideward(s):
            west, x, east = lines[s]
            return (2.0 / 3.0) * jnp.where(at_first, west, east) + (1.0 / 3.0) * x

        sidewards = [sideward(s) for s in range(slots)]
        columns = [w + 7.0 * x + e for w, x, e in lines]
        for m in range(third_y):
            x = lines[m + 1][1]
            value = mine(m) + (NUDGING / 81.0) * (columns[m] + 7.0 * columns[m + 1] + columns[m + 2])
            for q in range(3):
                lane_of = 8 * m + q
                first, last = edges[:, lane_of : lane_of + 1], edges[:, lane_of + 3 : lane_of + 4]
                scale = jnp.where(at_first, first, jnp.where(at_last, last, 0.0))
                value = value + scale * sidewards[m + q]
            for side, at in ((0, 0), (1, third_y - 1)):
                if m == at:
                    for q in range(3):
                        value = value + jnp.where(row == side, ghosts[q], 0.0) * outward(side, q)
            rows_ref[m] = x + weight * (value - x)
        rows_ref[third_y] = weight * mine(third_y)


def later_kernel(
    levels,
    west_ref,
    south_ref,
    field_ref,
    east_ref,
    north_ref,
    level_ref,
    middle_ref,
    other_ref,
    parent_ref,
    blend_ref,
    out_ref,
    fine_ref,
    side_ref,
    northern_ref,
    southern_ref,
):
    height, breadth = level_ref.shape
    third_y = height // 3
    slots = third_y + 2
    tile, row, lev = place()
    nest = tile == lax.axis_size("tiles") - 1

    @pl.when(nest)
    def _():
        slabs = [middle_ref[s] + other_ref[s] for s in range(slots + 1)]
        cells, ring = refine(slabs[:slots], slabs[slots], height, breadth, row)
        fine_ref[...] = cells[:, :breadth]
        side_ref[...] = cells[:, breadth:]
        zero = jnp.zeros_like(ring)
        northern_ref[...] = jnp.where(row == 0, ring, zero)
        southern_ref[...] = jnp.where(row == 0, zero, ring)
        full_step(
            out_ref,
            field_ref,
            east_ref,
            north_ref,
            level_ref,
            levels,
            lev,
            True,
            northern_ref,
            southern_ref,
            side_ref,
            fine_ref,
        )

    @pl.when(jnp.logical_not(nest))
    def _():
        out_ref[...] = parent_ref[...]
        start = west_ref[1] - tile * breadth
        top = south_ref[1] + row * third_y - row * height
        for m in range(third_y):
            place_row(out_ref, levels, top + m, start, blend_ref[m])


def last_kernel(
    levels, west_ref, south_ref, given_ref, speeds_ref, blend_ref, rows_ref, out_hbm, out_ref, sems
):
    pieces, size, _ = given_ref.shape
    breadth = pieces * LANES
    height = size // levels
    third_y = height // 3
    tile, row, _ = place()
    nest = tile == lax.axis_size("tiles") - 1
    out_ref[...] = given_ref[...]

    @pl.when(nest)
    def _():
        inner = inner_line(height, row)
        halo = ghost_weight(join_slabs(speeds_ref, pieces, pieces), row == 1) * join_slabs(rows_ref, 0, pieces)
        store_line(out_ref, levels, inner, load_line(out_ref, levels, inner) + halo)

    @pl.when(jnp.logical_not(nest))
    def _():
        start = west_ref[1] - tile * breadth
        top = south_ref[1] + (1 - row) * third_y - row * height
        for m in range(third_y):
            value = rows_ref[m]
            if m == 0:
                value = value + jnp.where(row == 0, blend_ref[third_y], 0.0)
            if m == third_y - 1:
                value = value + jnp.where(row == 1, blend_ref[third_y], 0.0)
            place_row(out_ref, levels, top + m, start, value)
        near = jnp.where(row == 0, third_y - 1, 0)
        line = south_ref[1] + row * third_y - row * height + near
        place_row(out_ref, levels, line, start, blend_ref[near] + rows_ref[third_y])

    copies = [
        pltpu.make_async_copy(out_ref.at[c], out_hbm.at[:, pl.ds(c * LANES, LANES)], sems.at[c])
        for c in range(pieces)
    ]
    for copy in copies:
        copy.start()
    for copy in copies:
        copy.wait()


def call(kernel, outs, inputs, places, scratch=(), flops=0, out_place="v", aliases=()):
    spaces = {"s": pltpu.SMEM, "v": pltpu.VMEM, "h": pltpu.HBM}
    outs = [spaces[out_place](out, jnp.float32) if isinstance(out, tuple) else out for out in outs]
    moved = sum(4 * math.prod(out.shape) for out in outs) + sum(array.nbytes for array in inputs)
    inputs = [
        array if p == "v" else pltpu.with_memory_space_constraint(array, spaces[p])
        for array, p in zip(inputs, places)
    ]
    return pl.pallas_call(
        kernel,
        out_shape=outs,
        in_specs=[pl.BlockSpec(memory_space=spaces[p]) for p in places],
        out_specs=[pl.BlockSpec(memory_space=out.memory_space) for out in outs],
        scratch_shapes=[pltpu.VMEM(s, jnp.float32) if isinstance(s, tuple) else s for s in scratch],
        input_output_aliases=dict(aliases),
        compiler_params=pltpu.CompilerParams(vmem_limit_bytes=32 * 1024 * 1024),
        cost_estimate=pl.CostEstimate(flops=flops, bytes_accessed=moved, transcendentals=0),
    )(*inputs)


def per_device_paired(air_state, wind_east, wind_north, feedback_weight, nest_west, nest_south):
    levels, height, breadth = air_state.shape
    third_y = height // 3
    pieces = breadth // LANES
    slots = third_y + 2
    tile_count = lax.axis_size("tiles")
    size = levels * height
    flat = (size, breadth)
    chunked = (pieces, size, LANES)
    air, east, north = (array.reshape(flat) for array in (air_state, wind_east, wind_north))
    weight = jnp.broadcast_to(feedback_weight[:, None], (levels, LANES))
    swap = [(0, 1), (1, 0)]

    def slabs(count):
        return (count, levels, LANES)

    def kernel(body):
        return functools.partial(body, levels)

    rows, air_pieces, west, south = call(
        kernel(pack_kernel),
        [slabs(slots + 1 + pieces), chunked, pltpu.SMEM((2,), jnp.int32), pltpu.SMEM((2,), jnp.int32)],
        [nest_west, nest_south, air, north],
        "hhhh",
        [chunked, pltpu.SemaphoreType.DMA((2 * pieces + 2,))],
    )
    own, level, speeds, edges = call(
        kernel(own_kernel),
        [slabs(slots + 1), (height, breadth), slabs(2 * pieces), (levels, LANES)],
        [west, south, air_pieces, east, north],
        "ssvvv",
        flops=30 * size * breadth,
    )
    rows = lax.ppermute(rows, "rows", swap)
    level = lax.ppermute(level, "lev", swap)
    where = [(t, r, l) for t in range(tile_count) for r in range(2) for l in range(2)]
    at = {position: i for i, position in enumerate(where)}

    def over_tiles(message, step, *without):
        pairs = []
        for t, r, l in where:
            idle = t in without or (t ^ step) in without
            pairs.append((at[t, r, l], at[(t, r, 1 - l) if idle else (t ^ step, r, l)]))
        return lax.ppermute(message, ("tiles", "rows", "lev"), pairs)

    halo = over_tiles(edges, 3, 0)
    eastern = nest_west[1] > breadth
    rows, halo, eastern, weight = lax.optimization_barrier((rows, halo, eastern, weight))
    window = own + rows[: slots + 1]
    around = [(t, (t - 1) % tile_count) for t in range(tile_count)]
    starting = [
        over_tiles(window, 1),
        over_tiles(window, 2, 0),
        lax.ppermute(window, "tiles", around),
    ]
    sides = [(size, LANES), (levels, breadth), (levels, breadth)]
    early, other = call(
        kernel(early_kernel),
        [chunked, slabs(slots + 1)],
        [west, south, air, east, north, rows, level, starting[0]],
        "ssvvvvvv",
        sides,
        flops=30 * size * breadth,
    )
    early, other = call(
        kernel(middle_kernel),
        [chunked, slabs(slots + 1)],
        [west, south, air, east, north, rows, level, halo, starting[0], early, other],
        "ssvvvvvvvvv",
        sides,
        flops=30 * size * breadth,
        aliases=[(9, 0), (10, 1)],
    )
    other = lax.ppermute(other, "rows", swap)
    first, edge, own = call(
        kernel(first_kernel),
        [chunked, (height, breadth), slabs(slots + 1)],
        [west, south, early, east, speeds, *starting[::-1]],
        "ssvvvvvv",
        flops=10 * size * breadth,
    )
    level = lax.ppermute(edge, "lev", swap)
    (part,) = call(
        kernel(average_kernel),
        [slabs(slots + 1)],
        [first, east, north, rows],
        "vvvv",
        [flat, (height, breadth)],
        flops=30 * size * breadth,
    )
    message, side_message = call(
        kernel(message_kernel),
        [slabs(slots + 1), slabs(slots + 1 + WEIGHTS)],
        [level, part, starting[1], own, other],
        "vvvvv",
    )
    def finish(western, arrays):
        west, south, weight, first, east, north, level, message, side_message, early, speeds, coefs = arrays
        if western:
            other, beside = over_tiles(message, 3, 1), over_tiles(side_message, 1, 3)
        else:
            other, beside = over_tiles(message, 1, 0), over_tiles(side_message, 3, 0)
        middle = over_tiles(message, 2, 0)
        (blend,) = call(
            functools.partial(blend_kernel, levels, western),
            [slabs(third_y + 1)],
            [weight, first, message, beside, middle, other, *coefs],
            "v" * 8,
        )
        rows = lax.ppermute(blend, "rows", swap)
        (later,) = call(
            kernel(later_kernel),
            [chunked],
            [west, south, first, east, north, level, middle, other, early, blend],
            "ss" + "v" * 8,
            [flat, *sides],
            flops=30 * size * breadth,
        )
        (out,) = call(
            kernel(last_kernel),
            [flat],
            [west, south, later, speeds, blend, rows],
            "ssvvvv",
            [chunked, pltpu.SemaphoreType.DMA((pieces,))],
            out_place="h",
        )
        return out

    arrays = (west, south, weight, first, east, north, level, message, side_message, early, speeds)
    arrays += ((starting[1], starting[0]),)
    out = lax.cond(
        eastern,
        functools.partial(finish, False),
        functools.partial(finish, True),
        arrays,
    )
    return out.reshape(air_state.shape)


def solution(mesh):
    in_specs = (
        P(("members", "lev"), "rows", "tiles"),
        P(("members", "lev"), "rows", "tiles"),
        P(("members", "lev"), "rows", "tiles"),
        P("lev"),
        P("members"),
        P("members"),
    )
    out_specs = P(("members", "lev"), "rows", "tiles")
    paired = mesh.shape["tiles"] == 4 and mesh.shape["rows"] == 2 and mesh.shape["lev"] == 2
    return jax.shard_map(
        per_device_paired if paired else per_device, mesh=mesh, in_specs=in_specs, out_specs=out_specs, check_vma=False
    )
```

```python
import functools
import math

import jax
import jax.numpy as jnp
import numpy as np
from jax import lax
from jax.experimental import pallas as pl
from jax.experimental.pallas import tpu as pltpu
from jax.sharding import PartitionSpec as P

VERTICAL_MIX = 0.1
PARENT_MIXING = 0.04
NEST_MIXING = 0.18
NEST_ADVECT = 1.5
NUDGING = 0.2


def padded_2(array, sides, width):
    for axis, dim in sides:
        size, length = (lax.axis_size(axis), array.shape[dim])
        up = [(i, (i + 1) % size) for i in range(size - 1)]
        down = [(j, i) for i, j in up]
        last = lax.slice_in_dim(array, length - width, length, axis=dim)
        first = lax.slice_in_dim(array, 0, width, axis=dim)
        before = lax.ppermute(last, axis, up)
        after = lax.ppermute(first, axis, down)
        array = jnp.concatenate([before, array, after], axis=dim)
    return array


def interp_table(cells):
    extended = jnp.arange(cells + 2, dtype=jnp.int32) - 1
    coarse = jnp.floor_divide(extended, 3)
    offset = extended - 3 * coarse
    fraction = jnp.abs(offset - 1).astype(jnp.float32) / 3.0
    nearest = coarse + 1
    beside = nearest + (offset - 1)
    slots = jnp.arange(cells // 3 + 2, dtype=jnp.int32)[:, None]
    first_part = jnp.where(
        slots == nearest[None, :], 1.0 - fraction[None, :], jnp.zeros((), jnp.float32)
    )
    second_part = jnp.where(slots == beside[None, :], fraction[None, :], jnp.zeros((), jnp.float32))
    return first_part + second_part


def tendency(padded, speed_east, speed_north, advect_scale, mixing_scale):
    centre = padded[1:-1, 1:-1, 1:-1]
    eastern = padded[1:-1, 1:-1, 2:]
    western = padded[1:-1, 1:-1, :-2]
    southern = padded[1:-1, 2:, 1:-1]
    northern = padded[1:-1, :-2, 1:-1]
    upper = padded[2:, 1:-1, 1:-1]
    lower = padded[:-2, 1:-1, 1:-1]
    advect = speed_east * (eastern - western) + speed_north * (southern - northern)
    horizontal = eastern + western + southern + northern - 4.0 * centre
    vertical = upper + lower - 2.0 * centre
    return -0.5 * advect_scale * advect + mixing_scale * horizontal + VERTICAL_MIX * vertical


def padded_block(block_field):
    return padded_2(block_field, (("tiles", 2), ("rows", 1), ("lev", 0)), 1)


def per_device(air_state, wind_east, wind_north, feedback_weight, nest_west, nest_south):
    levels, height, breadth = air_state.shape
    tile_count = lax.axis_size("tiles")
    row_count = lax.axis_size("rows")
    tile_index = lax.axis_index("tiles")
    row_index = lax.axis_index("rows")
    parent_tiles = 3 * tile_count // 4
    nest_tiles = tile_count - parent_tiles
    in_nest = tile_index >= parent_tiles
    nest_tile = tile_index - parent_tiles
    cross_x = breadth // 3 + 2
    cross_y = height // 3 + 2
    third_x = breadth // 3
    third_y = height // 3
    first_x = tile_index * breadth
    first_y = row_index * height
    columns = jnp.arange(breadth, dtype=jnp.int32)
    lines = jnp.arange(height, dtype=jnp.int32)
    targets_x = jnp.arange(tile_count, dtype=jnp.int32)
    targets_y = jnp.arange(row_count, dtype=jnp.int32)
    highest = lax.Precision.HIGHEST
    table_x = interp_table(breadth)
    table_y = interp_table(height)
    zero_value = jnp.zeros((), jnp.float32)

    def boundary(source, substep):
        anchor_x = nest_west[substep] + (targets_x - parent_tiles) * third_x - 1
        slot_x = jnp.arange(cross_x, dtype=jnp.int32)
        pick_x = (
            (first_x + columns)[None, :, None] == anchor_x[:, None, None] + slot_x[None, None, :]
        ) & (targets_x >= parent_tiles)[:, None, None]
        pick_x = pick_x.astype(jnp.float32)
        anchor_y = nest_south[substep] + targets_y * third_y - 1
        slot_y = jnp.arange(cross_y, dtype=jnp.int32)
        pick_y = (
            (first_y + lines)[None, :, None] == anchor_y[:, None, None] + slot_y[None, None, :]
        ).astype(jnp.float32)
        pieces = jnp.einsum("lyi,tij->tlyj", source, pick_x, precision=highest)
        merged = lax.all_to_all(pieces, "tiles", split_axis=0, concat_axis=0, tiled=True).sum(
            axis=0
        )
        pieces = jnp.einsum("lyj,ryw->rlwj", merged, pick_y, precision=highest)
        window = lax.all_to_all(pieces, "rows", split_axis=0, concat_axis=0, tiled=True).sum(axis=0)
        along = jnp.einsum("lwj,je->lwe", window, table_x, precision=highest)
        return jnp.einsum("lwe,wf->lfe", along, table_y, precision=highest)

    def assemble(block_field, fine):
        padded = padded_block(block_field)
        fine_padded = jnp.pad(fine, ((1, 1), (0, 0), (0, 0)))
        column_place = lax.broadcasted_iota(jnp.int32, padded.shape, 2)
        line_place = lax.broadcasted_iota(jnp.int32, padded.shape, 1)
        outside = (column_place == 0) & (nest_tile == 0) | (column_place == breadth + 1) & (
            nest_tile == nest_tiles - 1
        )
        outside = (
            outside
            | (line_place == 0) & (row_index == 0)
            | (line_place == height + 1) & (row_index == row_count - 1)
        )
        padded = jnp.where(outside & in_nest, fine_padded, padded)
        seam_cells = (column_place == breadth + 1) & (tile_index == parent_tiles - 1)
        return jnp.where(seam_cells, zero_value, padded)

    advect_scale = jnp.where(in_nest, jnp.float32(NEST_ADVECT), jnp.float32(1.0))
    mixing_scale = jnp.where(in_nest, jnp.float32(NEST_MIXING), jnp.float32(PARENT_MIXING))
    fine_first = boundary(air_state, 0)
    change = tendency(
        assemble(air_state, fine_first), wind_east, wind_north, advect_scale, mixing_scale
    )
    nudging_term = jnp.where(in_nest, NUDGING * (fine_first[:, 1:-1, 1:-1] - air_state), zero_value)
    step_one = air_state + change + nudging_term
    fine_second = boundary(step_one, 1)
    change = tendency(
        assemble(step_one, fine_second), wind_east, wind_north, advect_scale, mixing_scale
    )
    nested_two = step_one + change + NUDGING * (fine_second[:, 1:-1, 1:-1] - step_one)
    step_two = jnp.where(in_nest, nested_two, step_one)
    coarse = step_two.reshape(levels, third_y, 3, third_x, 3).mean(axis=(2, 4))
    avg_columns = jnp.arange(third_x, dtype=jnp.int32)
    avg_lines = jnp.arange(third_y, dtype=jnp.int32)
    west_last = nest_west[1]
    south_last = nest_south[1]
    place_x = (
        (west_last + (targets_x - parent_tiles) * third_x)[:, None, None]
        + avg_columns[None, :, None]
        == (first_x + columns)[None, None, :]
    ) & (targets_x >= parent_tiles)[:, None, None]
    place_x = place_x.astype(jnp.float32)
    place_y = (
        (south_last + targets_y * third_y)[:, None, None] + avg_lines[None, :, None]
        == (first_y + lines)[None, None, :]
    ).astype(jnp.float32)
    parent_y = south_last + row_index * third_y + avg_lines
    send_y = (jnp.floor_divide(parent_y, height)[None, :] == targets_y[:, None]) & in_nest
    pieces = jnp.where(send_y[:, None, :, None], coarse[None], zero_value)
    received = lax.all_to_all(pieces, "rows", split_axis=0, concat_axis=0, tiled=True)
    spread = jnp.einsum("slba,sby->lya", received, place_y, precision=highest)
    parent_x = west_last + nest_tile * third_x + avg_columns
    send_x = jnp.floor_divide(parent_x, breadth)[None, :] == targets_x[:, None]
    pieces = jnp.where(send_x[:, None, None, :], spread[None], zero_value)
    received = lax.all_to_all(pieces, "tiles", split_axis=0, concat_axis=0, tiled=True)
    placed = jnp.einsum("slya,sai->lyi", received, place_x, precision=highest)
    global_x = (first_x + columns)[None, None, :]
    global_y = (first_y + lines)[None, :, None]
    covered = (global_x >= west_last) & (global_x < west_last + nest_tiles * third_x)
    covered = covered & (global_y >= south_last) & (global_y < south_last + row_count * third_y)
    covered = covered & jnp.logical_not(in_nest)
    blended = step_two + feedback_weight[:, None, None] * (placed - step_two)
    return jnp.where(covered, blended, step_two)


LANES = 128
FIRST_LANE = 32
LAST_LANE = 96
EAST_LANE = 64
WEIGHTS = 4


def iota(shape, dim):
    return lax.broadcasted_iota(jnp.int32, shape, dim)


def split_level(place, height):
    level = ((place.astype(jnp.float32) + 0.5) * (1.0 / height)).astype(jnp.int32)
    return level, place - level * height


def table(values):
    return values.astype(jnp.float32).astype(jnp.bfloat16)


def parts_of(array):
    high = array.astype(jnp.bfloat16)
    low = (array - high.astype(jnp.float32)).astype(jnp.bfloat16)
    return high, low


def dot(left, right):
    return jnp.dot(left, right, preferred_element_type=jnp.float32)


def from_left(weights, array):
    high, low = parts_of(array)
    return dot(weights, high) + dot(weights, low)


def from_right(array, weights):
    high, low = parts_of(array)
    return dot(high, weights) + dot(low, weights)


def hat(distance):
    return jnp.maximum(0, 3 - jnp.abs(distance - 1))


def place():
    return lax.axis_index("tiles"), lax.axis_index("rows"), lax.axis_index("lev")


def level_table(levels, height):
    shape = (levels, levels * height)
    level, _ = split_level(iota(shape, 1), height)
    return table(iota(shape, 0) == level)


def spread_table(levels, height):
    shape = (levels * height, levels)
    level, _ = split_level(iota(shape, 0), height)
    return table(iota(shape, 1) == level)


def load_line(ref, levels, line):
    rows = pl.ds(line, levels, stride=ref.shape[1] // levels)
    return jnp.concatenate([ref[c, rows, :] for c in range(ref.shape[0])], axis=1)


def store_line(ref, levels, line, value):
    rows = pl.ds(line, levels, stride=ref.shape[1] // levels)
    for c in range(ref.shape[0]):
        ref[c, rows, :] = value[:, c * LANES : (c + 1) * LANES]


def load_level(ref, height, l):
    rows = pl.ds(l * height, height)
    if len(ref.shape) == 2:
        return ref[rows, :]
    return jnp.concatenate([ref[c, rows, :] for c in range(ref.shape[0])], axis=1)


def store_level(ref, height, l, value):
    rows = pl.ds(l * height, height)
    if len(ref.shape) == 2:
        ref[rows, :] = value
    else:
        for c in range(ref.shape[0]):
            ref[c, rows, :] = value[:, c * LANES : (c + 1) * LANES]


def store_slabs(ref, first, wide):
    for i in range(wide.shape[1] // LANES):
        ref[first + i] = wide[:, i * LANES : (i + 1) * LANES]


def join_slabs(ref, first, count):
    return jnp.concatenate([ref[first + i] for i in range(count)], axis=1)


def column_pieces(start, pieces):
    first = (start + 64 * LANES) // LANES - 64
    offset = start - first * LANES
    held = [(c >= 0) & (c < pieces) for c in (first, first + 1)]
    return [jnp.clip(c, 0, pieces - 1) for c in (first, first + 1)], held, offset


def pack_window(ref, field_ref, levels, top, start):
    pieces, size, _ = field_ref.shape
    height = size // levels
    slots = ref.shape[0] - 1
    lane = iota((levels, LANES), 1)
    (left, right), (left_held, right_held), offset = column_pieces(start, pieces)
    before = lax.rem(offset + LANES - 1, LANES)
    (beside, _), (beside_held, _), _ = column_pieces(start - 1, pieces)
    in_left = lane < LANES - offset
    held = jnp.where(in_left, left_held.astype(jnp.float32), right_held.astype(jnp.float32))
    west_held, east_held = beside_held.astype(jnp.float32), right_held.astype(jnp.float32)
    turn = lax.rem(LANES - offset, LANES)
    extra = jnp.zeros((levels, LANES), jnp.float32)
    for slot in range(slots):
        line = top + slot
        there = ((line >= 0) & (line < height)).astype(jnp.float32)
        rows = pl.ds(jnp.clip(line, 0, height - 1), levels, stride=height)
        near, far, west = field_ref[left, rows, :], field_ref[right, rows, :], field_ref[beside, rows, :]
        ref[slot] = jnp.where(in_left, pltpu.roll(near, turn, 1), pltpu.roll(far, turn, 1)) * (held * there)
        west = pltpu.roll(west, lax.rem(LANES + slot - before, LANES), 1) * (west_held * there)
        east = pltpu.roll(far, lax.rem(LANES + EAST_LANE + slot - offset, LANES), 1) * (east_held * there)
        extra = jnp.where(lane == slot, west, jnp.where(lane == EAST_LANE + slot, east, extra))
    ref[slots] = extra


def place_row(ref, levels, line, start, value):
    pieces, size, _ = ref.shape
    height = size // levels
    lane = iota((levels, LANES), 1)
    at, held, offset = column_pieces(start, pieces)
    value = pltpu.roll(value, offset, 1)
    there = (line >= 0) & (line < height)
    rows = pl.ds(jnp.clip(line, 0, height - 1), levels, stride=height)
    for c in range(2):
        mine = (lane >= offset) if c == 0 else (lane < offset)
        ref[at[c], rows, :] = jnp.where(mine & (held[c] & there), value, ref[at[c], rows, :])


def pack_edges(field_ref, levels):
    height = field_ref.shape[1] // levels
    lane = iota((levels, LANES), 1)
    packed = jnp.zeros((levels, LANES), jnp.float32)
    for line in range(height):
        rows = pl.ds(line, levels, stride=height)
        first = field_ref[0, rows, :]
        last = field_ref[field_ref.shape[0] - 1, rows, :]
        packed = jnp.where(lane == FIRST_LANE + line, pltpu.roll(first, FIRST_LANE + line, 1), packed)
        packed = jnp.where(lane == LAST_LANE + line, pltpu.roll(last, LAST_LANE + line + 1, 1), packed)
    return packed


def neighbour_columns(even, odd, parent_tiles, tile):
    is_odd = tile % 2 == 1
    west = jnp.where(is_odd, even, odd)
    east = jnp.where(is_odd, odd, even)
    west = jnp.where(tile == 0, jnp.zeros_like(west), west)
    east = jnp.where(tile >= parent_tiles - 1, jnp.zeros_like(east), east)
    return jnp.where(iota(west.shape, 1) < LAST_LANE, east, west)


def unpack_edges(columns, levels, height):
    wide = from_left(spread_table(levels, height), columns)
    lane = iota(wide.shape, 1)
    _, line = split_level(iota(wide.shape, 0), height)
    west = jnp.sum(jnp.where(lane == line + LAST_LANE, wide, 0.0), axis=1, keepdims=True)
    east = jnp.sum(jnp.where(lane == line + FIRST_LANE, wide, 0.0), axis=1, keepdims=True)
    return jnp.where(lane == 0, west, jnp.where(lane == 1, east, 0.0))


def refine(slabs, extra, height, breadth, row):
    slots, levels = len(slabs), extra.shape[0]
    beside = [pltpu.roll(extra, LANES - s, 1) if s else extra for s in range(slots)]
    window = jnp.concatenate([jnp.concatenate(slabs, axis=0), jnp.concatenate(beside, axis=0)], axis=1)
    shape = (2 * LANES, breadth + LANES)
    slot, cell = iota(shape, 0), iota(shape, 1)
    held = (slot <= LANES) | (slot == LANES + EAST_LANE)
    at = jnp.where(slot < LANES, slot, jnp.where(slot == LANES, -1, LANES))
    cell = jnp.where(cell == breadth, -1, jnp.where(cell == breadth + 1, breadth, cell))
    across = jnp.where(held & (cell <= breadth), hat(cell - 3 * at), 0)
    wide = from_right(window, table(across)) * (1.0 / 9.0)
    shape = (levels * height, slots * levels)
    taken = iota(shape, 1)
    slot = taken // levels
    level, line = split_level(iota(shape, 0), height)
    along = jnp.where(taken - slot * levels == level, hat(line - 3 * (slot - 1)), 0)
    cells = from_left(table(along), wide)
    ring = jnp.where(
        row == 0,
        2.0 * wide[:levels] + wide[levels : 2 * levels],
        2.0 * wide[(slots - 1) * levels :] + wide[(slots - 2) * levels : (slots - 1) * levels],
    )
    return cells, ring[:, :breadth]


def beside_rows(x, north, south):
    height = x.shape[0]
    line = iota(x.shape, 0)
    northern = jnp.where(line == 0, north, pltpu.roll(x, 1, 0))
    southern = jnp.where(line == height - 1, south, pltpu.roll(x, height - 1, 0))
    return northern, southern


def beside_columns(x, west, east):
    breadth = x.shape[1]
    column = iota(x.shape, 1)
    western = jnp.where(column == 0, west, pltpu.roll(x, 1, 1))
    eastern = jnp.where(column == breadth - 1, east, pltpu.roll(x, breadth - 1, 1))
    return western, eastern


def change_of(x, sides, u, v, upper, lower, nest):
    advect_scale = NEST_ADVECT if nest else 1.0
    mixing_scale = NEST_MIXING if nest else PARENT_MIXING
    northern, southern, western, eastern = sides
    advect = u * (eastern - western) + v * (southern - northern)
    horizontal = eastern + western + southern + northern - 4.0 * x
    vertical = upper + lower - 2.0 * x
    return -0.5 * advect_scale * advect + mixing_scale * horizontal + VERTICAL_MIX * vertical


def ghost_weight(speed, before):
    return jnp.where(before, 0.5 * NEST_ADVECT, -0.5 * NEST_ADVECT) * speed + NEST_MIXING


def full_step(out_ref, field_ref, u_ref, v_ref, level_ref, levels, lev, nest, north, south, side, fine):
    height, breadth = level_ref.shape
    zero = jnp.zeros((height, breadth), jnp.float32)

    def block(ref, l):
        return load_level(ref, height, l)

    for l in range(levels):
        x = block(field_ref, l)
        lower = block(field_ref, l - 1) if l else jnp.where(lev == 1, level_ref[...], zero)
        upper = block(field_ref, l + 1) if l < levels - 1 else jnp.where(lev == 0, level_ref[...], zero)
        rows = [0.0 if ref is None else ref[pl.ds(l, 1), :] for ref in (north, south)]
        if side is None:
            columns = (0.0, 0.0)
        else:
            beside = side[pl.ds(l * height, height), :]
            columns = (beside[:, 0:1], beside[:, 1:2])
        sides = beside_rows(x, *rows) + beside_columns(x, *columns)
        fresh = x + change_of(x, sides, block(u_ref, l), block(v_ref, l), upper, lower, nest)
        if nest:
            fresh = fresh - NUDGING * x if fine is None else fresh + NUDGING * (block(fine, l) - x)
        store_level(out_ref, height, l, fresh)


def inner_line(height, row):
    return jnp.where(row == 0, height - 1, 0)


def edge_level(ref, height, lev):
    last = ref.shape[1] // height - 1
    return jnp.where(lev == 0, load_level(ref, height, last), load_level(ref, height, 0))


def ghost_row_weights(ghost, breadth):
    cell, third = iota((breadth, 3 * LANES), 0), iota((breadth, 3 * LANES), 1)
    kind = third // LANES
    offset = cell - 3 * (third - kind * LANES)
    middle = jnp.where(offset == 1, 3, jnp.where((offset == 0) | (offset == 2), 2, 0))
    weight = jnp.where(kind == 1, middle, jnp.where(offset == kind, 1, 0))
    return from_right(ghost, table(weight)) * (1.0 / 27.0)


def ghost_column_weights(first, last, levels, height):
    shape = (levels * height, LANES)
    lane = iota(shape, 1)
    _, line = split_level(iota(shape, 0), height)
    block = lane // 8
    inside = lane - block * 8
    eastern = inside >= 3
    kind = jnp.where(eastern, inside - 3, inside)
    offset = line - 3 * block
    middle = jnp.where(offset == 1, 3, jnp.where((offset == 0) | (offset == 2), 2, 0))
    weight = jnp.where(kind == 1, middle, jnp.where(offset == kind, 1, 0))
    weight = jnp.where((inside < 6) & (block < height // 3), weight, 0).astype(jnp.float32)
    columns = jnp.where(eastern, last, first) * weight
    return from_left(level_table(levels, height), columns) * (1.0 / 27.0)


def pack_kernel(
    levels, west_hbm, south_hbm, air_hbm, north_hbm, rows_ref, air_ref, west_ref, south_ref, north_ref, sems
):
    pieces, size, _ = air_ref.shape
    breadth = pieces * LANES
    height = size // levels
    third_y = height // 3
    slots = rows_ref.shape[0] - 1 - pieces
    tile, row, _ = place()
    nest = tile == lax.axis_size("tiles") - 1
    inner = inner_line(height, row)

    def column_copies(source, target, first):
        return [
            pltpu.make_async_copy(source.at[:, pl.ds(c * LANES, LANES)], target.at[c], sems.at[first + c])
            for c in range(pieces)
        ]

    copies = column_copies(air_hbm, air_ref, 0)
    copies.append(pltpu.make_async_copy(west_hbm, west_ref, sems.at[2 * pieces]))
    copies.append(pltpu.make_async_copy(south_hbm, south_ref, sems.at[2 * pieces + 1]))
    speeds = column_copies(north_hbm, north_ref, pieces)
    for copy in copies:
        copy.start()

    @pl.when(nest)
    def _():
        for copy in speeds:
            copy.start()

    for copy in copies:
        copy.wait()
    store_slabs(rows_ref, slots + 1, load_line(air_ref, levels, inner))
    part = rows_ref.at[pl.ds(0, slots + 1)]

    @pl.when(nest)
    def _():
        for copy in speeds:
            copy.wait()
        part[...] = jnp.zeros_like(part)
        store_slabs(rows_ref, WEIGHTS, load_line(north_ref, levels, inner))

    @pl.when(jnp.logical_not(nest))
    def _():
        start = west_ref[0] - tile * breadth
        top = south_ref[0] - 1 - row * height
        pack_window(part, air_ref, levels, top + (1 - row) * third_y, start)


def own_kernel(
    levels, west_ref, south_ref, air_ref, east_ref, north_ref, own_ref, level_ref, speeds_ref, edges_ref
):
    pieces, size, _ = air_ref.shape
    breadth = pieces * LANES
    height = size // levels
    third_y = height // 3
    slots = own_ref.shape[0] - 1
    tile, row, lev = place()
    nest = tile == lax.axis_size("tiles") - 1
    level_ref[...] = edge_level(air_ref, height, lev)

    @pl.when(nest)
    def _():
        inner = inner_line(height, row)
        shape = (2 * levels, size)
        taken = iota(shape, 0)
        level, line = split_level(iota(shape, 1), height)
        wanted = jnp.where(taken < levels, height - 1 - inner, inner)
        picked = table((lax.rem(taken, levels) == level) & (line == wanted))
        speeds = from_left(picked, north_ref[...])
        outer = speeds[:levels]
        store_slabs(speeds_ref, 0, outer)
        store_slabs(speeds_ref, pieces, speeds[levels:])
        own_ref[...] = jnp.zeros_like(own_ref)
        edges_ref[...] = jnp.zeros_like(edges_ref)
        store_slabs(own_ref, 0, ghost_row_weights(ghost_weight(outer, row == 0), breadth))
        first = ghost_weight(east_ref[:, 0:1], True)
        last = ghost_weight(east_ref[:, breadth - 1 : breadth], False)
        own_ref[WEIGHTS - 1] = ghost_column_weights(first, last, levels, height)

    @pl.when(jnp.logical_not(nest))
    def _():
        start = west_ref[0] - tile * breadth
        top = south_ref[0] - 1 - row * height
        pack_window(own_ref, air_ref, levels, top + row * third_y, start)
        edges_ref[...] = pack_edges(air_ref, levels)
        own_ref[slots] = own_ref[slots] + edges_ref[...]
        speeds_ref[...] = jnp.zeros_like(speeds_ref)


def set_halo(rows_ref, first, northern_ref, southern_ref, row):
    halo = join_slabs(rows_ref, first, rows_ref.shape[0] - first)
    zero = jnp.zeros_like(halo)
    northern_ref[...] = jnp.where(row == 0, zero, halo)
    southern_ref[...] = jnp.where(row == 0, halo, zero)


def parent_step(
    levels, west_ref, south_ref, shared, rows_ref, columns, field_ref, other_ref, side_ref, northern_ref, southern_ref
):
    height = side_ref.shape[0] // levels
    slots = other_ref.shape[0] - 1
    tile, row, lev = place()
    set_halo(rows_ref, slots + 1, northern_ref, southern_ref, row)
    side_ref[...] = unpack_edges(columns, levels, height)
    full_step(field_ref, *shared, levels, lev, False, northern_ref, southern_ref, side_ref, None)
    start = west_ref[1] - tile * field_ref.shape[0] * LANES
    top = south_ref[1] - 1 - row * height
    pack_window(other_ref, field_ref, levels, top + (1 - row) * (height // 3), start)


def early_kernel(
    levels,
    west_ref,
    south_ref,
    air_ref,
    east_ref,
    north_ref,
    rows_ref,
    level_ref,
    one_ref,
    field_ref,
    other_ref,
    side_ref,
    northern_ref,
    southern_ref,
):
    slots = other_ref.shape[0] - 1
    tile_count = lax.axis_size("tiles")
    tile, row, lev = place()
    shared = (air_ref, east_ref, north_ref, level_ref)

    @pl.when(tile == tile_count - 1)
    def _():
        set_halo(rows_ref, slots + 1, northern_ref, southern_ref, row)
        full_step(field_ref, *shared, levels, lev, True, northern_ref, southern_ref, None, None)
        other_ref[...] = jnp.zeros_like(other_ref)

    @pl.when(tile == 0)
    def _():
        columns = neighbour_columns(one_ref[slots], one_ref[slots], tile_count - 1, tile)
        refs = (field_ref, other_ref, side_ref, northern_ref, southern_ref)
        parent_step(levels, west_ref, south_ref, shared, rows_ref, columns, *refs)


def middle_kernel(
    levels,
    west_ref,
    south_ref,
    air_ref,
    east_ref,
    north_ref,
    rows_ref,
    level_ref,
    three_ref,
    one_ref,
    given_field_ref,
    given_other_ref,
    field_ref,
    other_ref,
    side_ref,
    northern_ref,
    southern_ref,
):
    slots = other_ref.shape[0] - 1
    tile_count = lax.axis_size("tiles")
    tile, _, _ = place()
    shared = (air_ref, east_ref, north_ref, level_ref)

    @pl.when((tile > 0) & (tile < tile_count - 1))
    def _():
        columns = neighbour_columns(one_ref[slots], three_ref[...], tile_count - 1, tile)
        refs = (field_ref, other_ref, side_ref, northern_ref, southern_ref)
        parent_step(levels, west_ref, south_ref, shared, rows_ref, columns, *refs)


def first_kernel(
    levels,
    west_ref,
    south_ref,
    early_ref,
    east_ref,
    speeds_ref,
    three_ref,
    two_ref,
    one_ref,
    field_ref,
    edge_ref,
    own_ref,
):
    pieces, size, _ = early_ref.shape
    height, breadth = edge_ref.shape
    slots = one_ref.shape[0] - 1
    tile, row, lev = place()
    nest = tile == lax.axis_size("tiles") - 1

    @pl.when(jnp.logical_not(nest))
    def _():
        edge_ref[...] = jnp.zeros_like(edge_ref)
        start = west_ref[1] - tile * breadth
        top = south_ref[1] - 1 - row * height
        pack_window(own_ref, early_ref, levels, top + row * (height // 3), start)

    @pl.when(nest)
    def _():
        slabs = [one_ref[s] + two_ref[s] + three_ref[s] for s in range(slots + 1)]
        cells, ring = refine(slabs[:slots], slabs[slots], height, breadth, row)
        lane = iota((size, LANES), 1)
        for c in range(pieces):
            piece = slice(c * LANES, (c + 1) * LANES)
            value = early_ref[c] + NUDGING * cells[:, piece]
            if c == 0:
                ghost = ghost_weight(east_ref[:, piece], True) * cells[:, breadth : breadth + 1]
                value = value + jnp.where(lane == 0, ghost, 0.0)
            if c == pieces - 1:
                ghost = ghost_weight(east_ref[:, piece], False) * cells[:, breadth + 1 : breadth + 2]
                value = value + jnp.where(lane == LANES - 1, ghost, 0.0)
            field_ref[c] = value
        outer = height - 1 - inner_line(height, row)
        ghost = ghost_weight(join_slabs(speeds_ref, 0, pieces), row == 0) * ring
        store_line(field_ref, levels, outer, load_line(field_ref, levels, outer) + ghost)
        edge_ref[...] = edge_level(field_ref, height, lev)


def average_kernel(levels, field_ref, east_ref, north_ref, rows_ref, message_ref, part_ref, nothing_ref):
    pieces, size, _ = field_ref.shape
    height, breadth = nothing_ref.shape
    third_y = height // 3
    tile, row, lev = place()

    @pl.when(tile == lax.axis_size("tiles") - 1)
    def _():
        nothing_ref[...] = jnp.zeros_like(nothing_ref)
        full_step(part_ref, field_ref, east_ref, north_ref, nothing_ref, levels, lev, True, None, None, None, None)
        sums = sums_table(breadth)
        shape = (third_y * levels, size)
        taken = iota(shape, 0)
        block = taken // levels
        level, line = split_level(iota(shape, 1), height)
        offset = line - 3 * block
        rows = table((taken - block * levels == level) & (offset >= 0) & (offset <= 2))
        means = from_left(rows, from_right(part_ref[...], sums)) * (1.0 / 9.0)
        for m in range(third_y):
            message_ref[m] = means[m * levels : (m + 1) * levels]
        shared = load_line(field_ref, levels, inner_line(height, row))
        shared = ghost_weight(join_slabs(rows_ref, WEIGHTS, pieces), row == 0) * shared
        message_ref[third_y] = from_right(shared, sums) * (1.0 / 9.0)
        for i in range(third_y + 1, message_ref.shape[0]):
            message_ref[i] = jnp.zeros((levels, LANES), jnp.float32)


def sums_table(breadth):
    offset = iota((breadth, LANES), 0) - 3 * iota((breadth, LANES), 1)
    return table((offset >= 0) & (offset <= 2))


def pack_column(slabs, extra, slot):
    lane = iota(extra.shape, 1)
    packed = jnp.where(slot == -1, extra, pltpu.roll(extra, LANES - EAST_LANE, 1))
    inside = (slot >= 0) & (slot < LANES)
    for s, slab in enumerate(slabs):
        turned = pltpu.roll(slab, lax.rem(s - slot + 64 * LANES, LANES), 1)
        packed = jnp.where((lane == s) & inside, turned, packed)
    return packed


def message_kernel(
    levels, west_ref, level_ref, part_ref, coef_ref, own_ref, other_ref, message_ref, side_ref
):
    height, breadth = level_ref.shape
    third_y = height // 3
    tile, row, lev = place()
    nest = tile == lax.axis_size("tiles") - 1

    @pl.when(jnp.logical_not(nest))
    def _():
        message_ref[...] = own_ref[...] + other_ref[...]
        slots = message_ref.shape[0] - 1
        first = tile * breadth - west_ref[1]
        lane = iota((levels, LANES), 1)
        columns = [
            pack_column([message_ref[s] for s in range(slots)], message_ref[slots], slot)
            for slot in (first, first + breadth - 1)
        ]
        side_ref[0] = jnp.where(lane < EAST_LANE, columns[0], pltpu.roll(columns[1], EAST_LANE, 1))

    @pl.when(nest)
    def _():
        offset = iota((third_y, height), 1) - 3 * iota((third_y, height), 0)
        rows = table((offset >= 0) & (offset <= 2))
        across = from_left(rows, from_right(level_ref[...], sums_table(breadth))) * (VERTICAL_MIX / 9.0)
        at_edge = iota((levels, LANES), 0) == jnp.where(lev == 0, levels - 1, 0)
        for m in range(third_y):
            message_ref[m] = part_ref[m] + jnp.where(at_edge, across[m : m + 1], 0.0)
        for i in range(third_y, message_ref.shape[0]):
            message_ref[i] = part_ref[i]
        side_ref[0] = jnp.zeros((levels, LANES), jnp.float32)

    side_ref[pl.ds(1, WEIGHTS)] = coef_ref[pl.ds(0, WEIGHTS)]


def blend_kernel(
    levels,
    western,
    west_ref,
    weight_ref,
    field_ref,
    window_ref,
    beside_ref,
    middle_ref,
    other_ref,
    coef_middle_ref,
    coef_near_ref,
    rows_ref,
):
    pieces, size, _ = field_ref.shape
    height = size // levels
    third_y = height // 3
    slots = third_y + 2
    tile_count = lax.axis_size("tiles")
    tile, row, _ = place()
    nest = tile == tile_count - 1

    @pl.when(nest)
    def _():
        store_slabs(rows_ref, 0, load_line(field_ref, levels, inner_line(height, row)))
        for i in range(pieces, rows_ref.shape[0]):
            rows_ref[i] = jnp.zeros((levels, LANES), jnp.float32)

    @pl.when(jnp.logical_not(nest))
    def _():
        paired = (tile == 1) | (tile == (0 if western else 2))

        def mine(i):
            return jnp.where(tile == 1, middle_ref[i], other_ref[i])

        def coefficient(i):
            other = beside_ref[1 + i] if western else coef_near_ref[i]
            return jnp.where(tile == 1, coef_middle_ref[i], other)

        breadth = pieces * LANES
        partner_east = tile == (0 if western else 1)
        slot = jnp.where(partner_east, (tile + 1) * breadth, tile * breadth - 1) - west_ref[1]
        column = jnp.where(partner_east, beside_ref[0], pltpu.roll(beside_ref[0], LANES - EAST_LANE, 1))
        lane = iota((levels, LANES), 1)

        def whole(s):
            return jnp.where(paired & (lane == slot), column[:, s : s + 1], window_ref[s])

        weight = weight_ref[:, 0:1]
        extra = window_ref[slots]
        extra = jnp.where(paired & (slot == -1) & (lane < EAST_LANE), column, extra)
        east_column = pltpu.roll(column, EAST_LANE, 1)
        extra = jnp.where(paired & (slot == LANES) & (lane >= EAST_LANE), east_column, extra)
        at_first, at_last = lane == 0, lane == LANES - 1
        lines = []
        for s in range(slots):
            x = whole(s)
            west = jnp.where(at_first, extra[:, s : s + 1], pltpu.roll(x, 1, 1))
            last = EAST_LANE + s
            east = jnp.where(at_last, extra[:, last : last + 1], pltpu.roll(x, LANES - 1, 1))
            lines.append((west, x, east))
        edges = coefficient(WEIGHTS - 1)
        ghosts = [coefficient(q) for q in range(3)]

        def outward(side, q):
            near = lines[1] if side == 0 else lines[slots - 2]
            far = lines[0] if side == 0 else lines[slots - 1]
            return (2.0 / 3.0) * far[q] + (1.0 / 3.0) * near[q]

        def sideward(s):
            west, x, east = lines[s]
            return (2.0 / 3.0) * jnp.where(at_first, west, east) + (1.0 / 3.0) * x

        sidewards = [sideward(s) for s in range(slots)]
        columns = [w + 7.0 * x + e for w, x, e in lines]
        for m in range(third_y):
            x = lines[m + 1][1]
            value = mine(m) + (NUDGING / 81.0) * (columns[m] + 7.0 * columns[m + 1] + columns[m + 2])
            for q in range(3):
                lane_of = 8 * m + q
                first, last = edges[:, lane_of : lane_of + 1], edges[:, lane_of + 3 : lane_of + 4]
                scale = jnp.where(at_first, first, jnp.where(at_last, last, 0.0))
                value = value + scale * sidewards[m + q]
            for side, at in ((0, 0), (1, third_y - 1)):
                if m == at:
                    for q in range(3):
                        value = value + jnp.where(row == side, ghosts[q], 0.0) * outward(side, q)
            rows_ref[m] = x + weight * (value - x)
        rows_ref[third_y] = weight * mine(third_y)


def later_kernel(
    levels,
    west_ref,
    south_ref,
    field_ref,
    east_ref,
    north_ref,
    level_ref,
    middle_ref,
    other_ref,
    parent_ref,
    blend_ref,
    out_ref,
    fine_ref,
    side_ref,
    northern_ref,
    southern_ref,
):
    height, breadth = level_ref.shape
    third_y = height // 3
    slots = third_y + 2
    tile, row, lev = place()
    nest = tile == lax.axis_size("tiles") - 1

    @pl.when(nest)
    def _():
        slabs = [middle_ref[s] + other_ref[s] for s in range(slots + 1)]
        cells, ring = refine(slabs[:slots], slabs[slots], height, breadth, row)
        fine_ref[...] = cells[:, :breadth]
        side_ref[...] = cells[:, breadth:]
        zero = jnp.zeros_like(ring)
        northern_ref[...] = jnp.where(row == 0, ring, zero)
        southern_ref[...] = jnp.where(row == 0, zero, ring)
        full_step(
            out_ref,
            field_ref,
            east_ref,
            north_ref,
            level_ref,
            levels,
            lev,
            True,
            northern_ref,
            southern_ref,
            side_ref,
            fine_ref,
        )

    @pl.when(jnp.logical_not(nest))
    def _():
        out_ref[...] = parent_ref[...]
        start = west_ref[1] - tile * breadth
        top = south_ref[1] + row * third_y - row * height
        for m in range(third_y):
            place_row(out_ref, levels, top + m, start, blend_ref[m])


def last_kernel(
    levels, west_ref, south_ref, given_ref, speeds_ref, blend_ref, rows_ref, out_hbm, out_ref, sems
):
    pieces, size, _ = given_ref.shape
    breadth = pieces * LANES
    height = size // levels
    third_y = height // 3
    tile, row, _ = place()
    nest = tile == lax.axis_size("tiles") - 1
    out_ref[...] = given_ref[...]

    @pl.when(nest)
    def _():
        inner = inner_line(height, row)
        halo = ghost_weight(join_slabs(speeds_ref, pieces, pieces), row == 1) * join_slabs(rows_ref, 0, pieces)
        store_line(out_ref, levels, inner, load_line(out_ref, levels, inner) + halo)

    @pl.when(jnp.logical_not(nest))
    def _():
        start = west_ref[1] - tile * breadth
        top = south_ref[1] + (1 - row) * third_y - row * height
        for m in range(third_y):
            value = rows_ref[m]
            if m == 0:
                value = value + jnp.where(row == 0, blend_ref[third_y], 0.0)
            if m == third_y - 1:
                value = value + jnp.where(row == 1, blend_ref[third_y], 0.0)
            place_row(out_ref, levels, top + m, start, value)
        near = jnp.where(row == 0, third_y - 1, 0)
        line = south_ref[1] + row * third_y - row * height + near
        place_row(out_ref, levels, line, start, blend_ref[near] + rows_ref[third_y])

    copies = [
        pltpu.make_async_copy(out_ref.at[c], out_hbm.at[:, pl.ds(c * LANES, LANES)], sems.at[c])
        for c in range(pieces)
    ]
    for copy in copies:
        copy.start()
    for copy in copies:
        copy.wait()


def call(kernel, outs, inputs, places, scratch=(), flops=0, out_place="v", aliases=()):
    spaces = {"s": pltpu.SMEM, "v": pltpu.VMEM, "h": pltpu.HBM}
    outs = [spaces[out_place](out, jnp.float32) if isinstance(out, tuple) else out for out in outs]
    moved = sum(4 * math.prod(out.shape) for out in outs) + sum(array.nbytes for array in inputs)
    inputs = [
        array if p == "v" else pltpu.with_memory_space_constraint(array, spaces[p])
        for array, p in zip(inputs, places)
    ]
    return pl.pallas_call(
        kernel,
        out_shape=outs,
        in_specs=[pl.BlockSpec(memory_space=spaces[p]) for p in places],
        out_specs=[pl.BlockSpec(memory_space=out.memory_space) for out in outs],
        scratch_shapes=[pltpu.VMEM(s, jnp.float32) if isinstance(s, tuple) else s for s in scratch],
        input_output_aliases=dict(aliases),
        compiler_params=pltpu.CompilerParams(vmem_limit_bytes=32 * 1024 * 1024),
        cost_estimate=pl.CostEstimate(flops=flops, bytes_accessed=moved, transcendentals=0),
    )(*inputs)


def per_device_paired(air_state, wind_east, wind_north, feedback_weight, nest_west, nest_south):
    levels, height, breadth = air_state.shape
    third_y = height // 3
    pieces = breadth // LANES
    slots = third_y + 2
    tile_count = lax.axis_size("tiles")
    size = levels * height
    flat = (size, breadth)
    chunked = (pieces, size, LANES)
    air, east, north = (array.reshape(flat) for array in (air_state, wind_east, wind_north))
    weight = jnp.broadcast_to(feedback_weight[:, None], (levels, LANES))
    swap = [(0, 1), (1, 0)]

    def slabs(count):
        return (count, levels, LANES)

    def kernel(body):
        return functools.partial(body, levels)

    rows, air_pieces, west, south = call(
        kernel(pack_kernel),
        [slabs(slots + 1 + pieces), chunked, pltpu.SMEM((2,), jnp.int32), pltpu.SMEM((2,), jnp.int32)],
        [nest_west, nest_south, air, north],
        "hhhh",
        [chunked, pltpu.SemaphoreType.DMA((2 * pieces + 2,))],
    )
    own, level, speeds, edges = call(
        kernel(own_kernel),
        [slabs(slots + 1), (height, breadth), slabs(2 * pieces), (levels, LANES)],
        [west, south, air_pieces, east, north],
        "ssvvv",
        flops=30 * size * breadth,
    )
    rows = lax.ppermute(rows, "rows", swap)
    level = lax.ppermute(level, "lev", swap)
    where = [(t, r, l) for t in range(tile_count) for r in range(2) for l in range(2)]
    at = {position: i for i, position in enumerate(where)}

    def over_tiles(message, step, *without):
        pairs = []
        for t, r, l in where:
            idle = t in without or (t ^ step) in without
            pairs.append((at[t, r, l], at[(t, r, 1 - l) if idle else (t ^ step, r, l)]))
        return lax.ppermute(message, ("tiles", "rows", "lev"), pairs)

    halo = over_tiles(edges, 3, 0)
    eastern = nest_west[1] > breadth
    rows, halo, eastern, weight = lax.optimization_barrier((rows, halo, eastern, weight))
    window = own + rows[: slots + 1]
    around = [(t, (t - 1) % tile_count) for t in range(tile_count)]
    starting = [
        over_tiles(window, 1),
        over_tiles(window, 2, 0),
        lax.ppermute(window, "tiles", around),
    ]
    sides = [(size, LANES), (levels, breadth), (levels, breadth)]
    early, other = call(
        kernel(early_kernel),
        [chunked, slabs(slots + 1)],
        [west, south, air, east, north, rows, level, starting[0]],
        "ssvvvvvv",
        sides,
        flops=30 * size * breadth,
    )
    early, other = call(
        kernel(middle_kernel),
        [chunked, slabs(slots + 1)],
        [west, south, air, east, north, rows, level, halo, starting[0], early, other],
        "ssvvvvvvvvv",
        sides,
        flops=30 * size * breadth,
        aliases=[(9, 0), (10, 1)],
    )
    other = lax.ppermute(other, "rows", swap)
    first, edge, own = call(
        kernel(first_kernel),
        [chunked, (height, breadth), slabs(slots + 1)],
        [west, south, early, east, speeds, *starting[::-1]],
        "ssvvvvvv",
        flops=10 * size * breadth,
    )
    level = lax.ppermute(edge, "lev", swap)
    (part,) = call(
        kernel(average_kernel),
        [slabs(slots + 1)],
        [first, east, north, rows],
        "vvvv",
        [flat, (height, breadth)],
        flops=30 * size * breadth,
    )
    message, side_message = call(
        kernel(message_kernel),
        [slabs(slots + 1), slabs(1 + WEIGHTS)],
        [west, level, part, starting[1], own, other],
        "svvvvv",
    )
    def finish(western, arrays):
        west, south, weight, first, east, north, level, message, side_message, early, speeds, coefs = arrays
        if western:
            other, beside = over_tiles(message, 3, 1), over_tiles(side_message, 1, 3)
        else:
            other, beside = over_tiles(message, 1, 0), over_tiles(side_message, 3, 0)
        middle = over_tiles(message, 2, 0)
        (blend,) = call(
            functools.partial(blend_kernel, levels, western),
            [slabs(third_y + 1)],
            [west, weight, first, message, beside, middle, other, *coefs],
            "s" + "v" * 8,
        )
        rows = lax.ppermute(blend, "rows", swap)
        (later,) = call(
            kernel(later_kernel),
            [chunked],
            [west, south, first, east, north, level, middle, other, early, blend],
            "ss" + "v" * 8,
            [flat, *sides],
            flops=30 * size * breadth,
        )
        (out,) = call(
            kernel(last_kernel),
            [flat],
            [west, south, later, speeds, blend, rows],
            "ssvvvv",
            [chunked, pltpu.SemaphoreType.DMA((pieces,))],
            out_place="h",
        )
        return out

    arrays = (west, south, weight, first, east, north, level, message, side_message, early, speeds)
    arrays += ((starting[1], starting[0]),)
    out = lax.cond(
        eastern,
        functools.partial(finish, False),
        functools.partial(finish, True),
        arrays,
    )
    return out.reshape(air_state.shape)


def solution(mesh):
    in_specs = (
        P(("members", "lev"), "rows", "tiles"),
        P(("members", "lev"), "rows", "tiles"),
        P(("members", "lev"), "rows", "tiles"),
        P("lev"),
        P("members"),
        P("members"),
    )
    out_specs = P(("members", "lev"), "rows", "tiles")
    paired = mesh.shape["tiles"] == 4 and mesh.shape["rows"] == 2 and mesh.shape["lev"] == 2
    return jax.shard_map(
        per_device_paired if paired else per_device, mesh=mesh, in_specs=in_specs, out_specs=out_specs, check_vma=False
    )
```

```python
import functools
import math

import jax
import jax.numpy as jnp
import numpy as np
from jax import lax
from jax.experimental import pallas as pl
from jax.experimental.pallas import tpu as pltpu
from jax.sharding import PartitionSpec as P

VERTICAL_MIX = 0.1
PARENT_MIXING = 0.04
NEST_MIXING = 0.18
NEST_ADVECT = 1.5
NUDGING = 0.2


def padded_2(array, sides, width):
    for axis, dim in sides:
        size, length = (lax.axis_size(axis), array.shape[dim])
        up = [(i, (i + 1) % size) for i in range(size - 1)]
        down = [(j, i) for i, j in up]
        last = lax.slice_in_dim(array, length - width, length, axis=dim)
        first = lax.slice_in_dim(array, 0, width, axis=dim)
        before = lax.ppermute(last, axis, up)
        after = lax.ppermute(first, axis, down)
        array = jnp.concatenate([before, array, after], axis=dim)
    return array


def interp_table(cells):
    extended = jnp.arange(cells + 2, dtype=jnp.int32) - 1
    coarse = jnp.floor_divide(extended, 3)
    offset = extended - 3 * coarse
    fraction = jnp.abs(offset - 1).astype(jnp.float32) / 3.0
    nearest = coarse + 1
    beside = nearest + (offset - 1)
    slots = jnp.arange(cells // 3 + 2, dtype=jnp.int32)[:, None]
    first_part = jnp.where(
        slots == nearest[None, :], 1.0 - fraction[None, :], jnp.zeros((), jnp.float32)
    )
    second_part = jnp.where(slots == beside[None, :], fraction[None, :], jnp.zeros((), jnp.float32))
    return first_part + second_part


def tendency(padded, speed_east, speed_north, advect_scale, mixing_scale):
    centre = padded[1:-1, 1:-1, 1:-1]
    eastern = padded[1:-1, 1:-1, 2:]
    western = padded[1:-1, 1:-1, :-2]
    southern = padded[1:-1, 2:, 1:-1]
    northern = padded[1:-1, :-2, 1:-1]
    upper = padded[2:, 1:-1, 1:-1]
    lower = padded[:-2, 1:-1, 1:-1]
    advect = speed_east * (eastern - western) + speed_north * (southern - northern)
    horizontal = eastern + western + southern + northern - 4.0 * centre
    vertical = upper + lower - 2.0 * centre
    return -0.5 * advect_scale * advect + mixing_scale * horizontal + VERTICAL_MIX * vertical


def padded_block(block_field):
    return padded_2(block_field, (("tiles", 2), ("rows", 1), ("lev", 0)), 1)


def per_device(air_state, wind_east, wind_north, feedback_weight, nest_west, nest_south):
    levels, height, breadth = air_state.shape
    tile_count = lax.axis_size("tiles")
    row_count = lax.axis_size("rows")
    tile_index = lax.axis_index("tiles")
    row_index = lax.axis_index("rows")
    parent_tiles = 3 * tile_count // 4
    nest_tiles = tile_count - parent_tiles
    in_nest = tile_index >= parent_tiles
    nest_tile = tile_index - parent_tiles
    cross_x = breadth // 3 + 2
    cross_y = height // 3 + 2
    third_x = breadth // 3
    third_y = height // 3
    first_x = tile_index * breadth
    first_y = row_index * height
    columns = jnp.arange(breadth, dtype=jnp.int32)
    lines = jnp.arange(height, dtype=jnp.int32)
    targets_x = jnp.arange(tile_count, dtype=jnp.int32)
    targets_y = jnp.arange(row_count, dtype=jnp.int32)
    highest = lax.Precision.HIGHEST
    table_x = interp_table(breadth)
    table_y = interp_table(height)
    zero_value = jnp.zeros((), jnp.float32)

    def boundary(source, substep):
        anchor_x = nest_west[substep] + (targets_x - parent_tiles) * third_x - 1
        slot_x = jnp.arange(cross_x, dtype=jnp.int32)
        pick_x = (
            (first_x + columns)[None, :, None] == anchor_x[:, None, None] + slot_x[None, None, :]
        ) & (targets_x >= parent_tiles)[:, None, None]
        pick_x = pick_x.astype(jnp.float32)
        anchor_y = nest_south[substep] + targets_y * third_y - 1
        slot_y = jnp.arange(cross_y, dtype=jnp.int32)
        pick_y = (
            (first_y + lines)[None, :, None] == anchor_y[:, None, None] + slot_y[None, None, :]
        ).astype(jnp.float32)
        pieces = jnp.einsum("lyi,tij->tlyj", source, pick_x, precision=highest)
        merged = lax.all_to_all(pieces, "tiles", split_axis=0, concat_axis=0, tiled=True).sum(
            axis=0
        )
        pieces = jnp.einsum("lyj,ryw->rlwj", merged, pick_y, precision=highest)
        window = lax.all_to_all(pieces, "rows", split_axis=0, concat_axis=0, tiled=True).sum(axis=0)
        along = jnp.einsum("lwj,je->lwe", window, table_x, precision=highest)
        return jnp.einsum("lwe,wf->lfe", along, table_y, precision=highest)

    def assemble(block_field, fine):
        padded = padded_block(block_field)
        fine_padded = jnp.pad(fine, ((1, 1), (0, 0), (0, 0)))
        column_place = lax.broadcasted_iota(jnp.int32, padded.shape, 2)
        line_place = lax.broadcasted_iota(jnp.int32, padded.shape, 1)
        outside = (column_place == 0) & (nest_tile == 0) | (column_place == breadth + 1) & (
            nest_tile == nest_tiles - 1
        )
        outside = (
            outside
            | (line_place == 0) & (row_index == 0)
            | (line_place == height + 1) & (row_index == row_count - 1)
        )
        padded = jnp.where(outside & in_nest, fine_padded, padded)
        seam_cells = (column_place == breadth + 1) & (tile_index == parent_tiles - 1)
        return jnp.where(seam_cells, zero_value, padded)

    advect_scale = jnp.where(in_nest, jnp.float32(NEST_ADVECT), jnp.float32(1.0))
    mixing_scale = jnp.where(in_nest, jnp.float32(NEST_MIXING), jnp.float32(PARENT_MIXING))
    fine_first = boundary(air_state, 0)
    change = tendency(
        assemble(air_state, fine_first), wind_east, wind_north, advect_scale, mixing_scale
    )
    nudging_term = jnp.where(in_nest, NUDGING * (fine_first[:, 1:-1, 1:-1] - air_state), zero_value)
    step_one = air_state + change + nudging_term
    fine_second = boundary(step_one, 1)
    change = tendency(
        assemble(step_one, fine_second), wind_east, wind_north, advect_scale, mixing_scale
    )
    nested_two = step_one + change + NUDGING * (fine_second[:, 1:-1, 1:-1] - step_one)
    step_two = jnp.where(in_nest, nested_two, step_one)
    coarse = step_two.reshape(levels, third_y, 3, third_x, 3).mean(axis=(2, 4))
    avg_columns = jnp.arange(third_x, dtype=jnp.int32)
    avg_lines = jnp.arange(third_y, dtype=jnp.int32)
    west_last = nest_west[1]
    south_last = nest_south[1]
    place_x = (
        (west_last + (targets_x - parent_tiles) * third_x)[:, None, None]
        + avg_columns[None, :, None]
        == (first_x + columns)[None, None, :]
    ) & (targets_x >= parent_tiles)[:, None, None]
    place_x = place_x.astype(jnp.float32)
    place_y = (
        (south_last + targets_y * third_y)[:, None, None] + avg_lines[None, :, None]
        == (first_y + lines)[None, None, :]
    ).astype(jnp.float32)
    parent_y = south_last + row_index * third_y + avg_lines
    send_y = (jnp.floor_divide(parent_y, height)[None, :] == targets_y[:, None]) & in_nest
    pieces = jnp.where(send_y[:, None, :, None], coarse[None], zero_value)
    received = lax.all_to_all(pieces, "rows", split_axis=0, concat_axis=0, tiled=True)
    spread = jnp.einsum("slba,sby->lya", received, place_y, precision=highest)
    parent_x = west_last + nest_tile * third_x + avg_columns
    send_x = jnp.floor_divide(parent_x, breadth)[None, :] == targets_x[:, None]
    pieces = jnp.where(send_x[:, None, None, :], spread[None], zero_value)
    received = lax.all_to_all(pieces, "tiles", split_axis=0, concat_axis=0, tiled=True)
    placed = jnp.einsum("slya,sai->lyi", received, place_x, precision=highest)
    global_x = (first_x + columns)[None, None, :]
    global_y = (first_y + lines)[None, :, None]
    covered = (global_x >= west_last) & (global_x < west_last + nest_tiles * third_x)
    covered = covered & (global_y >= south_last) & (global_y < south_last + row_count * third_y)
    covered = covered & jnp.logical_not(in_nest)
    blended = step_two + feedback_weight[:, None, None] * (placed - step_two)
    return jnp.where(covered, blended, step_two)


LANES = 128
FIRST_LANE = 32
LAST_LANE = 96
EAST_LANE = 64
WEIGHTS = 4


def iota(shape, dim):
    return lax.broadcasted_iota(jnp.int32, shape, dim)


def split_level(place, height):
    level = ((place.astype(jnp.float32) + 0.5) * (1.0 / height)).astype(jnp.int32)
    return level, place - level * height


def table(values):
    return values.astype(jnp.float32).astype(jnp.bfloat16)


def parts_of(array):
    high = array.astype(jnp.bfloat16)
    low = (array - high.astype(jnp.float32)).astype(jnp.bfloat16)
    return high, low


def dot(left, right):
    return jnp.dot(left, right, preferred_element_type=jnp.float32)


def from_left(weights, array):
    high, low = parts_of(array)
    return dot(weights, high) + dot(weights, low)


def from_right(array, weights):
    high, low = parts_of(array)
    return dot(high, weights) + dot(low, weights)


def hat(distance):
    return jnp.maximum(0, 3 - jnp.abs(distance - 1))


def place():
    return lax.axis_index("tiles"), lax.axis_index("rows"), lax.axis_index("lev")


def level_table(levels, height):
    shape = (levels, levels * height)
    level, _ = split_level(iota(shape, 1), height)
    return table(iota(shape, 0) == level)


def spread_table(levels, height):
    shape = (levels * height, levels)
    level, _ = split_level(iota(shape, 0), height)
    return table(iota(shape, 1) == level)


def load_line(ref, levels, line):
    rows = pl.ds(line, levels, stride=ref.shape[1] // levels)
    return jnp.concatenate([ref[c, rows, :] for c in range(ref.shape[0])], axis=1)


def store_line(ref, levels, line, value):
    rows = pl.ds(line, levels, stride=ref.shape[1] // levels)
    for c in range(ref.shape[0]):
        ref[c, rows, :] = value[:, c * LANES : (c + 1) * LANES]


def load_level(ref, height, l):
    rows = pl.ds(l * height, height)
    if len(ref.shape) == 2:
        return ref[rows, :]
    return jnp.concatenate([ref[c, rows, :] for c in range(ref.shape[0])], axis=1)


def store_level(ref, height, l, value):
    rows = pl.ds(l * height, height)
    if len(ref.shape) == 2:
        ref[rows, :] = value
    else:
        for c in range(ref.shape[0]):
            ref[c, rows, :] = value[:, c * LANES : (c + 1) * LANES]


def store_slabs(ref, first, wide):
    for i in range(wide.shape[1] // LANES):
        ref[first + i] = wide[:, i * LANES : (i + 1) * LANES]


def join_slabs(ref, first, count):
    return jnp.concatenate([ref[first + i] for i in range(count)], axis=1)


def column_pieces(start, pieces):
    first = (start + 64 * LANES) // LANES - 64
    offset = start - first * LANES
    held = [(c >= 0) & (c < pieces) for c in (first, first + 1)]
    return [jnp.clip(c, 0, pieces - 1) for c in (first, first + 1)], held, offset


def pack_window(ref, field_ref, levels, top, start):
    pieces, size, _ = field_ref.shape
    height = size // levels
    slots = ref.shape[0] - 1
    lane = iota((levels, LANES), 1)
    (left, right), (left_held, right_held), offset = column_pieces(start, pieces)
    before = lax.rem(offset + LANES - 1, LANES)
    (beside, _), (beside_held, _), _ = column_pieces(start - 1, pieces)
    in_left = lane < LANES - offset
    held = jnp.where(in_left, left_held.astype(jnp.float32), right_held.astype(jnp.float32))
    west_held, east_held = beside_held.astype(jnp.float32), right_held.astype(jnp.float32)
    turn = lax.rem(LANES - offset, LANES)
    extra = jnp.zeros((levels, LANES), jnp.float32)
    for slot in range(slots):
        line = top + slot
        there = ((line >= 0) & (line < height)).astype(jnp.float32)
        rows = pl.ds(jnp.clip(line, 0, height - 1), levels, stride=height)
        near, far, west = field_ref[left, rows, :], field_ref[right, rows, :], field_ref[beside, rows, :]
        ref[slot] = jnp.where(in_left, pltpu.roll(near, turn, 1), pltpu.roll(far, turn, 1)) * (held * there)
        west = pltpu.roll(west, lax.rem(LANES + slot - before, LANES), 1) * (west_held * there)
        east = pltpu.roll(far, lax.rem(LANES + EAST_LANE + slot - offset, LANES), 1) * (east_held * there)
        extra = jnp.where(lane == slot, west, jnp.where(lane == EAST_LANE + slot, east, extra))
    ref[slots] = extra


def place_row(ref, levels, line, start, value):
    pieces, size, _ = ref.shape
    height = size // levels
    lane = iota((levels, LANES), 1)
    at, held, offset = column_pieces(start, pieces)
    value = pltpu.roll(value, offset, 1)
    there = (line >= 0) & (line < height)
    rows = pl.ds(jnp.clip(line, 0, height - 1), levels, stride=height)
    for c in range(2):
        mine = (lane >= offset) if c == 0 else (lane < offset)
        ref[at[c], rows, :] = jnp.where(mine & (held[c] & there), value, ref[at[c], rows, :])


def pack_edges(field_ref, levels):
    height = field_ref.shape[1] // levels
    lane = iota((levels, LANES), 1)
    packed = jnp.zeros((levels, LANES), jnp.float32)
    for line in range(height):
        rows = pl.ds(line, levels, stride=height)
        first = field_ref[0, rows, :]
        last = field_ref[field_ref.shape[0] - 1, rows, :]
        packed = jnp.where(lane == FIRST_LANE + line, pltpu.roll(first, FIRST_LANE + line, 1), packed)
        packed = jnp.where(lane == LAST_LANE + line, pltpu.roll(last, LAST_LANE + line + 1, 1), packed)
    return packed


def neighbour_columns(even, odd, parent_tiles, tile):
    is_odd = tile % 2 == 1
    west = jnp.where(is_odd, even, odd)
    east = jnp.where(is_odd, odd, even)
    west = jnp.where(tile == 0, jnp.zeros_like(west), west)
    east = jnp.where(tile >= parent_tiles - 1, jnp.zeros_like(east), east)
    return jnp.where(iota(west.shape, 1) < LAST_LANE, east, west)


def unpack_edges(columns, levels, height):
    wide = from_left(spread_table(levels, height), columns)
    lane = iota(wide.shape, 1)
    _, line = split_level(iota(wide.shape, 0), height)
    west = jnp.sum(jnp.where(lane == line + LAST_LANE, wide, 0.0), axis=1, keepdims=True)
    east = jnp.sum(jnp.where(lane == line + FIRST_LANE, wide, 0.0), axis=1, keepdims=True)
    return jnp.where(lane == 0, west, jnp.where(lane == 1, east, 0.0))


def refine(slabs, extra, height, breadth, row):
    slots, levels = len(slabs), extra.shape[0]
    beside = [pltpu.roll(extra, LANES - s, 1) if s else extra for s in range(slots)]
    window = jnp.concatenate([jnp.concatenate(slabs, axis=0), jnp.concatenate(beside, axis=0)], axis=1)
    shape = (2 * LANES, breadth + LANES)
    slot, cell = iota(shape, 0), iota(shape, 1)
    held = (slot <= LANES) | (slot == LANES + EAST_LANE)
    at = jnp.where(slot < LANES, slot, jnp.where(slot == LANES, -1, LANES))
    cell = jnp.where(cell == breadth, -1, jnp.where(cell == breadth + 1, breadth, cell))
    across = jnp.where(held & (cell <= breadth), hat(cell - 3 * at), 0)
    wide = from_right(window, table(across)) * (1.0 / 9.0)
    shape = (levels * height, slots * levels)
    taken = iota(shape, 1)
    slot = taken // levels
    level, line = split_level(iota(shape, 0), height)
    along = jnp.where(taken - slot * levels == level, hat(line - 3 * (slot - 1)), 0)
    cells = from_left(table(along), wide)
    ring = jnp.where(
        row == 0,
        2.0 * wide[:levels] + wide[levels : 2 * levels],
        2.0 * wide[(slots - 1) * levels :] + wide[(slots - 2) * levels : (slots - 1) * levels],
    )
    return cells, ring[:, :breadth]


def beside_rows(x, north, south):
    height = x.shape[0]
    line = iota(x.shape, 0)
    northern = jnp.where(line == 0, north, pltpu.roll(x, 1, 0))
    southern = jnp.where(line == height - 1, south, pltpu.roll(x, height - 1, 0))
    return northern, southern


def beside_columns(x, west, east):
    breadth = x.shape[1]
    column = iota(x.shape, 1)
    western = jnp.where(column == 0, west, pltpu.roll(x, 1, 1))
    eastern = jnp.where(column == breadth - 1, east, pltpu.roll(x, breadth - 1, 1))
    return western, eastern


def change_of(x, sides, u, v, upper, lower, nest):
    advect_scale = NEST_ADVECT if nest else 1.0
    mixing_scale = NEST_MIXING if nest else PARENT_MIXING
    northern, southern, western, eastern = sides
    advect = u * (eastern - western) + v * (southern - northern)
    horizontal = eastern + western + southern + northern - 4.0 * x
    vertical = upper + lower - 2.0 * x
    return -0.5 * advect_scale * advect + mixing_scale * horizontal + VERTICAL_MIX * vertical


def ghost_weight(speed, before):
    return jnp.where(before, 0.5 * NEST_ADVECT, -0.5 * NEST_ADVECT) * speed + NEST_MIXING


def full_step(out_ref, field_ref, u_ref, v_ref, level_ref, levels, lev, nest, north, south, side, fine):
    height, breadth = level_ref.shape
    zero = jnp.zeros((height, breadth), jnp.float32)

    def block(ref, l):
        return load_level(ref, height, l)

    for l in range(levels):
        x = block(field_ref, l)
        lower = block(field_ref, l - 1) if l else jnp.where(lev == 1, level_ref[...], zero)
        upper = block(field_ref, l + 1) if l < levels - 1 else jnp.where(lev == 0, level_ref[...], zero)
        rows = [0.0 if ref is None else ref[pl.ds(l, 1), :] for ref in (north, south)]
        if side is None:
            columns = (0.0, 0.0)
        else:
            beside = side[pl.ds(l * height, height), :]
            columns = (beside[:, 0:1], beside[:, 1:2])
        sides = beside_rows(x, *rows) + beside_columns(x, *columns)
        fresh = x + change_of(x, sides, block(u_ref, l), block(v_ref, l), upper, lower, nest)
        if nest:
            fresh = fresh - NUDGING * x if fine is None else fresh + NUDGING * (block(fine, l) - x)
        store_level(out_ref, height, l, fresh)


def inner_line(height, row):
    return jnp.where(row == 0, height - 1, 0)


def edge_level(ref, height, lev):
    last = ref.shape[1] // height - 1
    return jnp.where(lev == 0, load_level(ref, height, last), load_level(ref, height, 0))


def ghost_row_weights(ghost, breadth):
    cell, third = iota((breadth, 3 * LANES), 0), iota((breadth, 3 * LANES), 1)
    kind = third // LANES
    offset = cell - 3 * (third - kind * LANES)
    middle = jnp.where(offset == 1, 3, jnp.where((offset == 0) | (offset == 2), 2, 0))
    weight = jnp.where(kind == 1, middle, jnp.where(offset == kind, 1, 0))
    return from_right(ghost, table(weight)) * (1.0 / 27.0)


def ghost_column_weights(first, last, levels, height):
    shape = (levels * height, LANES)
    lane = iota(shape, 1)
    _, line = split_level(iota(shape, 0), height)
    block = lane // 8
    inside = lane - block * 8
    eastern = inside >= 3
    kind = jnp.where(eastern, inside - 3, inside)
    offset = line - 3 * block
    middle = jnp.where(offset == 1, 3, jnp.where((offset == 0) | (offset == 2), 2, 0))
    weight = jnp.where(kind == 1, middle, jnp.where(offset == kind, 1, 0))
    weight = jnp.where((inside < 6) & (block < height // 3), weight, 0).astype(jnp.float32)
    columns = jnp.where(eastern, last, first) * weight
    return from_left(level_table(levels, height), columns) * (1.0 / 27.0)


def pack_kernel(
    levels,
    west_hbm,
    south_hbm,
    weight_hbm,
    air_hbm,
    north_hbm,
    rows_ref,
    air_ref,
    west_ref,
    south_ref,
    weight_ref,
    north_ref,
    sems,
):
    pieces, size, _ = air_ref.shape
    breadth = pieces * LANES
    height = size // levels
    third_y = height // 3
    slots = rows_ref.shape[0] - 1 - pieces
    tile, row, _ = place()
    nest = tile == lax.axis_size("tiles") - 1
    inner = inner_line(height, row)

    def column_copies(source, target, first):
        return [
            pltpu.make_async_copy(source.at[:, pl.ds(c * LANES, LANES)], target.at[c], sems.at[first + c])
            for c in range(pieces)
        ]

    copies = column_copies(air_hbm, air_ref, 0)
    copies.append(pltpu.make_async_copy(west_hbm, west_ref, sems.at[2 * pieces]))
    copies.append(pltpu.make_async_copy(south_hbm, south_ref, sems.at[2 * pieces + 1]))
    copies.append(pltpu.make_async_copy(weight_hbm, weight_ref, sems.at[2 * pieces + 2]))
    speeds = column_copies(north_hbm, north_ref, pieces)
    for copy in copies:
        copy.start()

    @pl.when(nest)
    def _():
        for copy in speeds:
            copy.start()

    for copy in copies:
        copy.wait()
    store_slabs(rows_ref, slots + 1, load_line(air_ref, levels, inner))
    part = rows_ref.at[pl.ds(0, slots + 1)]

    @pl.when(nest)
    def _():
        for copy in speeds:
            copy.wait()
        part[...] = jnp.zeros_like(part)
        store_slabs(rows_ref, WEIGHTS, load_line(north_ref, levels, inner))

    @pl.when(jnp.logical_not(nest))
    def _():
        start = west_ref[0] - tile * breadth
        top = south_ref[0] - 1 - row * height
        pack_window(part, air_ref, levels, top + (1 - row) * third_y, start)


def own_kernel(
    levels, west_ref, south_ref, air_ref, east_ref, north_ref, own_ref, level_ref, speeds_ref, edges_ref
):
    pieces, size, _ = air_ref.shape
    breadth = pieces * LANES
    height = size // levels
    third_y = height // 3
    slots = own_ref.shape[0] - 1
    tile, row, lev = place()
    nest = tile == lax.axis_size("tiles") - 1
    level_ref[...] = edge_level(air_ref, height, lev)

    @pl.when(nest)
    def _():
        inner = inner_line(height, row)
        shape = (2 * levels, size)
        taken = iota(shape, 0)
        level, line = split_level(iota(shape, 1), height)
        wanted = jnp.where(taken < levels, height - 1 - inner, inner)
        picked = table((lax.rem(taken, levels) == level) & (line == wanted))
        speeds = from_left(picked, north_ref[...])
        outer = speeds[:levels]
        store_slabs(speeds_ref, 0, outer)
        store_slabs(speeds_ref, pieces, speeds[levels:])
        own_ref[...] = jnp.zeros_like(own_ref)
        edges_ref[...] = jnp.zeros_like(edges_ref)
        store_slabs(own_ref, 0, ghost_row_weights(ghost_weight(outer, row == 0), breadth))
        first = ghost_weight(east_ref[:, 0:1], True)
        last = ghost_weight(east_ref[:, breadth - 1 : breadth], False)
        own_ref[WEIGHTS - 1] = ghost_column_weights(first, last, levels, height)

    @pl.when(jnp.logical_not(nest))
    def _():
        start = west_ref[0] - tile * breadth
        top = south_ref[0] - 1 - row * height
        pack_window(own_ref, air_ref, levels, top + row * third_y, start)
        edges = pack_edges(air_ref, levels)
        edges_ref[0] = edges
        own_ref[slots] = own_ref[slots] + edges
        speeds_ref[...] = jnp.zeros_like(speeds_ref)


def set_halo(rows_ref, first, northern_ref, southern_ref, row):
    halo = join_slabs(rows_ref, first, rows_ref.shape[0] - first)
    zero = jnp.zeros_like(halo)
    northern_ref[...] = jnp.where(row == 0, zero, halo)
    southern_ref[...] = jnp.where(row == 0, halo, zero)


def parent_step(
    levels, west_ref, south_ref, shared, rows_ref, columns, field_ref, other_ref, side_ref, northern_ref, southern_ref
):
    height = side_ref.shape[0] // levels
    slots = other_ref.shape[0] - 1
    tile, row, lev = place()
    set_halo(rows_ref, slots + 1, northern_ref, southern_ref, row)
    side_ref[...] = unpack_edges(columns, levels, height)
    full_step(field_ref, *shared, levels, lev, False, northern_ref, southern_ref, side_ref, None)
    start = west_ref[1] - tile * field_ref.shape[0] * LANES
    top = south_ref[1] - 1 - row * height
    pack_window(other_ref, field_ref, levels, top + (1 - row) * (height // 3), start)


def early_kernel(
    levels,
    west_ref,
    south_ref,
    air_ref,
    east_ref,
    north_ref,
    rows_ref,
    level_ref,
    one_ref,
    field_ref,
    other_ref,
    side_ref,
    northern_ref,
    southern_ref,
):
    slots = other_ref.shape[0] - 1
    tile_count = lax.axis_size("tiles")
    tile, row, lev = place()
    shared = (air_ref, east_ref, north_ref, level_ref)

    @pl.when(tile == tile_count - 1)
    def _():
        set_halo(rows_ref, slots + 1, northern_ref, southern_ref, row)
        full_step(field_ref, *shared, levels, lev, True, northern_ref, southern_ref, None, None)
        other_ref[...] = jnp.zeros_like(other_ref)

    @pl.when(tile == 0)
    def _():
        columns = neighbour_columns(one_ref[slots], one_ref[slots], tile_count - 1, tile)
        refs = (field_ref, other_ref, side_ref, northern_ref, southern_ref)
        parent_step(levels, west_ref, south_ref, shared, rows_ref, columns, *refs)


def middle_kernel(
    levels,
    west_ref,
    south_ref,
    air_ref,
    east_ref,
    north_ref,
    rows_ref,
    level_ref,
    three_ref,
    one_ref,
    given_field_ref,
    given_other_ref,
    field_ref,
    other_ref,
    side_ref,
    northern_ref,
    southern_ref,
):
    slots = other_ref.shape[0] - 1
    tile_count = lax.axis_size("tiles")
    tile, _, _ = place()
    shared = (air_ref, east_ref, north_ref, level_ref)

    @pl.when((tile > 0) & (tile < tile_count - 1))
    def _():
        columns = neighbour_columns(one_ref[slots], three_ref[0], tile_count - 1, tile)
        refs = (field_ref, other_ref, side_ref, northern_ref, southern_ref)
        parent_step(levels, west_ref, south_ref, shared, rows_ref, columns, *refs)


def first_kernel(
    levels,
    west_ref,
    south_ref,
    early_ref,
    east_ref,
    speeds_ref,
    three_ref,
    two_ref,
    one_ref,
    field_ref,
    edge_ref,
    own_ref,
):
    pieces, size, _ = early_ref.shape
    height, breadth = edge_ref.shape
    slots = one_ref.shape[0] - 1
    tile, row, lev = place()
    nest = tile == lax.axis_size("tiles") - 1

    @pl.when(jnp.logical_not(nest))
    def _():
        edge_ref[...] = jnp.zeros_like(edge_ref)
        start = west_ref[1] - tile * breadth
        top = south_ref[1] - 1 - row * height
        pack_window(own_ref, early_ref, levels, top + row * (height // 3), start)

    @pl.when(nest)
    def _():
        slabs = [one_ref[s] + two_ref[s] + three_ref[s] for s in range(slots + 1)]
        cells, ring = refine(slabs[:slots], slabs[slots], height, breadth, row)
        lane = iota((size, LANES), 1)
        for c in range(pieces):
            piece = slice(c * LANES, (c + 1) * LANES)
            value = early_ref[c] + NUDGING * cells[:, piece]
            if c == 0:
                ghost = ghost_weight(east_ref[:, piece], True) * cells[:, breadth : breadth + 1]
                value = value + jnp.where(lane == 0, ghost, 0.0)
            if c == pieces - 1:
                ghost = ghost_weight(east_ref[:, piece], False) * cells[:, breadth + 1 : breadth + 2]
                value = value + jnp.where(lane == LANES - 1, ghost, 0.0)
            field_ref[c] = value
        outer = height - 1 - inner_line(height, row)
        ghost = ghost_weight(join_slabs(speeds_ref, 0, pieces), row == 0) * ring
        store_line(field_ref, levels, outer, load_line(field_ref, levels, outer) + ghost)
        edge_ref[...] = edge_level(field_ref, height, lev)


def average_kernel(levels, field_ref, east_ref, north_ref, rows_ref, message_ref, part_ref, nothing_ref):
    pieces, size, _ = field_ref.shape
    height, breadth = nothing_ref.shape
    third_y = height // 3
    tile, row, lev = place()

    @pl.when(tile == lax.axis_size("tiles") - 1)
    def _():
        nothing_ref[...] = jnp.zeros_like(nothing_ref)
        full_step(part_ref, field_ref, east_ref, north_ref, nothing_ref, levels, lev, True, None, None, None, None)
        sums = sums_table(breadth)
        shape = (third_y * levels, size)
        taken = iota(shape, 0)
        block = taken // levels
        level, line = split_level(iota(shape, 1), height)
        offset = line - 3 * block
        rows = table((taken - block * levels == level) & (offset >= 0) & (offset <= 2))
        means = from_left(rows, from_right(part_ref[...], sums)) * (1.0 / 9.0)
        for m in range(third_y):
            message_ref[m] = means[m * levels : (m + 1) * levels]
        shared = load_line(field_ref, levels, inner_line(height, row))
        shared = ghost_weight(join_slabs(rows_ref, WEIGHTS, pieces), row == 0) * shared
        message_ref[third_y] = from_right(shared, sums) * (1.0 / 9.0)
        for i in range(third_y + 1, message_ref.shape[0]):
            message_ref[i] = jnp.zeros((levels, LANES), jnp.float32)


def sums_table(breadth):
    offset = iota((breadth, LANES), 0) - 3 * iota((breadth, LANES), 1)
    return table((offset >= 0) & (offset <= 2))


def pack_column(slabs, extra, slot):
    lane = iota(extra.shape, 1)
    packed = jnp.where(slot == -1, extra, pltpu.roll(extra, LANES - EAST_LANE, 1))
    inside = (slot >= 0) & (slot < LANES)
    for s, slab in enumerate(slabs):
        turned = pltpu.roll(slab, lax.rem(s - slot + 64 * LANES, LANES), 1)
        packed = jnp.where((lane == s) & inside, turned, packed)
    return packed


def message_kernel(
    levels, west_ref, level_ref, part_ref, coef_ref, own_ref, other_ref, message_ref, side_ref
):
    height, breadth = level_ref.shape
    third_y = height // 3
    tile, row, lev = place()
    nest = tile == lax.axis_size("tiles") - 1

    @pl.when(jnp.logical_not(nest))
    def _():
        message_ref[...] = own_ref[...] + other_ref[...]
        slots = message_ref.shape[0] - 1
        first = tile * breadth - west_ref[1]
        lane = iota((levels, LANES), 1)
        columns = [
            pack_column([message_ref[s] for s in range(slots)], message_ref[slots], slot)
            for slot in (first, first + breadth - 1)
        ]
        side_ref[0] = jnp.where(lane < EAST_LANE, columns[0], pltpu.roll(columns[1], EAST_LANE, 1))

    @pl.when(nest)
    def _():
        offset = iota((third_y, height), 1) - 3 * iota((third_y, height), 0)
        rows = table((offset >= 0) & (offset <= 2))
        across = from_left(rows, from_right(level_ref[...], sums_table(breadth))) * (VERTICAL_MIX / 9.0)
        at_edge = iota((levels, LANES), 0) == jnp.where(lev == 0, levels - 1, 0)
        for m in range(third_y):
            message_ref[m] = part_ref[m] + jnp.where(at_edge, across[m : m + 1], 0.0)
        for i in range(third_y, message_ref.shape[0]):
            message_ref[i] = part_ref[i]
        side_ref[0] = jnp.zeros((levels, LANES), jnp.float32)

    side_ref[pl.ds(1, WEIGHTS)] = coef_ref[pl.ds(0, WEIGHTS)]


def blend_kernel(
    levels,
    western,
    west_ref,
    weight_ref,
    field_ref,
    window_ref,
    beside_ref,
    middle_ref,
    other_ref,
    coef_middle_ref,
    coef_near_ref,
    rows_ref,
):
    pieces, size, _ = field_ref.shape
    height = size // levels
    third_y = height // 3
    slots = third_y + 2
    tile_count = lax.axis_size("tiles")
    tile, row, _ = place()
    nest = tile == tile_count - 1

    @pl.when(nest)
    def _():
        store_slabs(rows_ref, 0, load_line(field_ref, levels, inner_line(height, row)))
        for i in range(pieces, rows_ref.shape[0]):
            rows_ref[i] = jnp.zeros((levels, LANES), jnp.float32)

    @pl.when(jnp.logical_not(nest))
    def _():
        paired = (tile == 1) | (tile == (0 if western else 2))

        def mine(i):
            return jnp.where(tile == 1, middle_ref[i], other_ref[i])

        def coefficient(i):
            other = beside_ref[1 + i] if western else coef_near_ref[i]
            return jnp.where(tile == 1, coef_middle_ref[i], other)

        breadth = pieces * LANES
        partner_east = tile == (0 if western else 1)
        slot = jnp.where(partner_east, (tile + 1) * breadth, tile * breadth - 1) - west_ref[1]
        column = jnp.where(partner_east, beside_ref[0], pltpu.roll(beside_ref[0], LANES - EAST_LANE, 1))
        lane = iota((levels, LANES), 1)

        def whole(s):
            return jnp.where(paired & (lane == slot), column[:, s : s + 1], window_ref[s])

        level = iota((levels, LANES), 0)
        weight = jnp.zeros((levels, LANES), jnp.float32)
        for l in range(levels):
            weight = jnp.where(level == l, weight_ref[l], weight)
        extra = window_ref[slots]
        extra = jnp.where(paired & (slot == -1) & (lane < EAST_LANE), column, extra)
        east_column = pltpu.roll(column, EAST_LANE, 1)
        extra = jnp.where(paired & (slot == LANES) & (lane >= EAST_LANE), east_column, extra)
        at_first, at_last = lane == 0, lane == LANES - 1
        lines = []
        for s in range(slots):
            x = whole(s)
            west = jnp.where(at_first, extra[:, s : s + 1], pltpu.roll(x, 1, 1))
            last = EAST_LANE + s
            east = jnp.where(at_last, extra[:, last : last + 1], pltpu.roll(x, LANES - 1, 1))
            lines.append((west, x, east))
        edges = coefficient(WEIGHTS - 1)
        ghosts = [coefficient(q) for q in range(3)]

        def outward(side, q):
            near = lines[1] if side == 0 else lines[slots - 2]
            far = lines[0] if side == 0 else lines[slots - 1]
            return (2.0 / 3.0) * far[q] + (1.0 / 3.0) * near[q]

        def sideward(s):
            west, x, east = lines[s]
            return (2.0 / 3.0) * jnp.where(at_first, west, east) + (1.0 / 3.0) * x

        sidewards = [sideward(s) for s in range(slots)]
        columns = [w + 7.0 * x + e for w, x, e in lines]
        for m in range(third_y):
            x = lines[m + 1][1]
            value = mine(m) + (NUDGING / 81.0) * (columns[m] + 7.0 * columns[m + 1] + columns[m + 2])
            for q in range(3):
                lane_of = 8 * m + q
                first, last = edges[:, lane_of : lane_of + 1], edges[:, lane_of + 3 : lane_of + 4]
                scale = jnp.where(at_first, first, jnp.where(at_last, last, 0.0))
                value = value + scale * sidewards[m + q]
            for side, at in ((0, 0), (1, third_y - 1)):
                if m == at:
                    for q in range(3):
                        value = value + jnp.where(row == side, ghosts[q], 0.0) * outward(side, q)
            rows_ref[m] = x + weight * (value - x)
        rows_ref[third_y] = weight * mine(third_y)


def later_kernel(
    levels,
    west_ref,
    south_ref,
    field_ref,
    east_ref,
    north_ref,
    level_ref,
    middle_ref,
    other_ref,
    parent_ref,
    blend_ref,
    out_ref,
    fine_ref,
    side_ref,
    northern_ref,
    southern_ref,
):
    height, breadth = level_ref.shape
    third_y = height // 3
    slots = third_y + 2
    tile, row, lev = place()
    nest = tile == lax.axis_size("tiles") - 1

    @pl.when(nest)
    def _():
        slabs = [middle_ref[s] + other_ref[s] for s in range(slots + 1)]
        cells, ring = refine(slabs[:slots], slabs[slots], height, breadth, row)
        fine_ref[...] = cells[:, :breadth]
        side_ref[...] = cells[:, breadth:]
        zero = jnp.zeros_like(ring)
        northern_ref[...] = jnp.where(row == 0, ring, zero)
        southern_ref[...] = jnp.where(row == 0, zero, ring)
        full_step(
            out_ref,
            field_ref,
            east_ref,
            north_ref,
            level_ref,
            levels,
            lev,
            True,
            northern_ref,
            southern_ref,
            side_ref,
            fine_ref,
        )

    @pl.when(jnp.logical_not(nest))
    def _():
        out_ref[...] = parent_ref[...]
        start = west_ref[1] - tile * breadth
        top = south_ref[1] + row * third_y - row * height
        for m in range(third_y):
            place_row(out_ref, levels, top + m, start, blend_ref[m])


def last_kernel(
    levels, west_ref, south_ref, given_ref, speeds_ref, blend_ref, rows_ref, out_hbm, out_ref, sems
):
    pieces, size, _ = given_ref.shape
    breadth = pieces * LANES
    height = size // levels
    third_y = height // 3
    tile, row, _ = place()
    nest = tile == lax.axis_size("tiles") - 1
    out_ref[...] = given_ref[...]

    @pl.when(nest)
    def _():
        inner = inner_line(height, row)
        halo = ghost_weight(join_slabs(speeds_ref, pieces, pieces), row == 1) * join_slabs(rows_ref, 0, pieces)
        store_line(out_ref, levels, inner, load_line(out_ref, levels, inner) + halo)

    @pl.when(jnp.logical_not(nest))
    def _():
        start = west_ref[1] - tile * breadth
        top = south_ref[1] + (1 - row) * third_y - row * height
        for m in range(third_y):
            value = rows_ref[m]
            if m == 0:
                value = value + jnp.where(row == 0, blend_ref[third_y], 0.0)
            if m == third_y - 1:
                value = value + jnp.where(row == 1, blend_ref[third_y], 0.0)
            place_row(out_ref, levels, top + m, start, value)
        near = jnp.where(row == 0, third_y - 1, 0)
        line = south_ref[1] + row * third_y - row * height + near
        place_row(out_ref, levels, line, start, blend_ref[near] + rows_ref[third_y])

    copies = [
        pltpu.make_async_copy(out_ref.at[c], out_hbm.at[:, pl.ds(c * LANES, LANES)], sems.at[c])
        for c in range(pieces)
    ]
    for copy in copies:
        copy.start()
    for copy in copies:
        copy.wait()


def call(kernel, outs, inputs, places, scratch=(), flops=0, out_place="v", aliases=()):
    spaces = {"s": pltpu.SMEM, "v": pltpu.VMEM, "h": pltpu.HBM}
    outs = [spaces[out_place](out, jnp.float32) if isinstance(out, tuple) else out for out in outs]
    moved = sum(4 * math.prod(out.shape) for out in outs) + sum(array.nbytes for array in inputs)
    inputs = [
        array if p == "v" else pltpu.with_memory_space_constraint(array, spaces[p])
        for array, p in zip(inputs, places)
    ]
    return pl.pallas_call(
        kernel,
        out_shape=outs,
        in_specs=[pl.BlockSpec(memory_space=spaces[p]) for p in places],
        out_specs=[pl.BlockSpec(memory_space=out.memory_space) for out in outs],
        scratch_shapes=[pltpu.VMEM(s, jnp.float32) if isinstance(s, tuple) else s for s in scratch],
        input_output_aliases=dict(aliases),
        compiler_params=pltpu.CompilerParams(vmem_limit_bytes=32 * 1024 * 1024),
        cost_estimate=pl.CostEstimate(flops=flops, bytes_accessed=moved, transcendentals=0),
    )(*inputs)


def per_device_paired(air_state, wind_east, wind_north, feedback_weight, nest_west, nest_south):
    levels, height, breadth = air_state.shape
    third_y = height // 3
    pieces = breadth // LANES
    slots = third_y + 2
    tile_count = lax.axis_size("tiles")
    size = levels * height
    flat = (size, breadth)
    chunked = (pieces, size, LANES)
    air, east, north = (array.reshape(flat) for array in (air_state, wind_east, wind_north))
    swap = [(0, 1), (1, 0)]

    def slabs(count):
        return (count, levels, LANES)

    def kernel(body):
        return functools.partial(body, levels)

    rows, air_pieces, west, south, weight = call(
        kernel(pack_kernel),
        [
            slabs(slots + 1 + pieces),
            chunked,
            pltpu.SMEM((2,), jnp.int32),
            pltpu.SMEM((2,), jnp.int32),
            pltpu.SMEM((levels,), jnp.float32),
        ],
        [nest_west, nest_south, feedback_weight, air, north],
        "hhhhh",
        [chunked, pltpu.SemaphoreType.DMA((2 * pieces + 3,))],
    )
    own, level, speeds, edges = call(
        kernel(own_kernel),
        [slabs(slots + 1), (height, breadth), slabs(2 * pieces), slabs(slots + 2)],
        [west, south, air_pieces, east, north],
        "ssvvv",
        flops=30 * size * breadth,
    )
    rows = lax.ppermute(rows, "rows", swap)
    level = lax.ppermute(level, "lev", swap)
    where = [(t, r, l) for t in range(tile_count) for r in range(2) for l in range(2)]
    at = {position: i for i, position in enumerate(where)}

    def over_tiles(message, step, *without):
        pairs = []
        for t, r, l in where:
            idle = t in without or (t ^ step) in without
            pairs.append((at[t, r, l], at[(t, r, 1 - l) if idle else (t ^ step, r, l)]))
        return lax.ppermute(message, ("tiles", "rows", "lev"), pairs)

    halo = over_tiles(edges, 3, 0)
    eastern = nest_west[1] > breadth
    rows, eastern = lax.optimization_barrier((rows, eastern))
    window = own + rows[: slots + 1]
    around = [(t, (t - 1) % tile_count) for t in range(tile_count)]
    starting = [
        over_tiles(window, 1),
        over_tiles(window, 2, 0),
        lax.ppermute(window, "tiles", around),
    ]
    sides = [(size, LANES), (levels, breadth), (levels, breadth)]
    early, other = call(
        kernel(early_kernel),
        [chunked, slabs(slots + 1)],
        [west, south, air, east, north, rows, level, starting[0]],
        "ssvvvvvv",
        sides,
        flops=30 * size * breadth,
    )
    early, other = call(
        kernel(middle_kernel),
        [chunked, slabs(slots + 1)],
        [west, south, air, east, north, rows, level, halo, starting[0], early, other],
        "ssvvvvvvvvv",
        sides,
        flops=30 * size * breadth,
        aliases=[(9, 0), (10, 1)],
    )
    other = lax.ppermute(other, "rows", swap)
    first, edge, own = call(
        kernel(first_kernel),
        [chunked, (height, breadth), slabs(slots + 1)],
        [west, south, early, east, speeds, *starting[::-1]],
        "ssvvvvvv",
        flops=10 * size * breadth,
    )
    level = lax.ppermute(edge, "lev", swap)
    (part,) = call(
        kernel(average_kernel),
        [slabs(slots + 1)],
        [first, east, north, rows],
        "vvvv",
        [flat, (height, breadth)],
        flops=30 * size * breadth,
    )
    message, side_message = call(
        kernel(message_kernel),
        [slabs(slots + 1), slabs(1 + WEIGHTS)],
        [west, level, part, starting[1], own, other],
        "svvvvv",
    )
    def finish(western, arrays):
        west, south, weight, first, east, north, level, message, side_message, early, speeds, coefs = arrays
        if western:
            other, beside = over_tiles(message, 3, 1), over_tiles(side_message, 1, 3)
        else:
            other, beside = over_tiles(message, 1, 0), over_tiles(side_message, 3, 0)
        middle = over_tiles(message, 2, 0)
        (blend,) = call(
            functools.partial(blend_kernel, levels, western),
            [slabs(third_y + 1)],
            [west, weight, first, message, beside, middle, other, *coefs],
            "ss" + "v" * 7,
        )
        rows = lax.ppermute(blend, "rows", swap)
        (later,) = call(
            kernel(later_kernel),
            [chunked],
            [west, south, first, east, north, level, middle, other, early, blend],
            "ss" + "v" * 8,
            [flat, *sides],
            flops=30 * size * breadth,
        )
        (out,) = call(
            kernel(last_kernel),
            [flat],
            [west, south, later, speeds, blend, rows],
            "ssvvvv",
            [chunked, pltpu.SemaphoreType.DMA((pieces,))],
            out_place="h",
        )
        return out

    arrays = (west, south, weight, first, east, north, level, message, side_message, early, speeds)
    arrays += ((starting[1], starting[0]),)
    out = lax.cond(
        eastern,
        functools.partial(finish, False),
        functools.partial(finish, True),
        arrays,
    )
    return out.reshape(air_state.shape)


def solution(mesh):
    in_specs = (
        P(("members", "lev"), "rows", "tiles"),
        P(("members", "lev"), "rows", "tiles"),
        P(("members", "lev"), "rows", "tiles"),
        P("lev"),
        P("members"),
        P("members"),
    )
    out_specs = P(("members", "lev"), "rows", "tiles")
    paired = mesh.shape["tiles"] == 4 and mesh.shape["rows"] == 2 and mesh.shape["lev"] == 2
    return jax.shard_map(
        per_device_paired if paired else per_device, mesh=mesh, in_specs=in_specs, out_specs=out_specs, check_vma=False
    )
```

```python
import functools
import math

import jax
import jax.numpy as jnp
import numpy as np
from jax import lax
from jax.experimental import pallas as pl
from jax.experimental.pallas import tpu as pltpu
from jax.sharding import PartitionSpec as P

VERTICAL_MIX = 0.1
PARENT_MIXING = 0.04
NEST_MIXING = 0.18
NEST_ADVECT = 1.5
NUDGING = 0.2


def padded_2(array, sides, width):
    for axis, dim in sides:
        size, length = (lax.axis_size(axis), array.shape[dim])
        up = [(i, (i + 1) % size) for i in range(size - 1)]
        down = [(j, i) for i, j in up]
        last = lax.slice_in_dim(array, length - width, length, axis=dim)
        first = lax.slice_in_dim(array, 0, width, axis=dim)
        before = lax.ppermute(last, axis, up)
        after = lax.ppermute(first, axis, down)
        array = jnp.concatenate([before, array, after], axis=dim)
    return array


def interp_table(cells):
    extended = jnp.arange(cells + 2, dtype=jnp.int32) - 1
    coarse = jnp.floor_divide(extended, 3)
    offset = extended - 3 * coarse
    fraction = jnp.abs(offset - 1).astype(jnp.float32) / 3.0
    nearest = coarse + 1
    beside = nearest + (offset - 1)
    slots = jnp.arange(cells // 3 + 2, dtype=jnp.int32)[:, None]
    first_part = jnp.where(
        slots == nearest[None, :], 1.0 - fraction[None, :], jnp.zeros((), jnp.float32)
    )
    second_part = jnp.where(slots == beside[None, :], fraction[None, :], jnp.zeros((), jnp.float32))
    return first_part + second_part


def tendency(padded, speed_east, speed_north, advect_scale, mixing_scale):
    centre = padded[1:-1, 1:-1, 1:-1]
    eastern = padded[1:-1, 1:-1, 2:]
    western = padded[1:-1, 1:-1, :-2]
    southern = padded[1:-1, 2:, 1:-1]
    northern = padded[1:-1, :-2, 1:-1]
    upper = padded[2:, 1:-1, 1:-1]
    lower = padded[:-2, 1:-1, 1:-1]
    advect = speed_east * (eastern - western) + speed_north * (southern - northern)
    horizontal = eastern + western + southern + northern - 4.0 * centre
    vertical = upper + lower - 2.0 * centre
    return -0.5 * advect_scale * advect + mixing_scale * horizontal + VERTICAL_MIX * vertical


def padded_block(block_field):
    return padded_2(block_field, (("tiles", 2), ("rows", 1), ("lev", 0)), 1)


def per_device(air_state, wind_east, wind_north, feedback_weight, nest_west, nest_south):
    levels, height, breadth = air_state.shape
    tile_count = lax.axis_size("tiles")
    row_count = lax.axis_size("rows")
    tile_index = lax.axis_index("tiles")
    row_index = lax.axis_index("rows")
    parent_tiles = 3 * tile_count // 4
    nest_tiles = tile_count - parent_tiles
    in_nest = tile_index >= parent_tiles
    nest_tile = tile_index - parent_tiles
    cross_x = breadth // 3 + 2
    cross_y = height // 3 + 2
    third_x = breadth // 3
    third_y = height // 3
    first_x = tile_index * breadth
    first_y = row_index * height
    columns = jnp.arange(breadth, dtype=jnp.int32)
    lines = jnp.arange(height, dtype=jnp.int32)
    targets_x = jnp.arange(tile_count, dtype=jnp.int32)
    targets_y = jnp.arange(row_count, dtype=jnp.int32)
    highest = lax.Precision.HIGHEST
    table_x = interp_table(breadth)
    table_y = interp_table(height)
    zero_value = jnp.zeros((), jnp.float32)

    def boundary(source, substep):
        anchor_x = nest_west[substep] + (targets_x - parent_tiles) * third_x - 1
        slot_x = jnp.arange(cross_x, dtype=jnp.int32)
        pick_x = (
            (first_x + columns)[None, :, None] == anchor_x[:, None, None] + slot_x[None, None, :]
        ) & (targets_x >= parent_tiles)[:, None, None]
        pick_x = pick_x.astype(jnp.float32)
        anchor_y = nest_south[substep] + targets_y * third_y - 1
        slot_y = jnp.arange(cross_y, dtype=jnp.int32)
        pick_y = (
            (first_y + lines)[None, :, None] == anchor_y[:, None, None] + slot_y[None, None, :]
        ).astype(jnp.float32)
        pieces = jnp.einsum("lyi,tij->tlyj", source, pick_x, precision=highest)
        merged = lax.all_to_all(pieces, "tiles", split_axis=0, concat_axis=0, tiled=True).sum(
            axis=0
        )
        pieces = jnp.einsum("lyj,ryw->rlwj", merged, pick_y, precision=highest)
        window = lax.all_to_all(pieces, "rows", split_axis=0, concat_axis=0, tiled=True).sum(axis=0)
        along = jnp.einsum("lwj,je->lwe", window, table_x, precision=highest)
        return jnp.einsum("lwe,wf->lfe", along, table_y, precision=highest)

    def assemble(block_field, fine):
        padded = padded_block(block_field)
        fine_padded = jnp.pad(fine, ((1, 1), (0, 0), (0, 0)))
        column_place = lax.broadcasted_iota(jnp.int32, padded.shape, 2)
        line_place = lax.broadcasted_iota(jnp.int32, padded.shape, 1)
        outside = (column_place == 0) & (nest_tile == 0) | (column_place == breadth + 1) & (
            nest_tile == nest_tiles - 1
        )
        outside = (
            outside
            | (line_place == 0) & (row_index == 0)
            | (line_place == height + 1) & (row_index == row_count - 1)
        )
        padded = jnp.where(outside & in_nest, fine_padded, padded)
        seam_cells = (column_place == breadth + 1) & (tile_index == parent_tiles - 1)
        return jnp.where(seam_cells, zero_value, padded)

    advect_scale = jnp.where(in_nest, jnp.float32(NEST_ADVECT), jnp.float32(1.0))
    mixing_scale = jnp.where(in_nest, jnp.float32(NEST_MIXING), jnp.float32(PARENT_MIXING))
    fine_first = boundary(air_state, 0)
    change = tendency(
        assemble(air_state, fine_first), wind_east, wind_north, advect_scale, mixing_scale
    )
    nudging_term = jnp.where(in_nest, NUDGING * (fine_first[:, 1:-1, 1:-1] - air_state), zero_value)
    step_one = air_state + change + nudging_term
    fine_second = boundary(step_one, 1)
    change = tendency(
        assemble(step_one, fine_second), wind_east, wind_north, advect_scale, mixing_scale
    )
    nested_two = step_one + change + NUDGING * (fine_second[:, 1:-1, 1:-1] - step_one)
    step_two = jnp.where(in_nest, nested_two, step_one)
    coarse = step_two.reshape(levels, third_y, 3, third_x, 3).mean(axis=(2, 4))
    avg_columns = jnp.arange(third_x, dtype=jnp.int32)
    avg_lines = jnp.arange(third_y, dtype=jnp.int32)
    west_last = nest_west[1]
    south_last = nest_south[1]
    place_x = (
        (west_last + (targets_x - parent_tiles) * third_x)[:, None, None]
        + avg_columns[None, :, None]
        == (first_x + columns)[None, None, :]
    ) & (targets_x >= parent_tiles)[:, None, None]
    place_x = place_x.astype(jnp.float32)
    place_y = (
        (south_last + targets_y * third_y)[:, None, None] + avg_lines[None, :, None]
        == (first_y + lines)[None, None, :]
    ).astype(jnp.float32)
    parent_y = south_last + row_index * third_y + avg_lines
    send_y = (jnp.floor_divide(parent_y, height)[None, :] == targets_y[:, None]) & in_nest
    pieces = jnp.where(send_y[:, None, :, None], coarse[None], zero_value)
    received = lax.all_to_all(pieces, "rows", split_axis=0, concat_axis=0, tiled=True)
    spread = jnp.einsum("slba,sby->lya", received, place_y, precision=highest)
    parent_x = west_last + nest_tile * third_x + avg_columns
    send_x = jnp.floor_divide(parent_x, breadth)[None, :] == targets_x[:, None]
    pieces = jnp.where(send_x[:, None, None, :], spread[None], zero_value)
    received = lax.all_to_all(pieces, "tiles", split_axis=0, concat_axis=0, tiled=True)
    placed = jnp.einsum("slya,sai->lyi", received, place_x, precision=highest)
    global_x = (first_x + columns)[None, None, :]
    global_y = (first_y + lines)[None, :, None]
    covered = (global_x >= west_last) & (global_x < west_last + nest_tiles * third_x)
    covered = covered & (global_y >= south_last) & (global_y < south_last + row_count * third_y)
    covered = covered & jnp.logical_not(in_nest)
    blended = step_two + feedback_weight[:, None, None] * (placed - step_two)
    return jnp.where(covered, blended, step_two)


LANES = 128
FIRST_LANE = 32
LAST_LANE = 96
EAST_LANE = 64
WEIGHTS = 4


def iota(shape, dim):
    return lax.broadcasted_iota(jnp.int32, shape, dim)


def split_level(place, height):
    level = ((place.astype(jnp.float32) + 0.5) * (1.0 / height)).astype(jnp.int32)
    return level, place - level * height


def table(values):
    return values.astype(jnp.float32).astype(jnp.bfloat16)


def parts_of(array):
    high = array.astype(jnp.bfloat16)
    low = (array - high.astype(jnp.float32)).astype(jnp.bfloat16)
    return high, low


def dot(left, right):
    return jnp.dot(left, right, preferred_element_type=jnp.float32)


def from_left(weights, array):
    high, low = parts_of(array)
    return dot(weights, high) + dot(weights, low)


def from_right(array, weights):
    high, low = parts_of(array)
    return dot(high, weights) + dot(low, weights)


def hat(distance):
    return jnp.maximum(0, 3 - jnp.abs(distance - 1))


def place():
    return lax.axis_index("tiles"), lax.axis_index("rows"), lax.axis_index("lev")


def level_table(levels, height):
    shape = (levels, levels * height)
    level, _ = split_level(iota(shape, 1), height)
    return table(iota(shape, 0) == level)


def spread_table(levels, height):
    shape = (levels * height, levels)
    level, _ = split_level(iota(shape, 0), height)
    return table(iota(shape, 1) == level)


def load_line(ref, levels, line):
    rows = pl.ds(line, levels, stride=ref.shape[1] // levels)
    return jnp.concatenate([ref[c, rows, :] for c in range(ref.shape[0])], axis=1)


def store_line(ref, levels, line, value):
    rows = pl.ds(line, levels, stride=ref.shape[1] // levels)
    for c in range(ref.shape[0]):
        ref[c, rows, :] = value[:, c * LANES : (c + 1) * LANES]


def load_level(ref, height, l):
    rows = pl.ds(l * height, height)
    if len(ref.shape) == 2:
        return ref[rows, :]
    return jnp.concatenate([ref[c, rows, :] for c in range(ref.shape[0])], axis=1)


def store_level(ref, height, l, value):
    rows = pl.ds(l * height, height)
    if len(ref.shape) == 2:
        ref[rows, :] = value
    else:
        for c in range(ref.shape[0]):
            ref[c, rows, :] = value[:, c * LANES : (c + 1) * LANES]


def store_slabs(ref, first, wide):
    for i in range(wide.shape[1] // LANES):
        ref[first + i] = wide[:, i * LANES : (i + 1) * LANES]


def join_slabs(ref, first, count):
    return jnp.concatenate([ref[first + i] for i in range(count)], axis=1)


def column_pieces(start, pieces):
    first = (start + 64 * LANES) // LANES - 64
    offset = start - first * LANES
    held = [(c >= 0) & (c < pieces) for c in (first, first + 1)]
    return [jnp.clip(c, 0, pieces - 1) for c in (first, first + 1)], held, offset


def pack_window(ref, field_ref, levels, top, start):
    pieces, size, _ = field_ref.shape
    height = size // levels
    slots = ref.shape[0] - 1
    lane = iota((levels, LANES), 1)
    (left, right), (left_held, right_held), offset = column_pieces(start, pieces)
    before = lax.rem(offset + LANES - 1, LANES)
    (beside, _), (beside_held, _), _ = column_pieces(start - 1, pieces)
    in_left = lane < LANES - offset
    held = jnp.where(in_left, left_held.astype(jnp.float32), right_held.astype(jnp.float32))
    west_held, east_held = beside_held.astype(jnp.float32), right_held.astype(jnp.float32)
    turn = lax.rem(LANES - offset, LANES)
    extra = jnp.zeros((levels, LANES), jnp.float32)
    for slot in range(slots):
        line = top + slot
        there = ((line >= 0) & (line < height)).astype(jnp.float32)
        rows = pl.ds(jnp.clip(line, 0, height - 1), levels, stride=height)
        near, far, west = field_ref[left, rows, :], field_ref[right, rows, :], field_ref[beside, rows, :]
        ref[slot] = jnp.where(in_left, pltpu.roll(near, turn, 1), pltpu.roll(far, turn, 1)) * (held * there)
        west = pltpu.roll(west, lax.rem(LANES + slot - before, LANES), 1) * (west_held * there)
        east = pltpu.roll(far, lax.rem(LANES + EAST_LANE + slot - offset, LANES), 1) * (east_held * there)
        extra = jnp.where(lane == slot, west, jnp.where(lane == EAST_LANE + slot, east, extra))
    ref[slots] = extra


def place_row(ref, levels, line, start, value):
    pieces, size, _ = ref.shape
    height = size // levels
    lane = iota((levels, LANES), 1)
    at, held, offset = column_pieces(start, pieces)
    value = pltpu.roll(value, offset, 1)
    there = (line >= 0) & (line < height)
    rows = pl.ds(jnp.clip(line, 0, height - 1), levels, stride=height)
    for c in range(2):
        mine = (lane >= offset) if c == 0 else (lane < offset)
        ref[at[c], rows, :] = jnp.where(mine & (held[c] & there), value, ref[at[c], rows, :])


def pack_edges(field_ref, levels):
    height = field_ref.shape[1] // levels
    lane = iota((levels, LANES), 1)
    packed = jnp.zeros((levels, LANES), jnp.float32)
    for line in range(height):
        rows = pl.ds(line, levels, stride=height)
        first = field_ref[0, rows, :]
        last = field_ref[field_ref.shape[0] - 1, rows, :]
        packed = jnp.where(lane == FIRST_LANE + line, pltpu.roll(first, FIRST_LANE + line, 1), packed)
        packed = jnp.where(lane == LAST_LANE + line, pltpu.roll(last, LAST_LANE + line + 1, 1), packed)
    return packed


def neighbour_columns(even, odd, parent_tiles, tile):
    is_odd = tile % 2 == 1
    west = jnp.where(is_odd, even, odd)
    east = jnp.where(is_odd, odd, even)
    west = jnp.where(tile == 0, jnp.zeros_like(west), west)
    east = jnp.where(tile >= parent_tiles - 1, jnp.zeros_like(east), east)
    return jnp.where(iota(west.shape, 1) < LAST_LANE, east, west)


def unpack_edges(columns, levels, height):
    wide = from_left(spread_table(levels, height), columns)
    lane = iota(wide.shape, 1)
    _, line = split_level(iota(wide.shape, 0), height)
    west = jnp.sum(jnp.where(lane == line + LAST_LANE, wide, 0.0), axis=1, keepdims=True)
    east = jnp.sum(jnp.where(lane == line + FIRST_LANE, wide, 0.0), axis=1, keepdims=True)
    return jnp.where(lane == 0, west, jnp.where(lane == 1, east, 0.0))


def refine(slabs, extra, height, breadth, row):
    slots, levels = len(slabs), extra.shape[0]
    beside = [pltpu.roll(extra, LANES - s, 1) if s else extra for s in range(slots)]
    window = jnp.concatenate([jnp.concatenate(slabs, axis=0), jnp.concatenate(beside, axis=0)], axis=1)
    shape = (2 * LANES, breadth + LANES)
    slot, cell = iota(shape, 0), iota(shape, 1)
    held = (slot <= LANES) | (slot == LANES + EAST_LANE)
    at = jnp.where(slot < LANES, slot, jnp.where(slot == LANES, -1, LANES))
    cell = jnp.where(cell == breadth, -1, jnp.where(cell == breadth + 1, breadth, cell))
    across = jnp.where(held & (cell <= breadth), hat(cell - 3 * at), 0)
    wide = from_right(window, table(across)) * (1.0 / 9.0)
    shape = (levels * height, slots * levels)
    taken = iota(shape, 1)
    slot = taken // levels
    level, line = split_level(iota(shape, 0), height)
    along = jnp.where(taken - slot * levels == level, hat(line - 3 * (slot - 1)), 0)
    cells = from_left(table(along), wide)
    ring = jnp.where(
        row == 0,
        2.0 * wide[:levels] + wide[levels : 2 * levels],
        2.0 * wide[(slots - 1) * levels :] + wide[(slots - 2) * levels : (slots - 1) * levels],
    )
    return cells, ring[:, :breadth]


def beside_rows(x, north, south):
    height = x.shape[0]
    line = iota(x.shape, 0)
    northern = jnp.where(line == 0, north, pltpu.roll(x, 1, 0))
    southern = jnp.where(line == height - 1, south, pltpu.roll(x, height - 1, 0))
    return northern, southern


def beside_columns(x, west, east):
    breadth = x.shape[1]
    column = iota(x.shape, 1)
    western = jnp.where(column == 0, west, pltpu.roll(x, 1, 1))
    eastern = jnp.where(column == breadth - 1, east, pltpu.roll(x, breadth - 1, 1))
    return western, eastern


def change_of(x, sides, u, v, upper, lower, nest):
    advect_scale = NEST_ADVECT if nest else 1.0
    mixing_scale = NEST_MIXING if nest else PARENT_MIXING
    northern, southern, western, eastern = sides
    advect = u * (eastern - western) + v * (southern - northern)
    horizontal = eastern + western + southern + northern - 4.0 * x
    vertical = upper + lower - 2.0 * x
    return -0.5 * advect_scale * advect + mixing_scale * horizontal + VERTICAL_MIX * vertical


def ghost_weight(speed, before):
    return jnp.where(before, 0.5 * NEST_ADVECT, -0.5 * NEST_ADVECT) * speed + NEST_MIXING


def full_step(out_ref, field_ref, u_ref, v_ref, level_ref, levels, lev, nest, north, south, side, fine):
    height, breadth = level_ref.shape
    zero = jnp.zeros((height, breadth), jnp.float32)

    def block(ref, l):
        return load_level(ref, height, l)

    for l in range(levels):
        x = block(field_ref, l)
        lower = block(field_ref, l - 1) if l else jnp.where(lev == 1, level_ref[...], zero)
        upper = block(field_ref, l + 1) if l < levels - 1 else jnp.where(lev == 0, level_ref[...], zero)
        rows = [0.0 if ref is None else ref[pl.ds(l, 1), :] for ref in (north, south)]
        if side is None:
            columns = (0.0, 0.0)
        else:
            beside = side[pl.ds(l * height, height), :]
            columns = (beside[:, 0:1], beside[:, 1:2])
        sides = beside_rows(x, *rows) + beside_columns(x, *columns)
        fresh = x + change_of(x, sides, block(u_ref, l), block(v_ref, l), upper, lower, nest)
        if nest:
            fresh = fresh - NUDGING * x if fine is None else fresh + NUDGING * (block(fine, l) - x)
        store_level(out_ref, height, l, fresh)


def inner_line(height, row):
    return jnp.where(row == 0, height - 1, 0)


def edge_level(ref, height, lev):
    last = ref.shape[1] // height - 1
    return jnp.where(lev == 0, load_level(ref, height, last), load_level(ref, height, 0))


def ghost_row_weights(ghost, breadth):
    cell, third = iota((breadth, 3 * LANES), 0), iota((breadth, 3 * LANES), 1)
    kind = third // LANES
    offset = cell - 3 * (third - kind * LANES)
    middle = jnp.where(offset == 1, 3, jnp.where((offset == 0) | (offset == 2), 2, 0))
    weight = jnp.where(kind == 1, middle, jnp.where(offset == kind, 1, 0))
    return from_right(ghost, table(weight)) * (1.0 / 27.0)


def ghost_column_weights(first, last, levels, height):
    shape = (levels * height, LANES)
    lane = iota(shape, 1)
    _, line = split_level(iota(shape, 0), height)
    block = lane // 8
    inside = lane - block * 8
    eastern = inside >= 3
    kind = jnp.where(eastern, inside - 3, inside)
    offset = line - 3 * block
    middle = jnp.where(offset == 1, 3, jnp.where((offset == 0) | (offset == 2), 2, 0))
    weight = jnp.where(kind == 1, middle, jnp.where(offset == kind, 1, 0))
    weight = jnp.where((inside < 6) & (block < height // 3), weight, 0).astype(jnp.float32)
    columns = jnp.where(eastern, last, first) * weight
    return from_left(level_table(levels, height), columns) * (1.0 / 27.0)


def pack_kernel(
    levels,
    west_hbm,
    south_hbm,
    weight_hbm,
    air_hbm,
    north_hbm,
    rows_ref,
    air_ref,
    west_ref,
    south_ref,
    weight_ref,
    north_ref,
    sems,
):
    pieces, size, _ = air_ref.shape
    breadth = pieces * LANES
    height = size // levels
    third_y = height // 3
    slots = rows_ref.shape[0] - 1 - pieces
    tile, row, _ = place()
    nest = tile == lax.axis_size("tiles") - 1
    inner = inner_line(height, row)

    def column_copies(source, target, first):
        return [
            pltpu.make_async_copy(source.at[:, pl.ds(c * LANES, LANES)], target.at[c], sems.at[first + c])
            for c in range(pieces)
        ]

    copies = column_copies(air_hbm, air_ref, 0)
    copies.append(pltpu.make_async_copy(west_hbm, west_ref, sems.at[2 * pieces]))
    copies.append(pltpu.make_async_copy(south_hbm, south_ref, sems.at[2 * pieces + 1]))
    copies.append(pltpu.make_async_copy(weight_hbm, weight_ref, sems.at[2 * pieces + 2]))
    speeds = column_copies(north_hbm, north_ref, pieces)
    for copy in copies:
        copy.start()

    @pl.when(nest)
    def _():
        for copy in speeds:
            copy.start()

    for copy in copies:
        copy.wait()
    store_slabs(rows_ref, slots + 1, load_line(air_ref, levels, inner))
    part = rows_ref.at[pl.ds(0, slots + 1)]

    @pl.when(nest)
    def _():
        for copy in speeds:
            copy.wait()
        part[...] = jnp.zeros_like(part)
        store_slabs(rows_ref, WEIGHTS, load_line(north_ref, levels, inner))

    @pl.when(jnp.logical_not(nest))
    def _():
        start = west_ref[0] - tile * breadth
        top = south_ref[0] - 1 - row * height
        pack_window(part, air_ref, levels, top + (1 - row) * third_y, start)


def own_kernel(
    levels, west_ref, south_ref, air_ref, east_ref, north_ref, own_ref, level_ref, speeds_ref, edges_ref
):
    pieces, size, _ = air_ref.shape
    breadth = pieces * LANES
    height = size // levels
    third_y = height // 3
    slots = own_ref.shape[0] - 1
    tile, row, lev = place()
    nest = tile == lax.axis_size("tiles") - 1
    level_ref[...] = edge_level(air_ref, height, lev)

    @pl.when(nest)
    def _():
        inner = inner_line(height, row)
        shape = (2 * levels, size)
        taken = iota(shape, 0)
        level, line = split_level(iota(shape, 1), height)
        wanted = jnp.where(taken < levels, height - 1 - inner, inner)
        picked = table((lax.rem(taken, levels) == level) & (line == wanted))
        speeds = from_left(picked, north_ref[...])
        outer = speeds[:levels]
        store_slabs(speeds_ref, 0, outer)
        store_slabs(speeds_ref, pieces, speeds[levels:])
        own_ref[...] = jnp.zeros_like(own_ref)
        edges_ref[...] = jnp.zeros_like(edges_ref)
        store_slabs(own_ref, 0, ghost_row_weights(ghost_weight(outer, row == 0), breadth))
        first = ghost_weight(east_ref[:, 0:1], True)
        last = ghost_weight(east_ref[:, breadth - 1 : breadth], False)
        own_ref[WEIGHTS - 1] = ghost_column_weights(first, last, levels, height)

    @pl.when(jnp.logical_not(nest))
    def _():
        start = west_ref[0] - tile * breadth
        top = south_ref[0] - 1 - row * height
        pack_window(own_ref, air_ref, levels, top + row * third_y, start)
        edges = pack_edges(air_ref, levels)
        edges_ref[...] = jnp.zeros_like(edges_ref)
        edges_ref[0] = edges
        own_ref[slots] = own_ref[slots] + edges
        speeds_ref[...] = jnp.zeros_like(speeds_ref)


def set_halo(rows_ref, first, northern_ref, southern_ref, row):
    halo = join_slabs(rows_ref, first, rows_ref.shape[0] - first)
    zero = jnp.zeros_like(halo)
    northern_ref[...] = jnp.where(row == 0, zero, halo)
    southern_ref[...] = jnp.where(row == 0, halo, zero)


def parent_step(
    levels, west_ref, south_ref, shared, rows_ref, columns, field_ref, other_ref, side_ref, northern_ref, southern_ref
):
    height = side_ref.shape[0] // levels
    slots = other_ref.shape[0] - 1
    tile, row, lev = place()
    set_halo(rows_ref, slots + 1, northern_ref, southern_ref, row)
    side_ref[...] = unpack_edges(columns, levels, height)
    full_step(field_ref, *shared, levels, lev, False, northern_ref, southern_ref, side_ref, None)
    start = west_ref[1] - tile * field_ref.shape[0] * LANES
    top = south_ref[1] - 1 - row * height
    pack_window(other_ref, field_ref, levels, top + (1 - row) * (height // 3), start)


def early_kernel(
    levels,
    west_ref,
    south_ref,
    air_ref,
    east_ref,
    north_ref,
    rows_ref,
    level_ref,
    one_ref,
    field_ref,
    other_ref,
    side_ref,
    northern_ref,
    southern_ref,
):
    slots = other_ref.shape[0] - 1
    tile_count = lax.axis_size("tiles")
    tile, row, lev = place()
    shared = (air_ref, east_ref, north_ref, level_ref)

    @pl.when(tile == tile_count - 1)
    def _():
        set_halo(rows_ref, slots + 1, northern_ref, southern_ref, row)
        full_step(field_ref, *shared, levels, lev, True, northern_ref, southern_ref, None, None)
        other_ref[...] = jnp.zeros_like(other_ref)

    @pl.when(tile == 0)
    def _():
        columns = neighbour_columns(one_ref[slots], one_ref[slots], tile_count - 1, tile)
        refs = (field_ref, other_ref, side_ref, northern_ref, southern_ref)
        parent_step(levels, west_ref, south_ref, shared, rows_ref, columns, *refs)


def middle_kernel(
    levels,
    west_ref,
    south_ref,
    air_ref,
    east_ref,
    north_ref,
    rows_ref,
    level_ref,
    three_ref,
    one_ref,
    given_field_ref,
    given_other_ref,
    field_ref,
    other_ref,
    side_ref,
    northern_ref,
    southern_ref,
):
    slots = other_ref.shape[0] - 1
    tile_count = lax.axis_size("tiles")
    tile, _, _ = place()
    shared = (air_ref, east_ref, north_ref, level_ref)

    @pl.when((tile > 0) & (tile < tile_count - 1))
    def _():
        columns = neighbour_columns(one_ref[slots], three_ref[0], tile_count - 1, tile)
        refs = (field_ref, other_ref, side_ref, northern_ref, southern_ref)
        parent_step(levels, west_ref, south_ref, shared, rows_ref, columns, *refs)


def first_kernel(
    levels,
    west_ref,
    south_ref,
    early_ref,
    east_ref,
    speeds_ref,
    three_ref,
    two_ref,
    one_ref,
    field_ref,
    edge_ref,
    own_ref,
):
    pieces, size, _ = early_ref.shape
    height, breadth = edge_ref.shape
    slots = one_ref.shape[0] - 1
    tile, row, lev = place()
    nest = tile == lax.axis_size("tiles") - 1

    @pl.when(jnp.logical_not(nest))
    def _():
        edge_ref[...] = jnp.zeros_like(edge_ref)
        start = west_ref[1] - tile * breadth
        top = south_ref[1] - 1 - row * height
        pack_window(own_ref, early_ref, levels, top + row * (height // 3), start)

    @pl.when(nest)
    def _():
        slabs = [one_ref[s] + two_ref[s] + three_ref[s] for s in range(slots + 1)]
        cells, ring = refine(slabs[:slots], slabs[slots], height, breadth, row)
        lane = iota((size, LANES), 1)
        for c in range(pieces):
            piece = slice(c * LANES, (c + 1) * LANES)
            value = early_ref[c] + NUDGING * cells[:, piece]
            if c == 0:
                ghost = ghost_weight(east_ref[:, piece], True) * cells[:, breadth : breadth + 1]
                value = value + jnp.where(lane == 0, ghost, 0.0)
            if c == pieces - 1:
                ghost = ghost_weight(east_ref[:, piece], False) * cells[:, breadth + 1 : breadth + 2]
                value = value + jnp.where(lane == LANES - 1, ghost, 0.0)
            field_ref[c] = value
        outer = height - 1 - inner_line(height, row)
        ghost = ghost_weight(join_slabs(speeds_ref, 0, pieces), row == 0) * ring
        store_line(field_ref, levels, outer, load_line(field_ref, levels, outer) + ghost)
        edge_ref[...] = edge_level(field_ref, height, lev)


def average_kernel(levels, field_ref, east_ref, north_ref, rows_ref, message_ref, part_ref, nothing_ref):
    pieces, size, _ = field_ref.shape
    height, breadth = nothing_ref.shape
    third_y = height // 3
    tile, row, lev = place()

    @pl.when(tile == lax.axis_size("tiles") - 1)
    def _():
        nothing_ref[...] = jnp.zeros_like(nothing_ref)
        full_step(part_ref, field_ref, east_ref, north_ref, nothing_ref, levels, lev, True, None, None, None, None)
        sums = sums_table(breadth)
        shape = (third_y * levels, size)
        taken = iota(shape, 0)
        block = taken // levels
        level, line = split_level(iota(shape, 1), height)
        offset = line - 3 * block
        rows = table((taken - block * levels == level) & (offset >= 0) & (offset <= 2))
        means = from_left(rows, from_right(part_ref[...], sums)) * (1.0 / 9.0)
        for m in range(third_y):
            message_ref[m] = means[m * levels : (m + 1) * levels]
        shared = load_line(field_ref, levels, inner_line(height, row))
        shared = ghost_weight(join_slabs(rows_ref, WEIGHTS, pieces), row == 0) * shared
        message_ref[third_y] = from_right(shared, sums) * (1.0 / 9.0)
        for i in range(third_y + 1, message_ref.shape[0]):
            message_ref[i] = jnp.zeros((levels, LANES), jnp.float32)


def sums_table(breadth):
    offset = iota((breadth, LANES), 0) - 3 * iota((breadth, LANES), 1)
    return table((offset >= 0) & (offset <= 2))


def pack_column(slabs, extra, slot):
    lane = iota(extra.shape, 1)
    packed = jnp.where(slot == -1, extra, pltpu.roll(extra, LANES - EAST_LANE, 1))
    inside = (slot >= 0) & (slot < LANES)
    for s, slab in enumerate(slabs):
        turned = pltpu.roll(slab, lax.rem(s - slot + 64 * LANES, LANES), 1)
        packed = jnp.where((lane == s) & inside, turned, packed)
    return packed


def message_kernel(
    levels, west_ref, level_ref, part_ref, coef_ref, own_ref, other_ref, message_ref, far_ref, side_ref
):
    height, breadth = level_ref.shape
    third_y = height // 3
    tile, row, lev = place()
    nest = tile == lax.axis_size("tiles") - 1

    @pl.when(jnp.logical_not(nest))
    def _():
        message_ref[...] = own_ref[...] + other_ref[...]
        far_ref[pl.ds(0, message_ref.shape[0])] = message_ref[...]
        for i in range(message_ref.shape[0], far_ref.shape[0]):
            far_ref[i] = jnp.zeros((levels, LANES), jnp.float32)
        slots = message_ref.shape[0] - 1
        first = tile * breadth - west_ref[1]
        lane = iota((levels, LANES), 1)
        columns = [
            pack_column([message_ref[s] for s in range(slots)], message_ref[slots], slot)
            for slot in (first, first + breadth - 1)
        ]
        side_ref[...] = jnp.where(lane < EAST_LANE, columns[0], pltpu.roll(columns[1], EAST_LANE, 1))

    @pl.when(nest)
    def _():
        offset = iota((third_y, height), 1) - 3 * iota((third_y, height), 0)
        rows = table((offset >= 0) & (offset <= 2))
        across = from_left(rows, from_right(level_ref[...], sums_table(breadth))) * (VERTICAL_MIX / 9.0)
        at_edge = iota((levels, LANES), 0) == jnp.where(lev == 0, levels - 1, 0)
        for m in range(third_y):
            message_ref[m] = part_ref[m] + jnp.where(at_edge, across[m : m + 1], 0.0)
        for i in range(third_y, message_ref.shape[0]):
            message_ref[i] = part_ref[i]
        far_ref[pl.ds(0, third_y + 1)] = message_ref[pl.ds(0, third_y + 1)]
        far_ref[pl.ds(third_y + 1, WEIGHTS)] = coef_ref[pl.ds(0, WEIGHTS)]
        side_ref[...] = jnp.zeros_like(side_ref)


def blend_kernel(
    levels,
    western,
    west_ref,
    weight_ref,
    field_ref,
    window_ref,
    beside_ref,
    middle_ref,
    other_ref,
    coef_middle_ref,
    coef_near_ref,
    rows_ref,
):
    pieces, size, _ = field_ref.shape
    height = size // levels
    third_y = height // 3
    slots = third_y + 2
    tile_count = lax.axis_size("tiles")
    tile, row, _ = place()
    nest = tile == tile_count - 1

    @pl.when(nest)
    def _():
        store_slabs(rows_ref, 0, load_line(field_ref, levels, inner_line(height, row)))
        for i in range(pieces, rows_ref.shape[0]):
            rows_ref[i] = jnp.zeros((levels, LANES), jnp.float32)

    @pl.when(jnp.logical_not(nest))
    def _():
        paired = (tile == 1) | (tile == (0 if western else 2))

        def mine(i):
            return jnp.where(tile == 1, middle_ref[i], other_ref[i])

        def coefficient(i):
            other = other_ref[third_y + 1 + i] if western else coef_near_ref[i]
            return jnp.where(tile == 1, coef_middle_ref[i], other)

        breadth = pieces * LANES
        partner_east = tile == (0 if western else 1)
        slot = jnp.where(partner_east, (tile + 1) * breadth, tile * breadth - 1) - west_ref[1]
        column = jnp.where(partner_east, beside_ref[...], pltpu.roll(beside_ref[...], LANES - EAST_LANE, 1))
        lane = iota((levels, LANES), 1)

        def whole(s):
            return jnp.where(paired & (lane == slot), column[:, s : s + 1], window_ref[s])

        level = iota((levels, LANES), 0)
        weight = jnp.zeros((levels, LANES), jnp.float32)
        for l in range(levels):
            weight = jnp.where(level == l, weight_ref[l], weight)
        extra = window_ref[slots]
        extra = jnp.where(paired & (slot == -1) & (lane < EAST_LANE), column, extra)
        east_column = pltpu.roll(column, EAST_LANE, 1)
        extra = jnp.where(paired & (slot == LANES) & (lane >= EAST_LANE), east_column, extra)
        at_first, at_last = lane == 0, lane == LANES - 1
        lines = []
        for s in range(slots):
            x = whole(s)
            west = jnp.where(at_first, extra[:, s : s + 1], pltpu.roll(x, 1, 1))
            last = EAST_LANE + s
            east = jnp.where(at_last, extra[:, last : last + 1], pltpu.roll(x, LANES - 1, 1))
            lines.append((west, x, east))
        edges = coefficient(WEIGHTS - 1)
        ghosts = [coefficient(q) for q in range(3)]

        def outward(side, q):
            near = lines[1] if side == 0 else lines[slots - 2]
            far = lines[0] if side == 0 else lines[slots - 1]
            return (2.0 / 3.0) * far[q] + (1.0 / 3.0) * near[q]

        def sideward(s):
            west, x, east = lines[s]
            return (2.0 / 3.0) * jnp.where(at_first, west, east) + (1.0 / 3.0) * x

        sidewards = [sideward(s) for s in range(slots)]
        columns = [w + 7.0 * x + e for w, x, e in lines]
        for m in range(third_y):
            x = lines[m + 1][1]
            value = mine(m) + (NUDGING / 81.0) * (columns[m] + 7.0 * columns[m + 1] + columns[m + 2])
            for q in range(3):
                lane_of = 8 * m + q
                first, last = edges[:, lane_of : lane_of + 1], edges[:, lane_of + 3 : lane_of + 4]
                scale = jnp.where(at_first, first, jnp.where(at_last, last, 0.0))
                value = value + scale * sidewards[m + q]
            for side, at in ((0, 0), (1, third_y - 1)):
                if m == at:
                    for q in range(3):
                        value = value + jnp.where(row == side, ghosts[q], 0.0) * outward(side, q)
            rows_ref[m] = x + weight * (value - x)
        rows_ref[third_y] = weight * mine(third_y)


def later_kernel(
    levels,
    west_ref,
    south_ref,
    field_ref,
    east_ref,
    north_ref,
    level_ref,
    middle_ref,
    other_ref,
    parent_ref,
    blend_ref,
    out_ref,
    fine_ref,
    side_ref,
    northern_ref,
    southern_ref,
):
    height, breadth = level_ref.shape
    third_y = height // 3
    slots = third_y + 2
    tile, row, lev = place()
    nest = tile == lax.axis_size("tiles") - 1

    @pl.when(nest)
    def _():
        slabs = [middle_ref[s] + other_ref[s] for s in range(slots + 1)]
        cells, ring = refine(slabs[:slots], slabs[slots], height, breadth, row)
        fine_ref[...] = cells[:, :breadth]
        side_ref[...] = cells[:, breadth:]
        zero = jnp.zeros_like(ring)
        northern_ref[...] = jnp.where(row == 0, ring, zero)
        southern_ref[...] = jnp.where(row == 0, zero, ring)
        full_step(
            out_ref,
            field_ref,
            east_ref,
            north_ref,
            level_ref,
            levels,
            lev,
            True,
            northern_ref,
            southern_ref,
            side_ref,
            fine_ref,
        )

    @pl.when(jnp.logical_not(nest))
    def _():
        out_ref[...] = parent_ref[...]
        start = west_ref[1] - tile * breadth
        top = south_ref[1] + row * third_y - row * height
        for m in range(third_y):
            place_row(out_ref, levels, top + m, start, blend_ref[m])


def last_kernel(
    levels, west_ref, south_ref, given_ref, speeds_ref, blend_ref, rows_ref, out_hbm, out_ref, sems
):
    pieces, size, _ = out_ref.shape
    breadth = pieces * LANES
    height = size // levels
    third_y = height // 3
    tile, row, _ = place()
    nest = tile == lax.axis_size("tiles") - 1

    @pl.when(nest)
    def _():
        inner = inner_line(height, row)
        halo = ghost_weight(join_slabs(speeds_ref, pieces, pieces), row == 1) * join_slabs(rows_ref, 0, pieces)
        store_line(out_ref, levels, inner, load_line(out_ref, levels, inner) + halo)

    @pl.when(jnp.logical_not(nest))
    def _():
        start = west_ref[1] - tile * breadth
        top = south_ref[1] + (1 - row) * third_y - row * height
        for m in range(third_y):
            value = rows_ref[m]
            if m == 0:
                value = value + jnp.where(row == 0, blend_ref[third_y], 0.0)
            if m == third_y - 1:
                value = value + jnp.where(row == 1, blend_ref[third_y], 0.0)
            place_row(out_ref, levels, top + m, start, value)
        near = jnp.where(row == 0, third_y - 1, 0)
        line = south_ref[1] + row * third_y - row * height + near
        place_row(out_ref, levels, line, start, blend_ref[near] + rows_ref[third_y])

    copies = [
        pltpu.make_async_copy(out_ref.at[c], out_hbm.at[:, pl.ds(c * LANES, LANES)], sems.at[c])
        for c in range(pieces)
    ]
    for copy in copies:
        copy.start()
    for copy in copies:
        copy.wait()


def call(kernel, outs, inputs, places, scratch=(), flops=0, aliases=()):
    spaces = {"s": pltpu.SMEM, "v": pltpu.VMEM, "h": pltpu.HBM}
    outs = [pltpu.VMEM(out, jnp.float32) if isinstance(out, tuple) else out for out in outs]
    moved = sum(4 * math.prod(out.shape) for out in outs) + sum(array.nbytes for array in inputs)
    inputs = [
        array if p == "v" else pltpu.with_memory_space_constraint(array, spaces[p])
        for array, p in zip(inputs, places)
    ]
    return pl.pallas_call(
        kernel,
        out_shape=outs,
        in_specs=[pl.BlockSpec(memory_space=spaces[p]) for p in places],
        out_specs=[pl.BlockSpec(memory_space=out.memory_space) for out in outs],
        scratch_shapes=[pltpu.VMEM(s, jnp.float32) if isinstance(s, tuple) else s for s in scratch],
        input_output_aliases=dict(aliases),
        compiler_params=pltpu.CompilerParams(vmem_limit_bytes=32 * 1024 * 1024),
        cost_estimate=pl.CostEstimate(flops=flops, bytes_accessed=moved, transcendentals=0),
    )(*inputs)


def per_device_paired(air_state, wind_east, wind_north, feedback_weight, nest_west, nest_south):
    levels, height, breadth = air_state.shape
    third_y = height // 3
    pieces = breadth // LANES
    slots = third_y + 2
    tile_count = lax.axis_size("tiles")
    size = levels * height
    flat = (size, breadth)
    chunked = (pieces, size, LANES)
    air, east, north = (array.reshape(flat) for array in (air_state, wind_east, wind_north))
    swap = [(0, 1), (1, 0)]

    def slabs(count):
        return (count, levels, LANES)

    def kernel(body):
        return functools.partial(body, levels)

    rows, air_pieces, west, south, weight = call(
        kernel(pack_kernel),
        [
            slabs(slots + 1 + pieces),
            chunked,
            pltpu.SMEM((2,), jnp.int32),
            pltpu.SMEM((2,), jnp.int32),
            pltpu.SMEM((levels,), jnp.float32),
        ],
        [nest_west, nest_south, feedback_weight, air, north],
        "hhhhh",
        [chunked, pltpu.SemaphoreType.DMA((2 * pieces + 3,))],
    )
    own, level, speeds, edges = call(
        kernel(own_kernel),
        [slabs(slots + 1), (height, breadth), slabs(2 * pieces), slabs(slots + 2)],
        [west, south, air_pieces, east, north],
        "ssvvv",
        flops=30 * size * breadth,
    )
    rows = lax.ppermute(rows, "rows", swap)
    level = lax.ppermute(level, "lev", swap)
    where = [(t, r, l) for t in range(tile_count) for r in range(2) for l in range(2)]
    at = {position: i for i, position in enumerate(where)}

    def over_tiles(message, step, *without):
        pairs = []
        for t, r, l in where:
            idle = t in without or (t ^ step) in without
            pairs.append((at[t, r, l], at[(t, r, 1 - l) if idle else (t ^ step, r, l)]))
        return lax.ppermute(message, ("tiles", "rows", "lev"), pairs)

    halo = over_tiles(edges, 3, 0)
    eastern = nest_west[1] > breadth
    rows, eastern = lax.optimization_barrier((rows, eastern))
    window = own + rows[: slots + 1]
    own_0 = own
    around = [(t, (t - 1) % tile_count) for t in range(tile_count)]
    starting = [
        over_tiles(window, 1),
        over_tiles(window, 2, 0),
        lax.ppermute(window, "tiles", around),
    ]
    sides = [(size, LANES), (levels, breadth), (levels, breadth)]
    early, other = call(
        kernel(early_kernel),
        [chunked, slabs(slots + 1)],
        [west, south, air, east, north, rows, level, starting[0]],
        "ssvvvvvv",
        sides,
        flops=30 * size * breadth,
    )
    early, other = call(
        kernel(middle_kernel),
        [chunked, slabs(slots + 1)],
        [west, south, air, east, north, rows, level, halo, starting[0], early, other],
        "ssvvvvvvvvv",
        sides,
        flops=30 * size * breadth,
        aliases=[(9, 0), (10, 1)],
    )
    other = lax.ppermute(other, "rows", swap)
    first, edge, own = call(
        kernel(first_kernel),
        [chunked, (height, breadth), slabs(slots + 1)],
        [west, south, early, east, speeds, *starting[::-1]],
        "ssvvvvvv",
        flops=10 * size * breadth,
    )
    level = lax.ppermute(edge, "lev", swap)
    (part,) = call(
        kernel(average_kernel),
        [slabs(slots + 1)],
        [first, east, north, rows],
        "vvvv",
        [flat, (height, breadth)],
        flops=30 * size * breadth,
    )
    message, far_message, side_message = call(
        kernel(message_kernel),
        [slabs(slots + 1), slabs(third_y + 1 + WEIGHTS), (levels, LANES)],
        [west, level, part, own_0, own, other],
        "svvvvv",
    )
    def finish(western, arrays):
        west, south, weight, first, east, north, level, message, far_message, side_message, early, speeds, coefs = arrays
        if western:
            other, beside = over_tiles(far_message, 3, 1), over_tiles(side_message, 1, 3)
        else:
            other, beside = over_tiles(message, 1, 0), over_tiles(side_message, 3, 0)
        middle = over_tiles(message, 2, 0)
        (blend,) = call(
            functools.partial(blend_kernel, levels, western),
            [slabs(third_y + 1)],
            [west, weight, first, message, beside, middle, other, *coefs],
            "ss" + "v" * 7,
        )
        rows = lax.ppermute(blend, "rows", swap)
        (later,) = call(
            kernel(later_kernel),
            [chunked],
            [west, south, first, east, north, level, middle, other, early, blend],
            "ss" + "v" * 8,
            [flat, *sides],
            flops=30 * size * breadth,
        )
        out, _ = call(
            kernel(last_kernel),
            [pltpu.HBM(flat, jnp.float32), chunked],
            [west, south, later, speeds, blend, rows],
            "ssvvvv",
            [pltpu.SemaphoreType.DMA((pieces,))],
            aliases=[(2, 1)],
        )
        return out

    arrays = (west, south, weight, first, east, north, level, message, far_message, side_message, early, speeds)
    arrays += ((starting[1], starting[0]),)
    out = lax.cond(
        eastern,
        functools.partial(finish, False),
        functools.partial(finish, True),
        arrays,
    )
    return out.reshape(air_state.shape)


def solution(mesh):
    in_specs = (
        P(("members", "lev"), "rows", "tiles"),
        P(("members", "lev"), "rows", "tiles"),
        P(("members", "lev"), "rows", "tiles"),
        P("lev"),
        P("members"),
        P("members"),
    )
    out_specs = P(("members", "lev"), "rows", "tiles")
    paired = mesh.shape["tiles"] == 4 and mesh.shape["rows"] == 2 and mesh.shape["lev"] == 2
    return jax.shard_map(
        per_device_paired if paired else per_device, mesh=mesh, in_specs=in_specs, out_specs=out_specs, check_vma=False
    )
```

```python
import functools
import math

import jax
import jax.numpy as jnp
import numpy as np
from jax import lax
from jax.experimental import pallas as pl
from jax.experimental.pallas import tpu as pltpu
from jax.sharding import PartitionSpec as P

VERTICAL_MIX = 0.1
PARENT_MIXING = 0.04
NEST_MIXING = 0.18
NEST_ADVECT = 1.5
NUDGING = 0.2


def padded_2(array, sides, width):
    for axis, dim in sides:
        size, length = (lax.axis_size(axis), array.shape[dim])
        up = [(i, (i + 1) % size) for i in range(size - 1)]
        down = [(j, i) for i, j in up]
        last = lax.slice_in_dim(array, length - width, length, axis=dim)
        first = lax.slice_in_dim(array, 0, width, axis=dim)
        before = lax.ppermute(last, axis, up)
        after = lax.ppermute(first, axis, down)
        array = jnp.concatenate([before, array, after], axis=dim)
    return array


def interp_table(cells):
    extended = jnp.arange(cells + 2, dtype=jnp.int32) - 1
    coarse = jnp.floor_divide(extended, 3)
    offset = extended - 3 * coarse
    fraction = jnp.abs(offset - 1).astype(jnp.float32) / 3.0
    nearest = coarse + 1
    beside = nearest + (offset - 1)
    slots = jnp.arange(cells // 3 + 2, dtype=jnp.int32)[:, None]
    first_part = jnp.where(
        slots == nearest[None, :], 1.0 - fraction[None, :], jnp.zeros((), jnp.float32)
    )
    second_part = jnp.where(slots == beside[None, :], fraction[None, :], jnp.zeros((), jnp.float32))
    return first_part + second_part


def tendency(padded, speed_east, speed_north, advect_scale, mixing_scale):
    centre = padded[1:-1, 1:-1, 1:-1]
    eastern = padded[1:-1, 1:-1, 2:]
    western = padded[1:-1, 1:-1, :-2]
    southern = padded[1:-1, 2:, 1:-1]
    northern = padded[1:-1, :-2, 1:-1]
    upper = padded[2:, 1:-1, 1:-1]
    lower = padded[:-2, 1:-1, 1:-1]
    advect = speed_east * (eastern - western) + speed_north * (southern - northern)
    horizontal = eastern + western + southern + northern - 4.0 * centre
    vertical = upper + lower - 2.0 * centre
    return -0.5 * advect_scale * advect + mixing_scale * horizontal + VERTICAL_MIX * vertical


def padded_block(block_field):
    return padded_2(block_field, (("tiles", 2), ("rows", 1), ("lev", 0)), 1)


def per_device(air_state, wind_east, wind_north, feedback_weight, nest_west, nest_south):
    levels, height, breadth = air_state.shape
    tile_count = lax.axis_size("tiles")
    row_count = lax.axis_size("rows")
    tile_index = lax.axis_index("tiles")
    row_index = lax.axis_index("rows")
    parent_tiles = 3 * tile_count // 4
    nest_tiles = tile_count - parent_tiles
    in_nest = tile_index >= parent_tiles
    nest_tile = tile_index - parent_tiles
    cross_x = breadth // 3 + 2
    cross_y = height // 3 + 2
    third_x = breadth // 3
    third_y = height // 3
    first_x = tile_index * breadth
    first_y = row_index * height
    columns = jnp.arange(breadth, dtype=jnp.int32)
    lines = jnp.arange(height, dtype=jnp.int32)
    targets_x = jnp.arange(tile_count, dtype=jnp.int32)
    targets_y = jnp.arange(row_count, dtype=jnp.int32)
    highest = lax.Precision.HIGHEST
    table_x = interp_table(breadth)
    table_y = interp_table(height)
    zero_value = jnp.zeros((), jnp.float32)

    def boundary(source, substep):
        anchor_x = nest_west[substep] + (targets_x - parent_tiles) * third_x - 1
        slot_x = jnp.arange(cross_x, dtype=jnp.int32)
        pick_x = (
            (first_x + columns)[None, :, None] == anchor_x[:, None, None] + slot_x[None, None, :]
        ) & (targets_x >= parent_tiles)[:, None, None]
        pick_x = pick_x.astype(jnp.float32)
        anchor_y = nest_south[substep] + targets_y * third_y - 1
        slot_y = jnp.arange(cross_y, dtype=jnp.int32)
        pick_y = (
            (first_y + lines)[None, :, None] == anchor_y[:, None, None] + slot_y[None, None, :]
        ).astype(jnp.float32)
        pieces = jnp.einsum("lyi,tij->tlyj", source, pick_x, precision=highest)
        merged = lax.all_to_all(pieces, "tiles", split_axis=0, concat_axis=0, tiled=True).sum(
            axis=0
        )
        pieces = jnp.einsum("lyj,ryw->rlwj", merged, pick_y, precision=highest)
        window = lax.all_to_all(pieces, "rows", split_axis=0, concat_axis=0, tiled=True).sum(axis=0)
        along = jnp.einsum("lwj,je->lwe", window, table_x, precision=highest)
        return jnp.einsum("lwe,wf->lfe", along, table_y, precision=highest)

    def assemble(block_field, fine):
        padded = padded_block(block_field)
        fine_padded = jnp.pad(fine, ((1, 1), (0, 0), (0, 0)))
        column_place = lax.broadcasted_iota(jnp.int32, padded.shape, 2)
        line_place = lax.broadcasted_iota(jnp.int32, padded.shape, 1)
        outside = (column_place == 0) & (nest_tile == 0) | (column_place == breadth + 1) & (
            nest_tile == nest_tiles - 1
        )
        outside = (
            outside
            | (line_place == 0) & (row_index == 0)
            | (line_place == height + 1) & (row_index == row_count - 1)
        )
        padded = jnp.where(outside & in_nest, fine_padded, padded)
        seam_cells = (column_place == breadth + 1) & (tile_index == parent_tiles - 1)
        return jnp.where(seam_cells, zero_value, padded)

    advect_scale = jnp.where(in_nest, jnp.float32(NEST_ADVECT), jnp.float32(1.0))
    mixing_scale = jnp.where(in_nest, jnp.float32(NEST_MIXING), jnp.float32(PARENT_MIXING))
    fine_first = boundary(air_state, 0)
    change = tendency(
        assemble(air_state, fine_first), wind_east, wind_north, advect_scale, mixing_scale
    )
    nudging_term = jnp.where(in_nest, NUDGING * (fine_first[:, 1:-1, 1:-1] - air_state), zero_value)
    step_one = air_state + change + nudging_term
    fine_second = boundary(step_one, 1)
    change = tendency(
        assemble(step_one, fine_second), wind_east, wind_north, advect_scale, mixing_scale
    )
    nested_two = step_one + change + NUDGING * (fine_second[:, 1:-1, 1:-1] - step_one)
    step_two = jnp.where(in_nest, nested_two, step_one)
    coarse = step_two.reshape(levels, third_y, 3, third_x, 3).mean(axis=(2, 4))
    avg_columns = jnp.arange(third_x, dtype=jnp.int32)
    avg_lines = jnp.arange(third_y, dtype=jnp.int32)
    west_last = nest_west[1]
    south_last = nest_south[1]
    place_x = (
        (west_last + (targets_x - parent_tiles) * third_x)[:, None, None]
        + avg_columns[None, :, None]
        == (first_x + columns)[None, None, :]
    ) & (targets_x >= parent_tiles)[:, None, None]
    place_x = place_x.astype(jnp.float32)
    place_y = (
        (south_last + targets_y * third_y)[:, None, None] + avg_lines[None, :, None]
        == (first_y + lines)[None, None, :]
    ).astype(jnp.float32)
    parent_y = south_last + row_index * third_y + avg_lines
    send_y = (jnp.floor_divide(parent_y, height)[None, :] == targets_y[:, None]) & in_nest
    pieces = jnp.where(send_y[:, None, :, None], coarse[None], zero_value)
    received = lax.all_to_all(pieces, "rows", split_axis=0, concat_axis=0, tiled=True)
    spread = jnp.einsum("slba,sby->lya", received, place_y, precision=highest)
    parent_x = west_last + nest_tile * third_x + avg_columns
    send_x = jnp.floor_divide(parent_x, breadth)[None, :] == targets_x[:, None]
    pieces = jnp.where(send_x[:, None, None, :], spread[None], zero_value)
    received = lax.all_to_all(pieces, "tiles", split_axis=0, concat_axis=0, tiled=True)
    placed = jnp.einsum("slya,sai->lyi", received, place_x, precision=highest)
    global_x = (first_x + columns)[None, None, :]
    global_y = (first_y + lines)[None, :, None]
    covered = (global_x >= west_last) & (global_x < west_last + nest_tiles * third_x)
    covered = covered & (global_y >= south_last) & (global_y < south_last + row_count * third_y)
    covered = covered & jnp.logical_not(in_nest)
    blended = step_two + feedback_weight[:, None, None] * (placed - step_two)
    return jnp.where(covered, blended, step_two)


LANES = 128
FIRST_LANE = 32
LAST_LANE = 96
EAST_LANE = 64
WEIGHTS = 4


def iota(shape, dim):
    return lax.broadcasted_iota(jnp.int32, shape, dim)


def split_level(place, height):
    level = ((place.astype(jnp.float32) + 0.5) * (1.0 / height)).astype(jnp.int32)
    return level, place - level * height


def table(values):
    return values.astype(jnp.float32).astype(jnp.bfloat16)


def parts_of(array):
    high = array.astype(jnp.bfloat16)
    low = (array - high.astype(jnp.float32)).astype(jnp.bfloat16)
    return high, low


def dot(left, right):
    return jnp.dot(left, right, preferred_element_type=jnp.float32)


def from_left(weights, array):
    high, low = parts_of(array)
    return dot(weights, high) + dot(weights, low)


def from_right(array, weights):
    high, low = parts_of(array)
    return dot(high, weights) + dot(low, weights)


def hat(distance):
    return jnp.maximum(0, 3 - jnp.abs(distance - 1))


def place():
    return lax.axis_index("tiles"), lax.axis_index("rows"), lax.axis_index("lev")


def level_table(levels, height):
    shape = (levels, levels * height)
    level, _ = split_level(iota(shape, 1), height)
    return table(iota(shape, 0) == level)


def spread_table(levels, height):
    shape = (levels * height, levels)
    level, _ = split_level(iota(shape, 0), height)
    return table(iota(shape, 1) == level)


def load_line(ref, levels, line):
    rows = pl.ds(line, levels, stride=ref.shape[1] // levels)
    return jnp.concatenate([ref[c, rows, :] for c in range(ref.shape[0])], axis=1)


def store_line(ref, levels, line, value):
    rows = pl.ds(line, levels, stride=ref.shape[1] // levels)
    for c in range(ref.shape[0]):
        ref[c, rows, :] = value[:, c * LANES : (c + 1) * LANES]


def load_level(ref, height, l):
    rows = pl.ds(l * height, height)
    if len(ref.shape) == 2:
        return ref[rows, :]
    return jnp.concatenate([ref[c, rows, :] for c in range(ref.shape[0])], axis=1)


def store_level(ref, height, l, value):
    rows = pl.ds(l * height, height)
    if len(ref.shape) == 2:
        ref[rows, :] = value
    else:
        for c in range(ref.shape[0]):
            ref[c, rows, :] = value[:, c * LANES : (c + 1) * LANES]


def store_slabs(ref, first, wide):
    for i in range(wide.shape[1] // LANES):
        ref[first + i] = wide[:, i * LANES : (i + 1) * LANES]


def join_slabs(ref, first, count):
    return jnp.concatenate([ref[first + i] for i in range(count)], axis=1)


def column_pieces(start, pieces):
    first = (start + 64 * LANES) // LANES - 64
    offset = start - first * LANES
    held = [(c >= 0) & (c < pieces) for c in (first, first + 1)]
    return [jnp.clip(c, 0, pieces - 1) for c in (first, first + 1)], held, offset


def pack_window(ref, field_ref, levels, top, start):
    pieces, size, _ = field_ref.shape
    height = size // levels
    slots = ref.shape[0] - 1
    lane = iota((levels, LANES), 1)
    (left, right), (left_held, right_held), offset = column_pieces(start, pieces)
    before = lax.rem(offset + LANES - 1, LANES)
    (beside, _), (beside_held, _), _ = column_pieces(start - 1, pieces)
    in_left = lane < LANES - offset
    held = jnp.where(in_left, left_held.astype(jnp.float32), right_held.astype(jnp.float32))
    west_held, east_held = beside_held.astype(jnp.float32), right_held.astype(jnp.float32)
    turn = lax.rem(LANES - offset, LANES)
    extra = jnp.zeros((levels, LANES), jnp.float32)
    for slot in range(slots):
        line = top + slot
        there = ((line >= 0) & (line < height)).astype(jnp.float32)
        rows = pl.ds(jnp.clip(line, 0, height - 1), levels, stride=height)
        near, far, west = field_ref[left, rows, :], field_ref[right, rows, :], field_ref[beside, rows, :]
        ref[slot] = jnp.where(in_left, pltpu.roll(near, turn, 1), pltpu.roll(far, turn, 1)) * (held * there)
        west = pltpu.roll(west, lax.rem(LANES + slot - before, LANES), 1) * (west_held * there)
        east = pltpu.roll(far, lax.rem(LANES + EAST_LANE + slot - offset, LANES), 1) * (east_held * there)
        extra = jnp.where(lane == slot, west, jnp.where(lane == EAST_LANE + slot, east, extra))
    ref[slots] = extra


def place_row(ref, levels, line, start, value):
    pieces, size, _ = ref.shape
    height = size // levels
    lane = iota((levels, LANES), 1)
    at, held, offset = column_pieces(start, pieces)
    value = pltpu.roll(value, offset, 1)
    there = (line >= 0) & (line < height)
    rows = pl.ds(jnp.clip(line, 0, height - 1), levels, stride=height)
    for c in range(2):
        mine = (lane >= offset) if c == 0 else (lane < offset)
        ref[at[c], rows, :] = jnp.where(mine & (held[c] & there), value, ref[at[c], rows, :])


def pack_edges(field_ref, levels):
    height = field_ref.shape[1] // levels
    lane = iota((levels, LANES), 1)
    packed = jnp.zeros((levels, LANES), jnp.float32)
    for line in range(height):
        rows = pl.ds(line, levels, stride=height)
        first = field_ref[0, rows, :]
        last = field_ref[field_ref.shape[0] - 1, rows, :]
        packed = jnp.where(lane == FIRST_LANE + line, pltpu.roll(first, FIRST_LANE + line, 1), packed)
        packed = jnp.where(lane == LAST_LANE + line, pltpu.roll(last, LAST_LANE + line + 1, 1), packed)
    return packed


def neighbour_columns(even, odd, parent_tiles, tile):
    is_odd = tile % 2 == 1
    west = jnp.where(is_odd, even, odd)
    east = jnp.where(is_odd, odd, even)
    west = jnp.where(tile == 0, jnp.zeros_like(west), west)
    east = jnp.where(tile >= parent_tiles - 1, jnp.zeros_like(east), east)
    return jnp.where(iota(west.shape, 1) < LAST_LANE, east, west)


def unpack_edges(columns, levels, height):
    wide = from_left(spread_table(levels, height), columns)
    lane = iota(wide.shape, 1)
    _, line = split_level(iota(wide.shape, 0), height)
    west = jnp.sum(jnp.where(lane == line + LAST_LANE, wide, 0.0), axis=1, keepdims=True)
    east = jnp.sum(jnp.where(lane == line + FIRST_LANE, wide, 0.0), axis=1, keepdims=True)
    return jnp.where(lane == 0, west, jnp.where(lane == 1, east, 0.0))


def refine(slabs, extra, height, breadth, row):
    slots, levels = len(slabs), extra.shape[0]
    beside = [pltpu.roll(extra, LANES - s, 1) if s else extra for s in range(slots)]
    window = jnp.concatenate([jnp.concatenate(slabs, axis=0), jnp.concatenate(beside, axis=0)], axis=1)
    shape = (2 * LANES, breadth + LANES)
    slot, cell = iota(shape, 0), iota(shape, 1)
    held = (slot <= LANES) | (slot == LANES + EAST_LANE)
    at = jnp.where(slot < LANES, slot, jnp.where(slot == LANES, -1, LANES))
    cell = jnp.where(cell == breadth, -1, jnp.where(cell == breadth + 1, breadth, cell))
    across = jnp.where(held & (cell <= breadth), hat(cell - 3 * at), 0)
    wide = from_right(window, table(across)) * (1.0 / 9.0)
    shape = (levels * height, slots * levels)
    taken = iota(shape, 1)
    slot = taken // levels
    level, line = split_level(iota(shape, 0), height)
    along = jnp.where(taken - slot * levels == level, hat(line - 3 * (slot - 1)), 0)
    cells = from_left(table(along), wide)
    ring = jnp.where(
        row == 0,
        2.0 * wide[:levels] + wide[levels : 2 * levels],
        2.0 * wide[(slots - 1) * levels :] + wide[(slots - 2) * levels : (slots - 1) * levels],
    )
    return cells, ring[:, :breadth]


def beside_rows(x, north, south):
    height = x.shape[0]
    line = iota(x.shape, 0)
    northern = jnp.where(line == 0, north, pltpu.roll(x, 1, 0))
    southern = jnp.where(line == height - 1, south, pltpu.roll(x, height - 1, 0))
    return northern, southern


def beside_columns(x, west, east):
    breadth = x.shape[1]
    column = iota(x.shape, 1)
    western = jnp.where(column == 0, west, pltpu.roll(x, 1, 1))
    eastern = jnp.where(column == breadth - 1, east, pltpu.roll(x, breadth - 1, 1))
    return western, eastern


def change_of(x, sides, u, v, upper, lower, nest):
    advect_scale = NEST_ADVECT if nest else 1.0
    mixing_scale = NEST_MIXING if nest else PARENT_MIXING
    northern, southern, western, eastern = sides
    advect = u * (eastern - western) + v * (southern - northern)
    horizontal = eastern + western + southern + northern - 4.0 * x
    vertical = upper + lower - 2.0 * x
    return -0.5 * advect_scale * advect + mixing_scale * horizontal + VERTICAL_MIX * vertical


def ghost_weight(speed, before):
    return jnp.where(before, 0.5 * NEST_ADVECT, -0.5 * NEST_ADVECT) * speed + NEST_MIXING


def full_step(out_ref, field_ref, u_ref, v_ref, level_ref, levels, lev, nest, north, south, side, fine):
    height, breadth = level_ref.shape
    zero = jnp.zeros((height, breadth), jnp.float32)

    def block(ref, l):
        return load_level(ref, height, l)

    for l in range(levels):
        x = block(field_ref, l)
        lower = block(field_ref, l - 1) if l else jnp.where(lev == 1, level_ref[...], zero)
        upper = block(field_ref, l + 1) if l < levels - 1 else jnp.where(lev == 0, level_ref[...], zero)
        rows = [0.0 if ref is None else ref[pl.ds(l, 1), :] for ref in (north, south)]
        if side is None:
            columns = (0.0, 0.0)
        else:
            beside = side[pl.ds(l * height, height), :]
            columns = (beside[:, 0:1], beside[:, 1:2])
        sides = beside_rows(x, *rows) + beside_columns(x, *columns)
        fresh = x + change_of(x, sides, block(u_ref, l), block(v_ref, l), upper, lower, nest)
        if nest:
            fresh = fresh - NUDGING * x if fine is None else fresh + NUDGING * (block(fine, l) - x)
        store_level(out_ref, height, l, fresh)


def inner_line(height, row):
    return jnp.where(row == 0, height - 1, 0)


def edge_level(ref, height, lev):
    last = ref.shape[1] // height - 1
    return jnp.where(lev == 0, load_level(ref, height, last), load_level(ref, height, 0))


def ghost_row_weights(ghost, breadth):
    cell, third = iota((breadth, 3 * LANES), 0), iota((breadth, 3 * LANES), 1)
    kind = third // LANES
    offset = cell - 3 * (third - kind * LANES)
    middle = jnp.where(offset == 1, 3, jnp.where((offset == 0) | (offset == 2), 2, 0))
    weight = jnp.where(kind == 1, middle, jnp.where(offset == kind, 1, 0))
    return from_right(ghost, table(weight)) * (1.0 / 27.0)


def ghost_column_weights(first, last, levels, height):
    shape = (levels * height, LANES)
    lane = iota(shape, 1)
    _, line = split_level(iota(shape, 0), height)
    block = lane // 8
    inside = lane - block * 8
    eastern = inside >= 3
    kind = jnp.where(eastern, inside - 3, inside)
    offset = line - 3 * block
    middle = jnp.where(offset == 1, 3, jnp.where((offset == 0) | (offset == 2), 2, 0))
    weight = jnp.where(kind == 1, middle, jnp.where(offset == kind, 1, 0))
    weight = jnp.where((inside < 6) & (block < height // 3), weight, 0).astype(jnp.float32)
    columns = jnp.where(eastern, last, first) * weight
    return from_left(level_table(levels, height), columns) * (1.0 / 27.0)


def pack_kernel(
    levels,
    west_hbm,
    south_hbm,
    weight_hbm,
    air_hbm,
    north_hbm,
    rows_ref,
    air_ref,
    west_ref,
    south_ref,
    weight_ref,
    north_ref,
    sems,
):
    pieces, size, _ = air_ref.shape
    breadth = pieces * LANES
    height = size // levels
    third_y = height // 3
    slots = rows_ref.shape[0] - 1 - pieces
    tile, row, _ = place()
    nest = tile == lax.axis_size("tiles") - 1
    inner = inner_line(height, row)

    def column_copies(source, target, first):
        return [
            pltpu.make_async_copy(source.at[:, pl.ds(c * LANES, LANES)], target.at[c], sems.at[first + c])
            for c in range(pieces)
        ]

    copies = column_copies(air_hbm, air_ref, 0)
    copies.append(pltpu.make_async_copy(west_hbm, west_ref, sems.at[2 * pieces]))
    copies.append(pltpu.make_async_copy(south_hbm, south_ref, sems.at[2 * pieces + 1]))
    copies.append(pltpu.make_async_copy(weight_hbm, weight_ref, sems.at[2 * pieces + 2]))
    speeds = column_copies(north_hbm, north_ref, pieces)
    for copy in copies:
        copy.start()

    @pl.when(nest)
    def _():
        for copy in speeds:
            copy.start()

    for copy in copies:
        copy.wait()
    store_slabs(rows_ref, slots + 1, load_line(air_ref, levels, inner))
    part = rows_ref.at[pl.ds(0, slots + 1)]

    @pl.when(nest)
    def _():
        for copy in speeds:
            copy.wait()
        part[...] = jnp.zeros_like(part)
        store_slabs(rows_ref, WEIGHTS, load_line(north_ref, levels, inner))

    @pl.when(jnp.logical_not(nest))
    def _():
        start = west_ref[0] - tile * breadth
        top = south_ref[0] - 1 - row * height
        pack_window(part, air_ref, levels, top + (1 - row) * third_y, start)


def own_kernel(
    levels, west_ref, south_ref, air_ref, east_ref, north_ref, own_ref, level_ref, speeds_ref, edges_ref
):
    pieces, size, _ = air_ref.shape
    breadth = pieces * LANES
    height = size // levels
    third_y = height // 3
    slots = own_ref.shape[0] - 1
    tile, row, lev = place()
    nest = tile == lax.axis_size("tiles") - 1
    level_ref[...] = edge_level(air_ref, height, lev)

    @pl.when(nest)
    def _():
        inner = inner_line(height, row)
        shape = (2 * levels, size)
        taken = iota(shape, 0)
        level, line = split_level(iota(shape, 1), height)
        wanted = jnp.where(taken < levels, height - 1 - inner, inner)
        picked = table((lax.rem(taken, levels) == level) & (line == wanted))
        speeds = from_left(picked, north_ref[...])
        outer = speeds[:levels]
        store_slabs(speeds_ref, 0, outer)
        store_slabs(speeds_ref, pieces, speeds[levels:])
        own_ref[...] = jnp.zeros_like(own_ref)
        edges_ref[...] = jnp.zeros_like(edges_ref)
        store_slabs(own_ref, 0, ghost_row_weights(ghost_weight(outer, row == 0), breadth))
        first = ghost_weight(east_ref[:, 0:1], True)
        last = ghost_weight(east_ref[:, breadth - 1 : breadth], False)
        own_ref[WEIGHTS - 1] = ghost_column_weights(first, last, levels, height)

    @pl.when(jnp.logical_not(nest))
    def _():
        start = west_ref[0] - tile * breadth
        top = south_ref[0] - 1 - row * height
        pack_window(own_ref, air_ref, levels, top + row * third_y, start)
        edges = pack_edges(air_ref, levels)
        edges_ref[...] = jnp.zeros_like(edges_ref)
        edges_ref[0] = edges
        own_ref[slots] = own_ref[slots] + edges
        speeds_ref[...] = jnp.zeros_like(speeds_ref)


def set_halo(rows_ref, first, northern_ref, southern_ref, row):
    halo = join_slabs(rows_ref, first, rows_ref.shape[0] - first)
    zero = jnp.zeros_like(halo)
    northern_ref[...] = jnp.where(row == 0, zero, halo)
    southern_ref[...] = jnp.where(row == 0, halo, zero)


def early_kernel(
    levels,
    air_ref,
    east_ref,
    north_ref,
    rows_ref,
    level_ref,
    field_ref,
    northern_ref,
    southern_ref,
):
    tile, row, lev = place()
    nest = tile == lax.axis_size("tiles") - 1
    set_halo(rows_ref, rows_ref.shape[0] - field_ref.shape[0], northern_ref, southern_ref, row)
    shared = (field_ref, air_ref, east_ref, north_ref, level_ref, levels, lev)

    @pl.when(nest)
    def _():
        full_step(*shared, True, northern_ref, southern_ref, None, None)

    @pl.when(jnp.logical_not(nest))
    def _():
        full_step(*shared, False, northern_ref, southern_ref, None, None)


def middle_kernel(levels, west_ref, south_ref, east_ref, three_ref, one_ref, given_ref, field_ref, other_ref):
    pieces, size, _ = field_ref.shape
    height, breadth = size // levels, pieces * LANES
    slots = other_ref.shape[0] - 1
    tile_count = lax.axis_size("tiles")
    tile, row, _ = place()
    nest = tile == tile_count - 1

    @pl.when(nest)
    def _():
        other_ref[...] = jnp.zeros_like(other_ref)

    @pl.when(jnp.logical_not(nest))
    def _():
        columns = neighbour_columns(one_ref[slots], three_ref[0], tile_count - 1, tile)
        side = unpack_edges(columns, levels, height)
        lane = iota((size, LANES), 1)
        west = (0.5 * east_ref[:, pl.ds(0, LANES)] + PARENT_MIXING) * side[:, 0:1]
        field_ref[0] = field_ref[0] + jnp.where(lane == 0, west, 0.0)
        east = (-0.5 * east_ref[:, pl.ds(breadth - LANES, LANES)] + PARENT_MIXING) * side[:, 1:2]
        field_ref[pieces - 1] = field_ref[pieces - 1] + jnp.where(lane == LANES - 1, east, 0.0)
        start = west_ref[1] - tile * breadth
        top = south_ref[1] - 1 - row * height
        pack_window(other_ref, field_ref, levels, top + (1 - row) * (height // 3), start)


def first_kernel(
    levels,
    west_ref,
    south_ref,
    early_ref,
    east_ref,
    speeds_ref,
    three_ref,
    two_ref,
    one_ref,
    field_ref,
    edge_ref,
    own_ref,
):
    pieces, size, _ = early_ref.shape
    height, breadth = edge_ref.shape
    slots = one_ref.shape[0] - 1
    tile, row, lev = place()
    nest = tile == lax.axis_size("tiles") - 1

    @pl.when(jnp.logical_not(nest))
    def _():
        edge_ref[...] = jnp.zeros_like(edge_ref)
        start = west_ref[1] - tile * breadth
        top = south_ref[1] - 1 - row * height
        pack_window(own_ref, early_ref, levels, top + row * (height // 3), start)

    @pl.when(nest)
    def _():
        slabs = [one_ref[s] + two_ref[s] + three_ref[s] for s in range(slots + 1)]
        cells, ring = refine(slabs[:slots], slabs[slots], height, breadth, row)
        lane = iota((size, LANES), 1)
        for c in range(pieces):
            piece = slice(c * LANES, (c + 1) * LANES)
            value = early_ref[c] + NUDGING * cells[:, piece]
            if c == 0:
                ghost = ghost_weight(east_ref[:, piece], True) * cells[:, breadth : breadth + 1]
                value = value + jnp.where(lane == 0, ghost, 0.0)
            if c == pieces - 1:
                ghost = ghost_weight(east_ref[:, piece], False) * cells[:, breadth + 1 : breadth + 2]
                value = value + jnp.where(lane == LANES - 1, ghost, 0.0)
            field_ref[c] = value
        outer = height - 1 - inner_line(height, row)
        ghost = ghost_weight(join_slabs(speeds_ref, 0, pieces), row == 0) * ring
        store_line(field_ref, levels, outer, load_line(field_ref, levels, outer) + ghost)
        edge_ref[...] = edge_level(field_ref, height, lev)


def average_kernel(levels, field_ref, east_ref, north_ref, rows_ref, message_ref, part_ref, nothing_ref):
    pieces, size, _ = field_ref.shape
    height, breadth = nothing_ref.shape
    third_y = height // 3
    tile, row, lev = place()

    @pl.when(tile == lax.axis_size("tiles") - 1)
    def _():
        nothing_ref[...] = jnp.zeros_like(nothing_ref)
        full_step(part_ref, field_ref, east_ref, north_ref, nothing_ref, levels, lev, True, None, None, None, None)
        sums = sums_table(breadth)
        shape = (third_y * levels, size)
        taken = iota(shape, 0)
        block = taken // levels
        level, line = split_level(iota(shape, 1), height)
        offset = line - 3 * block
        rows = table((taken - block * levels == level) & (offset >= 0) & (offset <= 2))
        means = from_left(rows, from_right(part_ref[...], sums)) * (1.0 / 9.0)
        for m in range(third_y):
            message_ref[m] = means[m * levels : (m + 1) * levels]
        shared = load_line(field_ref, levels, inner_line(height, row))
        shared = ghost_weight(join_slabs(rows_ref, WEIGHTS, pieces), row == 0) * shared
        message_ref[third_y] = from_right(shared, sums) * (1.0 / 9.0)
        for i in range(third_y + 1, message_ref.shape[0]):
            message_ref[i] = jnp.zeros((levels, LANES), jnp.float32)


def sums_table(breadth):
    offset = iota((breadth, LANES), 0) - 3 * iota((breadth, LANES), 1)
    return table((offset >= 0) & (offset <= 2))


def pack_column(slabs, extra, slot):
    lane = iota(extra.shape, 1)
    packed = jnp.where(slot == -1, extra, pltpu.roll(extra, LANES - EAST_LANE, 1))
    inside = (slot >= 0) & (slot < LANES)
    for s, slab in enumerate(slabs):
        turned = pltpu.roll(slab, lax.rem(s - slot + 64 * LANES, LANES), 1)
        packed = jnp.where((lane == s) & inside, turned, packed)
    return packed


def message_kernel(
    levels, west_ref, level_ref, part_ref, coef_ref, own_ref, other_ref, message_ref, far_ref, side_ref
):
    height, breadth = level_ref.shape
    third_y = height // 3
    tile, row, lev = place()
    nest = tile == lax.axis_size("tiles") - 1

    @pl.when(jnp.logical_not(nest))
    def _():
        message_ref[...] = own_ref[...] + other_ref[...]
        far_ref[pl.ds(0, message_ref.shape[0])] = message_ref[...]
        for i in range(message_ref.shape[0], far_ref.shape[0]):
            far_ref[i] = jnp.zeros((levels, LANES), jnp.float32)
        slots = message_ref.shape[0] - 1
        first = tile * breadth - west_ref[1]
        lane = iota((levels, LANES), 1)
        columns = [
            pack_column([message_ref[s] for s in range(slots)], message_ref[slots], slot)
            for slot in (first, first + breadth - 1)
        ]
        side_ref[...] = jnp.where(lane < EAST_LANE, columns[0], pltpu.roll(columns[1], EAST_LANE, 1))

    @pl.when(nest)
    def _():
        offset = iota((third_y, height), 1) - 3 * iota((third_y, height), 0)
        rows = table((offset >= 0) & (offset <= 2))
        across = from_left(rows, from_right(level_ref[...], sums_table(breadth))) * (VERTICAL_MIX / 9.0)
        at_edge = iota((levels, LANES), 0) == jnp.where(lev == 0, levels - 1, 0)
        for m in range(third_y):
            message_ref[m] = part_ref[m] + jnp.where(at_edge, across[m : m + 1], 0.0)
        for i in range(third_y, message_ref.shape[0]):
            message_ref[i] = part_ref[i]
        far_ref[pl.ds(0, third_y + 1)] = message_ref[pl.ds(0, third_y + 1)]
        far_ref[pl.ds(third_y + 1, WEIGHTS)] = coef_ref[pl.ds(0, WEIGHTS)]
        side_ref[...] = jnp.zeros_like(side_ref)


def blend_kernel(
    levels,
    western,
    west_ref,
    weight_ref,
    field_ref,
    window_ref,
    beside_ref,
    middle_ref,
    other_ref,
    coef_middle_ref,
    coef_near_ref,
    rows_ref,
):
    pieces, size, _ = field_ref.shape
    height = size // levels
    third_y = height // 3
    slots = third_y + 2
    tile_count = lax.axis_size("tiles")
    tile, row, _ = place()
    nest = tile == tile_count - 1

    @pl.when(nest)
    def _():
        store_slabs(rows_ref, 0, load_line(field_ref, levels, inner_line(height, row)))
        for i in range(pieces, rows_ref.shape[0]):
            rows_ref[i] = jnp.zeros((levels, LANES), jnp.float32)

    @pl.when(jnp.logical_not(nest))
    def _():
        paired = (tile == 1) | (tile == (0 if western else 2))

        def mine(i):
            return jnp.where(tile == 1, middle_ref[i], other_ref[i])

        def coefficient(i):
            other = other_ref[third_y + 1 + i] if western else coef_near_ref[i]
            return jnp.where(tile == 1, coef_middle_ref[i], other)

        breadth = pieces * LANES
        partner_east = tile == (0 if western else 1)
        slot = jnp.where(partner_east, (tile + 1) * breadth, tile * breadth - 1) - west_ref[1]
        column = jnp.where(partner_east, beside_ref[...], pltpu.roll(beside_ref[...], LANES - EAST_LANE, 1))
        lane = iota((levels, LANES), 1)

        def whole(s):
            return jnp.where(paired & (lane == slot), column[:, s : s + 1], window_ref[s])

        level = iota((levels, LANES), 0)
        weight = jnp.zeros((levels, LANES), jnp.float32)
        for l in range(levels):
            weight = jnp.where(level == l, weight_ref[l], weight)
        extra = window_ref[slots]
        extra = jnp.where(paired & (slot == -1) & (lane < EAST_LANE), column, extra)
        east_column = pltpu.roll(column, EAST_LANE, 1)
        extra = jnp.where(paired & (slot == LANES) & (lane >= EAST_LANE), east_column, extra)
        at_first, at_last = lane == 0, lane == LANES - 1
        lines = []
        for s in range(slots):
            x = whole(s)
            west = jnp.where(at_first, extra[:, s : s + 1], pltpu.roll(x, 1, 1))
            last = EAST_LANE + s
            east = jnp.where(at_last, extra[:, last : last + 1], pltpu.roll(x, LANES - 1, 1))
            lines.append((west, x, east))
        edges = coefficient(WEIGHTS - 1)
        ghosts = [coefficient(q) for q in range(3)]

        def outward(side, q):
            near = lines[1] if side == 0 else lines[slots - 2]
            far = lines[0] if side == 0 else lines[slots - 1]
            return (2.0 / 3.0) * far[q] + (1.0 / 3.0) * near[q]

        def sideward(s):
            west, x, east = lines[s]
            return (2.0 / 3.0) * jnp.where(at_first, west, east) + (1.0 / 3.0) * x

        sidewards = [sideward(s) for s in range(slots)]
        columns = [w + 7.0 * x + e for w, x, e in lines]
        for m in range(third_y):
            x = lines[m + 1][1]
            value = mine(m) + (NUDGING / 81.0) * (columns[m] + 7.0 * columns[m + 1] + columns[m + 2])
            for q in range(3):
                lane_of = 8 * m + q
                first, last = edges[:, lane_of : lane_of + 1], edges[:, lane_of + 3 : lane_of + 4]
                scale = jnp.where(at_first, first, jnp.where(at_last, last, 0.0))
                value = value + scale * sidewards[m + q]
            for side, at in ((0, 0), (1, third_y - 1)):
                if m == at:
                    for q in range(3):
                        value = value + jnp.where(row == side, ghosts[q], 0.0) * outward(side, q)
            rows_ref[m] = x + weight * (value - x)
        rows_ref[third_y] = weight * mine(third_y)


def later_kernel(
    levels,
    west_ref,
    south_ref,
    field_ref,
    east_ref,
    north_ref,
    level_ref,
    middle_ref,
    other_ref,
    parent_ref,
    blend_ref,
    out_ref,
    fine_ref,
    side_ref,
    northern_ref,
    southern_ref,
):
    height, breadth = level_ref.shape
    third_y = height // 3
    slots = third_y + 2
    tile, row, lev = place()
    nest = tile == lax.axis_size("tiles") - 1

    @pl.when(nest)
    def _():
        slabs = [middle_ref[s] + other_ref[s] for s in range(slots + 1)]
        cells, ring = refine(slabs[:slots], slabs[slots], height, breadth, row)
        fine_ref[...] = cells[:, :breadth]
        side_ref[...] = cells[:, breadth:]
        zero = jnp.zeros_like(ring)
        northern_ref[...] = jnp.where(row == 0, ring, zero)
        southern_ref[...] = jnp.where(row == 0, zero, ring)
        full_step(
            out_ref,
            field_ref,
            east_ref,
            north_ref,
            level_ref,
            levels,
            lev,
            True,
            northern_ref,
            southern_ref,
            side_ref,
            fine_ref,
        )

    @pl.when(jnp.logical_not(nest))
    def _():
        out_ref[...] = parent_ref[...]
        start = west_ref[1] - tile * breadth
        top = south_ref[1] + row * third_y - row * height
        for m in range(third_y):
            place_row(out_ref, levels, top + m, start, blend_ref[m])


def last_kernel(
    levels, west_ref, south_ref, given_ref, speeds_ref, blend_ref, rows_ref, out_hbm, out_ref, sems
):
    pieces, size, _ = out_ref.shape
    breadth = pieces * LANES
    height = size // levels
    third_y = height // 3
    tile, row, _ = place()
    nest = tile == lax.axis_size("tiles") - 1

    @pl.when(nest)
    def _():
        inner = inner_line(height, row)
        halo = ghost_weight(join_slabs(speeds_ref, pieces, pieces), row == 1) * join_slabs(rows_ref, 0, pieces)
        store_line(out_ref, levels, inner, load_line(out_ref, levels, inner) + halo)

    @pl.when(jnp.logical_not(nest))
    def _():
        start = west_ref[1] - tile * breadth
        top = south_ref[1] + (1 - row) * third_y - row * height
        for m in range(third_y):
            value = rows_ref[m]
            if m == 0:
                value = value + jnp.where(row == 0, blend_ref[third_y], 0.0)
            if m == third_y - 1:
                value = value + jnp.where(row == 1, blend_ref[third_y], 0.0)
            place_row(out_ref, levels, top + m, start, value)
        near = jnp.where(row == 0, third_y - 1, 0)
        line = south_ref[1] + row * third_y - row * height + near
        place_row(out_ref, levels, line, start, blend_ref[near] + rows_ref[third_y])

    copies = [
        pltpu.make_async_copy(out_ref.at[c], out_hbm.at[:, pl.ds(c * LANES, LANES)], sems.at[c])
        for c in range(pieces)
    ]
    for copy in copies:
        copy.start()
    for copy in copies:
        copy.wait()


def call(kernel, outs, inputs, places, scratch=(), flops=0, aliases=()):
    spaces = {"s": pltpu.SMEM, "v": pltpu.VMEM, "h": pltpu.HBM}
    outs = [pltpu.VMEM(out, jnp.float32) if isinstance(out, tuple) else out for out in outs]
    moved = sum(4 * math.prod(out.shape) for out in outs) + sum(array.nbytes for array in inputs)
    inputs = [
        array if p == "v" else pltpu.with_memory_space_constraint(array, spaces[p])
        for array, p in zip(inputs, places)
    ]
    return pl.pallas_call(
        kernel,
        out_shape=outs,
        in_specs=[pl.BlockSpec(memory_space=spaces[p]) for p in places],
        out_specs=[pl.BlockSpec(memory_space=out.memory_space) for out in outs],
        scratch_shapes=[pltpu.VMEM(s, jnp.float32) if isinstance(s, tuple) else s for s in scratch],
        input_output_aliases=dict(aliases),
        compiler_params=pltpu.CompilerParams(vmem_limit_bytes=32 * 1024 * 1024),
        cost_estimate=pl.CostEstimate(flops=flops, bytes_accessed=moved, transcendentals=0),
    )(*inputs)


def per_device_paired(air_state, wind_east, wind_north, feedback_weight, nest_west, nest_south):
    levels, height, breadth = air_state.shape
    third_y = height // 3
    pieces = breadth // LANES
    slots = third_y + 2
    tile_count = lax.axis_size("tiles")
    size = levels * height
    flat = (size, breadth)
    chunked = (pieces, size, LANES)
    air, east, north = (array.reshape(flat) for array in (air_state, wind_east, wind_north))
    swap = [(0, 1), (1, 0)]

    def slabs(count):
        return (count, levels, LANES)

    def kernel(body):
        return functools.partial(body, levels)

    rows, air_pieces, west, south, weight = call(
        kernel(pack_kernel),
        [
            slabs(slots + 1 + pieces),
            chunked,
            pltpu.SMEM((2,), jnp.int32),
            pltpu.SMEM((2,), jnp.int32),
            pltpu.SMEM((levels,), jnp.float32),
        ],
        [nest_west, nest_south, feedback_weight, air, north],
        "hhhhh",
        [chunked, pltpu.SemaphoreType.DMA((2 * pieces + 3,))],
    )
    own, level, speeds, edges = call(
        kernel(own_kernel),
        [slabs(slots + 1), (height, breadth), slabs(2 * pieces), slabs(slots + 2)],
        [west, south, air_pieces, east, north],
        "ssvvv",
        flops=30 * size * breadth,
    )
    rows = lax.ppermute(rows, "rows", swap)
    level = lax.ppermute(level, "lev", swap)
    where = [(t, r, l) for t in range(tile_count) for r in range(2) for l in range(2)]
    at = {position: i for i, position in enumerate(where)}

    def over_tiles(message, step, *without):
        pairs = []
        for t, r, l in where:
            idle = t in without or (t ^ step) in without
            pairs.append((at[t, r, l], at[(t, r, 1 - l) if idle else (t ^ step, r, l)]))
        return lax.ppermute(message, ("tiles", "rows", "lev"), pairs)

    halo = over_tiles(edges, 3, 0)
    eastern = nest_west[1] > breadth
    rows, eastern = lax.optimization_barrier((rows, eastern))
    window = own + rows[: slots + 1]
    own_0 = own
    around = [(t, (t - 1) % tile_count) for t in range(tile_count)]
    starting = [
        over_tiles(window, 1),
        over_tiles(window, 2, 0),
        lax.ppermute(window, "tiles", around),
    ]
    sides = [(size, LANES), (levels, breadth), (levels, breadth)]
    (early,) = call(
        kernel(early_kernel),
        [chunked],
        [air, east, north, rows, level],
        "vvvvv",
        sides[1:],
        flops=30 * size * breadth,
    )
    early, other = call(
        kernel(middle_kernel),
        [chunked, slabs(slots + 1)],
        [west, south, east, halo, starting[0], early],
        "ssvvvv",
        flops=10 * size * breadth,
        aliases=[(5, 0)],
    )
    other = lax.ppermute(other, "rows", swap)
    first, edge, own = call(
        kernel(first_kernel),
        [chunked, (height, breadth), slabs(slots + 1)],
        [west, south, early, east, speeds, *starting[::-1]],
        "ssvvvvvv",
        flops=10 * size * breadth,
    )
    level = lax.ppermute(edge, "lev", swap)
    (part,) = call(
        kernel(average_kernel),
        [slabs(slots + 1)],
        [first, east, north, rows],
        "vvvv",
        [flat, (height, breadth)],
        flops=30 * size * breadth,
    )
    message, far_message, side_message = call(
        kernel(message_kernel),
        [slabs(slots + 1), slabs(third_y + 1 + WEIGHTS), (levels, LANES)],
        [west, level, part, own_0, own, other],
        "svvvvv",
    )
    def finish(western, arrays):
        west, south, weight, first, east, north, level, message, far_message, side_message, early, speeds, coefs = arrays
        if western:
            other, beside = over_tiles(far_message, 3, 1), over_tiles(side_message, 1, 3)
        else:
            other, beside = over_tiles(message, 1, 0), over_tiles(side_message, 3, 0)
        middle = over_tiles(message, 2, 0)
        (blend,) = call(
            functools.partial(blend_kernel, levels, western),
            [slabs(third_y + 1)],
            [west, weight, first, message, beside, middle, other, *coefs],
            "ss" + "v" * 7,
        )
        rows = lax.ppermute(blend, "rows", swap)
        (later,) = call(
            kernel(later_kernel),
            [chunked],
            [west, south, first, east, north, level, middle, other, early, blend],
            "ss" + "v" * 8,
            [flat, *sides],
            flops=30 * size * breadth,
        )
        out, _ = call(
            kernel(last_kernel),
            [pltpu.HBM(flat, jnp.float32), chunked],
            [west, south, later, speeds, blend, rows],
            "ssvvvv",
            [pltpu.SemaphoreType.DMA((pieces,))],
            aliases=[(2, 1)],
        )
        return out

    arrays = (west, south, weight, first, east, north, level, message, far_message, side_message, early, speeds)
    arrays += ((starting[1], starting[0]),)
    out = lax.cond(
        eastern,
        functools.partial(finish, False),
        functools.partial(finish, True),
        arrays,
    )
    return out.reshape(air_state.shape)


def solution(mesh):
    in_specs = (
        P(("members", "lev"), "rows", "tiles"),
        P(("members", "lev"), "rows", "tiles"),
        P(("members", "lev"), "rows", "tiles"),
        P("lev"),
        P("members"),
        P("members"),
    )
    out_specs = P(("members", "lev"), "rows", "tiles")
    paired = mesh.shape["tiles"] == 4 and mesh.shape["rows"] == 2 and mesh.shape["lev"] == 2
    return jax.shard_map(
        per_device_paired if paired else per_device, mesh=mesh, in_specs=in_specs, out_specs=out_specs, check_vma=False
    )
```

```python
import functools
import math

import jax
import jax.numpy as jnp
import numpy as np
from jax import lax
from jax.experimental import pallas as pl
from jax.experimental.pallas import tpu as pltpu
from jax.sharding import PartitionSpec as P

VERTICAL_MIX = 0.1
PARENT_MIXING = 0.04
NEST_MIXING = 0.18
NEST_ADVECT = 1.5
NUDGING = 0.2


def padded_2(array, sides, width):
    for axis, dim in sides:
        size, length = (lax.axis_size(axis), array.shape[dim])
        up = [(i, (i + 1) % size) for i in range(size - 1)]
        down = [(j, i) for i, j in up]
        last = lax.slice_in_dim(array, length - width, length, axis=dim)
        first = lax.slice_in_dim(array, 0, width, axis=dim)
        before = lax.ppermute(last, axis, up)
        after = lax.ppermute(first, axis, down)
        array = jnp.concatenate([before, array, after], axis=dim)
    return array


def interp_table(cells):
    extended = jnp.arange(cells + 2, dtype=jnp.int32) - 1
    coarse = jnp.floor_divide(extended, 3)
    offset = extended - 3 * coarse
    fraction = jnp.abs(offset - 1).astype(jnp.float32) / 3.0
    nearest = coarse + 1
    beside = nearest + (offset - 1)
    slots = jnp.arange(cells // 3 + 2, dtype=jnp.int32)[:, None]
    first_part = jnp.where(
        slots == nearest[None, :], 1.0 - fraction[None, :], jnp.zeros((), jnp.float32)
    )
    second_part = jnp.where(slots == beside[None, :], fraction[None, :], jnp.zeros((), jnp.float32))
    return first_part + second_part


def tendency(padded, speed_east, speed_north, advect_scale, mixing_scale):
    centre = padded[1:-1, 1:-1, 1:-1]
    eastern = padded[1:-1, 1:-1, 2:]
    western = padded[1:-1, 1:-1, :-2]
    southern = padded[1:-1, 2:, 1:-1]
    northern = padded[1:-1, :-2, 1:-1]
    upper = padded[2:, 1:-1, 1:-1]
    lower = padded[:-2, 1:-1, 1:-1]
    advect = speed_east * (eastern - western) + speed_north * (southern - northern)
    horizontal = eastern + western + southern + northern - 4.0 * centre
    vertical = upper + lower - 2.0 * centre
    return -0.5 * advect_scale * advect + mixing_scale * horizontal + VERTICAL_MIX * vertical


def padded_block(block_field):
    return padded_2(block_field, (("tiles", 2), ("rows", 1), ("lev", 0)), 1)


def per_device(air_state, wind_east, wind_north, feedback_weight, nest_west, nest_south):
    levels, height, breadth = air_state.shape
    tile_count = lax.axis_size("tiles")
    row_count = lax.axis_size("rows")
    tile_index = lax.axis_index("tiles")
    row_index = lax.axis_index("rows")
    parent_tiles = 3 * tile_count // 4
    nest_tiles = tile_count - parent_tiles
    in_nest = tile_index >= parent_tiles
    nest_tile = tile_index - parent_tiles
    cross_x = breadth // 3 + 2
    cross_y = height // 3 + 2
    third_x = breadth // 3
    third_y = height // 3
    first_x = tile_index * breadth
    first_y = row_index * height
    columns = jnp.arange(breadth, dtype=jnp.int32)
    lines = jnp.arange(height, dtype=jnp.int32)
    targets_x = jnp.arange(tile_count, dtype=jnp.int32)
    targets_y = jnp.arange(row_count, dtype=jnp.int32)
    highest = lax.Precision.HIGHEST
    table_x = interp_table(breadth)
    table_y = interp_table(height)
    zero_value = jnp.zeros((), jnp.float32)

    def boundary(source, substep):
        anchor_x = nest_west[substep] + (targets_x - parent_tiles) * third_x - 1
        slot_x = jnp.arange(cross_x, dtype=jnp.int32)
        pick_x = (
            (first_x + columns)[None, :, None] == anchor_x[:, None, None] + slot_x[None, None, :]
        ) & (targets_x >= parent_tiles)[:, None, None]
        pick_x = pick_x.astype(jnp.float32)
        anchor_y = nest_south[substep] + targets_y * third_y - 1
        slot_y = jnp.arange(cross_y, dtype=jnp.int32)
        pick_y = (
            (first_y + lines)[None, :, None] == anchor_y[:, None, None] + slot_y[None, None, :]
        ).astype(jnp.float32)
        pieces = jnp.einsum("lyi,tij->tlyj", source, pick_x, precision=highest)
        merged = lax.all_to_all(pieces, "tiles", split_axis=0, concat_axis=0, tiled=True).sum(
            axis=0
        )
        pieces = jnp.einsum("lyj,ryw->rlwj", merged, pick_y, precision=highest)
        window = lax.all_to_all(pieces, "rows", split_axis=0, concat_axis=0, tiled=True).sum(axis=0)
        along = jnp.einsum("lwj,je->lwe", window, table_x, precision=highest)
        return jnp.einsum("lwe,wf->lfe", along, table_y, precision=highest)

    def assemble(block_field, fine):
        padded = padded_block(block_field)
        fine_padded = jnp.pad(fine, ((1, 1), (0, 0), (0, 0)))
        column_place = lax.broadcasted_iota(jnp.int32, padded.shape, 2)
        line_place = lax.broadcasted_iota(jnp.int32, padded.shape, 1)
        outside = (column_place == 0) & (nest_tile == 0) | (column_place == breadth + 1) & (
            nest_tile == nest_tiles - 1
        )
        outside = (
            outside
            | (line_place == 0) & (row_index == 0)
            | (line_place == height + 1) & (row_index == row_count - 1)
        )
        padded = jnp.where(outside & in_nest, fine_padded, padded)
        seam_cells = (column_place == breadth + 1) & (tile_index == parent_tiles - 1)
        return jnp.where(seam_cells, zero_value, padded)

    advect_scale = jnp.where(in_nest, jnp.float32(NEST_ADVECT), jnp.float32(1.0))
    mixing_scale = jnp.where(in_nest, jnp.float32(NEST_MIXING), jnp.float32(PARENT_MIXING))
    fine_first = boundary(air_state, 0)
    change = tendency(
        assemble(air_state, fine_first), wind_east, wind_north, advect_scale, mixing_scale
    )
    nudging_term = jnp.where(in_nest, NUDGING * (fine_first[:, 1:-1, 1:-1] - air_state), zero_value)
    step_one = air_state + change + nudging_term
    fine_second = boundary(step_one, 1)
    change = tendency(
        assemble(step_one, fine_second), wind_east, wind_north, advect_scale, mixing_scale
    )
    nested_two = step_one + change + NUDGING * (fine_second[:, 1:-1, 1:-1] - step_one)
    step_two = jnp.where(in_nest, nested_two, step_one)
    coarse = step_two.reshape(levels, third_y, 3, third_x, 3).mean(axis=(2, 4))
    avg_columns = jnp.arange(third_x, dtype=jnp.int32)
    avg_lines = jnp.arange(third_y, dtype=jnp.int32)
    west_last = nest_west[1]
    south_last = nest_south[1]
    place_x = (
        (west_last + (targets_x - parent_tiles) * third_x)[:, None, None]
        + avg_columns[None, :, None]
        == (first_x + columns)[None, None, :]
    ) & (targets_x >= parent_tiles)[:, None, None]
    place_x = place_x.astype(jnp.float32)
    place_y = (
        (south_last + targets_y * third_y)[:, None, None] + avg_lines[None, :, None]
        == (first_y + lines)[None, None, :]
    ).astype(jnp.float32)
    parent_y = south_last + row_index * third_y + avg_lines
    send_y = (jnp.floor_divide(parent_y, height)[None, :] == targets_y[:, None]) & in_nest
    pieces = jnp.where(send_y[:, None, :, None], coarse[None], zero_value)
    received = lax.all_to_all(pieces, "rows", split_axis=0, concat_axis=0, tiled=True)
    spread = jnp.einsum("slba,sby->lya", received, place_y, precision=highest)
    parent_x = west_last + nest_tile * third_x + avg_columns
    send_x = jnp.floor_divide(parent_x, breadth)[None, :] == targets_x[:, None]
    pieces = jnp.where(send_x[:, None, None, :], spread[None], zero_value)
    received = lax.all_to_all(pieces, "tiles", split_axis=0, concat_axis=0, tiled=True)
    placed = jnp.einsum("slya,sai->lyi", received, place_x, precision=highest)
    global_x = (first_x + columns)[None, None, :]
    global_y = (first_y + lines)[None, :, None]
    covered = (global_x >= west_last) & (global_x < west_last + nest_tiles * third_x)
    covered = covered & (global_y >= south_last) & (global_y < south_last + row_count * third_y)
    covered = covered & jnp.logical_not(in_nest)
    blended = step_two + feedback_weight[:, None, None] * (placed - step_two)
    return jnp.where(covered, blended, step_two)


LANES = 128
FIRST_LANE = 32
LAST_LANE = 96
EAST_LANE = 64
WEIGHTS = 4


def iota(shape, dim):
    return lax.broadcasted_iota(jnp.int32, shape, dim)


def split_level(place, height):
    level = ((place.astype(jnp.float32) + 0.5) * (1.0 / height)).astype(jnp.int32)
    return level, place - level * height


def table(values):
    return values.astype(jnp.float32).astype(jnp.bfloat16)


def parts_of(array):
    high = array.astype(jnp.bfloat16)
    low = (array - high.astype(jnp.float32)).astype(jnp.bfloat16)
    return high, low


def dot(left, right):
    return jnp.dot(left, right, preferred_element_type=jnp.float32)


def from_left(weights, array):
    high, low = parts_of(array)
    return dot(weights, high) + dot(weights, low)


def from_right(array, weights):
    high, low = parts_of(array)
    return dot(high, weights) + dot(low, weights)


def hat(distance):
    return jnp.maximum(0, 3 - jnp.abs(distance - 1))


def place():
    return lax.axis_index("tiles"), lax.axis_index("rows"), lax.axis_index("lev")


def level_table(levels, height):
    shape = (levels, levels * height)
    level, _ = split_level(iota(shape, 1), height)
    return table(iota(shape, 0) == level)


def spread_table(levels, height):
    shape = (levels * height, levels)
    level, _ = split_level(iota(shape, 0), height)
    return table(iota(shape, 1) == level)


def load_line(ref, levels, line):
    rows = pl.ds(line, levels, stride=ref.shape[1] // levels)
    return jnp.concatenate([ref[c, rows, :] for c in range(ref.shape[0])], axis=1)


def store_line(ref, levels, line, value):
    rows = pl.ds(line, levels, stride=ref.shape[1] // levels)
    for c in range(ref.shape[0]):
        ref[c, rows, :] = value[:, c * LANES : (c + 1) * LANES]


def load_level(ref, height, l):
    rows = pl.ds(l * height, height)
    if len(ref.shape) == 2:
        return ref[rows, :]
    return jnp.concatenate([ref[c, rows, :] for c in range(ref.shape[0])], axis=1)


def store_level(ref, height, l, value):
    rows = pl.ds(l * height, height)
    if len(ref.shape) == 2:
        ref[rows, :] = value
    else:
        for c in range(ref.shape[0]):
            ref[c, rows, :] = value[:, c * LANES : (c + 1) * LANES]


def store_slabs(ref, first, wide):
    for i in range(wide.shape[1] // LANES):
        ref[first + i] = wide[:, i * LANES : (i + 1) * LANES]


def join_slabs(ref, first, count):
    return jnp.concatenate([ref[first + i] for i in range(count)], axis=1)


def column_pieces(start, pieces):
    first = (start + 64 * LANES) // LANES - 64
    offset = start - first * LANES
    held = [(c >= 0) & (c < pieces) for c in (first, first + 1)]
    return [jnp.clip(c, 0, pieces - 1) for c in (first, first + 1)], held, offset


def pack_window(ref, field_ref, levels, top, start):
    pieces, size, _ = field_ref.shape
    height = size // levels
    slots = ref.shape[0] - 1
    lane = iota((levels, LANES), 1)
    (left, right), (left_held, right_held), offset = column_pieces(start, pieces)
    before = lax.rem(offset + LANES - 1, LANES)
    (beside, _), (beside_held, _), _ = column_pieces(start - 1, pieces)
    in_left = lane < LANES - offset
    held = jnp.where(in_left, left_held.astype(jnp.float32), right_held.astype(jnp.float32))
    west_held, east_held = beside_held.astype(jnp.float32), right_held.astype(jnp.float32)
    turn = lax.rem(LANES - offset, LANES)
    extra = jnp.zeros((levels, LANES), jnp.float32)
    for slot in range(slots):
        line = top + slot
        there = ((line >= 0) & (line < height)).astype(jnp.float32)
        rows = pl.ds(jnp.clip(line, 0, height - 1), levels, stride=height)
        near, far, west = field_ref[left, rows, :], field_ref[right, rows, :], field_ref[beside, rows, :]
        ref[slot] = jnp.where(in_left, pltpu.roll(near, turn, 1), pltpu.roll(far, turn, 1)) * (held * there)
        west = pltpu.roll(west, lax.rem(LANES + slot - before, LANES), 1) * (west_held * there)
        east = pltpu.roll(far, lax.rem(LANES + EAST_LANE + slot - offset, LANES), 1) * (east_held * there)
        extra = jnp.where(lane == slot, west, jnp.where(lane == EAST_LANE + slot, east, extra))
    ref[slots] = extra


def place_row(ref, levels, line, start, value):
    pieces, size, _ = ref.shape
    height = size // levels
    lane = iota((levels, LANES), 1)
    at, held, offset = column_pieces(start, pieces)
    value = pltpu.roll(value, offset, 1)
    there = (line >= 0) & (line < height)
    rows = pl.ds(jnp.clip(line, 0, height - 1), levels, stride=height)
    for c in range(2):
        mine = (lane >= offset) if c == 0 else (lane < offset)
        ref[at[c], rows, :] = jnp.where(mine & (held[c] & there), value, ref[at[c], rows, :])


def pack_edges(field_ref, levels):
    height = field_ref.shape[1] // levels
    lane = iota((levels, LANES), 1)
    packed = jnp.zeros((levels, LANES), jnp.float32)
    for line in range(height):
        rows = pl.ds(line, levels, stride=height)
        first = field_ref[0, rows, :]
        last = field_ref[field_ref.shape[0] - 1, rows, :]
        packed = jnp.where(lane == FIRST_LANE + line, pltpu.roll(first, FIRST_LANE + line, 1), packed)
        packed = jnp.where(lane == LAST_LANE + line, pltpu.roll(last, LAST_LANE + line + 1, 1), packed)
    return packed


def neighbour_columns(even, odd, parent_tiles, tile):
    is_odd = tile % 2 == 1
    west = jnp.where(is_odd, even, odd)
    east = jnp.where(is_odd, odd, even)
    west = jnp.where(tile == 0, jnp.zeros_like(west), west)
    east = jnp.where(tile >= parent_tiles - 1, jnp.zeros_like(east), east)
    return jnp.where(iota(west.shape, 1) < LAST_LANE, east, west)


def unpack_edges(columns, levels, height):
    wide = from_left(spread_table(levels, height), columns)
    lane = iota(wide.shape, 1)
    _, line = split_level(iota(wide.shape, 0), height)
    west = jnp.sum(jnp.where(lane == line + LAST_LANE, wide, 0.0), axis=1, keepdims=True)
    east = jnp.sum(jnp.where(lane == line + FIRST_LANE, wide, 0.0), axis=1, keepdims=True)
    return jnp.where(lane == 0, west, jnp.where(lane == 1, east, 0.0))


def refine(slabs, extra, height, breadth, row):
    slots, levels = len(slabs), extra.shape[0]
    beside = [pltpu.roll(extra, LANES - s, 1) if s else extra for s in range(slots)]
    window = jnp.concatenate([jnp.concatenate(slabs, axis=0), jnp.concatenate(beside, axis=0)], axis=1)
    shape = (2 * LANES, breadth + LANES)
    slot, cell = iota(shape, 0), iota(shape, 1)
    held = (slot <= LANES) | (slot == LANES + EAST_LANE)
    at = jnp.where(slot < LANES, slot, jnp.where(slot == LANES, -1, LANES))
    cell = jnp.where(cell == breadth, -1, jnp.where(cell == breadth + 1, breadth, cell))
    across = jnp.where(held & (cell <= breadth), hat(cell - 3 * at), 0)
    wide = from_right(window, table(across)) * (1.0 / 9.0)
    shape = (levels * height, slots * levels)
    taken = iota(shape, 1)
    slot = taken // levels
    level, line = split_level(iota(shape, 0), height)
    along = jnp.where(taken - slot * levels == level, hat(line - 3 * (slot - 1)), 0)
    cells = from_left(table(along), wide)
    ring = jnp.where(
        row == 0,
        2.0 * wide[:levels] + wide[levels : 2 * levels],
        2.0 * wide[(slots - 1) * levels :] + wide[(slots - 2) * levels : (slots - 1) * levels],
    )
    return cells, ring[:, :breadth]


def beside_rows(x, north, south):
    height = x.shape[0]
    line = iota(x.shape, 0)
    northern = jnp.where(line == 0, north, pltpu.roll(x, 1, 0))
    southern = jnp.where(line == height - 1, south, pltpu.roll(x, height - 1, 0))
    return northern, southern


def beside_columns(x, west, east):
    breadth = x.shape[1]
    column = iota(x.shape, 1)
    western = jnp.where(column == 0, west, pltpu.roll(x, 1, 1))
    eastern = jnp.where(column == breadth - 1, east, pltpu.roll(x, breadth - 1, 1))
    return western, eastern


def change_of(x, sides, u, v, upper, lower, nest):
    advect_scale = NEST_ADVECT if nest else 1.0
    mixing_scale = NEST_MIXING if nest else PARENT_MIXING
    northern, southern, western, eastern = sides
    advect = u * (eastern - western) + v * (southern - northern)
    horizontal = eastern + western + southern + northern - 4.0 * x
    vertical = upper + lower - 2.0 * x
    return -0.5 * advect_scale * advect + mixing_scale * horizontal + VERTICAL_MIX * vertical


def ghost_weight(speed, before):
    return jnp.where(before, 0.5 * NEST_ADVECT, -0.5 * NEST_ADVECT) * speed + NEST_MIXING


def full_step(out_ref, field_ref, u_ref, v_ref, level_ref, levels, lev, nest, north, south, side, fine):
    height, breadth = level_ref.shape
    zero = jnp.zeros((height, breadth), jnp.float32)

    def block(ref, l):
        return load_level(ref, height, l)

    for l in range(levels):
        x = block(field_ref, l)
        lower = block(field_ref, l - 1) if l else jnp.where(lev == 1, level_ref[...], zero)
        upper = block(field_ref, l + 1) if l < levels - 1 else jnp.where(lev == 0, level_ref[...], zero)
        rows = [0.0 if ref is None else ref[pl.ds(l, 1), :] for ref in (north, south)]
        if side is None:
            columns = (0.0, 0.0)
        else:
            beside = side[pl.ds(l * height, height), :]
            columns = (beside[:, 0:1], beside[:, 1:2])
        sides = beside_rows(x, *rows) + beside_columns(x, *columns)
        fresh = x + change_of(x, sides, block(u_ref, l), block(v_ref, l), upper, lower, nest)
        if nest:
            fresh = fresh - NUDGING * x if fine is None else fresh + NUDGING * (block(fine, l) - x)
        store_level(out_ref, height, l, fresh)


def inner_line(height, row):
    return jnp.where(row == 0, height - 1, 0)


def edge_level(ref, height, lev):
    last = ref.shape[1] // height - 1
    return jnp.where(lev == 0, load_level(ref, height, last), load_level(ref, height, 0))


def ghost_row_weights(ghost, breadth):
    cell, third = iota((breadth, 3 * LANES), 0), iota((breadth, 3 * LANES), 1)
    kind = third // LANES
    offset = cell - 3 * (third - kind * LANES)
    middle = jnp.where(offset == 1, 3, jnp.where((offset == 0) | (offset == 2), 2, 0))
    weight = jnp.where(kind == 1, middle, jnp.where(offset == kind, 1, 0))
    return from_right(ghost, table(weight)) * (1.0 / 27.0)


def ghost_column_weights(first, last, levels, height):
    shape = (levels * height, LANES)
    lane = iota(shape, 1)
    _, line = split_level(iota(shape, 0), height)
    block = lane // 8
    inside = lane - block * 8
    eastern = inside >= 3
    kind = jnp.where(eastern, inside - 3, inside)
    offset = line - 3 * block
    middle = jnp.where(offset == 1, 3, jnp.where((offset == 0) | (offset == 2), 2, 0))
    weight = jnp.where(kind == 1, middle, jnp.where(offset == kind, 1, 0))
    weight = jnp.where((inside < 6) & (block < height // 3), weight, 0).astype(jnp.float32)
    columns = jnp.where(eastern, last, first) * weight
    return from_left(level_table(levels, height), columns) * (1.0 / 27.0)


def pack_kernel(
    levels,
    west_hbm,
    south_hbm,
    weight_hbm,
    air_hbm,
    north_hbm,
    rows_ref,
    air_ref,
    west_ref,
    south_ref,
    weight_ref,
    north_ref,
    sems,
):
    pieces, size, _ = air_ref.shape
    breadth = pieces * LANES
    height = size // levels
    third_y = height // 3
    slots = rows_ref.shape[0] - 1 - pieces
    tile, row, _ = place()
    nest = tile == lax.axis_size("tiles") - 1
    inner = inner_line(height, row)

    def column_copies(source, target, first):
        return [
            pltpu.make_async_copy(source.at[:, pl.ds(c * LANES, LANES)], target.at[c], sems.at[first + c])
            for c in range(pieces)
        ]

    copies = column_copies(air_hbm, air_ref, 0)
    copies.append(pltpu.make_async_copy(west_hbm, west_ref, sems.at[2 * pieces]))
    copies.append(pltpu.make_async_copy(south_hbm, south_ref, sems.at[2 * pieces + 1]))
    copies.append(pltpu.make_async_copy(weight_hbm, weight_ref, sems.at[2 * pieces + 2]))
    speeds = column_copies(north_hbm, north_ref, pieces)
    for copy in copies:
        copy.start()

    @pl.when(nest)
    def _():
        for copy in speeds:
            copy.start()

    for copy in copies:
        copy.wait()
    store_slabs(rows_ref, slots + 1, load_line(air_ref, levels, inner))
    part = rows_ref.at[pl.ds(0, slots + 1)]

    @pl.when(nest)
    def _():
        for copy in speeds:
            copy.wait()
        part[...] = jnp.zeros_like(part)
        store_slabs(rows_ref, WEIGHTS, load_line(north_ref, levels, inner))

    @pl.when(jnp.logical_not(nest))
    def _():
        start = west_ref[0] - tile * breadth
        top = south_ref[0] - 1 - row * height
        pack_window(part, air_ref, levels, top + (1 - row) * third_y, start)


def own_kernel(
    levels, west_ref, south_ref, air_ref, east_ref, north_ref, own_ref, level_ref, speeds_ref, edges_ref
):
    pieces, size, _ = air_ref.shape
    breadth = pieces * LANES
    height = size // levels
    third_y = height // 3
    slots = own_ref.shape[0] - 1
    tile, row, lev = place()
    nest = tile == lax.axis_size("tiles") - 1
    level_ref[...] = edge_level(air_ref, height, lev)

    @pl.when(nest)
    def _():
        inner = inner_line(height, row)
        shape = (2 * levels, size)
        taken = iota(shape, 0)
        level, line = split_level(iota(shape, 1), height)
        wanted = jnp.where(taken < levels, height - 1 - inner, inner)
        picked = table((lax.rem(taken, levels) == level) & (line == wanted))
        speeds = from_left(picked, north_ref[...])
        outer = speeds[:levels]
        store_slabs(speeds_ref, 0, outer)
        store_slabs(speeds_ref, pieces, speeds[levels:])
        own_ref[...] = jnp.zeros_like(own_ref)
        edges_ref[...] = jnp.zeros_like(edges_ref)
        store_slabs(own_ref, 0, ghost_row_weights(ghost_weight(outer, row == 0), breadth))
        first = ghost_weight(east_ref[:, 0:1], True)
        last = ghost_weight(east_ref[:, breadth - 1 : breadth], False)
        own_ref[WEIGHTS - 1] = ghost_column_weights(first, last, levels, height)

    @pl.when(jnp.logical_not(nest))
    def _():
        start = west_ref[0] - tile * breadth
        top = south_ref[0] - 1 - row * height
        pack_window(own_ref, air_ref, levels, top + row * third_y, start)
        edges = pack_edges(air_ref, levels)
        edges_ref[...] = jnp.zeros_like(edges_ref)
        edges_ref[0] = edges
        own_ref[slots] = own_ref[slots] + edges
        speeds_ref[...] = jnp.zeros_like(speeds_ref)


def set_halo(rows_ref, first, northern_ref, southern_ref, row):
    halo = join_slabs(rows_ref, first, rows_ref.shape[0] - first)
    zero = jnp.zeros_like(halo)
    northern_ref[...] = jnp.where(row == 0, zero, halo)
    southern_ref[...] = jnp.where(row == 0, halo, zero)


def early_kernel(
    levels,
    air_ref,
    east_ref,
    north_ref,
    rows_ref,
    level_ref,
    field_ref,
    northern_ref,
    southern_ref,
):
    tile, row, lev = place()
    nest = tile == lax.axis_size("tiles") - 1
    set_halo(rows_ref, rows_ref.shape[0] - field_ref.shape[0], northern_ref, southern_ref, row)
    shared = (field_ref, air_ref, east_ref, north_ref, level_ref, levels, lev)

    @pl.when(nest)
    def _():
        full_step(*shared, True, northern_ref, southern_ref, None, None)

    @pl.when(jnp.logical_not(nest))
    def _():
        full_step(*shared, False, northern_ref, southern_ref, None, None)


def middle_kernel(levels, west_ref, south_ref, east_ref, three_ref, one_ref, given_ref, field_ref, other_ref):
    pieces, size, _ = field_ref.shape
    height, breadth = size // levels, pieces * LANES
    slots = other_ref.shape[0] - 1
    tile_count = lax.axis_size("tiles")
    tile, row, _ = place()
    nest = tile == tile_count - 1

    @pl.when(nest)
    def _():
        other_ref[...] = jnp.zeros_like(other_ref)

    @pl.when(jnp.logical_not(nest))
    def _():
        columns = neighbour_columns(one_ref[slots], three_ref[0], tile_count - 1, tile)
        side = unpack_edges(columns, levels, height)
        lane = iota((size, LANES), 1)
        west = (0.5 * east_ref[:, pl.ds(0, LANES)] + PARENT_MIXING) * side[:, 0:1]
        field_ref[0] = field_ref[0] + jnp.where(lane == 0, west, 0.0)
        east = (-0.5 * east_ref[:, pl.ds(breadth - LANES, LANES)] + PARENT_MIXING) * side[:, 1:2]
        field_ref[pieces - 1] = field_ref[pieces - 1] + jnp.where(lane == LANES - 1, east, 0.0)
        start = west_ref[1] - tile * breadth
        top = south_ref[1] - 1 - row * height
        pack_window(other_ref, field_ref, levels, top + (1 - row) * (height // 3), start)


def first_kernel(
    levels,
    west_ref,
    south_ref,
    early_ref,
    east_ref,
    speeds_ref,
    three_ref,
    one_ref,
    two_ref,
    field_ref,
    edge_ref,
    own_ref,
):
    pieces, size, _ = early_ref.shape
    height, breadth = edge_ref.shape
    slots = one_ref.shape[0] - 1
    tile, row, lev = place()
    nest = tile == lax.axis_size("tiles") - 1

    @pl.when(jnp.logical_not(nest))
    def _():
        edge_ref[...] = jnp.zeros_like(edge_ref)
        start = west_ref[1] - tile * breadth
        top = south_ref[1] - 1 - row * height
        pack_window(own_ref, early_ref, levels, top + row * (height // 3), start)

    @pl.when(nest)
    def _():
        slabs = [one_ref[s] + two_ref[s] + three_ref[s] for s in range(slots + 1)]
        cells, ring = refine(slabs[:slots], slabs[slots], height, breadth, row)
        lane = iota((size, LANES), 1)
        for c in range(pieces):
            piece = slice(c * LANES, (c + 1) * LANES)
            value = early_ref[c] + NUDGING * cells[:, piece]
            if c == 0:
                ghost = ghost_weight(east_ref[:, piece], True) * cells[:, breadth : breadth + 1]
                value = value + jnp.where(lane == 0, ghost, 0.0)
            if c == pieces - 1:
                ghost = ghost_weight(east_ref[:, piece], False) * cells[:, breadth + 1 : breadth + 2]
                value = value + jnp.where(lane == LANES - 1, ghost, 0.0)
            field_ref[c] = value
        outer = height - 1 - inner_line(height, row)
        ghost = ghost_weight(join_slabs(speeds_ref, 0, pieces), row == 0) * ring
        store_line(field_ref, levels, outer, load_line(field_ref, levels, outer) + ghost)
        edge_ref[...] = edge_level(field_ref, height, lev)


def average_kernel(levels, field_ref, east_ref, north_ref, rows_ref, message_ref, part_ref, nothing_ref):
    pieces, size, _ = field_ref.shape
    height, breadth = nothing_ref.shape
    third_y = height // 3
    tile, row, lev = place()

    @pl.when(tile == lax.axis_size("tiles") - 1)
    def _():
        nothing_ref[...] = jnp.zeros_like(nothing_ref)
        full_step(part_ref, field_ref, east_ref, north_ref, nothing_ref, levels, lev, True, None, None, None, None)
        sums = sums_table(breadth)
        shape = (third_y * levels, size)
        taken = iota(shape, 0)
        block = taken // levels
        level, line = split_level(iota(shape, 1), height)
        offset = line - 3 * block
        rows = table((taken - block * levels == level) & (offset >= 0) & (offset <= 2))
        means = from_left(rows, from_right(part_ref[...], sums)) * (1.0 / 9.0)
        for m in range(third_y):
            message_ref[m] = means[m * levels : (m + 1) * levels]
        shared = load_line(field_ref, levels, inner_line(height, row))
        shared = ghost_weight(join_slabs(rows_ref, WEIGHTS, pieces), row == 0) * shared
        message_ref[third_y] = from_right(shared, sums) * (1.0 / 9.0)
        for i in range(third_y + 1, message_ref.shape[0]):
            message_ref[i] = jnp.zeros((levels, LANES), jnp.float32)


def sums_table(breadth):
    offset = iota((breadth, LANES), 0) - 3 * iota((breadth, LANES), 1)
    return table((offset >= 0) & (offset <= 2))


def pack_column(slabs, extra, slot):
    lane = iota(extra.shape, 1)
    packed = jnp.where(slot == -1, extra, pltpu.roll(extra, LANES - EAST_LANE, 1))
    inside = (slot >= 0) & (slot < LANES)
    for s, slab in enumerate(slabs):
        turned = pltpu.roll(slab, lax.rem(s - slot + 64 * LANES, LANES), 1)
        packed = jnp.where((lane == s) & inside, turned, packed)
    return packed


def message_kernel(
    levels, west_ref, level_ref, part_ref, coef_ref, own_ref, other_ref, message_ref, far_ref, side_ref
):
    height, breadth = level_ref.shape
    third_y = height // 3
    tile, row, lev = place()
    nest = tile == lax.axis_size("tiles") - 1

    @pl.when(jnp.logical_not(nest))
    def _():
        message_ref[...] = own_ref[...] + other_ref[...]
        far_ref[pl.ds(0, message_ref.shape[0])] = message_ref[...]
        for i in range(message_ref.shape[0], far_ref.shape[0]):
            far_ref[i] = jnp.zeros((levels, LANES), jnp.float32)
        slots = message_ref.shape[0] - 1
        first = tile * breadth - west_ref[1]
        lane = iota((levels, LANES), 1)
        columns = [
            pack_column([message_ref[s] for s in range(slots)], message_ref[slots], slot)
            for slot in (first, first + breadth - 1)
        ]
        side_ref[...] = jnp.where(lane < EAST_LANE, columns[0], pltpu.roll(columns[1], EAST_LANE, 1))

    @pl.when(nest)
    def _():
        offset = iota((third_y, height), 1) - 3 * iota((third_y, height), 0)
        rows = table((offset >= 0) & (offset <= 2))
        across = from_left(rows, from_right(level_ref[...], sums_table(breadth))) * (VERTICAL_MIX / 9.0)
        at_edge = iota((levels, LANES), 0) == jnp.where(lev == 0, levels - 1, 0)
        for m in range(third_y):
            message_ref[m] = part_ref[m] + jnp.where(at_edge, across[m : m + 1], 0.0)
        for i in range(third_y, message_ref.shape[0]):
            message_ref[i] = part_ref[i]
        far_ref[pl.ds(0, third_y + 1)] = message_ref[pl.ds(0, third_y + 1)]
        far_ref[pl.ds(third_y + 1, WEIGHTS)] = coef_ref[pl.ds(0, WEIGHTS)]
        side_ref[...] = jnp.zeros_like(side_ref)


def blend_kernel(
    levels,
    western,
    west_ref,
    weight_ref,
    field_ref,
    window_ref,
    beside_ref,
    middle_ref,
    other_ref,
    coef_middle_ref,
    coef_near_ref,
    rows_ref,
):
    pieces, size, _ = field_ref.shape
    height = size // levels
    third_y = height // 3
    slots = third_y + 2
    tile_count = lax.axis_size("tiles")
    tile, row, _ = place()
    nest = tile == tile_count - 1

    @pl.when(nest)
    def _():
        store_slabs(rows_ref, 0, load_line(field_ref, levels, inner_line(height, row)))
        for i in range(pieces, rows_ref.shape[0]):
            rows_ref[i] = jnp.zeros((levels, LANES), jnp.float32)

    @pl.when(jnp.logical_not(nest))
    def _():
        paired = (tile == 1) | (tile == (0 if western else 2))

        def mine(i):
            return jnp.where(tile == 1, middle_ref[i], other_ref[i])

        def coefficient(i):
            other = other_ref[third_y + 1 + i] if western else coef_near_ref[i]
            return jnp.where(tile == 1, coef_middle_ref[i], other)

        breadth = pieces * LANES
        partner_east = tile == (0 if western else 1)
        slot = jnp.where(partner_east, (tile + 1) * breadth, tile * breadth - 1) - west_ref[1]
        column = jnp.where(partner_east, beside_ref[...], pltpu.roll(beside_ref[...], LANES - EAST_LANE, 1))
        lane = iota((levels, LANES), 1)

        def whole(s):
            return jnp.where(paired & (lane == slot), column[:, s : s + 1], window_ref[s])

        level = iota((levels, LANES), 0)
        weight = jnp.zeros((levels, LANES), jnp.float32)
        for l in range(levels):
            weight = jnp.where(level == l, weight_ref[l], weight)
        extra = window_ref[slots]
        extra = jnp.where(paired & (slot == -1) & (lane < EAST_LANE), column, extra)
        east_column = pltpu.roll(column, EAST_LANE, 1)
        extra = jnp.where(paired & (slot == LANES) & (lane >= EAST_LANE), east_column, extra)
        at_first, at_last = lane == 0, lane == LANES - 1
        lines = []
        for s in range(slots):
            x = whole(s)
            west = jnp.where(at_first, extra[:, s : s + 1], pltpu.roll(x, 1, 1))
            last = EAST_LANE + s
            east = jnp.where(at_last, extra[:, last : last + 1], pltpu.roll(x, LANES - 1, 1))
            lines.append((west, x, east))
        edges = coefficient(WEIGHTS - 1)
        ghosts = [coefficient(q) for q in range(3)]

        def outward(side, q):
            near = lines[1] if side == 0 else lines[slots - 2]
            far = lines[0] if side == 0 else lines[slots - 1]
            return (2.0 / 3.0) * far[q] + (1.0 / 3.0) * near[q]

        def sideward(s):
            west, x, east = lines[s]
            return (2.0 / 3.0) * jnp.where(at_first, west, east) + (1.0 / 3.0) * x

        sidewards = [sideward(s) for s in range(slots)]
        columns = [w + 7.0 * x + e for w, x, e in lines]
        for m in range(third_y):
            x = lines[m + 1][1]
            value = mine(m) + (NUDGING / 81.0) * (columns[m] + 7.0 * columns[m + 1] + columns[m + 2])
            for q in range(3):
                lane_of = 8 * m + q
                first, last = edges[:, lane_of : lane_of + 1], edges[:, lane_of + 3 : lane_of + 4]
                scale = jnp.where(at_first, first, jnp.where(at_last, last, 0.0))
                value = value + scale * sidewards[m + q]
            for side, at in ((0, 0), (1, third_y - 1)):
                if m == at:
                    for q in range(3):
                        value = value + jnp.where(row == side, ghosts[q], 0.0) * outward(side, q)
            rows_ref[m] = x + weight * (value - x)
        rows_ref[third_y] = weight * mine(third_y)


def later_kernel(
    levels,
    west_ref,
    south_ref,
    field_ref,
    east_ref,
    north_ref,
    level_ref,
    middle_ref,
    other_ref,
    parent_ref,
    blend_ref,
    out_ref,
    fine_ref,
    side_ref,
    northern_ref,
    southern_ref,
):
    height, breadth = level_ref.shape
    third_y = height // 3
    slots = third_y + 2
    tile, row, lev = place()
    nest = tile == lax.axis_size("tiles") - 1

    @pl.when(nest)
    def _():
        slabs = [middle_ref[s] + other_ref[s] for s in range(slots + 1)]
        cells, ring = refine(slabs[:slots], slabs[slots], height, breadth, row)
        fine_ref[...] = cells[:, :breadth]
        side_ref[...] = cells[:, breadth:]
        zero = jnp.zeros_like(ring)
        northern_ref[...] = jnp.where(row == 0, ring, zero)
        southern_ref[...] = jnp.where(row == 0, zero, ring)
        full_step(
            out_ref,
            field_ref,
            east_ref,
            north_ref,
            level_ref,
            levels,
            lev,
            True,
            northern_ref,
            southern_ref,
            side_ref,
            fine_ref,
        )

    @pl.when(jnp.logical_not(nest))
    def _():
        out_ref[...] = parent_ref[...]
        start = west_ref[1] - tile * breadth
        top = south_ref[1] + row * third_y - row * height
        for m in range(third_y):
            place_row(out_ref, levels, top + m, start, blend_ref[m])


def last_kernel(
    levels, west_ref, south_ref, given_ref, speeds_ref, blend_ref, rows_ref, out_hbm, out_ref, sems
):
    pieces, size, _ = out_ref.shape
    breadth = pieces * LANES
    height = size // levels
    third_y = height // 3
    tile, row, _ = place()
    nest = tile == lax.axis_size("tiles") - 1

    @pl.when(nest)
    def _():
        inner = inner_line(height, row)
        halo = ghost_weight(join_slabs(speeds_ref, pieces, pieces), row == 1) * join_slabs(rows_ref, 0, pieces)
        store_line(out_ref, levels, inner, load_line(out_ref, levels, inner) + halo)

    @pl.when(jnp.logical_not(nest))
    def _():
        start = west_ref[1] - tile * breadth
        top = south_ref[1] + (1 - row) * third_y - row * height
        for m in range(third_y):
            value = rows_ref[m]
            if m == 0:
                value = value + jnp.where(row == 0, blend_ref[third_y], 0.0)
            if m == third_y - 1:
                value = value + jnp.where(row == 1, blend_ref[third_y], 0.0)
            place_row(out_ref, levels, top + m, start, value)
        near = jnp.where(row == 0, third_y - 1, 0)
        line = south_ref[1] + row * third_y - row * height + near
        place_row(out_ref, levels, line, start, blend_ref[near] + rows_ref[third_y])

    copies = [
        pltpu.make_async_copy(out_ref.at[c], out_hbm.at[:, pl.ds(c * LANES, LANES)], sems.at[c])
        for c in range(pieces)
    ]
    for copy in copies:
        copy.start()
    for copy in copies:
        copy.wait()


def call(kernel, outs, inputs, places, scratch=(), flops=0, aliases=()):
    spaces = {"s": pltpu.SMEM, "v": pltpu.VMEM, "h": pltpu.HBM}
    outs = [pltpu.VMEM(out, jnp.float32) if isinstance(out, tuple) else out for out in outs]
    moved = sum(4 * math.prod(out.shape) for out in outs) + sum(array.nbytes for array in inputs)
    inputs = [
        array if p == "v" else pltpu.with_memory_space_constraint(array, spaces[p])
        for array, p in zip(inputs, places)
    ]
    return pl.pallas_call(
        kernel,
        out_shape=outs,
        in_specs=[pl.BlockSpec(memory_space=spaces[p]) for p in places],
        out_specs=[pl.BlockSpec(memory_space=out.memory_space) for out in outs],
        scratch_shapes=[pltpu.VMEM(s, jnp.float32) if isinstance(s, tuple) else s for s in scratch],
        input_output_aliases=dict(aliases),
        compiler_params=pltpu.CompilerParams(vmem_limit_bytes=32 * 1024 * 1024),
        cost_estimate=pl.CostEstimate(flops=flops, bytes_accessed=moved, transcendentals=0),
    )(*inputs)


def per_device_paired(air_state, wind_east, wind_north, feedback_weight, nest_west, nest_south):
    levels, height, breadth = air_state.shape
    third_y = height // 3
    pieces = breadth // LANES
    slots = third_y + 2
    tile_count = lax.axis_size("tiles")
    size = levels * height
    flat = (size, breadth)
    chunked = (pieces, size, LANES)
    air, east, north = (array.reshape(flat) for array in (air_state, wind_east, wind_north))
    swap = [(0, 1), (1, 0)]

    def slabs(count):
        return (count, levels, LANES)

    def kernel(body):
        return functools.partial(body, levels)

    rows, air_pieces, west, south, weight = call(
        kernel(pack_kernel),
        [
            slabs(slots + 1 + pieces),
            chunked,
            pltpu.SMEM((2,), jnp.int32),
            pltpu.SMEM((2,), jnp.int32),
            pltpu.SMEM((levels,), jnp.float32),
        ],
        [nest_west, nest_south, feedback_weight, air, north],
        "hhhhh",
        [chunked, pltpu.SemaphoreType.DMA((2 * pieces + 3,))],
    )
    own, level, speeds, edges = call(
        kernel(own_kernel),
        [slabs(slots + 1), (height, breadth), slabs(2 * pieces), slabs(slots + 2)],
        [west, south, air_pieces, east, north],
        "ssvvv",
        flops=30 * size * breadth,
    )
    rows = lax.ppermute(rows, "rows", swap)
    level = lax.ppermute(level, "lev", swap)
    where = [(t, r, l) for t in range(tile_count) for r in range(2) for l in range(2)]
    at = {position: i for i, position in enumerate(where)}

    def over_tiles(message, step, *without):
        pairs = []
        for t, r, l in where:
            idle = t in without or (t ^ step) in without
            pairs.append((at[t, r, l], at[(t, r, 1 - l) if idle else (t ^ step, r, l)]))
        return lax.ppermute(message, ("tiles", "rows", "lev"), pairs)

    halo = over_tiles(edges, 3, 0)
    eastern = nest_west[1] > breadth
    rows, eastern = lax.optimization_barrier((rows, eastern))
    window = own + rows[: slots + 1]
    own_0 = own
    around = [(t, (t - 1) % tile_count) for t in range(tile_count)]
    starting = [
        over_tiles(window, 1),
        over_tiles(window, 2, 0),
        lax.ppermute(window, "tiles", around),
    ]
    sides = [(size, LANES), (levels, breadth), (levels, breadth)]
    (early,) = call(
        kernel(early_kernel),
        [chunked],
        [air, east, north, rows, level],
        "vvvvv",
        sides[1:],
        flops=30 * size * breadth,
    )
    early, other = call(
        kernel(middle_kernel),
        [chunked, slabs(slots + 1)],
        [west, south, east, halo, starting[0], early],
        "ssvvvv",
        flops=10 * size * breadth,
        aliases=[(5, 0)],
    )
    other = lax.ppermute(other, "rows", swap)
    first, edge, own = call(
        kernel(first_kernel),
        [chunked, (height, breadth), slabs(slots + 1)],
        [west, south, early, east, speeds, starting[2], starting[0], starting[1]],
        "ssvvvvvv",
        flops=10 * size * breadth,
    )
    level = lax.ppermute(edge, "lev", swap)
    (part,) = call(
        kernel(average_kernel),
        [slabs(slots + 1)],
        [first, east, north, rows],
        "vvvv",
        [flat, (height, breadth)],
        flops=30 * size * breadth,
    )
    message, far_message, side_message = call(
        kernel(message_kernel),
        [slabs(slots + 1), slabs(third_y + 1 + WEIGHTS), (levels, LANES)],
        [west, level, part, own_0, own, other],
        "svvvvv",
    )
    def finish(western, arrays):
        west, south, weight, first, east, north, level, message, far_message, side_message, early, speeds, coefs = arrays
        if western:
            other, beside = over_tiles(far_message, 3, 1), over_tiles(side_message, 1, 3)
        else:
            other, beside = over_tiles(message, 1, 0), over_tiles(side_message, 3, 0)
        middle = over_tiles(message, 2, 0)
        (blend,) = call(
            functools.partial(blend_kernel, levels, western),
            [slabs(third_y + 1)],
            [west, weight, first, message, beside, middle, other, *coefs],
            "ss" + "v" * 7,
        )
        rows = lax.ppermute(blend, "rows", swap)
        (later,) = call(
            kernel(later_kernel),
            [chunked],
            [west, south, first, east, north, level, middle, other, early, blend],
            "ss" + "v" * 8,
            [flat, *sides],
            flops=30 * size * breadth,
        )
        out, _ = call(
            kernel(last_kernel),
            [pltpu.HBM(flat, jnp.float32), chunked],
            [west, south, later, speeds, blend, rows],
            "ssvvvv",
            [pltpu.SemaphoreType.DMA((pieces,))],
            aliases=[(2, 1)],
        )
        return out

    arrays = (west, south, weight, first, east, north, level, message, far_message, side_message, early, speeds)
    arrays += ((starting[1], starting[0]),)
    out = lax.cond(
        eastern,
        functools.partial(finish, False),
        functools.partial(finish, True),
        arrays,
    )
    return out.reshape(air_state.shape)


def solution(mesh):
    in_specs = (
        P(("members", "lev"), "rows", "tiles"),
        P(("members", "lev"), "rows", "tiles"),
        P(("members", "lev"), "rows", "tiles"),
        P("lev"),
        P("members"),
        P("members"),
    )
    out_specs = P(("members", "lev"), "rows", "tiles")
    paired = mesh.shape["tiles"] == 4 and mesh.shape["rows"] == 2 and mesh.shape["lev"] == 2
    return jax.shard_map(
        per_device_paired if paired else per_device, mesh=mesh, in_specs=in_specs, out_specs=out_specs, check_vma=False
    )
```
